128 devices in a mesh: dp: 8 (over x, core), fsdp: 16 (over z, y).
Axes of the slice: x: 4, y: 4, z: 4, core: 2. Of those that a mesh axis runs over, the one named last changes fastest.
Arguments:
- tokens: bfloat16 [65536, 1024], P(('dp', 'fsdp')), may hold values from -6 to 6
- cotangent: bfloat16 [65536, 1024], P(('dp', 'fsdp')), may hold values from -6 to 6
- lengths: int32 [128], P(('dp', 'fsdp')), may hold values from 85 to 512, as said below
- valid: int32 [65536], P(('dp', 'fsdp')), may hold values from 0 to 1, as said below
- owner_perm: int32 [96], replicated, may hold values from 0 to 95, each once
- w_qkv: float32 [1024, 3072], P(('dp', 'fsdp')), may hold values from -0.1875 to 0.1875
- w_out: float32 [1024, 1024], P(('dp', 'fsdp')), may hold values from -0.1875 to 0.1875
- w_up: float32 [1024, 4096], P(('dp', 'fsdp')), may hold values from -0.1875 to 0.1875
- w_down: float32 [1024, 4096], P(('dp', 'fsdp')), may hold values from -0.09375 to 0.09375
- vectors: float32 [22, 1024], P(None, ('dp', 'fsdp')), may hold values from -1.8 to 1.8
- head_scale: float32 [16], replicated, may hold values from 0.5 to 1.5
- left_stats: float32 [8, 96, 128, 128], P('dp', 'fsdp'), may hold values from 0 to 33554432, as said below
- right_stats: float32 [8, 96, 128, 128], P('dp', 'fsdp'), may hold values from 0 to 33554432, as said below
- left_roots: float32 [8, 96, 128, 128], P('dp', 'fsdp'), may hold values from -1 to 1, as said below
- right_roots: float32 [8, 96, 128, 128], P('dp', 'fsdp'), may hold values from -1 to 1, as said below
- vector_stats: float32 [22, 1024], P(None, ('dp', 'fsdp')), may hold values from 65536 to 262144
- head_stats: float32 [16], replicated, may hold values from 4194304 to 16777216
Outputs:
- output: bfloat16 [65536, 1024], P(('dp', 'fsdp'))
- input_grad: float32 [65536, 1024], P(('dp', 'fsdp'))
- grad_qkv: float32 [1024, 3072], P(('dp', 'fsdp'))
- grad_out: float32 [1024, 1024], P(('dp', 'fsdp'))
- grad_up: float32 [1024, 4096], P(('dp', 'fsdp'))
- grad_down: float32 [1024, 4096], P(('dp', 'fsdp'))
- vector_grads: float32 [22, 1024], P(None, ('dp', 'fsdp'))
- head_grads: float32 [16], replicated
- left_new: float32 [8, 96, 128, 128], P('dp', 'fsdp')
- right_new: float32 [8, 96, 128, 128], P('dp', 'fsdp')
- new_qkv: float32 [1024, 3072], P(('dp', 'fsdp'))
- new_out: float32 [1024, 1024], P(('dp', 'fsdp'))
- new_up: float32 [1024, 4096], P(('dp', 'fsdp'))
- new_down: float32 [1024, 4096], P(('dp', 'fsdp'))
- vector_stats_new: float32 [22, 1024], P(None, ('dp', 'fsdp'))
- vectors_new: float32 [22, 1024], P(None, ('dp', 'fsdp'))
- head_stats_new: float32 [16], replicated
- head_new: float32 [16], replicated
The draws below stay inside these ranges and needn't reach their ends.
Inputs may be any that keep to these rules, and one draw needn't show every extreme that they name: `lengths`: the last sequence's length is 512. `valid`: 0 at every position at or past its sequence's length. `owner_perm`: each column block once. `left_stats`: symmetric. `right_stats`: symmetric. `left_roots`: symmetric. `right_roots`: symmetric.
All inputs are finite; a program needn't handle non-finite values.
Results may differ from the reference program's by a relative error of at most 0.018.
Values may be sent and summed in bfloat16 or wider, within the bound.
No kernel may reach another device: no remote copies, remote signals or barrier semaphores. Data moves between devices by JAX's collectives and lax.ppermute only.
A program may use at most 256 MiB of HBM per device.

```python
import math
import jax
import jax.numpy as jnp
from jax import lax

D = 1024
FF = 4096
HEADS = 16
TOK_DEV = 512
TILE = 128
SEQS = 128
TOKENS = 65536
ROW_TILES = 8
COL_TILES = 96
VEC_ROWS = 22


def length_table(key):
    position = jnp.arange(SEQS, dtype=jnp.int32)
    floor_len = max(TOK_DEV // 6, 1)
    start = TOK_DEV // 4
    rising = start + (TOK_DEV - start) * position // max(SEQS - 1, 1)
    jitter = jax.random.randint(jax.random.fold_in(key, 3), (SEQS,), 0, TOK_DEV // 4 + 1)
    table = jnp.clip(rising - jitter, floor_len, TOK_DEV)
    return table.at[SEQS - 1].set(TOK_DEV).astype(jnp.int32)


def draw_lengths(key, part):
    return length_table(key)


def draw_valid(key, part):
    table = length_table(key)
    position = jnp.arange(TOK_DEV, dtype=jnp.int32)
    keeper = jax.random.randint(jax.random.fold_in(key, 7), (SEQS, TOK_DEV), 0, 20) >= 3
    inside = position[None, :] < table[:, None]
    return (inside & keeper).astype(jnp.int32).reshape(TOKENS)


def draw_vectors(key, part):
    row_index = jnp.arange(VEC_ROWS)[:, None]
    ratio_rows = FF // D
    is_gain = (row_index == 0) | (row_index == 4) | (row_index == 7) | (row_index >= 9 + ratio_rows) & (row_index < 9 + 2 * ratio_rows)
    first_key = jax.random.fold_in(key, 11)
    second_key = jax.random.fold_in(key, 12)
    gains = jax.random.uniform(first_key, (VEC_ROWS, D), jnp.float32, 0.6, 1.4)
    shifts = 0.3 * jnp.clip(jax.random.normal(second_key, (VEC_ROWS, D), jnp.float32), -6.0, 6.0)
    return jnp.where(is_gain, gains, shifts)


def identity_tile():
    index = jnp.arange(TILE)
    return (index[:, None] == index[None, :]).astype(jnp.float32)


def diagonal_stats(key):
    shape = (ROW_TILES, COL_TILES, TILE)
    diagonal = jnp.exp(jax.random.uniform(key, shape, jnp.float32, 0.0, math.log(4.0)))
    return TILE * TOKENS * diagonal[..., None] * identity_tile()


def root_matrix(key):
    scale_root = (2.0 * TILE * TOKENS) ** (-0.25)
    shape = (ROW_TILES, COL_TILES, TILE, TILE)
    diagonal = jax.random.uniform(jax.random.fold_in(key, 1), (ROW_TILES, COL_TILES, TILE), jnp.float32, 0.8, 1.2)
    noise = jnp.clip(jax.random.normal(jax.random.fold_in(key, 2), shape, jnp.float32), -6.0, 6.0)
    symmetric = (noise + jnp.swapaxes(noise, -1, -2)) * (0.35 / math.sqrt(2.0 * TILE))
    return scale_root * (diagonal[..., None] * identity_tile() + symmetric)


def draw_left_stats(key, part):
    return diagonal_stats(jax.random.fold_in(key, 21))


def draw_right_stats(key, part):
    return diagonal_stats(jax.random.fold_in(key, 22))


def draw_left_roots(key, part):
    return root_matrix(jax.random.fold_in(key, 23))


def draw_right_roots(key, part):
    return root_matrix(jax.random.fold_in(key, 24))


def block_levels(own_key, shape, cuts, least, high):
    level, own = 1.0, jax.random.fold_in(own_key, 6)
    for axis_at, parts in cuts:
        steps = jnp.exp(jax.random.uniform(jax.random.fold_in(own, axis_at), (parts,), jnp.float32, least / len(cuts), high / len(cuts)))
        level = level * jnp.repeat(steps, shape[axis_at] // parts).reshape([-1 if axis == axis_at else 1 for axis in range(len(shape))])
    return level


def scatter_about(stream_key, dims, spread, bound, shards=(), kind=jnp.bfloat16):
    values = spread * jax.random.normal(stream_key, dims, jnp.float32)
    if shards:
        values = values * block_levels(stream_key, dims, shards, -0.22, 0.18)
    return jnp.clip(values, -bound, bound).astype(kind)


def setup_inputs(seed: int = 0) -> dict:
    key_of = jax.random.split(jax.random.key(seed), 18)
    return {
        "tokens": scatter_about(key_of[0], (TOKENS, D), 1.0, 6.0, ((0, 128),)),
        "cotangent": scatter_about(key_of[1], (TOKENS, D), 1.0, 6.0, ((0, 128),)),
        "lengths": draw_lengths(jax.random.fold_in(key_of[17], 71), 0),
        "valid": draw_valid(jax.random.fold_in(key_of[17], 71), 0),
        "owner_perm": jax.random.permutation(key_of[4], COL_TILES).astype(jnp.int32),
        "w_qkv": scatter_about(key_of[5], (D, 3 * D), D ** -0.5, 0.1875, ((0, 128),), jnp.float32),
        "w_out": scatter_about(key_of[6], (D, D), D ** -0.5, 0.1875, ((0, 128),), jnp.float32),
        "w_up": scatter_about(key_of[7], (D, FF), D ** -0.5, 0.1875, ((0, 128),), jnp.float32),
        "w_down": scatter_about(key_of[8], (D, FF), FF ** -0.5, 0.09375, ((0, 128),), jnp.float32),
        "vectors": draw_vectors(jax.random.fold_in(key_of[17], 71), 0),
        "head_scale": jnp.clip(jax.random.uniform(key_of[10], (HEADS,), jnp.float32, 0.5, 1.5), 0.5, 1.5),
        "left_stats": draw_left_stats(jax.random.fold_in(key_of[17], 71), 0),
        "right_stats": draw_right_stats(jax.random.fold_in(key_of[17], 71), 0),
        "left_roots": draw_left_roots(jax.random.fold_in(key_of[17], 71), 0),
        "right_roots": draw_right_roots(jax.random.fold_in(key_of[17], 71), 0),
        "vector_stats": jnp.clip(jnp.exp(math.log(262144.0) - 1.3862944 * jax.random.uniform(key_of[15], (VEC_ROWS, D), jnp.float32) ** block_levels(key_of[15], (VEC_ROWS, D), ((1, 128),), -0.2, 0.2)), 65536.0, 262144.0),
        "head_stats": jnp.clip(jnp.exp(jax.random.uniform(key_of[16], (HEADS,), jnp.float32, math.log(4194304), math.log(16777216))), 4194304, 16777216),
    }


EPS = 1e-05
DECAY = 0.5
RATE_MATRIX = 0.1
RATE_VECTOR = 0.3
HIGHEST = lax.Precision.HIGHEST

@jax.custom_vjp
def low(v):
    return lax.optimization_barrier(v.astype(jnp.bfloat16)).astype(jnp.float32)

@jax.custom_vjp
def low_back(v):
    return v

def low_keep(v):
    return (low(v), None)

def low_pass(kept, grad):
    return (grad,)

def back_keep(v):
    return (v, None)

def back_low(kept, grad):
    return (low(grad),)
low.defvjp(low_keep, low_pass)
low_back.defvjp(back_keep, back_low)

def norm_rows(values, scale_row, shift_row):
    row_mean = lax.optimization_barrier(jnp.mean(values, axis=-1, keepdims=True))
    centered = values - row_mean
    variance = lax.optimization_barrier(jnp.mean(centered * centered, axis=-1, keepdims=True))
    return centered * lax.rsqrt(variance + EPS) * scale_row + shift_row

def layer_forward(tokens, w_qkv, w_out, w_up, w_down, vectors, head_scale, length):
    row_count, model_width = tokens.shape
    head_count = head_scale.shape[0]
    head_dim = model_width // head_count
    hidden_ratio = w_up.shape[1] // model_width
    up_bias = vectors[9:9 + hidden_ratio].reshape(-1)
    ffn_gain = vectors[9 + hidden_ratio:9 + 2 * hidden_ratio].reshape(-1)
    ffn_shift = vectors[9 + 2 * hidden_ratio:9 + 3 * hidden_ratio].reshape(-1)
    down_bias = vectors[9 + 3 * hidden_ratio]
    normed = low(norm_rows(tokens, vectors[0], vectors[1]))
    bias_full = jnp.concatenate([vectors[2], jnp.zeros((model_width,), jnp.float32), vectors[3]])
    projected = low(low_back(jnp.dot(normed, w_qkv, precision=HIGHEST) + bias_full))
    query_heads = projected[:, :model_width].reshape(row_count, head_count, head_dim)
    key_heads = projected[:, model_width:2 * model_width].reshape(row_count, head_count, head_dim)
    value_heads = projected[:, 2 * model_width:].reshape(row_count, head_count, head_dim)
    scores = low_back(jnp.einsum('qhd,khd->hqk', query_heads, key_heads, precision=HIGHEST) / math.sqrt(head_dim))
    position = jnp.arange(row_count)
    allowed = (position[None, :] <= position[:, None]) & (position[None, :] < length)
    masked = jnp.where(allowed[None], scores, -1e+30)
    largest = lax.optimization_barrier(jnp.max(masked, axis=-1, keepdims=True))
    exponent = jnp.exp(masked - largest)
    attention = low(exponent / lax.optimization_barrier(jnp.sum(exponent, axis=-1, keepdims=True)))
    mixed_heads = low_back(jnp.einsum('hqk,khd->qhd', attention, value_heads, precision=HIGHEST))
    scaled = low(mixed_heads * head_scale[None, :, None]).reshape(row_count, model_width)
    branch = low_back(jnp.dot(scaled, w_out, precision=HIGHEST) + vectors[6])
    attended = tokens + norm_rows(branch, vectors[4], vectors[5])
    normed_mid = low(norm_rows(attended, vectors[7], vectors[8]))
    hidden = low_back(jnp.dot(normed_mid, w_up, precision=HIGHEST) + up_bias)
    normed_top = low(norm_rows(jax.nn.gelu(hidden, approximate=False), ffn_gain, ffn_shift))
    return attended + jnp.dot(normed_top, w_down.T, precision=HIGHEST) + down_bias

def reference(tokens, cotangent, lengths, valid, owner_perm, w_qkv, w_out, w_up, w_down, vectors, head_scale, left_stats, right_stats, left_roots, right_roots, vector_stats, head_stats):
    model_width = tokens.shape[1]
    sequences = lengths.shape[0]
    params = (low(w_qkv), low(w_out), low(w_up), low(w_down), low(vectors), head_scale)
    seq_tokens = tokens.astype(jnp.float32).reshape(sequences, -1, model_width)
    upstream = (cotangent.astype(jnp.float32) * valid.astype(jnp.float32)[:, None]).reshape(sequences, -1, model_width)

    def one_sequence(totals, inputs):
        one_tokens, one_upstream, length = inputs

        def forward(token_rows, *weights):
            return layer_forward(token_rows, *weights, length)
        result, backward = jax.vjp(forward, one_tokens, *params)
        gradients = backward(one_upstream)
        totals = jax.tree.map(jnp.add, totals, tuple(gradients[1:]))
        return (totals, (result, gradients[0]))
    zeros = tuple((jnp.zeros(item.shape, jnp.float32) for item in params))
    totals, (results, input_rows) = lax.scan(one_sequence, zeros, (seq_tokens, upstream, lengths))
    grad_qkv, grad_out, grad_up, grad_down, vector_grads, head_grads = totals
    output = results.reshape(-1, model_width).astype(jnp.bfloat16)
    input_grad = input_rows.reshape(-1, model_width)
    column_grads = jnp.concatenate([grad_qkv, grad_out, grad_up, grad_down], axis=1)
    column_weights = jnp.concatenate([w_qkv, w_out, w_up, w_down], axis=1)

    def to_tiles(matrix):
        tiled = matrix.reshape(ROW_TILES, TILE, COL_TILES, TILE).transpose(0, 2, 1, 3)
        return jnp.take(tiled, owner_perm, axis=1)
    grad_tiles = to_tiles(column_grads)
    weight_tiles = to_tiles(column_weights)
    left_new = DECAY * left_stats + (1.0 - DECAY) * jnp.einsum('rsij,rskj->rsik', grad_tiles, grad_tiles, precision=HIGHEST)
    right_new = DECAY * right_stats + (1.0 - DECAY) * jnp.einsum('rsji,rsjk->rsik', grad_tiles, grad_tiles, precision=HIGHEST)
    right_side = jnp.einsum('rsij,rsjk->rsik', grad_tiles, right_roots, precision=HIGHEST)
    direction = jnp.einsum('rsij,rsjk->rsik', left_roots, right_side, precision=HIGHEST)
    new_tiles = weight_tiles - RATE_MATRIX * direction
    inverse = jnp.zeros((COL_TILES,), jnp.int32).at[owner_perm].set(jnp.arange(COL_TILES, dtype=jnp.int32))
    new_columns = jnp.take(new_tiles, inverse, axis=1).transpose(0, 2, 1, 3).reshape(model_width, -1)
    first_cut = 3 * model_width
    second_cut = first_cut + model_width
    third_cut = second_cut + w_up.shape[1]
    new_qkv = new_columns[:, :first_cut]
    new_out = new_columns[:, first_cut:second_cut]
    new_up = new_columns[:, second_cut:third_cut]
    new_down = new_columns[:, third_cut:]
    vector_stats_new = DECAY * vector_stats + (1.0 - DECAY) * vector_grads * vector_grads
    vectors_new = vectors - RATE_VECTOR * vector_grads * lax.rsqrt(vector_stats_new)
    head_stats_new = DECAY * head_stats + (1.0 - DECAY) * head_grads * head_grads
    head_new = head_scale - RATE_VECTOR * head_grads * lax.rsqrt(head_stats_new)
    return (output, input_grad, grad_qkv, grad_out, grad_up, grad_down, vector_grads, head_grads, left_new, right_new, new_qkv, new_out, new_up, new_down, vector_stats_new, vectors_new, head_stats_new, head_new)
```

```python
import math

import jax
import jax.numpy as jnp
from jax import lax
from jax.sharding import PartitionSpec as P

TILE = 128


EPS = 1e-05
DECAY = 0.5
RATE_MATRIX = 0.1
RATE_VECTOR = 0.3
HIGHEST = lax.Precision.HIGHEST


def norm_rows(values, scale_row, shift_row):
    row_mean = jnp.mean(values, axis=-1, keepdims=True)
    centered = values - row_mean
    variance = jnp.mean(centered * centered, axis=-1, keepdims=True)
    return centered * lax.rsqrt(variance + EPS) * scale_row + shift_row


def mlp_middle(hidden_in, gain_in, shift_in):
    return norm_rows(jax.nn.gelu(hidden_in, approximate=False), gain_in, shift_in)


def contract_last(left, right):
    return lax.dot_general(
        left, right, (((1,), (1,)), ((), ())), preferred_element_type=jnp.float32
    )


def contract_first(left, right):
    return lax.dot_general(
        left, right, (((0,), (0,)), ((), ())), preferred_element_type=jnp.float32
    )


def reduce_rows(left, right):
    tokens_here, rows = left.shape
    columns = right.shape[1]
    x_size, core_size = lax.axis_size("x"), lax.axis_size("core")
    plane = lax.axis_size("fsdp")
    me = lax.axis_index("core")
    by_core = left.reshape(tokens_here, x_size, core_size, -1)

    def rows_of(core):
        return lax.dynamic_index_in_dim(by_core, core, axis=2, keepdims=False).reshape(
            tokens_here, rows // core_size
        )

    sent = contract_first(rows_of(1 - me), right).astype(jnp.bfloat16)
    swapped = lax.ppermute(sent, "core", [(0, 1), (1, 0)])
    kept = (contract_first(rows_of(me), right) + swapped.astype(jnp.float32)).astype(jnp.bfloat16)
    half = columns // 2
    shard = rows // (x_size * core_size * plane)
    first = lax.psum_scatter(kept[:, :half], "x", scatter_dimension=0, tiled=True)
    first = lax.all_to_all(
        first.reshape(plane, shard, half), "fsdp", split_axis=0, concat_axis=0, tiled=True
    )
    first = jnp.sum(first.astype(jnp.float32), axis=0)
    second = kept[:, half:].reshape(x_size, plane, shard, columns - half).transpose(1, 0, 2, 3)
    second = lax.all_to_all(second, "fsdp", split_axis=0, concat_axis=0, tiled=True)
    second = jnp.sum(second.astype(jnp.float32), axis=0)
    second = lax.psum_scatter(
        second.reshape(x_size * shard, columns - half), "x", scatter_dimension=0, tiled=True
    )
    return jnp.concatenate([first, second], axis=1)


def owner_update(grad_owned, left_stats, right_stats, left_roots, right_roots):
    group_rows = grad_owned.shape[0]
    own_slots = grad_owned.shape[1]

    def as_tiles(block_rows):
        return block_rows.reshape(group_rows // TILE, TILE, own_slots, TILE).transpose(0, 2, 1, 3)

    grad_tiles = as_tiles(grad_owned)
    left_new = DECAY * left_stats + (1.0 - DECAY) * jnp.einsum(
        "rsij,rskj->rsik", grad_tiles, grad_tiles, precision=HIGHEST
    )
    right_new = DECAY * right_stats + (1.0 - DECAY) * jnp.einsum(
        "rsji,rsjk->rsik", grad_tiles, grad_tiles, precision=HIGHEST
    )
    right_side = jnp.einsum("rsij,rsjk->rsik", grad_tiles, right_roots, precision=HIGHEST)
    direction = jnp.einsum("rsij,rsjk->rsik", left_roots, right_side, precision=HIGHEST)
    direction = direction.transpose(0, 2, 1, 3).reshape(group_rows, own_slots, TILE)
    return (left_new, right_new, direction)


def shards(
    tokens,
    cotangent,
    lengths,
    valid,
    owner_perm,
    w_qkv,
    w_out,
    w_up,
    w_down,
    vectors,
    head_scale,
    left_stats,
    right_stats,
    left_roots,
    right_roots,
    vector_stats,
    head_stats,
):
    row_count, model_width = tokens.shape
    head_count = head_scale.shape[0]
    head_dim = model_width // head_count
    hidden_ratio = w_up.shape[1] // model_width
    root_dim = math.sqrt(head_dim)
    low_first = jnp.concatenate(
        [
            w_qkv.astype(jnp.bfloat16),
            w_out.astype(jnp.bfloat16),
            jnp.pad(vectors.astype(jnp.bfloat16).T, ((0, 0), (0, TILE - vectors.shape[0]))),
        ],
        axis=1,
    )
    qkv_cols = w_qkv.shape[1]
    out_cols = qkv_cols + w_out.shape[1]
    gathered_first = lax.all_gather(low_first, ("x", "core", "fsdp"), axis=0, tiled=True)
    gathered_qkv = gathered_first[:, :qkv_cols]
    gathered_out = gathered_first[:, qkv_cols:out_cols]
    gathered_vectors = gathered_first[:, out_cols : out_cols + vectors.shape[0]].T
    low_second = jnp.concatenate(
        [w_up.astype(jnp.bfloat16), w_down.astype(jnp.bfloat16)], axis=1
    )
    gathered_second = lax.all_gather(low_second, ("x", "core", "fsdp"), axis=0, tiled=True)
    gathered_up = gathered_second[:, : w_up.shape[1]]
    gathered_down = gathered_second[:, w_up.shape[1] :]
    vector_rows = gathered_vectors.astype(jnp.float32)
    up_bias = vector_rows[9 : 9 + hidden_ratio].reshape(-1)
    ffn_gain = vector_rows[9 + hidden_ratio : 9 + 2 * hidden_ratio].reshape(-1)
    ffn_shift = vector_rows[9 + 2 * hidden_ratio : 9 + 3 * hidden_ratio].reshape(-1)
    down_bias = vector_rows[9 + 3 * hidden_ratio]
    inputs = tokens.astype(jnp.float32)
    normed, first_back = jax.vjp(norm_rows, inputs, vector_rows[0], vector_rows[1])
    normed_low = normed.astype(jnp.bfloat16)
    bias_full = jnp.concatenate(
        [vector_rows[2], jnp.zeros((model_width,), jnp.float32), vector_rows[3]]
    )
    projected = (
        jnp.dot(normed_low, gathered_qkv, preferred_element_type=jnp.float32) + bias_full
    ).astype(jnp.bfloat16)
    query_heads = projected[:, :model_width].reshape(row_count, head_count, head_dim)
    key_heads = projected[:, model_width : 2 * model_width].reshape(row_count, head_count, head_dim)
    value_heads = projected[:, 2 * model_width :].reshape(row_count, head_count, head_dim)
    position = jnp.arange(row_count)
    allowed = (position[None, :] <= position[:, None]) & (position[None, :] < lengths[0])

    def masked_softmax(score_block):
        masked = jnp.where(allowed[None], score_block, -1e30)
        largest = jnp.max(masked, axis=-1, keepdims=True)
        exponent = jnp.exp(masked - largest)
        return exponent / jnp.sum(exponent, axis=-1, keepdims=True)

    scores = (
        jnp.einsum("qhd,khd->hqk", query_heads, key_heads, preferred_element_type=jnp.float32)
        / root_dim
    )
    attention, softmax_back = jax.vjp(masked_softmax, scores)
    attention_low = attention.astype(jnp.bfloat16)
    mixed_heads = jnp.einsum(
        "hqk,khd->qhd", attention_low, value_heads, preferred_element_type=jnp.float32
    )
    scaled_low = (
        (mixed_heads * head_scale[None, :, None])
        .astype(jnp.bfloat16)
        .reshape(row_count, model_width)
    )
    branch = jnp.dot(scaled_low, gathered_out, preferred_element_type=jnp.float32) + vector_rows[6]
    post_norm, post_back = jax.vjp(norm_rows, branch, vector_rows[4], vector_rows[5])
    attended = inputs + post_norm
    normed_mid, middle_back = jax.vjp(norm_rows, attended, vector_rows[7], vector_rows[8])
    normed_mid_low = normed_mid.astype(jnp.bfloat16)
    hidden = jnp.dot(normed_mid_low, gathered_up, preferred_element_type=jnp.float32) + up_bias
    normed_top, upper_back = jax.vjp(mlp_middle, hidden, ffn_gain, ffn_shift)
    normed_top_low = normed_top.astype(jnp.bfloat16)
    output = (attended + contract_last(normed_top_low, gathered_down) + down_bias).astype(
        jnp.bfloat16
    )
    upstream = cotangent.astype(jnp.float32) * valid.astype(jnp.float32)[:, None]
    upstream_low = upstream.astype(jnp.bfloat16)
    summed_down = reduce_rows(upstream_low, normed_top_low)
    grad_top = jnp.dot(upstream_low, gathered_down, preferred_element_type=jnp.float32)
    grad_hidden, grad_ffn_gain, grad_ffn_shift = upper_back(grad_top)
    grad_hidden_low = grad_hidden.astype(jnp.bfloat16)
    summed_up = reduce_rows(normed_mid_low, grad_hidden_low)
    grad_mid = contract_last(grad_hidden_low, gathered_up)
    grad_from_mid, grad_mid_gain, grad_mid_shift = middle_back(grad_mid)
    grad_attended = upstream + grad_from_mid
    mlp_vector_grads = jnp.concatenate(
        [
            grad_mid_gain[None],
            grad_mid_shift[None],
            jnp.sum(grad_hidden_low.astype(jnp.float32), axis=0).reshape(hidden_ratio, model_width),
            grad_ffn_gain.reshape(hidden_ratio, model_width),
            grad_ffn_shift.reshape(hidden_ratio, model_width),
            jnp.sum(upstream, axis=0)[None],
        ],
        axis=0,
    )
    grad_branch, grad_post_gain, grad_post_shift = post_back(grad_attended)
    grad_branch_low = grad_branch.astype(jnp.bfloat16)
    summed_out = reduce_rows(scaled_low, grad_branch_low)
    grad_scaled = contract_last(grad_branch_low, gathered_out).reshape(row_count, head_count, head_dim)
    grad_head = jnp.sum(grad_scaled * mixed_heads, axis=(0, 2))
    grad_mixed_low = (grad_scaled * head_scale[None, :, None]).astype(jnp.bfloat16)
    grad_attention = jnp.einsum(
        "qhd,khd->hqk", grad_mixed_low, value_heads, preferred_element_type=jnp.float32
    )
    grad_value = jnp.einsum(
        "hqk,qhd->khd", attention_low, grad_mixed_low, preferred_element_type=jnp.float32
    )
    grad_scores_low = softmax_back(grad_attention)[0].astype(jnp.bfloat16)
    grad_query = (
        jnp.einsum("hqk,khd->qhd", grad_scores_low, key_heads, preferred_element_type=jnp.float32)
        / root_dim
    )
    grad_key = (
        jnp.einsum("hqk,qhd->khd", grad_scores_low, query_heads, preferred_element_type=jnp.float32)
        / root_dim
    )
    grad_projected_low = jnp.concatenate(
        [
            grad_query.reshape(row_count, model_width),
            grad_key.reshape(row_count, model_width),
            grad_value.reshape(row_count, model_width),
        ],
        axis=1,
    ).astype(jnp.bfloat16)
    summed_qkv = reduce_rows(normed_low, grad_projected_low)
    grad_normed = contract_last(grad_projected_low, gathered_qkv)
    grad_from_first, grad_first_gain, grad_first_shift = first_back(grad_normed)
    input_grad = grad_attended + grad_from_first
    projected_sums = jnp.sum(grad_projected_low.astype(jnp.float32), axis=0)
    attn_vector_grads = jnp.stack(
        [
            grad_first_gain,
            grad_first_shift,
            projected_sums[:model_width],
            projected_sums[2 * model_width :],
            grad_post_gain,
            grad_post_shift,
            jnp.sum(grad_branch_low.astype(jnp.float32), axis=0),
        ],
        axis=0,
    )
    vector_partials = jnp.concatenate([attn_vector_grads, mlp_vector_grads], axis=0)
    devices = model_width // vectors.shape[1]
    small = jnp.concatenate(
        [
            vector_partials.reshape(-1, devices, vectors.shape[1])
            .transpose(1, 0, 2)
            .reshape(devices, -1),
            jnp.broadcast_to(grad_head[None], (devices, head_count)),
        ],
        axis=1,
    )
    small = jnp.sum(
        lax.all_to_all(small, ("x", "core", "fsdp"), split_axis=0, concat_axis=0, tiled=True), axis=0
    )
    vector_grads = small[: vectors.size].reshape(vectors.shape)
    head_total = small[vectors.size :]
    column_weights = jnp.concatenate([w_qkv, w_out, w_up, w_down], axis=1)
    shard_rows = column_weights.shape[0]
    tile_count = column_weights.shape[1] // TILE
    inverse = (
        jnp.zeros((tile_count,), jnp.int32)
        .at[owner_perm]
        .set(jnp.arange(tile_count, dtype=jnp.int32))
    )
    column_grads = jnp.concatenate([summed_qkv, summed_out, summed_up, summed_down], axis=1)
    grad_slots = jnp.take(
        column_grads.astype(jnp.bfloat16).reshape(shard_rows, tile_count, TILE), owner_perm, axis=1
    )
    grad_owned = lax.all_to_all(
        grad_slots, "fsdp", split_axis=1, concat_axis=0, tiled=True
    ).astype(jnp.float32)
    left_new, right_new, direction = owner_update(
        grad_owned, left_stats, right_stats, left_roots, right_roots
    )
    returned = lax.all_to_all(
        direction.astype(jnp.bfloat16), "fsdp", split_axis=0, concat_axis=1, tiled=True
    )
    vector_stats_new = DECAY * vector_stats + (1.0 - DECAY) * vector_grads * vector_grads
    vectors_new = vectors - RATE_VECTOR * vector_grads * lax.rsqrt(vector_stats_new)
    head_stats_new = DECAY * head_stats + (1.0 - DECAY) * head_total * head_total
    head_new = head_scale - RATE_VECTOR * head_total * lax.rsqrt(head_stats_new)
    steps = jnp.take(returned, inverse, axis=1).reshape(shard_rows, -1).astype(jnp.float32)
    new_columns = column_weights - RATE_MATRIX * steps
    first_cut = w_qkv.shape[1]
    second_cut = first_cut + w_out.shape[1]
    third_cut = second_cut + w_up.shape[1]
    new_qkv = new_columns[:, :first_cut]
    new_out = new_columns[:, first_cut:second_cut]
    new_up = new_columns[:, second_cut:third_cut]
    new_down = new_columns[:, third_cut:]
    return (
        output,
        input_grad,
        summed_qkv,
        summed_out,
        summed_up,
        summed_down,
        vector_grads,
        head_total,
        left_new,
        right_new,
        new_qkv,
        new_out,
        new_up,
        new_down,
        vector_stats_new,
        vectors_new,
        head_stats_new,
        head_new,
    )


def solution(mesh):
    placed = (
        P(("x", "core", "fsdp"), None),
        P(("x", "core", "fsdp"), None),
        P(("x", "core", "fsdp")),
        P(("x", "core", "fsdp")),
        P(),
        P(("x", "core", "fsdp"), None),
        P(("x", "core", "fsdp"), None),
        P(("x", "core", "fsdp"), None),
        P(("x", "core", "fsdp"), None),
        P(None, ("x", "core", "fsdp")),
        P(),
        P(("x", "core"), "fsdp", None, None),
        P(("x", "core"), "fsdp", None, None),
        P(("x", "core"), "fsdp", None, None),
        P(("x", "core"), "fsdp", None, None),
        P(None, ("x", "core", "fsdp")),
        P(),
    )
    dp, fsdp = mesh.devices.shape
    mesh = jax.sharding.Mesh(mesh.devices.reshape(dp // 2, 2, fsdp), ("x", "core", "fsdp"))
    return jax.shard_map(
        shards,
        mesh=mesh,
        in_specs=placed,
        out_specs=(
            P(("x", "core", "fsdp"), None),
            P(("x", "core", "fsdp"), None),
            P(("x", "core", "fsdp"), None),
            P(("x", "core", "fsdp"), None),
            P(("x", "core", "fsdp"), None),
            P(("x", "core", "fsdp"), None),
            P(None, ("x", "core", "fsdp")),
            P(),
            P(("x", "core"), "fsdp", None, None),
            P(("x", "core"), "fsdp", None, None),
            P(("x", "core", "fsdp"), None),
            P(("x", "core", "fsdp"), None),
            P(("x", "core", "fsdp"), None),
            P(("x", "core", "fsdp"), None),
            P(None, ("x", "core", "fsdp")),
            P(None, ("x", "core", "fsdp")),
            P(),
            P(),
        ),
        check_vma=False,
    )
```

```python
import functools
import math

import jax
import jax.numpy as jnp
from jax import lax
from jax.experimental import pallas as pl
from jax.experimental.pallas import tpu as pltpu
from jax.sharding import PartitionSpec as P

TILE = 128
EPS = 1e-05
DECAY = 0.5
RATE_MATRIX = 0.1
RATE_VECTOR = 0.3
HIGHEST = lax.Precision.HIGHEST
HEAD_AT = 24
VMEM_BYTES = 56 * 1024 * 1024
F32 = jnp.float32
BF16 = jnp.bfloat16


def dot_nn(left, right):
    return lax.dot_general(left, right, (((1,), (0,)), ((), ())), preferred_element_type=F32)


def dot_nt(left, right):
    return lax.dot_general(left, right, (((1,), (1,)), ((), ())), preferred_element_type=F32)


def dot_tn(left, right):
    return lax.dot_general(left, right, (((0,), (0,)), ((), ())), preferred_element_type=F32)


def row_stats(values):
    mean = jnp.mean(values, axis=-1, keepdims=True)
    centered = values - mean
    spread = lax.rsqrt(jnp.mean(centered * centered, axis=-1, keepdims=True) + EPS)
    return centered, spread


def norm_back(scaled_grad, unit, spread):
    mean_grad = jnp.mean(scaled_grad, axis=-1, keepdims=True)
    mean_both = jnp.mean(scaled_grad * unit, axis=-1, keepdims=True)
    return spread * (scaled_grad - mean_grad - unit * mean_both)


def lane_sum(values):
    total = values[:, :TILE]
    for at in range(TILE, values.shape[1], TILE):
        total = total + values[:, at : at + TILE]
    return total


def call(body, grid, in_specs, out_specs, out_shape, scratch=(), flops=0, bytes_accessed=0, scalars=0):
    return pl.pallas_call(
        body,
        out_shape=out_shape,
        grid_spec=pltpu.PrefetchScalarGridSpec(
            num_scalar_prefetch=scalars,
            grid=grid,
            in_specs=in_specs,
            out_specs=out_specs,
            scratch_shapes=list(scratch),
        ),
        compiler_params=pltpu.CompilerParams(vmem_limit_bytes=VMEM_BYTES),
        cost_estimate=pl.CostEstimate(
            flops=flops, bytes_accessed=bytes_accessed, transcendentals=0
        ),
    )


def whole(shape):
    return pl.BlockSpec(shape, lambda *_: (0,) * len(shape))


def after(*arrays):
    return [pl.BlockSpec(memory_space=pl.ANY) for _ in arrays]


def split_parity(values):
    blocks = [values[:, at : at + TILE] for at in range(0, values.shape[1], TILE)]
    return jnp.concatenate(blocks[0::2], axis=1), jnp.concatenate(blocks[1::2], axis=1)


def join_parity(even, odd):
    blocks = []
    for at in range(0, even.shape[1], TILE):
        blocks += [even[:, at : at + TILE], odd[:, at : at + TILE]]
    return jnp.concatenate(blocks, axis=1)


def project_body(
    core, tokens, vectors, own_qk, other_qk, own_vo, other_vo, normed, projected, parts
):
    part = pl.program_id(0)

    @pl.when(part == 0)
    def _():
        centered, spread = row_stats(tokens[...].astype(F32))
        low = (centered * spread * vectors[0:1, :] + vectors[1:2, :]).astype(BF16)
        normed[...] = low
        parts[0], parts[1] = split_parity(low)

    gate_q = jnp.where(part == 0, 1.0, 0.0).astype(F32)
    gate_v = jnp.where(part == 2, 1.0, 0.0).astype(F32)
    bias = gate_q * vectors[2:3, :] + gate_v * vectors[3:4, :]
    me = core[0]

    @pl.when(part < 2)
    def _():
        projected[...] = (
            dot_nn(parts[me], own_qk[...]) + dot_nn(parts[1 - me], other_qk[...]) + bias
        ).astype(BF16)

    @pl.when(part == 2)
    def _():
        projected[...] = (
            dot_nn(parts[me], own_vo[...]) + dot_nn(parts[1 - me], other_vo[...]) + bias
        ).astype(BF16)


def project(core, tokens, vectors, weights):
    rows, width = tokens.shape
    parts = 3
    third = pl.BlockSpec((width // 2, width), lambda part, *_: (0, jnp.minimum(part, 1)))
    last = pl.BlockSpec((width // 2, width), lambda part, *_: (0, 0))
    return call(
        project_body,
        (parts,),
        [whole((rows, width)), whole(vectors.shape), third, third, last, last],
        [whole((rows, width)), pl.BlockSpec((rows, width), lambda part, *_: (0, part))],
        [
            jax.ShapeDtypeStruct((rows, width), BF16),
            jax.ShapeDtypeStruct((rows, parts * width), BF16),
        ],
        scratch=[pltpu.VMEM((2, rows, width // 2), BF16)],
        flops=2 * rows * width * width * parts,
        bytes_accessed=2 * width * width * parts,
        scalars=1,
    )(core, tokens, vectors, *weights)


def attend_body(length, scales, queries, keys, values, mixed, scaled, weights):
    rows = queries.shape[0]
    head_dim = TILE // 2
    pair = pl.program_id(0)
    block = rows // 2
    lane = lax.broadcasted_iota(jnp.int32, (rows, TILE), 1)
    spot = lax.broadcasted_iota(jnp.int32, (rows, TILE), 0)
    hidden_key = jnp.where(spot < length[0], 0.0, -1e30).astype(BF16)
    one = jnp.ones((rows, TILE), BF16)
    zero = jnp.zeros((rows, TILE), BF16)
    query = queries[...] * jnp.asarray(1.0 / math.sqrt(head_dim), BF16)
    key = keys[...]
    value = values[...]
    causal = lax.broadcasted_iota(jnp.int32, (block, block), 1) <= lax.broadcasted_iota(
        jnp.int32, (block, block), 0
    )
    total = [jnp.zeros((block, TILE), F32) for _ in range(2)]
    for head in range(2):
        mine = (lane < head_dim) if head == 0 else (lane >= head_dim)
        spare = lane == (head_dim if head == 0 else 0)
        query_one = jnp.where(mine, query, jnp.where(spare, one, zero))
        key_one = jnp.where(mine, key, jnp.where(spare, hidden_key, zero))
        value_one = jnp.where(mine, value, zero)
        for part in range(2):
            seen = (part + 1) * block
            score = dot_nt(query_one[part * block : seen], key_one[:seen])
            last = jnp.where(causal, score[:, part * block :], -1e30)
            score = last if part == 0 else jnp.concatenate([score[:, :block], last], axis=1)
            top = jnp.max(score, axis=1, keepdims=True)
            grown = jnp.exp(score - top)
            share = (grown * (1.0 / jnp.sum(grown, axis=1, keepdims=True))).astype(BF16)
            if part == 0:
                weights[head, :, :block] = share
            else:
                weights[head, :, block:] = share
            total[part] = total[part] + dot_nn(share, value_one[:seen])
    scale_row = jnp.where(
        lax.broadcasted_iota(jnp.int32, (1, TILE), 1) < head_dim,
        scales[2 * pair],
        scales[2 * pair + 1],
    )
    for part in range(2):
        mixed[part * block : (part + 1) * block, :] = total[part]
        scaled[part * block : (part + 1) * block, :] = (total[part] * scale_row).astype(BF16)


def attend(length, scales, projected):
    rows, width3 = projected.shape
    width = width3 // 3
    pairs = width // TILE
    block = rows // 2
    return call(
        attend_body,
        (pairs,),
        [
            pl.BlockSpec((rows, TILE), lambda pair, *_: (0, pair)),
            pl.BlockSpec((rows, TILE), lambda pair, *_: (0, pairs + pair)),
            pl.BlockSpec((rows, TILE), lambda pair, *_: (0, 2 * pairs + pair)),
        ],
        [
            pl.BlockSpec((rows, TILE), lambda pair, *_: (0, pair)),
            pl.BlockSpec((rows, TILE), lambda pair, *_: (0, pair)),
            pl.BlockSpec((2, block, 3 * block), lambda pair, *_: (pair, 0, 0)),
        ],
        [
            jax.ShapeDtypeStruct((rows, width), F32),
            jax.ShapeDtypeStruct((rows, width), BF16),
            jax.ShapeDtypeStruct((2 * pairs, block, 3 * block), BF16),
        ],
        flops=4 * rows * rows * width,
        bytes_accessed=20 * rows * width,
        scalars=2,
    )(length, scales, projected, projected, projected)


def attend_back_body(queries, keys, values, mixed, grads, weights, _, out):
    rows = queries.shape[0]
    head_dim = TILE // 2
    block = rows // 2
    lane = lax.broadcasted_iota(jnp.int32, (rows, TILE), 1)
    zero = jnp.zeros((rows, TILE), BF16)
    query, key, value, grad = queries[...], keys[...], values[...], grads[...]
    both = grad.astype(F32) * mixed[...]
    q_total = [jnp.zeros((block, TILE), F32) for _ in range(2)]
    k_total = [jnp.zeros((block, TILE), F32) for _ in range(2)]
    v_total = [jnp.zeros((block, TILE), F32) for _ in range(2)]
    for head in range(2):
        mine = (lane < head_dim) if head == 0 else (lane >= head_dim)
        query_one = jnp.where(mine, query, zero)
        key_one = jnp.where(mine, key, zero)
        grad_one = jnp.where(mine, grad, zero)
        delta = jnp.sum(jnp.where(mine, both, 0.0), axis=1, keepdims=True)
        for part in range(2):
            at = part * block
            seen = at + block
            share = weights[head, :, :block] if part == 0 else weights[head, :, block:]
            into = dot_nt(grad_one[at:seen], value[:seen])
            slope = (share.astype(F32) * (into - delta[at:seen])).astype(BF16)
            q_total[part] = q_total[part] + dot_nn(slope, key_one[:seen])
            k_new = dot_tn(slope, query_one[at:seen])
            v_new = dot_tn(share, grad_one[at:seen])
            for into_part in range(part + 1):
                cut = slice(into_part * block, (into_part + 1) * block)
                k_total[into_part] = k_total[into_part] + k_new[cut]
                v_total[into_part] = v_total[into_part] + v_new[cut]
    root = 1.0 / math.sqrt(head_dim)
    for part in range(2):
        cut = slice(part * block, (part + 1) * block)
        out[0, cut, :] = (q_total[part] * root).astype(BF16)
        out[1, cut, :] = (k_total[part] * root).astype(BF16)
        out[2, cut, :] = v_total[part].astype(BF16)


def attend_back(projected, mixed, grads, weights, wait):
    rows, width3 = projected.shape
    width = width3 // 3
    pairs = width // TILE
    block = rows // 2
    by_pair = pl.BlockSpec((rows, TILE), lambda pair, *_: (0, pair))
    return call(
        attend_back_body,
        (pairs,),
        [
            by_pair,
            pl.BlockSpec((rows, TILE), lambda pair, *_: (0, pairs + pair)),
            pl.BlockSpec((rows, TILE), lambda pair, *_: (0, 2 * pairs + pair)),
            by_pair,
            by_pair,
            pl.BlockSpec((2, block, 3 * block), lambda pair, *_: (pair, 0, 0)),
            *after(wait),
        ],
        pl.BlockSpec((3, rows, TILE), lambda pair, *_: (0, 0, pair)),
        jax.ShapeDtypeStruct((3, rows, width), BF16),
        flops=10 * rows * rows * width,
        bytes_accessed=24 * rows * width,
    )(projected, projected, projected, mixed, grads, weights, wait)


def branch_body(core, scaled, own, other, tokens, vectors, branch, attended, normed, parts):
    parts[0], parts[1] = split_parity(scaled[...])
    me = core[0]
    value = dot_nn(parts[me], own[...]) + dot_nn(parts[1 - me], other[...]) + vectors[6:7, :]
    branch[...] = value
    centered, spread = row_stats(value)
    total = tokens[...].astype(F32) + centered * spread * vectors[4:5, :] + vectors[5:6, :]
    attended[...] = total
    centered, spread = row_stats(total)
    normed[...] = (centered * spread * vectors[7:8, :] + vectors[8:9, :]).astype(BF16)


def branch_out(core, scaled, weights, tokens, vectors):
    rows, width = scaled.shape
    block = rows // 4
    by_row = pl.BlockSpec((block, width), lambda at, *_: (at, 0))
    fourth = pl.BlockSpec((width // 2, width), lambda at, *_: (0, 1))
    return call(
        branch_body,
        (rows // block,),
        [by_row, fourth, fourth, by_row, whole(vectors.shape)],
        [by_row, by_row, by_row],
        [
            jax.ShapeDtypeStruct((rows, width), F32),
            jax.ShapeDtypeStruct((rows, width), F32),
            jax.ShapeDtypeStruct((rows, width), BF16),
        ],
        scratch=[pltpu.VMEM((2, block, width // 2), BF16)],
        flops=2 * rows * width * width,
        bytes_accessed=2 * width * width + 14 * rows * width,
        scalars=1,
    )(core, scaled, *weights[2:], tokens, vectors)


def branch_back_body(
    core, grad_attended, branch, own, other, mixed, scales, vectors, _, grad_branch, grad_mixed, sums, parts
):
    @pl.when(pl.program_id(0) == 0)
    def _():
        sums[...] = jnp.zeros_like(sums)

    grad = grad_attended[...]
    centered, spread = row_stats(branch[...])
    unit = centered * spread
    low = norm_back(grad * vectors[4:5, :], unit, spread).astype(BF16)
    grad_branch[...] = low
    me = core[0]
    parts[me] = dot_nt(low, own[...])
    parts[1 - me] = dot_nt(low, other[...])
    grad_scaled = join_parity(parts[0], parts[1])
    grad_mixed[...] = (grad_scaled * scales[0:1, :]).astype(BF16)
    sums[0:1, :] += jnp.sum(grad * unit, axis=0, keepdims=True)
    sums[1:2, :] += jnp.sum(grad, axis=0, keepdims=True)
    sums[2:3, :] += jnp.sum(low.astype(F32), axis=0, keepdims=True)
    sums[3:4, :] += jnp.sum(grad_scaled * mixed[...], axis=0, keepdims=True)


def branch_back(core, grad_attended, branch, weights, mixed, scales, vectors, wait):
    rows, width = branch.shape
    block = rows // 4
    by_row = pl.BlockSpec((block, width), lambda at, *_: (at, 0))
    fourth = pl.BlockSpec((width // 2, width), lambda at, *_: (0, 1))
    return call(
        branch_back_body,
        (rows // block,),
        [
            by_row,
            by_row,
            fourth,
            fourth,
            by_row,
            whole(scales.shape),
            whole(vectors.shape),
            *after(wait),
        ],
        [by_row, by_row, whole((8, width))],
        [
            jax.ShapeDtypeStruct((rows, width), BF16),
            jax.ShapeDtypeStruct((rows, width), BF16),
            jax.ShapeDtypeStruct((8, width), F32),
        ],
        scratch=[pltpu.VMEM((2, block, width // 2), F32)],
        flops=2 * rows * width * width,
        bytes_accessed=2 * width * width + 16 * rows * width,
        scalars=1,
    )(core, grad_attended, branch, *weights[2:], mixed, scales, vectors, wait)


def forward_ffn_body(
    steps, normed, attended, vectors, rows_of, up, down, output, top, kept, slope, stats, held, total, sums
):
    at = pl.program_id(0)
    width = held.shape[2]

    @pl.when(at == 0)
    def _():
        sums[...] = jnp.zeros_like(sums)

    @pl.when(at < steps)
    def _():
        hidden = dot_nn(normed[...], up[...]) + rows_of[0:1, :]
        cdf = 0.5 + 0.5 * lax.erf(hidden * math.sqrt(0.5))
        value = hidden * cdf
        slope[...] = (
            cdf + hidden * (jnp.exp(-0.5 * hidden * hidden) * (1.0 / math.sqrt(2.0 * math.pi)))
        ).astype(BF16)
        held[at] = value
        kept[...] = value.astype(BF16)
        sums[...] += lane_sum(value)

    @pl.when(at == steps)
    def _():
        count = steps * width
        mean = jnp.sum(sums[...], axis=1, keepdims=True) * (1.0 / count)
        square = jnp.zeros(sums.shape, F32)
        for block in range(steps):
            centered = held[block] - mean
            square = square + lane_sum(centered * centered)
        spread = lax.rsqrt(jnp.sum(square, axis=1, keepdims=True) * (1.0 / count) + EPS)
        stats[:, :TILE] = jnp.broadcast_to(mean, sums.shape)
        stats[:, TILE:] = jnp.broadcast_to(spread, sums.shape)
        total[...] = attended[...] + vectors[21:22, :]

    @pl.when(at >= steps)
    def _():
        mean = stats[:, 0:1]
        spread = stats[:, TILE : TILE + 1]
        value = held[at - steps]
        low = ((value - mean) * spread * rows_of[1:2, :] + rows_of[2:3, :]).astype(BF16)
        top[...] = low
        total[...] += dot_nt(low, down[...])

    @pl.when(at == 2 * steps - 1)
    def _():
        output[...] = total[...].astype(BF16)


def forward_ffn(normed, attended, vectors, wide_rows, both):
    rows, width = attended.shape
    hidden = both.shape[1] // 2
    block = 1024
    steps = hidden // block
    early = lambda at: (0, jnp.minimum(at, steps - 1))
    late = lambda at: (0, jnp.maximum(at - steps, 0))
    return call(
        functools.partial(forward_ffn_body, steps),
        (2 * steps,),
        [
            whole((rows, width)),
            whole((rows, width)),
            whole(vectors.shape),
            pl.BlockSpec((8, block), lambda at: (0, lax.rem(at, steps))),
            pl.BlockSpec((width, block), early),
            pl.BlockSpec((width, block), lambda at: (0, steps + jnp.maximum(at - steps, 0))),
        ],
        [
            whole((rows, width)),
            pl.BlockSpec((rows, block), late),
            pl.BlockSpec((rows, block), early),
            pl.BlockSpec((rows, block), early),
            whole((rows, 2 * TILE)),
        ],
        [
            jax.ShapeDtypeStruct((rows, width), BF16),
            jax.ShapeDtypeStruct((rows, hidden), BF16),
            jax.ShapeDtypeStruct((rows, hidden), BF16),
            jax.ShapeDtypeStruct((rows, hidden), BF16),
            jax.ShapeDtypeStruct((rows, 2 * TILE), F32),
        ],
        scratch=[
            pltpu.VMEM((steps, rows, block), F32),
            pltpu.VMEM((rows, width), F32),
            pltpu.VMEM((rows, TILE), F32),
        ],
        flops=4 * rows * width * hidden,
        bytes_accessed=4 * width * hidden + 6 * rows * hidden,
    )(normed, attended, vectors, wide_rows, both, both)


def backward_ffn_body(
    steps,
    upstream,
    attended,
    vectors,
    rows_of,
    stats,
    kept,
    slope,
    down,
    up,
    _,
    grad_attended,
    grad_hidden,
    wide_sums,
    sums,
    held,
    total,
    first,
    second,
):
    at = pl.program_id(0)
    count = steps * held.shape[2]
    mean = stats[:, 0:1]
    spread = stats[:, TILE : TILE + 1]

    @pl.when(at == 0)
    def _():
        first[...] = jnp.zeros_like(first)
        second[...] = jnp.zeros_like(second)
        total[...] = jnp.zeros_like(total)
        wide_sums[...] = jnp.zeros_like(wide_sums)

    @pl.when(at < steps)
    def _():
        grad = dot_nn(upstream[...], down[...])
        unit = (kept[...].astype(F32) - mean) * spread
        both = grad * unit
        wide_sums[at, 0:1, :] = jnp.sum(both, axis=0, keepdims=True)
        wide_sums[at, 1:2, :] = jnp.sum(grad, axis=0, keepdims=True)
        gain = rows_of[1:2, :]
        held[at] = grad * gain
        first[...] += lane_sum(grad * gain)
        second[...] += lane_sum(both * gain)

    @pl.when(at == steps)
    def _():
        scale = 1.0 / count
        first[...] = jnp.broadcast_to(
            jnp.sum(first[...], axis=1, keepdims=True) * scale, first.shape
        )
        second[...] = jnp.broadcast_to(
            jnp.sum(second[...], axis=1, keepdims=True) * scale, second.shape
        )

    @pl.when(at >= steps)
    def _():
        unit = (kept[...].astype(F32) - mean) * spread
        grad = spread * (held[at - steps] - first[:, 0:1] - unit * second[:, 0:1])
        low = (grad * slope[...].astype(F32)).astype(BF16)
        grad_hidden[...] = low
        wide_sums[at - steps, 2:3, :] = jnp.sum(low.astype(F32), axis=0, keepdims=True)
        total[...] += dot_nt(low, up[...])

    @pl.when(at == 2 * steps - 1)
    def _():
        grad = total[...]
        centered, mid_spread = row_stats(attended[...])
        unit = centered * mid_spread
        top = upstream[...].astype(F32)
        grad_attended[...] = top + norm_back(grad * vectors[7:8, :], unit, mid_spread)
        sums[0:1, :] = jnp.sum(grad * unit, axis=0, keepdims=True)
        sums[1:2, :] = jnp.sum(grad, axis=0, keepdims=True)
        sums[2:3, :] = jnp.sum(top, axis=0, keepdims=True)
        sums[3:8, :] = jnp.zeros((5, sums.shape[1]), F32)


def backward_ffn(upstream, attended, vectors, wide_rows, stats, kept, slope, both, wait):
    rows, width = attended.shape
    hidden = both.shape[1] // 2
    block = 1024
    steps = hidden // block
    late = lambda at: (0, jnp.maximum(at - steps, 0))
    turn = lambda at: (0, lax.rem(at, steps))
    return call(
        functools.partial(backward_ffn_body, steps),
        (2 * steps,),
        [
            whole((rows, width)),
            whole((rows, width)),
            whole(vectors.shape),
            pl.BlockSpec((8, block), turn),
            whole((rows, 2 * TILE)),
            pl.BlockSpec((rows, block), turn),
            pl.BlockSpec((rows, block), late),
            pl.BlockSpec((width, block), lambda at: (0, steps + jnp.minimum(at, steps - 1))),
            pl.BlockSpec((width, block), late),
            *after(wait),
        ],
        [
            whole((rows, width)),
            pl.BlockSpec((rows, block), late),
            whole((steps, 8, block)),
            whole((8, width)),
        ],
        [
            jax.ShapeDtypeStruct((rows, width), F32),
            jax.ShapeDtypeStruct((rows, hidden), BF16),
            jax.ShapeDtypeStruct((steps, 8, block), F32),
            jax.ShapeDtypeStruct((8, width), F32),
        ],
        scratch=[
            pltpu.VMEM((steps, rows, block), F32),
            pltpu.VMEM((rows, width), F32),
            pltpu.VMEM((rows, TILE), F32),
            pltpu.VMEM((rows, TILE), F32),
        ],
        flops=4 * rows * width * hidden,
        bytes_accessed=4 * width * hidden + 8 * rows * hidden,
    )(upstream, attended, vectors, wide_rows, stats, kept, slope, both, both, wait)


def input_back_body(
    core,
    grads,
    own_qk,
    other_qk,
    own_vo,
    other_vo,
    tokens,
    grad_attended,
    vectors,
    branch_sums,
    mid_sums,
    wide_sums,
    _,
    input_grad,
    turned,
    parts,
    sums,
):
    part = pl.program_id(0)
    me = core[0]
    grad_part = grads[...]

    @pl.when(part == 0)
    def _():
        parts[me] = dot_nt(grad_part, own_qk[...])
        parts[1 - me] = dot_nt(grad_part, other_qk[...])
        sums[...] = jnp.zeros_like(sums)
        sums[2:3, :] = jnp.sum(grad_part.astype(F32), axis=0, keepdims=True)

    @pl.when(part == 1)
    def _():
        parts[me] += dot_nt(grad_part, own_qk[...])
        parts[1 - me] += dot_nt(grad_part, other_qk[...])

    @pl.when(part == 2)
    def _():
        parts[me] += dot_nt(grad_part, own_vo[...])
        parts[1 - me] += dot_nt(grad_part, other_vo[...])
        grad = join_parity(parts[0], parts[1])
        centered, spread = row_stats(tokens[...].astype(F32))
        unit = centered * spread
        input_grad[...] = grad_attended[...] + norm_back(grad * vectors[0:1, :], unit, spread)
        sums[0:1, :] = jnp.sum(grad * unit, axis=0, keepdims=True)
        sums[1:2, :] = jnp.sum(grad, axis=0, keepdims=True)
        sums[3:4, :] = jnp.sum(grad_part.astype(F32), axis=0, keepdims=True)
        sums[4:7, :] = branch_sums[0:3, :]
        sums[7:9, :] = mid_sums[0:2, :]
        for row in range(wide_sums.shape[0]):
            sums[9 + row : 10 + row, :] = wide_sums[row, 2:3, :]
            sums[13 + row : 14 + row, :] = wide_sums[row, 0:1, :]
            sums[17 + row : 18 + row, :] = wide_sums[row, 1:2, :]
        sums[21:22, :] = mid_sums[2:3, :]
        width = sums.shape[1]
        head_dim = TILE // 2
        picks = (
            lax.broadcasted_iota(jnp.int32, (width, TILE), 0) // head_dim + HEAD_AT
            == lax.broadcasted_iota(jnp.int32, (width, TILE), 1)
        ).astype(F32)
        heads = lax.dot_general(
            branch_sums[...],
            picks,
            (((1,), (0,)), ((), ())),
            precision=HIGHEST,
            preferred_element_type=F32,
        )[3:4, :]
        for block in range(turned.shape[0]):
            turned[block] = (
                jnp.transpose(sums[:, block * TILE : (block + 1) * TILE]) + heads
            )


def input_back(core, grads, weights, tokens, grad_attended, vectors, sums, wait):
    rows, width = tokens.shape
    full = whole((rows, width))
    third = pl.BlockSpec((width // 2, width), lambda part, *_: (0, jnp.minimum(part, 1)))
    last = pl.BlockSpec((width // 2, width), lambda part, *_: (0, 0))
    return call(
        input_back_body,
        (3,),
        [
            pl.BlockSpec((None, rows, width), lambda part, *_: (part, 0, 0)),
            third,
            third,
            last,
            last,
            full,
            full,
            whole(vectors.shape),
            *[whole(item.shape) for item in sums],
            *after(wait),
        ],
        [full, whole((width // TILE, TILE, TILE))],
        [
            jax.ShapeDtypeStruct((rows, width), F32),
            jax.ShapeDtypeStruct((width // TILE, TILE, TILE), F32),
        ],
        scratch=[pltpu.VMEM((2, rows, width // 2), F32), pltpu.VMEM((TILE, width), F32)],
        flops=1,
        bytes_accessed=1,
        scalars=1,
    )(core, grads, *weights, tokens, grad_attended, vectors, *sums, wait)


def outer_body(two_lefts, adds, _, *refs):
    lefts = refs[: 4 * (1 + two_lefts)]
    refs = refs[4 * (1 + two_lefts) :]
    early, late, upper, lower = refs[:4]
    refs = refs[4:]
    if adds:
        add_first, add_second = refs[:2]
        refs = refs[2:]
    first, second = refs[:2]
    turned = refs[2:]
    at = pl.program_id(0)

    @pl.when(at == 0)
    def _():
        for which in range(1 + two_lefts):
            for block in range(4):
                turned[which][block * TILE : (block + 1) * TILE, :] = jnp.transpose(
                    lefts[4 * which + block][...]
                )

    def write_first(left, right):
        value = dot_nn(left[...], right[...])
        if adds:
            value = value + add_first[...].astype(F32)
        first[...] = value.astype(BF16)

    pl.when(at == 0)(lambda: write_first(turned[two_lefts], early))
    pl.when(at == 1)(lambda: write_first(turned[0], late))

    @pl.when(at >= 2)
    def _():
        above = dot_nn(turned[0][...], upper[...])
        below = dot_nn(turned[0][...], lower[...])
        plane, chips = second.shape[:2]
        for chip in range(chips):
            cut = slice(chip * 8 * plane, (chip + 1) * 8 * plane)
            value = jnp.concatenate(
                [
                    above[cut].reshape(plane, 8, above.shape[1]),
                    below[cut].reshape(plane, 8, below.shape[1]),
                ],
                axis=1,
            )
            if adds:
                value = value + add_second[:, chip].astype(F32)
            second[:, chip] = value.astype(BF16)


def outer(core, chips, left, rights, other_left=None, add=None, wait=()):
    rows, width = left.shape
    lefts = [left] if other_left is None else [left, other_left]
    half = width // 2
    plane = half // (8 * chips)

    def left_spec(block):
        return pl.BlockSpec((rows, TILE), lambda at, core, block=block: (0, 2 * block + core[0]))

    def right_spec(index, start, columns, low, high):
        def where(at, *_):
            column = start // columns + jnp.clip(at - low, 0, high)
            return (index, 0, column)

        return pl.BlockSpec((None, rows, columns), where)

    specs, operands = [], []
    for one in lefts:
        for block in range(4):
            specs.append(left_spec(block))
            operands.append(one)
    for (array, index, start), columns, low, high in zip(
        rights, (1024, 1024, 512, 512), (0, 0, 2, 2), (0, 0, 1, 1)
    ):
        specs.append(right_spec(index, start, columns, low, high))
        operands.append(array)
    part_specs = [
        pl.BlockSpec((half, 1024), lambda at, *_: (0, jnp.clip(at, 0, 1))),
        pl.BlockSpec((plane, chips, 16, 512), lambda at, *_: (0, 0, 0, jnp.clip(at - 2, 0, 1))),
    ]
    if add is not None:
        specs += part_specs
        operands += list(add)

    def body(core, *refs):
        used = len(operands)
        outer_body(len(lefts) - 1, add is not None, core, *refs[:used], *refs[used + len(wait) :])

    return call(
        body,
        (4,),
        specs + after(*wait),
        part_specs,
        [
            jax.ShapeDtypeStruct((half, 2048), BF16),
            jax.ShapeDtypeStruct((plane, chips, 16, 1024), BF16),
        ],
        scratch=[pltpu.VMEM((half, rows), BF16) for _ in lefts],
        flops=4 * rows * half * 2048,
        bytes_accessed=4 * half * 4096,
        scalars=1,
    )(core, *operands, *wait)


def to_slots_body(perm, down, up, attn, own, *refs):
    more, (grad_qkv, grad_out, grad_up, grad_down, slots, tiles) = refs[:3], refs[3:]
    rest = own[...]
    for one in more:
        rest = rest + one[...].astype(F32)
    width = grad_out.shape[1]
    half = down.shape[1]
    grad_out[...] = attn[:, :width]
    grad_qkv[:, :width] = attn[:, width : 2 * width]
    grad_qkv[:, width : 2 * width] = rest[32:40]
    grad_qkv[:, 2 * width :] = rest[40:48]
    for result, first, at in ((grad_down, down, 0), (grad_up, up, 16)):
        result[:, :half] = first[...]
        result[:, half : half + width] = rest[at : at + 8]
        result[:, half + width :] = rest[at + 8 : at + 16]
    column = 0
    for result in (grad_qkv, grad_out, grad_up, grad_down):
        for at in range(0, result.shape[1], TILE):
            tiles[column] = result[:, at : at + TILE]
            column += 1
    planes, pairs = slots.shape[:2]
    for slot in range(planes * pairs):
        pair = [tiles[perm[2 * slot + which]] for which in range(2)]
        slots[slot // pairs, slot % pairs] = jnp.concatenate(pair, axis=0).astype(BF16)


def to_slots(perm, down, up, attn, rest, plane, widths):
    arrays = [down, up, attn, *rest]
    pairs = perm.shape[0] // (2 * plane)
    shapes = [jax.ShapeDtypeStruct((8, columns), F32) for columns in widths]
    shapes.append(jax.ShapeDtypeStruct((plane, pairs, 16, TILE), BF16))
    return call(
        to_slots_body,
        (1,),
        [whole(item.shape) for item in arrays],
        [whole(item.shape) for item in shapes],
        shapes,
        scratch=[pltpu.VMEM((perm.shape[0], 8, TILE), F32)],
        bytes_accessed=8 * 8 * sum(widths),
        scalars=1,
    )(perm, *arrays)


def update_body(grads, left_stats, right_stats, left_roots, right_roots, left_new, right_new, back):
    planes, pairs = grads.shape[:2]
    for pair in range(pairs):
        block = grads[:, pair].astype(F32)
        moved = []
        for which in range(2):
            slot = 2 * pair + which
            grad = block[:, which * 8 : which * 8 + 8, :].reshape(TILE, TILE)
            low = grad.astype(BF16)
            left_new[slot] = DECAY * left_stats[slot] + (1.0 - DECAY) * dot_nt(low, low)
            right_new[slot] = DECAY * right_stats[slot] + (1.0 - DECAY) * dot_tn(low, low)
            step = jnp.dot(grad, right_roots[slot], precision=HIGHEST, preferred_element_type=F32)
            step = jnp.dot(left_roots[slot], step, precision=HIGHEST, preferred_element_type=F32)
            moved.append(step.reshape(planes, 8, TILE))
        back[:, pair] = jnp.concatenate(moved, axis=1).astype(BF16)


def update(grads, left_stats, right_stats, left_roots, right_roots):
    arrays = [item[0] for item in (left_stats, right_stats, left_roots, right_roots)]
    stats = jax.ShapeDtypeStruct(arrays[0].shape, F32)
    left_new, right_new, back = call(
        update_body,
        (1,),
        [whole(grads.shape)] + [whole(item.shape) for item in arrays],
        [whole(stats.shape), whole(stats.shape), whole(grads.shape)],
        [stats, stats, jax.ShapeDtypeStruct(grads.shape, BF16)],
        bytes_accessed=24 * arrays[0].size,
    )(grads, *arrays)
    return left_new[None], right_new[None], back


def apply_body(perm, moved, *refs):
    olds, news, tiles = refs[:4], refs[4:8], refs[8]
    pairs = moved.shape[1]
    for slot in range(moved.shape[0] * pairs):
        value = moved[slot // pairs, slot % pairs].astype(F32)
        tiles[perm[2 * slot]] = value[:8]
        tiles[perm[2 * slot + 1]] = value[8:]
    column = 0
    for old, new in zip(olds, news):
        for at in range(0, old.shape[1], TILE):
            cut = slice(at, at + TILE)
            new[:, cut] = old[:, cut] - RATE_MATRIX * tiles[column]
            column += 1


def apply_steps(perm, moved, weights):
    shapes = [jax.ShapeDtypeStruct(item.shape, F32) for item in weights]
    return call(
        apply_body,
        (1,),
        [whole(moved.shape)] + [whole(item.shape) for item in weights],
        [whole(item.shape) for item in shapes],
        shapes,
        scratch=[pltpu.VMEM((perm.shape[0], 8, TILE), F32)],
        bytes_accessed=10 * 8 * TILE * perm.shape[0],
        scalars=1,
    )(perm, moved, *weights)


def swap_cores(values):
    return lax.ppermute(values, "core", [(0, 1), (1, 0)])


def turn_chips(values, step):
    count = lax.axis_size("x")
    return lax.ppermute(values, "x", [(at, (at + step) % count) for at in range(count)])


def sum_parts(parts):
    return jnp.sum(parts.astype(F32), axis=0)


def shards(
    tokens,
    cotangent,
    lengths,
    valid,
    owner_perm,
    w_qkv,
    w_out,
    w_up,
    w_down,
    vectors,
    head_scale,
    left_stats,
    right_stats,
    left_roots,
    right_roots,
    vector_stats,
    head_stats,
):
    rows, width = tokens.shape
    heads = head_scale.shape[0]
    hidden = w_up.shape[1]
    ratio = hidden // width
    shard = w_up.shape[0]
    plane = lax.axis_size("fsdp")
    chips = lax.axis_size("x")
    core = lax.axis_index("core")
    core_arg = core.astype(jnp.int32).reshape(1)

    both = lax.all_gather(
        jnp.concatenate([w_up.astype(BF16), w_down.astype(BF16)], axis=1),
        ("x", "core", "fsdp"),
        axis=0,
        tiled=True,
    )
    low_qk = jnp.concatenate(
        [
            w_qkv[:, : 2 * width].astype(BF16),
            jnp.pad(vectors.astype(BF16).T, ((0, 0), (0, TILE - vectors.shape[0]))),
        ],
        axis=1,
    )
    low_vo = jnp.concatenate([w_qkv[:, 2 * width :].astype(BF16), w_out.astype(BF16)], axis=1)

    def to_plane(part, concat):
        spread = jnp.broadcast_to(part[None], (plane,) + part.shape)
        return lax.all_to_all(spread, "fsdp", split_axis=0, concat_axis=concat, tiled=True)

    place = lax.axis_index("x")

    def roll_chips(parts, start):
        twice = jnp.concatenate([parts, parts], axis=0)
        begin = [start] + [0] * (parts.ndim - 1)
        return lax.dynamic_slice(twice, begin, parts.shape, allow_negative_indices=False)

    def in_order(parts):
        return roll_chips(jnp.stack(parts[::-1]), chips - 1 - place)

    def to_chips(part):
        return in_order([part] + [turn_chips(part, step) for step in range(1, chips)])

    def across_chips(parts):
        ahead = roll_chips(parts, place)
        return [ahead[0]] + [turn_chips(ahead[step], step) for step in range(1, chips)]

    own_vo = to_plane(to_chips(low_vo), 2).reshape(width // 2, -1)
    own_qk = to_chips(to_plane(low_qk, 0).reshape(plane * shard, -1)).reshape(width // 2, -1)
    other_qk, other_vo = swap_cores(own_qk), swap_cores(own_vo)
    weights = (own_qk, other_qk, own_vo, other_vo)
    vector_at = 2 * width
    vector_pair = jnp.stack([own_qk[:, vector_at:], other_qk[:, vector_at:]])
    vector_pair = jnp.where(core == 0, vector_pair, vector_pair[::-1])
    vector_rows = (
        vector_pair.reshape(2, -1, TILE, TILE)
        .transpose(1, 0, 2, 3)
        .reshape(width, TILE)
        .T[:24]
        .astype(F32)
    )
    wide_rows = jnp.concatenate(
        [
            vector_rows[9 : 9 + 3 * ratio].reshape(3, hidden),
            jnp.zeros((5, hidden), F32),
        ],
        axis=0,
    )
    upstream = jnp.where(valid[:, None] != 0, cotangent, jnp.zeros_like(cotangent))
    scales = jnp.broadcast_to(jnp.repeat(head_scale, width // heads)[None], (8, width))

    normed, projected = project(core_arg, tokens, vector_rows, weights)
    mixed, scaled, attention = attend(lengths, head_scale, projected)
    branch, attended, normed_mid = branch_out(core_arg, scaled, weights, tokens, vector_rows)
    output, normed_top, kept, slope, stats = forward_ffn(
        normed_mid, attended, vector_rows, wide_rows, both
    )

    def over_x(part):
        return lax.psum_scatter(part, "x", scatter_dimension=0, tiled=True)

    def over_plane(part):
        return sum_parts(
            lax.all_to_all(
                part.reshape(plane, shard, -1), "fsdp", split_axis=0, concat_axis=0, tiled=True
            )
        )

    def plane_first(part):
        total = lax.all_to_all(part, "fsdp", split_axis=0, concat_axis=0, tiled=True)
        return sum_parts(total)

    def four(array):
        return [(array[None], 0, start) for start in (0, 1024, 2048, 3072)]

    sent_down = outer(1 - core_arg, chips, upstream, four(normed_top))
    down_first, down_second = outer(
        core_arg, chips, upstream, four(normed_top), add=[swap_cores(part) for part in sent_down]
    )
    down_rest = plane_first(down_second)
    down_part = over_plane(over_x(down_first))
    grad_attended, grad_hidden, wide_sums, mid_sums = backward_ffn(
        upstream, attended, vector_rows, wide_rows, stats, kept, slope, both, down_second
    )
    sent_up = outer(1 - core_arg, chips, normed_mid, four(grad_hidden))
    grad_branch, grad_mixed, branch_sums = branch_back(
        core_arg, grad_attended, branch, weights, mixed, scales, vector_rows, sent_up[1]
    )
    up_first, up_second = outer(
        core_arg,
        chips,
        normed_mid,
        four(grad_hidden),
        add=[swap_cores(part) for part in sent_up],
        wait=(grad_branch, down_rest, down_part),
    )
    up_rest = plane_first(up_second)
    up_part = over_plane(over_x(up_first))
    grads = attend_back(projected, mixed, grad_mixed, attention, up_second)
    rights = [(grad_branch[None], 0, 0), (grads, 0, 0), (grads, 1, 0), (grads, 2, 0)]
    sent_attn = outer(1 - core_arg, chips, normed, rights, other_left=scaled)
    attn_first, attn_second = outer(
        core_arg,
        chips,
        normed,
        rights,
        other_left=scaled,
        add=[swap_cores(part) for part in sent_attn],
        wait=(up_rest, up_part),
    )
    input_grad, turned = input_back(
        core_arg,
        grads,
        weights,
        tokens,
        grad_attended,
        vector_rows,
        (branch_sums, mid_sums, wide_sums),
        attn_second,
    )
    attn_rest = plane_first(attn_second)

    turned = turned.reshape(chips, 2, TILE, TILE)
    kept_sums = lax.dynamic_slice_in_dim(turned, core, 1, 1, allow_negative_indices=False)[:, 0]
    sent_sums = lax.dynamic_slice_in_dim(
        turned, 1 - core, 1, 1, allow_negative_indices=False
    )[:, 0]
    small = jnp.sum(in_order(across_chips(kept_sums + swap_cores(sent_sums))), axis=0)

    rest = jnp.concatenate([down_rest, up_rest, attn_rest], axis=1).astype(BF16)
    rest = across_chips(rest)
    rest[0] = rest[0].astype(F32)
    attn_part = over_plane(jnp.concatenate([over_x(attn_first), small.astype(BF16)], axis=1))
    vector_grads = attn_part[:, 2 * width :].T[: vectors.shape[0]]
    head_total = attn_part[0, 2 * width + HEAD_AT : 2 * width + HEAD_AT + heads]

    masters = (w_qkv, w_out, w_up, w_down)
    grad_qkv, grad_out, grad_up, grad_down, slots = to_slots(
        owner_perm,
        down_part,
        up_part,
        attn_part,
        rest,
        plane,
        [item.shape[1] for item in masters],
    )
    slots = lax.all_to_all(slots, "fsdp", split_axis=0, concat_axis=0, tiled=True)
    left_new, right_new, back = update(slots, left_stats, right_stats, left_roots, right_roots)
    back = lax.all_to_all(back, "fsdp", split_axis=0, concat_axis=0, tiled=True)
    new_qkv, new_out, new_up, new_down = apply_steps(owner_perm, back, masters)
    vector_stats_new = DECAY * vector_stats + (1.0 - DECAY) * vector_grads * vector_grads
    vectors_new = vectors - RATE_VECTOR * vector_grads * lax.rsqrt(vector_stats_new)
    head_stats_new = DECAY * head_stats + (1.0 - DECAY) * head_total * head_total
    head_new = head_scale - RATE_VECTOR * head_total * lax.rsqrt(head_stats_new)
    return (
        output,
        input_grad,
        grad_qkv,
        grad_out,
        grad_up,
        grad_down,
        vector_grads,
        head_total,
        left_new,
        right_new,
        new_qkv,
        new_out,
        new_up,
        new_down,
        vector_stats_new,
        vectors_new,
        head_stats_new,
        head_new,
    )


def solution(mesh):
    everywhere = ("x", "core", "fsdp")
    by_rows = P(everywhere, None)
    by_columns = P(None, everywhere)
    by_block = P(("x", "core"), "fsdp", None, None)
    dp, fsdp = mesh.devices.shape
    mesh = jax.sharding.Mesh(mesh.devices.reshape(dp // 2, 2, fsdp), everywhere)
    return jax.shard_map(
        shards,
        mesh=mesh,
        in_specs=(
            (by_rows, by_rows, P(everywhere), P(everywhere), P())
            + (by_rows,) * 4
            + (by_columns, P())
            + (by_block,) * 4
            + (by_columns, P())
        ),
        out_specs=(
            (by_rows,) * 6
            + (by_columns, P())
            + (by_block,) * 2
            + (by_rows,) * 4
            + (by_columns, by_columns, P(), P())
        ),
        check_vma=False,
    )
```

```python
import functools
import math

import jax
import jax.numpy as jnp
from jax import lax
from jax.experimental import pallas as pl
from jax.experimental.pallas import tpu as pltpu
from jax.sharding import PartitionSpec as P

TILE = 128
EPS = 1e-05
DECAY = 0.5
RATE_MATRIX = 0.1
RATE_VECTOR = 0.3
HIGHEST = lax.Precision.HIGHEST
HEAD_AT = 24
VMEM_BYTES = 56 * 1024 * 1024
F32 = jnp.float32
BF16 = jnp.bfloat16


def dot_nn(left, right):
    return lax.dot_general(left, right, (((1,), (0,)), ((), ())), preferred_element_type=F32)


def dot_nt(left, right):
    return lax.dot_general(left, right, (((1,), (1,)), ((), ())), preferred_element_type=F32)


def dot_tn(left, right):
    return lax.dot_general(left, right, (((0,), (0,)), ((), ())), preferred_element_type=F32)


def row_stats(values):
    mean = jnp.mean(values, axis=-1, keepdims=True)
    centered = values - mean
    spread = lax.rsqrt(jnp.mean(centered * centered, axis=-1, keepdims=True) + EPS)
    return centered, spread


def norm_back(scaled_grad, unit, spread):
    mean_grad = jnp.mean(scaled_grad, axis=-1, keepdims=True)
    mean_both = jnp.mean(scaled_grad * unit, axis=-1, keepdims=True)
    return spread * (scaled_grad - mean_grad - unit * mean_both)


def lane_sum(values):
    total = values[:, :TILE]
    for at in range(TILE, values.shape[1], TILE):
        total = total + values[:, at : at + TILE]
    return total


def call(body, grid, in_specs, out_specs, out_shape, scratch=(), flops=0, bytes_accessed=0, scalars=0):
    return pl.pallas_call(
        body,
        out_shape=out_shape,
        grid_spec=pltpu.PrefetchScalarGridSpec(
            num_scalar_prefetch=scalars,
            grid=grid,
            in_specs=in_specs,
            out_specs=out_specs,
            scratch_shapes=list(scratch),
        ),
        compiler_params=pltpu.CompilerParams(vmem_limit_bytes=VMEM_BYTES),
        cost_estimate=pl.CostEstimate(
            flops=7 * flops, bytes_accessed=bytes_accessed, transcendentals=0
        ),
    )


def whole(shape):
    return pl.BlockSpec(shape, lambda *_: (0,) * len(shape))


def after(*arrays):
    return [pl.BlockSpec(memory_space=pl.ANY) for _ in arrays]


def split_parity(values):
    blocks = [values[:, at : at + TILE] for at in range(0, values.shape[1], TILE)]
    return jnp.concatenate(blocks[0::2], axis=1), jnp.concatenate(blocks[1::2], axis=1)


def join_parity(even, odd):
    blocks = []
    for at in range(0, even.shape[1], TILE):
        blocks += [even[:, at : at + TILE], odd[:, at : at + TILE]]
    return jnp.concatenate(blocks, axis=1)


def turn_rows(left, turned, parity):
    for block in range(turned.shape[0] // TILE):
        at = pl.multiple_of((2 * block + parity) * TILE, TILE)
        turned[block * TILE : (block + 1) * TILE, :] = jnp.transpose(left[:, pl.ds(at, TILE)])


def by_owner(values, plane):
    rows, columns = values.shape
    chips = rows // (8 * plane)
    values = values.reshape(chips, plane, 8, columns)
    return jnp.concatenate([values[chip] for chip in range(chips)], axis=1)


def project_body(
    core, tokens, vectors, own_qk, other_qk, own_vo, other_vo, normed, projected, parts
):
    part = pl.program_id(0)

    @pl.when(part == 0)
    def _():
        centered, spread = row_stats(tokens[...].astype(F32))
        low = (centered * spread * vectors[0:1, :] + vectors[1:2, :]).astype(BF16)
        normed[...] = low
        parts[0], parts[1] = split_parity(low)

    gate_q = jnp.where(part == 0, 1.0, 0.0).astype(F32)
    gate_v = jnp.where(part == 2, 1.0, 0.0).astype(F32)
    bias = gate_q * vectors[2:3, :] + gate_v * vectors[3:4, :]
    me = core[0]

    @pl.when(part < 2)
    def _():
        projected[...] = (
            dot_nn(parts[me], own_qk[...]) + dot_nn(parts[1 - me], other_qk[...]) + bias
        ).astype(BF16)

    @pl.when(part == 2)
    def _():
        projected[...] = (
            dot_nn(parts[me], own_vo[...]) + dot_nn(parts[1 - me], other_vo[...]) + bias
        ).astype(BF16)


def project(core, tokens, vectors, weights):
    rows, width = tokens.shape
    parts = 3
    third = pl.BlockSpec((width // 2, width), lambda part, *_: (0, jnp.minimum(part, 1)))
    last = pl.BlockSpec((width // 2, width), lambda part, *_: (0, 0))
    return call(
        project_body,
        (parts,),
        [whole((rows, width)), whole(vectors.shape), third, third, last, last],
        [whole((rows, width)), pl.BlockSpec((rows, width), lambda part, *_: (0, part))],
        [
            jax.ShapeDtypeStruct((rows, width), BF16),
            jax.ShapeDtypeStruct((rows, parts * width), BF16),
        ],
        scratch=[pltpu.VMEM((2, rows, width // 2), BF16)],
        flops=2 * rows * width * width * parts,
        bytes_accessed=2 * width * width * parts,
        scalars=1,
    )(core, tokens, vectors, *weights)


def attend_body(length, scales, queries, keys, values, mixed, scaled, weights):
    rows = queries.shape[0]
    head_dim = TILE // 2
    pair = pl.program_id(0)
    block = rows // 2
    lane = lax.broadcasted_iota(jnp.int32, (rows, TILE), 1)
    spot = lax.broadcasted_iota(jnp.int32, (rows, TILE), 0)
    hidden_key = jnp.where(spot < length[0], 0.0, -1e30).astype(BF16)
    one = jnp.ones((rows, TILE), BF16)
    zero = jnp.zeros((rows, TILE), BF16)
    query = queries[...] * jnp.asarray(1.0 / math.sqrt(head_dim), BF16)
    key = keys[...]
    value = values[...]
    causal = lax.broadcasted_iota(jnp.int32, (block, block), 1) <= lax.broadcasted_iota(
        jnp.int32, (block, block), 0
    )
    total = [jnp.zeros((block, TILE), F32) for _ in range(2)]
    for head in range(2):
        mine = (lane < head_dim) if head == 0 else (lane >= head_dim)
        spare = lane == (head_dim if head == 0 else 0)
        query_one = jnp.where(mine, query, jnp.where(spare, one, zero))
        key_one = jnp.where(mine, key, jnp.where(spare, hidden_key, zero))
        value_one = jnp.where(mine, value, zero)
        for part in range(2):
            seen = (part + 1) * block
            score = dot_nt(query_one[part * block : seen], key_one[:seen])
            last = jnp.where(causal, score[:, part * block :], -1e30)
            score = last if part == 0 else jnp.concatenate([score[:, :block], last], axis=1)
            top = jnp.max(score, axis=1, keepdims=True)
            grown = jnp.exp(score - top)
            share = (grown * (1.0 / jnp.sum(grown, axis=1, keepdims=True))).astype(BF16)
            if part == 0:
                weights[head, :, :block] = share
            else:
                weights[head, :, block:] = share
            total[part] = total[part] + dot_nn(share, value_one[:seen])
    scale_row = jnp.where(
        lax.broadcasted_iota(jnp.int32, (1, TILE), 1) < head_dim,
        scales[2 * pair],
        scales[2 * pair + 1],
    )
    for part in range(2):
        mixed[part * block : (part + 1) * block, :] = total[part]
        scaled[part * block : (part + 1) * block, :] = (total[part] * scale_row).astype(BF16)


def attend(length, scales, projected):
    rows, width3 = projected.shape
    width = width3 // 3
    pairs = width // TILE
    block = rows // 2
    return call(
        attend_body,
        (pairs,),
        [
            pl.BlockSpec((rows, TILE), lambda pair, *_: (0, pair)),
            pl.BlockSpec((rows, TILE), lambda pair, *_: (0, pairs + pair)),
            pl.BlockSpec((rows, TILE), lambda pair, *_: (0, 2 * pairs + pair)),
        ],
        [
            pl.BlockSpec((rows, TILE), lambda pair, *_: (0, pair)),
            pl.BlockSpec((rows, TILE), lambda pair, *_: (0, pair)),
            pl.BlockSpec((2, block, 3 * block), lambda pair, *_: (pair, 0, 0)),
        ],
        [
            jax.ShapeDtypeStruct((rows, width), F32),
            jax.ShapeDtypeStruct((rows, width), BF16),
            jax.ShapeDtypeStruct((2 * pairs, block, 3 * block), BF16),
        ],
        flops=4 * rows * rows * width,
        bytes_accessed=20 * rows * width,
        scalars=2,
    )(length, scales, projected, projected, projected)


def attend_back_body(
    core, queries, keys, values, mixed, grads, weights, normed, _, __, out, sent_qk, sent_v, turned
):
    @pl.when(pl.program_id(0) == 0)
    def _():
        turn_rows(normed, turned, 1 - core[0])

    rows = queries.shape[0]
    head_dim = TILE // 2
    block = rows // 2
    lane = lax.broadcasted_iota(jnp.int32, (rows, TILE), 1)
    zero = jnp.zeros((rows, TILE), BF16)
    query, key, value, grad = queries[...], keys[...], values[...], grads[...]
    both = grad.astype(F32) * mixed[...]
    q_total = [jnp.zeros((block, TILE), F32) for _ in range(2)]
    k_total = [jnp.zeros((block, TILE), F32) for _ in range(2)]
    v_total = [jnp.zeros((block, TILE), F32) for _ in range(2)]
    for head in range(2):
        mine = (lane < head_dim) if head == 0 else (lane >= head_dim)
        query_one = jnp.where(mine, query, zero)
        key_one = jnp.where(mine, key, zero)
        grad_one = jnp.where(mine, grad, zero)
        delta = jnp.sum(jnp.where(mine, both, 0.0), axis=1, keepdims=True)
        for part in range(2):
            at = part * block
            seen = at + block
            share = weights[head, :, :block] if part == 0 else weights[head, :, block:]
            into = dot_nt(grad_one[at:seen], value[:seen])
            slope = (share.astype(F32) * (into - delta[at:seen])).astype(BF16)
            q_total[part] = q_total[part] + dot_nn(slope, key_one[:seen])
            k_new = dot_tn(slope, query_one[at:seen])
            v_new = dot_tn(share, grad_one[at:seen])
            for into_part in range(part + 1):
                cut = slice(into_part * block, (into_part + 1) * block)
                k_total[into_part] = k_total[into_part] + k_new[cut]
                v_total[into_part] = v_total[into_part] + v_new[cut]
    root = 1.0 / math.sqrt(head_dim)
    low_q = (jnp.concatenate(q_total, axis=0) * root).astype(BF16)
    low_k = (jnp.concatenate(k_total, axis=0) * root).astype(BF16)
    low_v = jnp.concatenate(v_total, axis=0).astype(BF16)
    out[0], out[1], out[2] = low_q, low_k, low_v
    sent = dot_nn(turned[...], jnp.concatenate([low_q, low_k, low_v], axis=1))
    sent_qk[0] = sent[:, :TILE].astype(BF16)
    sent_qk[1] = sent[:, TILE : 2 * TILE].astype(BF16)
    sent_v[...] = by_owner(sent[:, 2 * TILE :], sent_v.shape[0]).astype(BF16)


def attend_back(core, plane, projected, mixed, grads, weights, normed, wait):
    rows, width3 = projected.shape
    width = width3 // 3
    half = width // 2
    pairs = width // TILE
    block = rows // 2
    by_pair = pl.BlockSpec((rows, TILE), lambda pair, *_: (0, pair))
    return call(
        attend_back_body,
        (pairs,),
        [
            by_pair,
            pl.BlockSpec((rows, TILE), lambda pair, *_: (0, pairs + pair)),
            pl.BlockSpec((rows, TILE), lambda pair, *_: (0, 2 * pairs + pair)),
            by_pair,
            by_pair,
            pl.BlockSpec((2, block, 3 * block), lambda pair, *_: (pair, 0, 0)),
            whole((rows, width)),
            *after(*wait),
        ],
        [
            pl.BlockSpec((3, rows, TILE), lambda pair, *_: (0, 0, pair)),
            pl.BlockSpec((2, half, TILE), lambda pair, *_: (0, 0, pair)),
            pl.BlockSpec((plane, half // plane, TILE), lambda pair, *_: (0, 0, pair)),
        ],
        [
            jax.ShapeDtypeStruct((3, rows, width), BF16),
            jax.ShapeDtypeStruct((2, half, width), BF16),
            jax.ShapeDtypeStruct((plane, half // plane, width), BF16),
        ],
        scratch=[pltpu.VMEM((half, rows), BF16)],
        flops=10 * rows * rows * width,
        bytes_accessed=24 * rows * width,
        scalars=1,
    )(core, projected, projected, projected, mixed, grads, weights, normed, *wait)


def branch_body(core, scaled, own, other, tokens, vectors, branch, attended, normed, parts):
    parts[0], parts[1] = split_parity(scaled[...])
    me = core[0]
    value = dot_nn(parts[me], own[...]) + dot_nn(parts[1 - me], other[...]) + vectors[6:7, :]
    branch[...] = value
    centered, spread = row_stats(value)
    total = tokens[...].astype(F32) + centered * spread * vectors[4:5, :] + vectors[5:6, :]
    attended[...] = total
    centered, spread = row_stats(total)
    normed[...] = (centered * spread * vectors[7:8, :] + vectors[8:9, :]).astype(BF16)


def branch_out(core, scaled, weights, tokens, vectors):
    rows, width = scaled.shape
    block = rows // 4
    by_row = pl.BlockSpec((block, width), lambda at, *_: (at, 0))
    fourth = pl.BlockSpec((width // 2, width), lambda at, *_: (0, 1))
    return call(
        branch_body,
        (rows // block,),
        [by_row, fourth, fourth, by_row, whole(vectors.shape)],
        [by_row, by_row, by_row],
        [
            jax.ShapeDtypeStruct((rows, width), F32),
            jax.ShapeDtypeStruct((rows, width), F32),
            jax.ShapeDtypeStruct((rows, width), BF16),
        ],
        scratch=[pltpu.VMEM((2, block, width // 2), BF16)],
        flops=2 * rows * width * width,
        bytes_accessed=2 * width * width + 14 * rows * width,
        scalars=1,
    )(core, scaled, *weights[2:], tokens, vectors)


def branch_back_body(
    core,
    grad_attended,
    branch,
    own,
    other,
    mixed,
    scales,
    vectors,
    scaled,
    _,
    __,
    grad_branch,
    grad_mixed,
    sums,
    sent,
    staying,
    parts,
    lows,
    turned,
):
    at = pl.program_id(0)

    @pl.when(at == 0)
    def _():
        sums[...] = jnp.zeros_like(sums)

    grad = grad_attended[...]
    centered, spread = row_stats(branch[...])
    unit = centered * spread
    low = norm_back(grad * vectors[4:5, :], unit, spread).astype(BF16)
    grad_branch[...] = low
    lows[at] = low
    me = core[0]
    parts[me] = dot_nt(low, own[...])
    parts[1 - me] = dot_nt(low, other[...])
    grad_scaled = join_parity(parts[0], parts[1])
    grad_mixed[...] = (grad_scaled * scales[0:1, :]).astype(BF16)
    sums[0:1, :] += jnp.sum(grad * unit, axis=0, keepdims=True)
    sums[1:2, :] += jnp.sum(grad, axis=0, keepdims=True)
    sums[2:3, :] += jnp.sum(low.astype(F32), axis=0, keepdims=True)
    sums[3:4, :] += jnp.sum(grad_scaled * mixed[...], axis=0, keepdims=True)

    @pl.when(at == pl.num_programs(0) - 1)
    def _():
        right = lows[...].reshape(scaled.shape)
        turn_rows(scaled, turned, 1 - me)
        sent[...] = dot_nn(turned[...], right).astype(BF16)
        turn_rows(scaled, turned, me)
        staying[...] = dot_nn(turned[...], right)


def branch_back(core, grad_attended, branch, weights, mixed, scales, vectors, scaled, *wait):
    rows, width = branch.shape
    block = rows // 4
    by_row = pl.BlockSpec((block, width), lambda at, *_: (at, 0))
    fourth = pl.BlockSpec((width // 2, width), lambda at, *_: (0, 1))
    return call(
        branch_back_body,
        (rows // block,),
        [
            by_row,
            by_row,
            fourth,
            fourth,
            by_row,
            whole(scales.shape),
            whole(vectors.shape),
            whole(scaled.shape),
            *after(*wait),
        ],
        [by_row, by_row, whole((8, width)), whole((width // 2, width)), whole((width // 2, width))],
        [
            jax.ShapeDtypeStruct((rows, width), BF16),
            jax.ShapeDtypeStruct((rows, width), BF16),
            jax.ShapeDtypeStruct((8, width), F32),
            jax.ShapeDtypeStruct((width // 2, width), BF16),
            jax.ShapeDtypeStruct((width // 2, width), F32),
        ],
        scratch=[
            pltpu.VMEM((2, block, width // 2), F32),
            pltpu.VMEM((rows // block, block, width), BF16),
            pltpu.VMEM((width // 2, rows), BF16),
        ],
        flops=4 * rows * width * width,
        bytes_accessed=2 * width * width + 16 * rows * width,
        scalars=1,
    )(core, grad_attended, branch, *weights[2:], mixed, scales, vectors, scaled, *wait)


def send_part(values, step, first, second):
    @pl.when(step < 2)
    def _():
        first[...] = values.astype(BF16)

    @pl.when(step >= 2)
    def _():
        second[...] = by_owner(values, second.shape[0]).astype(BF16)


def part_specs(half, plane, start):
    return [
        pl.BlockSpec((half, 1024), lambda at, *_: (0, jnp.clip(at - start, 0, 1))),
        pl.BlockSpec(
            (plane, half // plane, 1024), lambda at, *_: (0, 0, jnp.clip(at - start - 2, 0, 1))
        ),
    ]


def part_shapes(half, plane):
    return [
        jax.ShapeDtypeStruct((half, 2048), BF16),
        jax.ShapeDtypeStruct((plane, half // plane, 2048), BF16),
    ]


def forward_ffn_body(
    steps,
    core,
    normed,
    attended,
    vectors,
    rows_of,
    up,
    down,
    upstream,
    output,
    top,
    kept,
    slope,
    stats,
    sent_first,
    sent_second,
    held,
    total,
    sums,
    turned,
):
    at = pl.program_id(0)
    width = held.shape[2]

    @pl.when(at == 0)
    def _():
        turn_rows(upstream, turned, 1 - core[0])
        sums[...] = jnp.zeros_like(sums)

    @pl.when(at < steps)
    def _():
        hidden = dot_nn(normed[...], up[...]) + rows_of[0:1, :]
        cdf = 0.5 + 0.5 * lax.erf(hidden * math.sqrt(0.5))
        value = hidden * cdf
        slope[...] = (
            cdf + hidden * (jnp.exp(-0.5 * hidden * hidden) * (1.0 / math.sqrt(2.0 * math.pi)))
        ).astype(BF16)
        held[at] = value
        kept[...] = value.astype(BF16)
        sums[...] += lane_sum(value)

    @pl.when(at == steps)
    def _():
        count = steps * width
        mean = jnp.sum(sums[...], axis=1, keepdims=True) * (1.0 / count)
        square = jnp.zeros(sums.shape, F32)
        for block in range(steps):
            centered = held[block] - mean
            square = square + lane_sum(centered * centered)
        spread = lax.rsqrt(jnp.sum(square, axis=1, keepdims=True) * (1.0 / count) + EPS)
        stats[:, :TILE] = jnp.broadcast_to(mean, sums.shape)
        stats[:, TILE:] = jnp.broadcast_to(spread, sums.shape)
        total[...] = attended[...] + vectors[21:22, :]

    @pl.when(at >= steps)
    def _():
        mean = stats[:, 0:1]
        spread = stats[:, TILE : TILE + 1]
        value = held[at - steps]
        low = ((value - mean) * spread * rows_of[1:2, :] + rows_of[2:3, :]).astype(BF16)
        top[...] = low
        total[...] += dot_nt(low, down[...])
        send_part(dot_nn(turned[...], low), at - steps, sent_first, sent_second)

    @pl.when(at == 2 * steps - 1)
    def _():
        output[...] = total[...].astype(BF16)


def forward_ffn(core, plane, normed, attended, vectors, wide_rows, both, upstream):
    rows, width = attended.shape
    hidden = both.shape[1] // 2
    block = 1024
    steps = hidden // block
    early = lambda at, *_: (0, jnp.minimum(at, steps - 1))
    late = lambda at, *_: (0, jnp.maximum(at - steps, 0))
    return call(
        functools.partial(forward_ffn_body, steps),
        (2 * steps,),
        [
            whole((rows, width)),
            whole((rows, width)),
            whole(vectors.shape),
            pl.BlockSpec((8, block), lambda at, *_: (0, lax.rem(at, steps))),
            pl.BlockSpec((width, block), early),
            pl.BlockSpec((width, block), lambda at, *_: (0, steps + jnp.maximum(at - steps, 0))),
            whole((rows, width)),
        ],
        [
            whole((rows, width)),
            pl.BlockSpec((rows, block), late),
            pl.BlockSpec((rows, block), early),
            pl.BlockSpec((rows, block), early),
            whole((rows, 2 * TILE)),
            *part_specs(width // 2, plane, steps),
        ],
        [
            jax.ShapeDtypeStruct((rows, width), BF16),
            jax.ShapeDtypeStruct((rows, hidden), BF16),
            jax.ShapeDtypeStruct((rows, hidden), BF16),
            jax.ShapeDtypeStruct((rows, hidden), BF16),
            jax.ShapeDtypeStruct((rows, 2 * TILE), F32),
            *part_shapes(width // 2, plane),
        ],
        scratch=[
            pltpu.VMEM((steps, rows, block), F32),
            pltpu.VMEM((rows, width), F32),
            pltpu.VMEM((rows, TILE), F32),
            pltpu.VMEM((width // 2, rows), BF16),
        ],
        flops=5 * rows * width * hidden,
        bytes_accessed=4 * width * hidden + 6 * rows * hidden,
        scalars=1,
    )(core, normed, attended, vectors, wide_rows, both, both, upstream)


def backward_ffn_body(
    steps,
    core,
    upstream,
    attended,
    vectors,
    rows_of,
    stats,
    kept,
    slope,
    down,
    up,
    normed,
    _,
    grad_attended,
    grad_hidden,
    wide_sums,
    sums,
    sent_first,
    sent_second,
    held,
    total,
    first,
    second,
    turned,
):
    at = pl.program_id(0)
    count = steps * held.shape[2]
    mean = stats[:, 0:1]
    spread = stats[:, TILE : TILE + 1]

    @pl.when(at == 0)
    def _():
        turn_rows(normed, turned, 1 - core[0])
        first[...] = jnp.zeros_like(first)
        second[...] = jnp.zeros_like(second)
        total[...] = jnp.zeros_like(total)
        wide_sums[...] = jnp.zeros_like(wide_sums)

    @pl.when(at < steps)
    def _():
        grad = dot_nn(upstream[...], down[...])
        unit = (kept[...].astype(F32) - mean) * spread
        both = grad * unit
        wide_sums[at, 0:1, :] = jnp.sum(both, axis=0, keepdims=True)
        wide_sums[at, 1:2, :] = jnp.sum(grad, axis=0, keepdims=True)
        gain = rows_of[1:2, :]
        held[at] = grad * gain
        first[...] += lane_sum(grad * gain)
        second[...] += lane_sum(both * gain)

    @pl.when(at == steps)
    def _():
        scale = 1.0 / count
        first[...] = jnp.broadcast_to(
            jnp.sum(first[...], axis=1, keepdims=True) * scale, first.shape
        )
        second[...] = jnp.broadcast_to(
            jnp.sum(second[...], axis=1, keepdims=True) * scale, second.shape
        )

    @pl.when(at >= steps)
    def _():
        unit = (kept[...].astype(F32) - mean) * spread
        grad = spread * (held[at - steps] - first[:, 0:1] - unit * second[:, 0:1])
        low = (grad * slope[...].astype(F32)).astype(BF16)
        grad_hidden[...] = low
        wide_sums[at - steps, 2:3, :] = jnp.sum(low.astype(F32), axis=0, keepdims=True)
        total[...] += dot_nt(low, up[...])
        send_part(dot_nn(turned[...], low), at - steps, sent_first, sent_second)

    @pl.when(at == 2 * steps - 1)
    def _():
        grad = total[...]
        centered, mid_spread = row_stats(attended[...])
        unit = centered * mid_spread
        top = upstream[...].astype(F32)
        grad_attended[...] = top + norm_back(grad * vectors[7:8, :], unit, mid_spread)
        sums[0:1, :] = jnp.sum(grad * unit, axis=0, keepdims=True)
        sums[1:2, :] = jnp.sum(grad, axis=0, keepdims=True)
        sums[2:3, :] = jnp.sum(top, axis=0, keepdims=True)
        sums[3:8, :] = jnp.zeros((5, sums.shape[1]), F32)


def backward_ffn(
    core, plane, upstream, attended, vectors, wide_rows, stats, kept, slope, both, normed, wait
):
    rows, width = attended.shape
    hidden = both.shape[1] // 2
    block = 1024
    steps = hidden // block
    late = lambda at, *_: (0, jnp.maximum(at - steps, 0))
    turn = lambda at, *_: (0, lax.rem(at, steps))
    return call(
        functools.partial(backward_ffn_body, steps),
        (2 * steps,),
        [
            whole((rows, width)),
            whole((rows, width)),
            whole(vectors.shape),
            pl.BlockSpec((8, block), turn),
            whole((rows, 2 * TILE)),
            pl.BlockSpec((rows, block), turn),
            pl.BlockSpec((rows, block), late),
            pl.BlockSpec((width, block), lambda at, *_: (0, steps + jnp.minimum(at, steps - 1))),
            pl.BlockSpec((width, block), late),
            whole((rows, width)),
            *after(wait),
        ],
        [
            whole((rows, width)),
            pl.BlockSpec((rows, block), late),
            whole((steps, 8, block)),
            whole((8, width)),
            *part_specs(width // 2, plane, steps),
        ],
        [
            jax.ShapeDtypeStruct((rows, width), F32),
            jax.ShapeDtypeStruct((rows, hidden), BF16),
            jax.ShapeDtypeStruct((steps, 8, block), F32),
            jax.ShapeDtypeStruct((8, width), F32),
            *part_shapes(width // 2, plane),
        ],
        scratch=[
            pltpu.VMEM((steps, rows, block), F32),
            pltpu.VMEM((rows, width), F32),
            pltpu.VMEM((rows, TILE), F32),
            pltpu.VMEM((rows, TILE), F32),
            pltpu.VMEM((width // 2, rows), BF16),
        ],
        flops=5 * rows * width * hidden,
        bytes_accessed=4 * width * hidden + 8 * rows * hidden,
        scalars=1,
    )(core, upstream, attended, vectors, wide_rows, stats, kept, slope, both, both, normed, wait)


def input_back_body(
    core,
    grads,
    own_qk,
    other_qk,
    own_vo,
    other_vo,
    tokens,
    grad_attended,
    vectors,
    branch_sums,
    mid_sums,
    wide_sums,
    input_grad,
    turned,
    parts,
    sums,
):
    part = pl.program_id(0)
    me = core[0]
    grad_part = grads[...]

    @pl.when(part == 0)
    def _():
        parts[me] = dot_nt(grad_part, own_qk[...])
        parts[1 - me] = dot_nt(grad_part, other_qk[...])
        sums[...] = jnp.zeros_like(sums)
        sums[2:3, :] = jnp.sum(grad_part.astype(F32), axis=0, keepdims=True)

    @pl.when(part == 1)
    def _():
        parts[me] += dot_nt(grad_part, own_qk[...])
        parts[1 - me] += dot_nt(grad_part, other_qk[...])

    @pl.when(part == 2)
    def _():
        parts[me] += dot_nt(grad_part, own_vo[...])
        parts[1 - me] += dot_nt(grad_part, other_vo[...])
        grad = join_parity(parts[0], parts[1])
        centered, spread = row_stats(tokens[...].astype(F32))
        unit = centered * spread
        input_grad[...] = grad_attended[...] + norm_back(grad * vectors[0:1, :], unit, spread)
        sums[0:1, :] = jnp.sum(grad * unit, axis=0, keepdims=True)
        sums[1:2, :] = jnp.sum(grad, axis=0, keepdims=True)
        sums[3:4, :] = jnp.sum(grad_part.astype(F32), axis=0, keepdims=True)
        sums[4:7, :] = branch_sums[0:3, :]
        sums[7:9, :] = mid_sums[0:2, :]
        for row in range(wide_sums.shape[0]):
            sums[9 + row : 10 + row, :] = wide_sums[row, 2:3, :]
            sums[13 + row : 14 + row, :] = wide_sums[row, 0:1, :]
            sums[17 + row : 18 + row, :] = wide_sums[row, 1:2, :]
        sums[21:22, :] = mid_sums[2:3, :]
        width = sums.shape[1]
        head_dim = TILE // 2
        picks = (
            lax.broadcasted_iota(jnp.int32, (width, TILE), 0) // head_dim + HEAD_AT
            == lax.broadcasted_iota(jnp.int32, (width, TILE), 1)
        ).astype(F32)
        heads = lax.dot_general(
            branch_sums[...],
            picks,
            (((1,), (0,)), ((), ())),
            precision=HIGHEST,
            preferred_element_type=F32,
        )[3:4, :]
        for block in range(turned.shape[0]):
            turned[block] = (
                jnp.transpose(sums[:, block * TILE : (block + 1) * TILE]) + heads
            )


def input_back(core, grads, weights, tokens, grad_attended, vectors, sums):
    rows, width = tokens.shape
    full = whole((rows, width))
    third = pl.BlockSpec((width // 2, width), lambda part, *_: (0, jnp.minimum(part, 1)))
    last = pl.BlockSpec((width // 2, width), lambda part, *_: (0, 0))
    return call(
        input_back_body,
        (3,),
        [
            pl.BlockSpec((None, rows, width), lambda part, *_: (part, 0, 0)),
            third,
            third,
            last,
            last,
            full,
            full,
            whole(vectors.shape),
            *[whole(item.shape) for item in sums],
        ],
        [full, whole((width // TILE, TILE, TILE))],
        [
            jax.ShapeDtypeStruct((rows, width), F32),
            jax.ShapeDtypeStruct((width // TILE, TILE, TILE), F32),
        ],
        scratch=[pltpu.VMEM((2, rows, width // 2), F32), pltpu.VMEM((TILE, width), F32)],
        flops=6 * rows * width * width,
        bytes_accessed=6 * width * width + 16 * rows * width,
        scalars=1,
    )(core, grads, *weights, tokens, grad_attended, vectors, *sums)


def outer_body(firsts, core, left, right, add_first, add_second, *refs):
    first, second, turned = refs[-3:]
    at = pl.program_id(0)

    @pl.when(at == 0)
    def _():
        turn_rows(left, turned, core[0])

    value = dot_nn(turned[...], right[...])

    @pl.when(at < firsts)
    def _():
        first[...] = (value + add_first[...].astype(F32)).astype(BF16)

    @pl.when(at >= firsts)
    def _():
        second[...] = (
            by_owner(value, second.shape[0]) + add_second[...].astype(F32)
        ).astype(BF16)


def outer(core, left, right, add, wait=()):
    rows, width = left.shape
    half = width // 2
    block = 1024
    add_first, add_second = add
    plane, owned = add_second.shape[:2]
    firsts = 2
    seconds = add_second.shape[2] // block
    if right.ndim == 2:
        right_spec = pl.BlockSpec((rows, block), lambda at, *_: (0, at))
        add_spec = pl.BlockSpec((half, block), lambda at, *_: (0, jnp.clip(at, 0, 1)))
    else:
        right_spec = pl.BlockSpec((None, rows, block), lambda at, *_: (at, 0, 0))
        add_spec = pl.BlockSpec((None, half, block), lambda at, *_: (jnp.clip(at, 0, 1), 0, 0))
    second_spec = pl.BlockSpec(
        (plane, owned, block), lambda at, *_: (0, 0, jnp.clip(at - firsts, 0, seconds - 1))
    )
    return call(
        functools.partial(outer_body, firsts),
        (firsts + seconds,),
        [whole((rows, width)), right_spec, add_spec, second_spec, *after(*wait)],
        [pl.BlockSpec((half, block), lambda at, *_: (0, jnp.clip(at, 0, 1))), second_spec],
        [
            jax.ShapeDtypeStruct((half, firsts * block), BF16),
            jax.ShapeDtypeStruct(add_second.shape, BF16),
        ],
        scratch=[pltpu.VMEM((half, rows), BF16)],
        flops=2 * rows * half * block * (firsts + seconds),
        bytes_accessed=6 * half * block * (firsts + seconds),
        scalars=1,
    )(core, left, right, add_first, add_second, *wait)


def to_slots_body(perm, down, parts, rest, *refs):
    grad_qkv, grad_out, grad_up, grad_down, slots, tiles = refs
    width = grad_out.shape[1]
    half = down.shape[1]
    grad_out[...] = parts[:, half : half + width]
    grad_qkv[:, : 2 * width] = parts[:, half + width : half + 3 * width]
    grad_qkv[:, 2 * width :] = rest[:, 2 * half :]
    grad_down[:, :half] = down[...]
    grad_down[:, half:] = rest[:, :half]
    grad_up[:, :half] = parts[:, :half]
    grad_up[:, half:] = rest[:, half : 2 * half]
    column = 0
    for result in (grad_qkv, grad_out, grad_up, grad_down):
        for at in range(0, result.shape[1], TILE):
            tiles[column] = result[:, at : at + TILE]
            column += 1
    planes, pairs = slots.shape[:2]
    for slot in range(planes * pairs):
        pair = [tiles[perm[2 * slot + which]] for which in range(2)]
        slots[slot // pairs, slot % pairs] = jnp.concatenate(pair, axis=0).astype(BF16)


def to_slots(perm, down, parts, rest, plane, widths):
    arrays = [down, parts, rest]
    pairs = perm.shape[0] // (2 * plane)
    shapes = [jax.ShapeDtypeStruct((8, columns), F32) for columns in widths]
    shapes.append(jax.ShapeDtypeStruct((plane, pairs, 16, TILE), BF16))
    return call(
        to_slots_body,
        (1,),
        [whole(item.shape) for item in arrays],
        [whole(item.shape) for item in shapes],
        shapes,
        scratch=[pltpu.VMEM((perm.shape[0], 8, TILE), F32)],
        bytes_accessed=8 * 8 * sum(widths),
        scalars=1,
    )(perm, *arrays)


def update_body(grads, left_stats, right_stats, left_roots, right_roots, left_new, right_new, back):
    planes, pairs = grads.shape[:2]
    for pair in range(pairs):
        block = grads[:, pair].astype(F32)
        moved = []
        for which in range(2):
            slot = 2 * pair + which
            grad = block[:, which * 8 : which * 8 + 8, :].reshape(TILE, TILE)
            low = grad.astype(BF16)
            left_new[slot] = DECAY * left_stats[slot] + (1.0 - DECAY) * dot_nt(low, low)
            right_new[slot] = DECAY * right_stats[slot] + (1.0 - DECAY) * dot_tn(low, low)
            step = jnp.dot(grad, right_roots[slot], precision=HIGHEST, preferred_element_type=F32)
            step = jnp.dot(left_roots[slot], step, precision=HIGHEST, preferred_element_type=F32)
            moved.append(step.reshape(planes, 8, TILE))
        back[:, pair] = jnp.concatenate(moved, axis=1).astype(BF16)


def update(grads, left_stats, right_stats, left_roots, right_roots):
    arrays = [item[0] for item in (left_stats, right_stats, left_roots, right_roots)]
    stats = jax.ShapeDtypeStruct(arrays[0].shape, F32)
    left_new, right_new, back = call(
        update_body,
        (1,),
        [whole(grads.shape)] + [whole(item.shape) for item in arrays],
        [whole(stats.shape), whole(stats.shape), whole(grads.shape)],
        [stats, stats, jax.ShapeDtypeStruct(grads.shape, BF16)],
        bytes_accessed=24 * arrays[0].size,
    )(grads, *arrays)
    return left_new[None], right_new[None], back


def apply_body(perm, moved, *refs):
    olds, news, tiles = refs[:4], refs[4:8], refs[8]
    pairs = moved.shape[1]
    for slot in range(moved.shape[0] * pairs):
        value = moved[slot // pairs, slot % pairs].astype(F32)
        tiles[perm[2 * slot]] = value[:8]
        tiles[perm[2 * slot + 1]] = value[8:]
    column = 0
    for old, new in zip(olds, news):
        for at in range(0, old.shape[1], TILE):
            cut = slice(at, at + TILE)
            new[:, cut] = old[:, cut] - RATE_MATRIX * tiles[column]
            column += 1


def apply_steps(perm, moved, weights):
    shapes = [jax.ShapeDtypeStruct(item.shape, F32) for item in weights]
    return call(
        apply_body,
        (1,),
        [whole(moved.shape)] + [whole(item.shape) for item in weights],
        [whole(item.shape) for item in shapes],
        shapes,
        scratch=[pltpu.VMEM((perm.shape[0], 8, TILE), F32)],
        bytes_accessed=10 * 8 * TILE * perm.shape[0],
        scalars=1,
    )(perm, moved, *weights)


def swap_cores(values):
    return lax.ppermute(values, "core", [(0, 1), (1, 0)])


def turn_chips(values, step):
    count = lax.axis_size("x")
    return lax.ppermute(values, "x", [(at, (at + step) % count) for at in range(count)])


def sum_parts(parts):
    return jnp.sum(parts.astype(F32), axis=0)


def shards(
    tokens,
    cotangent,
    lengths,
    valid,
    owner_perm,
    w_qkv,
    w_out,
    w_up,
    w_down,
    vectors,
    head_scale,
    left_stats,
    right_stats,
    left_roots,
    right_roots,
    vector_stats,
    head_stats,
):
    rows, width = tokens.shape
    heads = head_scale.shape[0]
    hidden = w_up.shape[1]
    ratio = hidden // width
    shard = w_up.shape[0]
    plane = lax.axis_size("fsdp")
    chips = lax.axis_size("x")
    core = lax.axis_index("core")
    core_arg = core.astype(jnp.int32).reshape(1)

    both = lax.all_gather(
        jnp.concatenate([w_up.astype(BF16), w_down.astype(BF16)], axis=1),
        ("x", "core", "fsdp"),
        axis=0,
        tiled=True,
    )
    low_qk = jnp.concatenate(
        [
            w_qkv[:, : 2 * width].astype(BF16),
            jnp.pad(vectors.astype(BF16).T, ((0, 0), (0, TILE - vectors.shape[0]))),
        ],
        axis=1,
    )
    low_vo = jnp.concatenate([w_qkv[:, 2 * width :].astype(BF16), w_out.astype(BF16)], axis=1)

    def to_plane(part, concat):
        spread = jnp.broadcast_to(part[None], (plane,) + part.shape)
        return lax.all_to_all(spread, "fsdp", split_axis=0, concat_axis=concat, tiled=True)

    place = lax.axis_index("x")

    def roll_chips(parts, start):
        twice = jnp.concatenate([parts, parts], axis=0)
        begin = [start] + [0] * (parts.ndim - 1)
        return lax.dynamic_slice(twice, begin, parts.shape, allow_negative_indices=False)

    def in_order(parts):
        return roll_chips(jnp.stack(parts[::-1]), chips - 1 - place)

    def to_chips(part):
        return in_order([part] + [turn_chips(part, step) for step in range(1, chips)])

    def across_chips(parts):
        ahead = roll_chips(parts, place)
        return [ahead[0]] + [turn_chips(ahead[step], step) for step in range(1, chips)]

    own_vo = to_plane(to_chips(low_vo), 2).reshape(width // 2, -1)
    own_qk = to_chips(to_plane(low_qk, 0).reshape(plane * shard, -1)).reshape(width // 2, -1)
    other_qk, other_vo = swap_cores(own_qk), swap_cores(own_vo)
    weights = (own_qk, other_qk, own_vo, other_vo)
    vector_at = 2 * width
    vector_pair = jnp.stack([own_qk[:, vector_at:], other_qk[:, vector_at:]])
    vector_pair = jnp.where(core == 0, vector_pair, vector_pair[::-1])
    vector_rows = (
        vector_pair.reshape(2, -1, TILE, TILE)
        .transpose(1, 0, 2, 3)
        .reshape(width, TILE)
        .T[:24]
        .astype(F32)
    )
    wide_rows = jnp.concatenate(
        [
            vector_rows[9 : 9 + 3 * ratio].reshape(3, hidden),
            jnp.zeros((5, hidden), F32),
        ],
        axis=0,
    )
    upstream = jnp.where(valid[:, None] != 0, cotangent, jnp.zeros_like(cotangent))
    scales = jnp.broadcast_to(jnp.repeat(head_scale, width // heads)[None], (8, width))

    normed, projected = project(core_arg, tokens, vector_rows, weights)
    mixed, scaled, attention = attend(lengths, head_scale, projected)
    branch, attended, normed_mid = branch_out(core_arg, scaled, weights, tokens, vector_rows)
    output, normed_top, kept, slope, stats, *sent_down = forward_ffn(
        core_arg, plane, normed_mid, attended, vector_rows, wide_rows, both, upstream
    )

    def over_x(part):
        return lax.psum_scatter(part, "x", scatter_dimension=0, tiled=True)

    def over_plane(part):
        return sum_parts(
            lax.all_to_all(
                part.reshape(plane, shard, -1), "fsdp", split_axis=0, concat_axis=0, tiled=True
            )
        )

    def plane_first(part):
        total = lax.all_to_all(part, "fsdp", split_axis=0, concat_axis=0, tiled=True)
        return sum_parts(total)

    down_first, down_second = outer(
        core_arg, upstream, normed_top, [swap_cores(part) for part in sent_down]
    )
    down_rest = plane_first(down_second)
    down_chips = over_x(down_first)
    down_part = over_plane(down_chips)
    grad_attended, grad_hidden, wide_sums, mid_sums, *sent_up = backward_ffn(
        core_arg,
        plane,
        upstream,
        attended,
        vector_rows,
        wide_rows,
        stats,
        kept,
        slope,
        both,
        normed_mid,
        down_second,
    )
    grad_branch, grad_mixed, branch_sums, out_sent, out_stays = branch_back(
        core_arg,
        grad_attended,
        branch,
        weights,
        mixed,
        scales,
        vector_rows,
        scaled,
        down_rest,
        down_chips,
    )
    up_first, up_second = outer(
        core_arg,
        normed_mid,
        grad_hidden,
        [swap_cores(part) for part in sent_up],
        wait=(grad_branch,),
    )
    up_second, _ = lax.optimization_barrier((up_second, down_part))
    up_rest = plane_first(up_second)
    out_first = (out_stays + swap_cores(out_sent).astype(F32)).astype(BF16)
    grads, *sent_attn = attend_back(
        core_arg,
        plane,
        projected,
        mixed,
        grad_mixed,
        attention,
        normed,
        (up_second, out_first),
    )
    input_grad, turned = input_back(
        core_arg,
        grads,
        weights,
        tokens,
        grad_attended,
        vector_rows,
        (branch_sums, mid_sums, wide_sums),
    )
    turned = turned.reshape(chips, 2, TILE, TILE)
    kept_sums = lax.dynamic_slice_in_dim(turned, core, 1, 1, allow_negative_indices=False)[:, 0]
    sent_sums = lax.dynamic_slice_in_dim(
        turned, 1 - core, 1, 1, allow_negative_indices=False
    )[:, 0]
    half_sums = kept_sums + swap_cores(sent_sums)
    attn_first, attn_second = outer(
        core_arg,
        normed,
        grads,
        [swap_cores(part) for part in sent_attn],
        wait=(half_sums, up_rest),
    )
    attn_rest = plane_first(attn_second)

    half_sums, _ = lax.optimization_barrier((half_sums, attn_second))
    small = jnp.sum(in_order(across_chips(half_sums)), axis=0)

    rest = jnp.concatenate([down_rest, up_rest, attn_rest], axis=1)
    rest = across_chips(rest.astype(BF16).reshape(chips, shard, -1))
    rest = sum(part.astype(F32) for part in rest)
    parts = over_plane(
        jnp.concatenate(
            [over_x(up_first), over_x(out_first), over_x(attn_first), small.astype(BF16)], axis=1
        )
    )
    small = parts[:, hidden // 2 + 3 * width :]
    vector_grads = small.T[: vectors.shape[0]]
    head_total = small[0, HEAD_AT : HEAD_AT + heads]

    masters = (w_qkv, w_out, w_up, w_down)
    grad_qkv, grad_out, grad_up, grad_down, slots = to_slots(
        owner_perm,
        down_part,
        parts,
        rest,
        plane,
        [item.shape[1] for item in masters],
    )
    slots = lax.all_to_all(slots, "fsdp", split_axis=0, concat_axis=0, tiled=True)
    left_new, right_new, back = update(slots, left_stats, right_stats, left_roots, right_roots)
    back = lax.all_to_all(back, "fsdp", split_axis=0, concat_axis=0, tiled=True)
    new_qkv, new_out, new_up, new_down = apply_steps(owner_perm, back, masters)
    vector_stats_new = DECAY * vector_stats + (1.0 - DECAY) * vector_grads * vector_grads
    vectors_new = vectors - RATE_VECTOR * vector_grads * lax.rsqrt(vector_stats_new)
    head_stats_new = DECAY * head_stats + (1.0 - DECAY) * head_total * head_total
    head_new = head_scale - RATE_VECTOR * head_total * lax.rsqrt(head_stats_new)
    return (
        output,
        input_grad,
        grad_qkv,
        grad_out,
        grad_up,
        grad_down,
        vector_grads,
        head_total,
        left_new,
        right_new,
        new_qkv,
        new_out,
        new_up,
        new_down,
        vector_stats_new,
        vectors_new,
        head_stats_new,
        head_new,
    )


def solution(mesh):
    everywhere = ("x", "core", "fsdp")
    by_rows = P(everywhere, None)
    by_columns = P(None, everywhere)
    by_block = P(("x", "core"), "fsdp", None, None)
    dp, fsdp = mesh.devices.shape
    mesh = jax.sharding.Mesh(mesh.devices.reshape(dp // 2, 2, fsdp), everywhere)
    return jax.shard_map(
        shards,
        mesh=mesh,
        in_specs=(
            (by_rows, by_rows, P(everywhere), P(everywhere), P())
            + (by_rows,) * 4
            + (by_columns, P())
            + (by_block,) * 4
            + (by_columns, P())
        ),
        out_specs=(
            (by_rows,) * 6
            + (by_columns, P())
            + (by_block,) * 2
            + (by_rows,) * 4
            + (by_columns, by_columns, P(), P())
        ),
        check_vma=False,
    )
```

```python
import functools
import math

import jax
import jax.numpy as jnp
from jax import lax
from jax.experimental import pallas as pl
from jax.experimental.pallas import tpu as pltpu
from jax.sharding import PartitionSpec as P

TILE = 128
EPS = 1e-05
DECAY = 0.5
RATE_MATRIX = 0.1
RATE_VECTOR = 0.3
HIGHEST = lax.Precision.HIGHEST
HEAD_AT = 24
VMEM_BYTES = 56 * 1024 * 1024
F32 = jnp.float32
BF16 = jnp.bfloat16


def dot_nn(left, right):
    return lax.dot_general(left, right, (((1,), (0,)), ((), ())), preferred_element_type=F32)


def dot_nt(left, right):
    return lax.dot_general(left, right, (((1,), (1,)), ((), ())), preferred_element_type=F32)


def dot_tn(left, right):
    return lax.dot_general(left, right, (((0,), (0,)), ((), ())), preferred_element_type=F32)


def row_stats(values):
    mean = jnp.mean(values, axis=-1, keepdims=True)
    centered = values - mean
    spread = lax.rsqrt(jnp.mean(centered * centered, axis=-1, keepdims=True) + EPS)
    return centered, spread


def norm_back(scaled_grad, unit, spread):
    mean_grad = jnp.mean(scaled_grad, axis=-1, keepdims=True)
    mean_both = jnp.mean(scaled_grad * unit, axis=-1, keepdims=True)
    return spread * (scaled_grad - mean_grad - unit * mean_both)


def lane_sum(values):
    total = values[:, :TILE]
    for at in range(TILE, values.shape[1], TILE):
        total = total + values[:, at : at + TILE]
    return total


def call(body, grid, in_specs, out_specs, out_shape, scratch=(), flops=0, bytes_accessed=0, scalars=0):
    return pl.pallas_call(
        body,
        out_shape=out_shape,
        grid_spec=pltpu.PrefetchScalarGridSpec(
            num_scalar_prefetch=scalars,
            grid=grid,
            in_specs=in_specs,
            out_specs=out_specs,
            scratch_shapes=list(scratch),
        ),
        compiler_params=pltpu.CompilerParams(vmem_limit_bytes=VMEM_BYTES),
        cost_estimate=pl.CostEstimate(
            flops=flops, bytes_accessed=bytes_accessed, transcendentals=0
        ),
    )


def whole(shape):
    return pl.BlockSpec(shape, lambda *_: (0,) * len(shape))


def after(*arrays):
    return [pl.BlockSpec(memory_space=pl.ANY) for _ in arrays]


def split_parity(values):
    blocks = [values[:, at : at + TILE] for at in range(0, values.shape[1], TILE)]
    return jnp.concatenate(blocks[0::2], axis=1), jnp.concatenate(blocks[1::2], axis=1)


def join_parity(even, odd):
    blocks = []
    for at in range(0, even.shape[1], TILE):
        blocks += [even[:, at : at + TILE], odd[:, at : at + TILE]]
    return jnp.concatenate(blocks, axis=1)


def turn_rows(left, turned, parity):
    for block in range(turned.shape[0] // TILE):
        at = pl.multiple_of((2 * block + parity) * TILE, TILE)
        turned[block * TILE : (block + 1) * TILE, :] = jnp.transpose(left[:, pl.ds(at, TILE)])


def by_owner(values, plane):
    rows, columns = values.shape
    chips = rows // (8 * plane)
    values = values.reshape(chips, plane, 8, columns)
    return jnp.concatenate([values[chip] for chip in range(chips)], axis=1)


def project_body(
    core, tokens, vectors, own_qk, other_qk, own_vo, other_vo, normed, projected, parts
):
    part = pl.program_id(0)

    @pl.when(part == 0)
    def _():
        centered, spread = row_stats(tokens[...].astype(F32))
        low = (centered * spread * vectors[0:1, :] + vectors[1:2, :]).astype(BF16)
        normed[...] = low
        parts[0], parts[1] = split_parity(low)

    gate_q = jnp.where(part == 0, 1.0, 0.0).astype(F32)
    gate_v = jnp.where(part == 2, 1.0, 0.0).astype(F32)
    bias = gate_q * vectors[2:3, :] + gate_v * vectors[3:4, :]
    me = core[0]

    @pl.when(part < 2)
    def _():
        projected[...] = (
            dot_nn(parts[me], own_qk[...]) + dot_nn(parts[1 - me], other_qk[...]) + bias
        ).astype(BF16)

    @pl.when(part == 2)
    def _():
        projected[...] = (
            dot_nn(parts[me], own_vo[...]) + dot_nn(parts[1 - me], other_vo[...]) + bias
        ).astype(BF16)


def project(core, tokens, vectors, weights):
    rows, width = tokens.shape
    parts = 3
    third = pl.BlockSpec((width // 2, width), lambda part, *_: (0, jnp.minimum(part, 1)))
    last = pl.BlockSpec((width // 2, width), lambda part, *_: (0, 0))
    return call(
        project_body,
        (parts,),
        [whole((rows, width)), whole(vectors.shape), third, third, last, last],
        [whole((rows, width)), pl.BlockSpec((rows, width), lambda part, *_: (0, part))],
        [
            jax.ShapeDtypeStruct((rows, width), BF16),
            jax.ShapeDtypeStruct((rows, parts * width), BF16),
        ],
        scratch=[pltpu.VMEM((2, rows, width // 2), BF16)],
        flops=2 * rows * width * width * parts,
        bytes_accessed=2 * width * width * parts,
        scalars=1,
    )(core, tokens, vectors, *weights)


def attend_body(length, scales, queries, keys, values, mixed, scaled, weights):
    rows = queries.shape[0]
    head_dim = TILE // 2
    pair = pl.program_id(0)
    block = rows // 2
    lane = lax.broadcasted_iota(jnp.int32, (rows, TILE), 1)
    spot = lax.broadcasted_iota(jnp.int32, (rows, TILE), 0)
    hidden_key = jnp.where(spot < length[0], 0.0, -1e30).astype(BF16)
    one = jnp.ones((rows, TILE), BF16)
    zero = jnp.zeros((rows, TILE), BF16)
    query = queries[...] * jnp.asarray(1.0 / math.sqrt(head_dim), BF16)
    key = keys[...]
    value = values[...]
    causal = lax.broadcasted_iota(jnp.int32, (block, block), 1) <= lax.broadcasted_iota(
        jnp.int32, (block, block), 0
    )
    total = [jnp.zeros((block, TILE), F32) for _ in range(2)]
    for head in range(2):
        mine = (lane < head_dim) if head == 0 else (lane >= head_dim)
        spare = lane == (head_dim if head == 0 else 0)
        query_one = jnp.where(mine, query, jnp.where(spare, one, zero))
        key_one = jnp.where(mine, key, jnp.where(spare, hidden_key, zero))
        value_one = jnp.where(mine, value, zero)
        for part in range(2):
            seen = (part + 1) * block
            score = dot_nt(query_one[part * block : seen], key_one[:seen])
            last = jnp.where(causal, score[:, part * block :], -1e30)
            score = last if part == 0 else jnp.concatenate([score[:, :block], last], axis=1)
            top = jnp.max(score, axis=1, keepdims=True)
            grown = jnp.exp(score - top)
            share = (grown * (1.0 / jnp.sum(grown, axis=1, keepdims=True))).astype(BF16)
            if part == 0:
                weights[head, :, :block] = share
            else:
                weights[head, :, block:] = share
            total[part] = total[part] + dot_nn(share, value_one[:seen])
    scale_row = jnp.where(
        lax.broadcasted_iota(jnp.int32, (1, TILE), 1) < head_dim,
        scales[2 * pair],
        scales[2 * pair + 1],
    )
    for part in range(2):
        mixed[part * block : (part + 1) * block, :] = total[part]
        scaled[part * block : (part + 1) * block, :] = (total[part] * scale_row).astype(BF16)


def attend(length, scales, projected):
    rows, width3 = projected.shape
    width = width3 // 3
    pairs = width // TILE
    block = rows // 2
    return call(
        attend_body,
        (pairs,),
        [
            pl.BlockSpec((rows, TILE), lambda pair, *_: (0, pair)),
            pl.BlockSpec((rows, TILE), lambda pair, *_: (0, pairs + pair)),
            pl.BlockSpec((rows, TILE), lambda pair, *_: (0, 2 * pairs + pair)),
        ],
        [
            pl.BlockSpec((rows, TILE), lambda pair, *_: (0, pair)),
            pl.BlockSpec((rows, TILE), lambda pair, *_: (0, pair)),
            pl.BlockSpec((2, block, 3 * block), lambda pair, *_: (pair, 0, 0)),
        ],
        [
            jax.ShapeDtypeStruct((rows, width), F32),
            jax.ShapeDtypeStruct((rows, width), BF16),
            jax.ShapeDtypeStruct((2 * pairs, block, 3 * block), BF16),
        ],
        flops=4 * rows * rows * width,
        bytes_accessed=20 * rows * width,
        scalars=2,
    )(length, scales, projected, projected, projected)


def attend_back_body(
    core, queries, keys, values, mixed, grads, weights, normed, _, out, sent_q, sent_k, sent_v, turned
):
    @pl.when(pl.program_id(0) == 0)
    def _():
        turn_rows(normed, turned, 1 - core[0])

    rows = queries.shape[0]
    head_dim = TILE // 2
    block = rows // 2
    lane = lax.broadcasted_iota(jnp.int32, (rows, TILE), 1)
    zero = jnp.zeros((rows, TILE), BF16)
    query, key, value, grad = queries[...], keys[...], values[...], grads[...]
    both = grad.astype(F32) * mixed[...]
    q_total = [jnp.zeros((block, TILE), F32) for _ in range(2)]
    k_total = [jnp.zeros((block, TILE), F32) for _ in range(2)]
    v_total = [jnp.zeros((block, TILE), F32) for _ in range(2)]
    for head in range(2):
        mine = (lane < head_dim) if head == 0 else (lane >= head_dim)
        query_one = jnp.where(mine, query, zero)
        key_one = jnp.where(mine, key, zero)
        grad_one = jnp.where(mine, grad, zero)
        delta = jnp.sum(jnp.where(mine, both, 0.0), axis=1, keepdims=True)
        for part in range(2):
            at = part * block
            seen = at + block
            share = weights[head, :, :block] if part == 0 else weights[head, :, block:]
            into = dot_nt(grad_one[at:seen], value[:seen])
            slope = (share.astype(F32) * (into - delta[at:seen])).astype(BF16)
            q_total[part] = q_total[part] + dot_nn(slope, key_one[:seen])
            k_new = dot_tn(slope, query_one[at:seen])
            v_new = dot_tn(share, grad_one[at:seen])
            for into_part in range(part + 1):
                cut = slice(into_part * block, (into_part + 1) * block)
                k_total[into_part] = k_total[into_part] + k_new[cut]
                v_total[into_part] = v_total[into_part] + v_new[cut]
    root = 1.0 / math.sqrt(head_dim)
    low_q = (jnp.concatenate(q_total, axis=0) * root).astype(BF16)
    low_k = (jnp.concatenate(k_total, axis=0) * root).astype(BF16)
    low_v = jnp.concatenate(v_total, axis=0).astype(BF16)
    out[0], out[1], out[2] = low_q, low_k, low_v
    values = dot_nn(turned[...], jnp.concatenate([low_q, low_k, low_v], axis=1)).astype(BF16)
    for which, sent in enumerate((sent_q, sent_k, sent_v)):
        sent[...] = values[:, which * TILE : (which + 1) * TILE]


def attend_back(core, projected, mixed, grads, weights, normed, wait):
    rows, width3 = projected.shape
    width = width3 // 3
    half = width // 2
    pairs = width // TILE
    block = rows // 2
    by_pair = pl.BlockSpec((rows, TILE), lambda pair, *_: (0, pair))
    return call(
        attend_back_body,
        (pairs,),
        [
            by_pair,
            pl.BlockSpec((rows, TILE), lambda pair, *_: (0, pairs + pair)),
            pl.BlockSpec((rows, TILE), lambda pair, *_: (0, 2 * pairs + pair)),
            by_pair,
            by_pair,
            pl.BlockSpec((2, block, 3 * block), lambda pair, *_: (pair, 0, 0)),
            whole((rows, width)),
            *after(*wait),
        ],
        [
            pl.BlockSpec((3, rows, TILE), lambda pair, *_: (0, 0, pair)),
            *[pl.BlockSpec((half, TILE), lambda pair, *_: (0, pair)) for _ in range(3)],
        ],
        [
            jax.ShapeDtypeStruct((3, rows, width), BF16),
            *[jax.ShapeDtypeStruct((half, width), BF16) for _ in range(3)],
        ],
        scratch=[pltpu.VMEM((half, rows), BF16)],
        flops=10 * rows * rows * width,
        bytes_accessed=24 * rows * width,
        scalars=1,
    )(core, projected, projected, projected, mixed, grads, weights, normed, *wait)


def branch_body(core, scaled, own, other, tokens, vectors, branch, attended, normed, parts):
    parts[0], parts[1] = split_parity(scaled[...])
    me = core[0]
    value = dot_nn(parts[me], own[...]) + dot_nn(parts[1 - me], other[...]) + vectors[6:7, :]
    branch[...] = value
    centered, spread = row_stats(value)
    total = tokens[...].astype(F32) + centered * spread * vectors[4:5, :] + vectors[5:6, :]
    attended[...] = total
    centered, spread = row_stats(total)
    normed[...] = (centered * spread * vectors[7:8, :] + vectors[8:9, :]).astype(BF16)


def branch_out(core, scaled, weights, tokens, vectors):
    rows, width = scaled.shape
    block = rows // 4
    by_row = pl.BlockSpec((block, width), lambda at, *_: (at, 0))
    fourth = pl.BlockSpec((width // 2, width), lambda at, *_: (0, 1))
    return call(
        branch_body,
        (rows // block,),
        [by_row, fourth, fourth, by_row, whole(vectors.shape)],
        [by_row, by_row, by_row],
        [
            jax.ShapeDtypeStruct((rows, width), F32),
            jax.ShapeDtypeStruct((rows, width), F32),
            jax.ShapeDtypeStruct((rows, width), BF16),
        ],
        scratch=[pltpu.VMEM((2, block, width // 2), BF16)],
        flops=2 * rows * width * width,
        bytes_accessed=2 * width * width + 14 * rows * width,
        scalars=1,
    )(core, scaled, *weights[2:], tokens, vectors)


def branch_back_body(
    core,
    grad_attended,
    branch,
    own,
    other,
    mixed,
    scales,
    vectors,
    scaled,
    _,
    __,
    grad_branch,
    grad_mixed,
    sums,
    sent,
    staying,
    parts,
    lows,
    turned,
):
    at = pl.program_id(0)

    @pl.when(at == 0)
    def _():
        sums[...] = jnp.zeros_like(sums)

    grad = grad_attended[...]
    centered, spread = row_stats(branch[...])
    unit = centered * spread
    low = norm_back(grad * vectors[4:5, :], unit, spread).astype(BF16)
    grad_branch[...] = low
    lows[at] = low
    me = core[0]
    parts[me] = dot_nt(low, own[...])
    parts[1 - me] = dot_nt(low, other[...])
    grad_scaled = join_parity(parts[0], parts[1])
    grad_mixed[...] = (grad_scaled * scales[0:1, :]).astype(BF16)
    sums[0:1, :] += jnp.sum(grad * unit, axis=0, keepdims=True)
    sums[1:2, :] += jnp.sum(grad, axis=0, keepdims=True)
    sums[2:3, :] += jnp.sum(low.astype(F32), axis=0, keepdims=True)
    sums[3:4, :] += jnp.sum(grad_scaled * mixed[...], axis=0, keepdims=True)

    @pl.when(at == pl.num_programs(0) - 1)
    def _():
        right = lows[...].reshape(scaled.shape)
        turn_rows(scaled, turned, 1 - me)
        sent[...] = dot_nn(turned[...], right).astype(BF16)
        turn_rows(scaled, turned, me)
        staying[...] = dot_nn(turned[...], right)


def branch_back(core, grad_attended, branch, weights, mixed, scales, vectors, scaled, *wait):
    rows, width = branch.shape
    block = rows // 4
    by_row = pl.BlockSpec((block, width), lambda at, *_: (at, 0))
    fourth = pl.BlockSpec((width // 2, width), lambda at, *_: (0, 1))
    return call(
        branch_back_body,
        (rows // block,),
        [
            by_row,
            by_row,
            fourth,
            fourth,
            by_row,
            whole(scales.shape),
            whole(vectors.shape),
            whole(scaled.shape),
            *after(*wait),
        ],
        [by_row, by_row, whole((8, width)), whole((width // 2, width)), whole((width // 2, width))],
        [
            jax.ShapeDtypeStruct((rows, width), BF16),
            jax.ShapeDtypeStruct((rows, width), BF16),
            jax.ShapeDtypeStruct((8, width), F32),
            jax.ShapeDtypeStruct((width // 2, width), BF16),
            jax.ShapeDtypeStruct((width // 2, width), F32),
        ],
        scratch=[
            pltpu.VMEM((2, block, width // 2), F32),
            pltpu.VMEM((rows // block, block, width), BF16),
            pltpu.VMEM((width // 2, rows), BF16),
        ],
        flops=4 * rows * width * width,
        bytes_accessed=2 * width * width + 16 * rows * width,
        scalars=1,
    )(core, grad_attended, branch, *weights[2:], mixed, scales, vectors, scaled, *wait)


def send_part(values, step, first, second):
    @pl.when(step < 2)
    def _():
        first[...] = values.astype(BF16)

    @pl.when(step >= 2)
    def _():
        second[...] = by_owner(values, second.shape[0]).astype(BF16)


def part_specs(half, plane, start):
    return [
        pl.BlockSpec((half, 1024), lambda at, *_: (0, jnp.clip(at - start, 0, 1))),
        pl.BlockSpec(
            (plane, half // plane, 1024), lambda at, *_: (0, 0, jnp.clip(at - start - 2, 0, 1))
        ),
    ]


def part_shapes(half, plane):
    return [
        jax.ShapeDtypeStruct((half, 2048), BF16),
        jax.ShapeDtypeStruct((plane, half // plane, 2048), BF16),
    ]


def forward_ffn_body(
    steps,
    core,
    normed,
    attended,
    vectors,
    rows_of,
    up,
    down,
    upstream,
    output,
    top,
    kept,
    slope,
    stats,
    sent_first,
    sent_second,
    held,
    total,
    sums,
    turned,
):
    at = pl.program_id(0)
    width = held.shape[2]

    @pl.when(at == 0)
    def _():
        turn_rows(upstream, turned, 1 - core[0])
        sums[...] = jnp.zeros_like(sums)

    @pl.when(at < steps)
    def _():
        hidden = dot_nn(normed[...], up[...]) + rows_of[0:1, :]
        cdf = 0.5 + 0.5 * lax.erf(hidden * math.sqrt(0.5))
        value = hidden * cdf
        slope[...] = (
            cdf + hidden * (jnp.exp(-0.5 * hidden * hidden) * (1.0 / math.sqrt(2.0 * math.pi)))
        ).astype(BF16)
        held[at] = value
        kept[...] = value.astype(BF16)
        sums[...] += lane_sum(value)

    @pl.when(at == steps)
    def _():
        count = steps * width
        mean = jnp.sum(sums[...], axis=1, keepdims=True) * (1.0 / count)
        square = jnp.zeros(sums.shape, F32)
        for block in range(steps):
            centered = held[block] - mean
            square = square + lane_sum(centered * centered)
        spread = lax.rsqrt(jnp.sum(square, axis=1, keepdims=True) * (1.0 / count) + EPS)
        stats[:, :TILE] = jnp.broadcast_to(mean, sums.shape)
        stats[:, TILE:] = jnp.broadcast_to(spread, sums.shape)
        total[...] = attended[...] + vectors[21:22, :]

    @pl.when(at >= steps)
    def _():
        mean = stats[:, 0:1]
        spread = stats[:, TILE : TILE + 1]
        value = held[at - steps]
        low = ((value - mean) * spread * rows_of[1:2, :] + rows_of[2:3, :]).astype(BF16)
        top[...] = low
        total[...] += dot_nt(low, down[...])
        send_part(dot_nn(turned[...], low), at - steps, sent_first, sent_second)

    @pl.when(at == 2 * steps - 1)
    def _():
        output[...] = total[...].astype(BF16)


def forward_ffn(core, plane, normed, attended, vectors, wide_rows, both, upstream):
    rows, width = attended.shape
    hidden = both.shape[1] // 2
    block = 1024
    steps = hidden // block
    early = lambda at, *_: (0, jnp.minimum(at, steps - 1))
    late = lambda at, *_: (0, jnp.maximum(at - steps, 0))
    return call(
        functools.partial(forward_ffn_body, steps),
        (2 * steps,),
        [
            whole((rows, width)),
            whole((rows, width)),
            whole(vectors.shape),
            pl.BlockSpec((8, block), lambda at, *_: (0, lax.rem(at, steps))),
            pl.BlockSpec((width, block), early),
            pl.BlockSpec((width, block), lambda at, *_: (0, steps + jnp.maximum(at - steps, 0))),
            whole((rows, width)),
        ],
        [
            whole((rows, width)),
            pl.BlockSpec((rows, block), late),
            pl.BlockSpec((rows, block), early),
            pl.BlockSpec((rows, block), early),
            whole((rows, 2 * TILE)),
            *part_specs(width // 2, plane, steps),
        ],
        [
            jax.ShapeDtypeStruct((rows, width), BF16),
            jax.ShapeDtypeStruct((rows, hidden), BF16),
            jax.ShapeDtypeStruct((rows, hidden), BF16),
            jax.ShapeDtypeStruct((rows, hidden), BF16),
            jax.ShapeDtypeStruct((rows, 2 * TILE), F32),
            *part_shapes(width // 2, plane),
        ],
        scratch=[
            pltpu.VMEM((steps, rows, block), F32),
            pltpu.VMEM((rows, width), F32),
            pltpu.VMEM((rows, TILE), F32),
            pltpu.VMEM((width // 2, rows), BF16),
        ],
        flops=5 * rows * width * hidden,
        bytes_accessed=4 * width * hidden + 6 * rows * hidden,
        scalars=1,
    )(core, normed, attended, vectors, wide_rows, both, both, upstream)


def backward_ffn_body(
    steps,
    core,
    upstream,
    attended,
    vectors,
    rows_of,
    stats,
    kept,
    slope,
    down,
    up,
    normed,
    _,
    grad_attended,
    grad_hidden,
    wide_sums,
    sums,
    sent_first,
    sent_second,
    held,
    total,
    first,
    second,
    turned,
):
    at = pl.program_id(0)
    count = steps * held.shape[2]
    mean = stats[:, 0:1]
    spread = stats[:, TILE : TILE + 1]

    @pl.when(at == 0)
    def _():
        turn_rows(normed, turned, 1 - core[0])
        first[...] = jnp.zeros_like(first)
        second[...] = jnp.zeros_like(second)
        total[...] = jnp.zeros_like(total)
        wide_sums[...] = jnp.zeros_like(wide_sums)

    @pl.when(at < steps)
    def _():
        grad = dot_nn(upstream[...], down[...])
        unit = (kept[...].astype(F32) - mean) * spread
        both = grad * unit
        wide_sums[at, 0:1, :] = jnp.sum(both, axis=0, keepdims=True)
        wide_sums[at, 1:2, :] = jnp.sum(grad, axis=0, keepdims=True)
        gain = rows_of[1:2, :]
        held[at] = grad * gain
        first[...] += lane_sum(grad * gain)
        second[...] += lane_sum(both * gain)

    @pl.when(at == steps)
    def _():
        scale = 1.0 / count
        first[...] = jnp.broadcast_to(
            jnp.sum(first[...], axis=1, keepdims=True) * scale, first.shape
        )
        second[...] = jnp.broadcast_to(
            jnp.sum(second[...], axis=1, keepdims=True) * scale, second.shape
        )

    @pl.when(at >= steps)
    def _():
        unit = (kept[...].astype(F32) - mean) * spread
        grad = spread * (held[at - steps] - first[:, 0:1] - unit * second[:, 0:1])
        low = (grad * slope[...].astype(F32)).astype(BF16)
        grad_hidden[...] = low
        wide_sums[at - steps, 2:3, :] = jnp.sum(low.astype(F32), axis=0, keepdims=True)
        total[...] += dot_nt(low, up[...])
        send_part(dot_nn(turned[...], low), at - steps, sent_first, sent_second)

    @pl.when(at == 2 * steps - 1)
    def _():
        grad = total[...]
        centered, mid_spread = row_stats(attended[...])
        unit = centered * mid_spread
        top = upstream[...].astype(F32)
        grad_attended[...] = top + norm_back(grad * vectors[7:8, :], unit, mid_spread)
        sums[0:1, :] = jnp.sum(grad * unit, axis=0, keepdims=True)
        sums[1:2, :] = jnp.sum(grad, axis=0, keepdims=True)
        sums[2:3, :] = jnp.sum(top, axis=0, keepdims=True)
        sums[3:8, :] = jnp.zeros((5, sums.shape[1]), F32)


def backward_ffn(
    core, plane, upstream, attended, vectors, wide_rows, stats, kept, slope, both, normed, wait
):
    rows, width = attended.shape
    hidden = both.shape[1] // 2
    block = 1024
    steps = hidden // block
    late = lambda at, *_: (0, jnp.maximum(at - steps, 0))
    turn = lambda at, *_: (0, lax.rem(at, steps))
    return call(
        functools.partial(backward_ffn_body, steps),
        (2 * steps,),
        [
            whole((rows, width)),
            whole((rows, width)),
            whole(vectors.shape),
            pl.BlockSpec((8, block), turn),
            whole((rows, 2 * TILE)),
            pl.BlockSpec((rows, block), turn),
            pl.BlockSpec((rows, block), late),
            pl.BlockSpec((width, block), lambda at, *_: (0, steps + jnp.minimum(at, steps - 1))),
            pl.BlockSpec((width, block), late),
            whole((rows, width)),
            *after(wait),
        ],
        [
            whole((rows, width)),
            pl.BlockSpec((rows, block), late),
            whole((steps, 8, block)),
            whole((8, width)),
            *part_specs(width // 2, plane, steps),
        ],
        [
            jax.ShapeDtypeStruct((rows, width), F32),
            jax.ShapeDtypeStruct((rows, hidden), BF16),
            jax.ShapeDtypeStruct((steps, 8, block), F32),
            jax.ShapeDtypeStruct((8, width), F32),
            *part_shapes(width // 2, plane),
        ],
        scratch=[
            pltpu.VMEM((steps, rows, block), F32),
            pltpu.VMEM((rows, width), F32),
            pltpu.VMEM((rows, TILE), F32),
            pltpu.VMEM((rows, TILE), F32),
            pltpu.VMEM((width // 2, rows), BF16),
        ],
        flops=5 * rows * width * hidden,
        bytes_accessed=4 * width * hidden + 8 * rows * hidden,
        scalars=1,
    )(core, upstream, attended, vectors, wide_rows, stats, kept, slope, both, both, normed, wait)


def input_back_body(
    core,
    grads,
    own_qk,
    other_qk,
    own_vo,
    other_vo,
    tokens,
    grad_attended,
    vectors,
    branch_sums,
    mid_sums,
    wide_sums,
    _,
    input_grad,
    turned,
    parts,
    sums,
):
    part = pl.program_id(0)
    me = core[0]
    grad_part = grads[...]

    @pl.when(part == 0)
    def _():
        parts[me] = dot_nt(grad_part, own_qk[...])
        parts[1 - me] = dot_nt(grad_part, other_qk[...])
        sums[...] = jnp.zeros_like(sums)
        sums[2:3, :] = jnp.sum(grad_part.astype(F32), axis=0, keepdims=True)

    @pl.when(part == 1)
    def _():
        parts[me] += dot_nt(grad_part, own_qk[...])
        parts[1 - me] += dot_nt(grad_part, other_qk[...])

    @pl.when(part == 2)
    def _():
        parts[me] += dot_nt(grad_part, own_vo[...])
        parts[1 - me] += dot_nt(grad_part, other_vo[...])
        grad = join_parity(parts[0], parts[1])
        centered, spread = row_stats(tokens[...].astype(F32))
        unit = centered * spread
        input_grad[...] = grad_attended[...] + norm_back(grad * vectors[0:1, :], unit, spread)
        sums[0:1, :] = jnp.sum(grad * unit, axis=0, keepdims=True)
        sums[1:2, :] = jnp.sum(grad, axis=0, keepdims=True)
        sums[3:4, :] = jnp.sum(grad_part.astype(F32), axis=0, keepdims=True)
        sums[4:7, :] = branch_sums[0:3, :]
        sums[7:9, :] = mid_sums[0:2, :]
        for row in range(wide_sums.shape[0]):
            sums[9 + row : 10 + row, :] = wide_sums[row, 2:3, :]
            sums[13 + row : 14 + row, :] = wide_sums[row, 0:1, :]
            sums[17 + row : 18 + row, :] = wide_sums[row, 1:2, :]
        sums[21:22, :] = mid_sums[2:3, :]
        width = sums.shape[1]
        head_dim = TILE // 2
        picks = (
            lax.broadcasted_iota(jnp.int32, (width, TILE), 0) // head_dim + HEAD_AT
            == lax.broadcasted_iota(jnp.int32, (width, TILE), 1)
        ).astype(F32)
        heads = lax.dot_general(
            branch_sums[...],
            picks,
            (((1,), (0,)), ((), ())),
            precision=HIGHEST,
            preferred_element_type=F32,
        )[3:4, :]
        for block in range(turned.shape[0]):
            turned[block] = (
                jnp.transpose(sums[:, block * TILE : (block + 1) * TILE]) + heads
            )


def input_back(core, grads, weights, tokens, grad_attended, vectors, sums, wait):
    rows, width = tokens.shape
    full = whole((rows, width))
    third = pl.BlockSpec((width // 2, width), lambda part, *_: (0, jnp.minimum(part, 1)))
    last = pl.BlockSpec((width // 2, width), lambda part, *_: (0, 0))
    return call(
        input_back_body,
        (3,),
        [
            pl.BlockSpec((None, rows, width), lambda part, *_: (part, 0, 0)),
            third,
            third,
            last,
            last,
            full,
            full,
            whole(vectors.shape),
            *[whole(item.shape) for item in sums],
            *after(wait),
        ],
        [full, whole((width // TILE, TILE, TILE))],
        [
            jax.ShapeDtypeStruct((rows, width), F32),
            jax.ShapeDtypeStruct((width // TILE, TILE, TILE), F32),
        ],
        scratch=[pltpu.VMEM((2, rows, width // 2), F32), pltpu.VMEM((TILE, width), F32)],
        flops=6 * rows * width * width,
        bytes_accessed=6 * width * width + 16 * rows * width,
        scalars=1,
    )(core, grads, *weights, tokens, grad_attended, vectors, *sums, wait)


def outer_body(firsts, more, core, left, right, add_first, add_second, *refs):
    first, second, turned = refs[-3:]
    at = pl.program_id(0)

    @pl.when(at == 0)
    def _():
        turn_rows(left, turned, core[0])

    value = dot_nn(turned[...], right[...])

    @pl.when(at < firsts)
    def _():
        first[...] = (value + add_first[...].astype(F32)).astype(BF16)

    if more:

        @pl.when(at == firsts)
        def _():
            first[...] = (refs[0][...] + refs[1][...].astype(F32)).astype(BF16)

    @pl.when(at >= firsts)
    def _():
        second[...] = (
            by_owner(value, second.shape[0]) + add_second[...].astype(F32)
        ).astype(BF16)


def outer(core, left, right, add, wait=(), more=()):
    rows, width = left.shape
    half = width // 2
    block = 1024
    add_first, add_second = add
    plane, owned = add_second.shape[:2]
    firsts = 2
    seconds = add_second.shape[2] // block
    right_spec = pl.BlockSpec((rows, block), lambda at, *_: (0, at))
    add_spec = pl.BlockSpec((half, block), lambda at, *_: (0, jnp.clip(at, 0, 1)))
    second_spec = pl.BlockSpec(
        (plane, owned, block), lambda at, *_: (0, 0, jnp.clip(at - firsts, 0, seconds - 1))
    )
    kinds = firsts + len(more) // 2
    out_specs = [
        pl.BlockSpec((half, block), lambda at, *_: (0, jnp.clip(at, 0, kinds - 1))),
        second_spec,
    ]
    out_shape = [
        jax.ShapeDtypeStruct((half, kinds * block), BF16),
        jax.ShapeDtypeStruct(add_second.shape, BF16),
    ]
    return call(
        functools.partial(outer_body, firsts, len(more) > 0),
        (firsts + seconds,),
        [
            whole((rows, width)),
            right_spec,
            add_spec,
            second_spec,
            *[whole(item.shape) for item in more],
            *after(*wait),
        ],
        out_specs,
        out_shape,
        scratch=[pltpu.VMEM((half, rows), BF16)],
        flops=2 * rows * half * block * (firsts + seconds),
        bytes_accessed=6 * half * block * (firsts + seconds),
        scalars=1,
    )(core, left, right, add_first, add_second, *more, *wait)


def outer_stack_body(core, left, right, *refs):
    adds, (out, turned) = refs[:3], refs[-2:]
    at = pl.program_id(0)

    @pl.when(at == 0)
    def _():
        turn_rows(left, turned, core[0])

    value = dot_nn(turned[...], right[...])
    for which, add in enumerate(adds):

        @pl.when(at == which)
        def _(add=add):
            out[...] = (value + add[...].astype(F32)).astype(BF16)


def outer_stack(core, left, rights, adds, *wait):
    count, rows, width = rights.shape
    half = width // 2
    return call(
        outer_stack_body,
        (count,),
        [
            whole((rows, width)),
            pl.BlockSpec((None, rows, width), lambda at, *_: (at, 0, 0)),
            *[whole((half, width)) for _ in adds],
            *after(*wait),
        ],
        pl.BlockSpec((half, width), lambda at, *_: (0, at)),
        jax.ShapeDtypeStruct((half, count * width), BF16),
        scratch=[pltpu.VMEM((half, rows), BF16)],
        flops=2 * rows * half * width * count,
        bytes_accessed=6 * half * width * count,
        scalars=1,
    )(core, left, rights, *adds, *wait)


def to_slots_body(perm, early, late, rest, *refs):
    grad_qkv, grad_out, grad_up, grad_down, slots, tiles = refs
    width = grad_out.shape[1]
    half = 2 * width
    grad_out[...] = early[:, half : half + width]
    grad_qkv[...] = late[:, : 3 * width]
    grad_down[:, :half] = early[:, half + width :]
    grad_down[:, half:] = rest[:, :half]
    grad_up[:, :half] = early[:, :half]
    grad_up[:, half:] = rest[:, half : 2 * half]
    column = 0
    for result in (grad_qkv, grad_out, grad_up, grad_down):
        for at in range(0, result.shape[1], TILE):
            tiles[column] = result[:, at : at + TILE]
            column += 1
    planes, pairs = slots.shape[:2]
    for slot in range(planes * pairs):
        pair = [tiles[perm[2 * slot + which]] for which in range(2)]
        slots[slot // pairs, slot % pairs] = jnp.concatenate(pair, axis=0).astype(BF16)


def to_slots(perm, early, late, rest, plane, widths):
    arrays = [early, late, rest]
    pairs = perm.shape[0] // (2 * plane)
    shapes = [jax.ShapeDtypeStruct((8, columns), F32) for columns in widths]
    shapes.append(jax.ShapeDtypeStruct((plane, pairs, 16, TILE), BF16))
    return call(
        to_slots_body,
        (1,),
        [whole(item.shape) for item in arrays],
        [whole(item.shape) for item in shapes],
        shapes,
        scratch=[pltpu.VMEM((perm.shape[0], 8, TILE), F32)],
        bytes_accessed=8 * 8 * sum(widths),
        scalars=1,
    )(perm, *arrays)


def update_body(grads, left_stats, right_stats, left_roots, right_roots, left_new, right_new, back):
    planes, pairs = grads.shape[:2]
    for pair in range(pairs):
        block = grads[:, pair].astype(F32)
        moved = []
        for which in range(2):
            slot = 2 * pair + which
            grad = block[:, which * 8 : which * 8 + 8, :].reshape(TILE, TILE)
            low = grad.astype(BF16)
            left_new[slot] = DECAY * left_stats[slot] + (1.0 - DECAY) * dot_nt(low, low)
            right_new[slot] = DECAY * right_stats[slot] + (1.0 - DECAY) * dot_tn(low, low)
            step = jnp.dot(grad, right_roots[slot], precision=HIGHEST, preferred_element_type=F32)
            step = jnp.dot(left_roots[slot], step, precision=HIGHEST, preferred_element_type=F32)
            moved.append(step.reshape(planes, 8, TILE))
        back[:, pair] = jnp.concatenate(moved, axis=1).astype(BF16)


def update(grads, left_stats, right_stats, left_roots, right_roots):
    arrays = [item[0] for item in (left_stats, right_stats, left_roots, right_roots)]
    stats = jax.ShapeDtypeStruct(arrays[0].shape, F32)
    left_new, right_new, back = call(
        update_body,
        (1,),
        [whole(grads.shape)] + [whole(item.shape) for item in arrays],
        [whole(stats.shape), whole(stats.shape), whole(grads.shape)],
        [stats, stats, jax.ShapeDtypeStruct(grads.shape, BF16)],
        bytes_accessed=24 * arrays[0].size,
    )(grads, *arrays)
    return left_new[None], right_new[None], back


def apply_body(perm, moved, *refs):
    olds, news, tiles = refs[:4], refs[4:8], refs[8]
    pairs = moved.shape[1]
    for slot in range(moved.shape[0] * pairs):
        value = moved[slot // pairs, slot % pairs].astype(F32)
        tiles[perm[2 * slot]] = value[:8]
        tiles[perm[2 * slot + 1]] = value[8:]
    column = 0
    for old, new in zip(olds, news):
        for at in range(0, old.shape[1], TILE):
            cut = slice(at, at + TILE)
            new[:, cut] = old[:, cut] - RATE_MATRIX * tiles[column]
            column += 1


def apply_steps(perm, moved, weights):
    shapes = [jax.ShapeDtypeStruct(item.shape, F32) for item in weights]
    return call(
        apply_body,
        (1,),
        [whole(moved.shape)] + [whole(item.shape) for item in weights],
        [whole(item.shape) for item in shapes],
        shapes,
        scratch=[pltpu.VMEM((perm.shape[0], 8, TILE), F32)],
        bytes_accessed=10 * 8 * TILE * perm.shape[0],
        scalars=1,
    )(perm, moved, *weights)


def swap_cores(values):
    return lax.ppermute(values, "core", [(0, 1), (1, 0)])


def turn_chips(values, step):
    count = lax.axis_size("x")
    return lax.ppermute(values, "x", [(at, (at + step) % count) for at in range(count)])


def sum_parts(parts):
    return jnp.sum(parts.astype(F32), axis=0)


def shards(
    tokens,
    cotangent,
    lengths,
    valid,
    owner_perm,
    w_qkv,
    w_out,
    w_up,
    w_down,
    vectors,
    head_scale,
    left_stats,
    right_stats,
    left_roots,
    right_roots,
    vector_stats,
    head_stats,
):
    rows, width = tokens.shape
    heads = head_scale.shape[0]
    hidden = w_up.shape[1]
    ratio = hidden // width
    shard = w_up.shape[0]
    plane = lax.axis_size("fsdp")
    chips = lax.axis_size("x")
    core = lax.axis_index("core")
    core_arg = core.astype(jnp.int32).reshape(1)

    both = lax.all_gather(
        jnp.concatenate([w_up.astype(BF16), w_down.astype(BF16)], axis=1),
        ("x", "core", "fsdp"),
        axis=0,
        tiled=True,
    )
    low_qk = jnp.concatenate(
        [
            w_qkv[:, : 2 * width].astype(BF16),
            jnp.pad(vectors.astype(BF16).T, ((0, 0), (0, TILE - vectors.shape[0]))),
        ],
        axis=1,
    )
    low_vo = jnp.concatenate([w_qkv[:, 2 * width :].astype(BF16), w_out.astype(BF16)], axis=1)

    def to_plane(part, concat):
        spread = jnp.broadcast_to(part[None], (plane,) + part.shape)
        return lax.all_to_all(spread, "fsdp", split_axis=0, concat_axis=concat, tiled=True)

    place = lax.axis_index("x")

    def roll_chips(parts, start):
        twice = jnp.concatenate([parts, parts], axis=0)
        begin = [start] + [0] * (parts.ndim - 1)
        return lax.dynamic_slice(twice, begin, parts.shape, allow_negative_indices=False)

    def in_order(parts):
        return roll_chips(jnp.stack(parts[::-1]), chips - 1 - place)

    def to_chips(part):
        return in_order([part] + [turn_chips(part, step) for step in range(1, chips)])

    def across_chips(parts):
        ahead = roll_chips(parts, place)
        return [ahead[0]] + [turn_chips(ahead[step], step) for step in range(1, chips)]

    own_vo = to_plane(to_chips(low_vo), 2).reshape(width // 2, -1)
    own_qk = to_chips(to_plane(low_qk, 0).reshape(plane * shard, -1)).reshape(width // 2, -1)
    other_qk, other_vo = swap_cores(own_qk), swap_cores(own_vo)
    weights = (own_qk, other_qk, own_vo, other_vo)
    vector_at = 2 * width
    vector_pair = jnp.stack([own_qk[:, vector_at:], other_qk[:, vector_at:]])
    vector_pair = jnp.where(core == 0, vector_pair, vector_pair[::-1])
    vector_rows = (
        vector_pair.reshape(2, -1, TILE, TILE)
        .transpose(1, 0, 2, 3)
        .reshape(width, TILE)
        .T[:24]
        .astype(F32)
    )
    wide_rows = jnp.concatenate(
        [
            vector_rows[9 : 9 + 3 * ratio].reshape(3, hidden),
            jnp.zeros((5, hidden), F32),
        ],
        axis=0,
    )
    upstream = jnp.where(valid[:, None] != 0, cotangent, jnp.zeros_like(cotangent))
    scales = jnp.broadcast_to(jnp.repeat(head_scale, width // heads)[None], (8, width))

    normed, projected = project(core_arg, tokens, vector_rows, weights)
    mixed, scaled, attention = attend(lengths, head_scale, projected)
    branch, attended, normed_mid = branch_out(core_arg, scaled, weights, tokens, vector_rows)
    output, normed_top, kept, slope, stats, *sent_down = forward_ffn(
        core_arg, plane, normed_mid, attended, vector_rows, wide_rows, both, upstream
    )

    def over_x(part):
        return lax.psum_scatter(part, "x", scatter_dimension=0, tiled=True)

    def over_plane(part):
        return sum_parts(
            lax.all_to_all(
                part.reshape(plane, shard, -1), "fsdp", split_axis=0, concat_axis=0, tiled=True
            )
        )

    def plane_first(part):
        total = lax.all_to_all(part, "fsdp", split_axis=0, concat_axis=0, tiled=True)
        return sum_parts(total)

    down_first, down_second = outer(
        core_arg, upstream, normed_top, [swap_cores(part) for part in sent_down]
    )
    down_rest = plane_first(down_second)
    down_chips = over_x(down_first)
    grad_attended, grad_hidden, wide_sums, mid_sums, *sent_up = backward_ffn(
        core_arg,
        plane,
        upstream,
        attended,
        vector_rows,
        wide_rows,
        stats,
        kept,
        slope,
        both,
        normed_mid,
        down_second,
    )
    grad_branch, grad_mixed, branch_sums, out_sent, out_stays = branch_back(
        core_arg,
        grad_attended,
        branch,
        weights,
        mixed,
        scales,
        vector_rows,
        scaled,
        down_rest,
        down_chips,
    )
    up_first, up_second = outer(
        core_arg,
        normed_mid,
        grad_hidden,
        [swap_cores(part) for part in sent_up],
        wait=(grad_branch,),
        more=(out_stays, swap_cores(out_sent)),
    )
    up_rest = plane_first(up_second)
    up_chips = over_x(up_first)
    grads, *sent_attn = attend_back(
        core_arg,
        projected,
        mixed,
        grad_mixed,
        attention,
        normed,
        (up_second,),
    )
    input_grad, turned = input_back(
        core_arg,
        grads,
        weights,
        tokens,
        grad_attended,
        vector_rows,
        (branch_sums, mid_sums, wide_sums),
        up_second,
    )

    turned = turned.reshape(chips, 2, TILE, TILE)
    kept_sums = lax.dynamic_slice_in_dim(turned, core, 1, 1, allow_negative_indices=False)[:, 0]
    sent_sums = lax.dynamic_slice_in_dim(
        turned, 1 - core, 1, 1, allow_negative_indices=False
    )[:, 0]
    half_sums = kept_sums + swap_cores(sent_sums)
    attn_first = outer_stack(
        core_arg, normed, grads, [swap_cores(part) for part in sent_attn], half_sums, up_rest
    )
    half_sums, _ = lax.optimization_barrier((half_sums, attn_first))
    small = jnp.sum(in_order(across_chips(half_sums)), axis=0)

    early_parts = over_plane(jnp.concatenate([up_chips, down_chips], axis=1))
    rest = jnp.concatenate([down_rest, up_rest], axis=1)
    rest = across_chips(rest.astype(BF16).reshape(chips, shard, -1))
    rest = sum(part.astype(F32) for part in rest)
    late_parts = over_plane(jnp.concatenate([over_x(attn_first), small.astype(BF16)], axis=1))
    small = late_parts[:, 3 * width :]
    vector_grads = small.T[: vectors.shape[0]]
    head_total = small[0, HEAD_AT : HEAD_AT + heads]

    masters = (w_qkv, w_out, w_up, w_down)
    grad_qkv, grad_out, grad_up, grad_down, slots = to_slots(
        owner_perm,
        early_parts,
        late_parts,
        rest,
        plane,
        [item.shape[1] for item in masters],
    )
    slots = lax.all_to_all(slots, "fsdp", split_axis=0, concat_axis=0, tiled=True)
    left_new, right_new, back = update(slots, left_stats, right_stats, left_roots, right_roots)
    back = lax.all_to_all(back, "fsdp", split_axis=0, concat_axis=0, tiled=True)
    new_qkv, new_out, new_up, new_down = apply_steps(owner_perm, back, masters)
    vector_stats_new = DECAY * vector_stats + (1.0 - DECAY) * vector_grads * vector_grads
    vectors_new = vectors - RATE_VECTOR * vector_grads * lax.rsqrt(vector_stats_new)
    head_stats_new = DECAY * head_stats + (1.0 - DECAY) * head_total * head_total
    head_new = head_scale - RATE_VECTOR * head_total * lax.rsqrt(head_stats_new)
    return (
        output,
        input_grad,
        grad_qkv,
        grad_out,
        grad_up,
        grad_down,
        vector_grads,
        head_total,
        left_new,
        right_new,
        new_qkv,
        new_out,
        new_up,
        new_down,
        vector_stats_new,
        vectors_new,
        head_stats_new,
        head_new,
    )


def solution(mesh):
    everywhere = ("x", "core", "fsdp")
    by_rows = P(everywhere, None)
    by_columns = P(None, everywhere)
    by_block = P(("x", "core"), "fsdp", None, None)
    dp, fsdp = mesh.devices.shape
    mesh = jax.sharding.Mesh(mesh.devices.reshape(dp // 2, 2, fsdp), everywhere)
    return jax.shard_map(
        shards,
        mesh=mesh,
        in_specs=(
            (by_rows, by_rows, P(everywhere), P(everywhere), P())
            + (by_rows,) * 4
            + (by_columns, P())
            + (by_block,) * 4
            + (by_columns, P())
        ),
        out_specs=(
            (by_rows,) * 6
            + (by_columns, P())
            + (by_block,) * 2
            + (by_rows,) * 4
            + (by_columns, by_columns, P(), P())
        ),
        check_vma=False,
    )
```

```python
import functools
import math

import jax
import jax.numpy as jnp
from jax import lax
from jax.experimental import pallas as pl
from jax.experimental.pallas import tpu as pltpu
from jax.sharding import PartitionSpec as P

TILE = 128
EPS = 1e-05
DECAY = 0.5
RATE_MATRIX = 0.1
RATE_VECTOR = 0.3
HIGHEST = lax.Precision.HIGHEST
HEAD_AT = 24
DOWN_FIRSTS = 3
UP_FIRSTS = 2
VMEM_BYTES = 56 * 1024 * 1024
F32 = jnp.float32
BF16 = jnp.bfloat16


def dot_nn(left, right):
    return lax.dot_general(left, right, (((1,), (0,)), ((), ())), preferred_element_type=F32)


def dot_nt(left, right):
    return lax.dot_general(left, right, (((1,), (1,)), ((), ())), preferred_element_type=F32)


def dot_tn(left, right):
    return lax.dot_general(left, right, (((0,), (0,)), ((), ())), preferred_element_type=F32)


def row_stats(values):
    mean = jnp.mean(values, axis=-1, keepdims=True)
    centered = values - mean
    spread = lax.rsqrt(jnp.mean(centered * centered, axis=-1, keepdims=True) + EPS)
    return centered, spread


def norm_back(scaled_grad, unit, spread):
    mean_grad = jnp.mean(scaled_grad, axis=-1, keepdims=True)
    mean_both = jnp.mean(scaled_grad * unit, axis=-1, keepdims=True)
    return spread * (scaled_grad - mean_grad - unit * mean_both)


def lane_sum(values):
    total = values[:, :TILE]
    for at in range(TILE, values.shape[1], TILE):
        total = total + values[:, at : at + TILE]
    return total


def call(body, grid, in_specs, out_specs, out_shape, scratch=(), flops=0, bytes_accessed=0, scalars=0):
    return pl.pallas_call(
        body,
        out_shape=out_shape,
        grid_spec=pltpu.PrefetchScalarGridSpec(
            num_scalar_prefetch=scalars,
            grid=grid,
            in_specs=in_specs,
            out_specs=out_specs,
            scratch_shapes=list(scratch),
        ),
        compiler_params=pltpu.CompilerParams(vmem_limit_bytes=VMEM_BYTES),
        cost_estimate=pl.CostEstimate(
            flops=flops, bytes_accessed=bytes_accessed, transcendentals=0
        ),
    )


def whole(shape):
    return pl.BlockSpec(shape, lambda *_: (0,) * len(shape))


def after(*arrays):
    return [pl.BlockSpec(memory_space=pl.ANY) for _ in arrays]


def split_parity(values):
    blocks = [values[:, at : at + TILE] for at in range(0, values.shape[1], TILE)]
    return jnp.concatenate(blocks[0::2], axis=1), jnp.concatenate(blocks[1::2], axis=1)


def join_parity(even, odd):
    blocks = []
    for at in range(0, even.shape[1], TILE):
        blocks += [even[:, at : at + TILE], odd[:, at : at + TILE]]
    return jnp.concatenate(blocks, axis=1)


def turn_rows(left, turned, parity):
    for block in range(turned.shape[0] // TILE):
        at = pl.multiple_of((2 * block + parity) * TILE, TILE)
        turned[block * TILE : (block + 1) * TILE, :] = jnp.transpose(left[:, pl.ds(at, TILE)])


def turn_all(left, turned):
    for at in range(0, turned.shape[0], TILE):
        turned[at : at + TILE, :] = jnp.transpose(left[:, at : at + TILE])


def by_owner(values, plane):
    rows, columns = values.shape
    chips = rows // (8 * plane)
    values = values.reshape(chips, plane, 8, columns)
    return jnp.concatenate([values[chip] for chip in range(chips)], axis=1)


def project_body(
    core, tokens, vectors, own_qk, other_qk, own_vo, other_vo, normed, projected, parts
):
    part = pl.program_id(0)

    @pl.when(part == 0)
    def _():
        centered, spread = row_stats(tokens[...].astype(F32))
        low = (centered * spread * vectors[0:1, :] + vectors[1:2, :]).astype(BF16)
        normed[...] = low
        parts[0], parts[1] = split_parity(low)

    gate_q = jnp.where(part == 0, 1.0, 0.0).astype(F32)
    gate_v = jnp.where(part == 2, 1.0, 0.0).astype(F32)
    bias = gate_q * vectors[2:3, :] + gate_v * vectors[3:4, :]
    me = core[0]

    @pl.when(part < 2)
    def _():
        projected[...] = (
            dot_nn(parts[me], own_qk[...]) + dot_nn(parts[1 - me], other_qk[...]) + bias
        ).astype(BF16)

    @pl.when(part == 2)
    def _():
        projected[...] = (
            dot_nn(parts[me], own_vo[...]) + dot_nn(parts[1 - me], other_vo[...]) + bias
        ).astype(BF16)


def project(core, tokens, vectors, weights):
    rows, width = tokens.shape
    parts = 3
    third = pl.BlockSpec((width // 2, width), lambda part, *_: (0, jnp.minimum(part, 1)))
    last = pl.BlockSpec((width // 2, width), lambda part, *_: (0, 0))
    return call(
        project_body,
        (parts,),
        [whole((rows, width)), whole(vectors.shape), third, third, last, last],
        [whole((rows, width)), pl.BlockSpec((rows, width), lambda part, *_: (0, part))],
        [
            jax.ShapeDtypeStruct((rows, width), BF16),
            jax.ShapeDtypeStruct((rows, parts * width), BF16),
        ],
        scratch=[pltpu.VMEM((2, rows, width // 2), BF16)],
        flops=2 * rows * width * width * parts,
        bytes_accessed=2 * width * width * parts,
        scalars=1,
    )(core, tokens, vectors, *weights)


def attend_body(length, scales, queries, keys, values, mixed, scaled, weights):
    rows = queries.shape[0]
    head_dim = TILE // 2
    pair = pl.program_id(0)
    block = rows // 2
    lane = lax.broadcasted_iota(jnp.int32, (rows, TILE), 1)
    spot = lax.broadcasted_iota(jnp.int32, (rows, TILE), 0)
    hidden_key = jnp.where(spot < length[0], 0.0, -1e30).astype(BF16)
    one = jnp.ones((rows, TILE), BF16)
    zero = jnp.zeros((rows, TILE), BF16)
    query = queries[...] * jnp.asarray(1.0 / math.sqrt(head_dim), BF16)
    key = keys[...]
    value = values[...]
    causal = lax.broadcasted_iota(jnp.int32, (block, block), 1) <= lax.broadcasted_iota(
        jnp.int32, (block, block), 0
    )
    total = [jnp.zeros((block, TILE), F32) for _ in range(2)]
    for head in range(2):
        mine = (lane < head_dim) if head == 0 else (lane >= head_dim)
        spare = lane == (head_dim if head == 0 else 0)
        query_one = jnp.where(mine, query, jnp.where(spare, one, zero))
        key_one = jnp.where(mine, key, jnp.where(spare, hidden_key, zero))
        value_one = jnp.where(mine, value, zero)
        for part in range(2):
            seen = (part + 1) * block
            score = dot_nt(query_one[part * block : seen], key_one[:seen])
            last = jnp.where(causal, score[:, part * block :], -1e30)
            score = last if part == 0 else jnp.concatenate([score[:, :block], last], axis=1)
            top = jnp.max(score, axis=1, keepdims=True)
            grown = jnp.exp(score - top)
            share = (grown * (1.0 / jnp.sum(grown, axis=1, keepdims=True))).astype(BF16)
            if part == 0:
                weights[head, :, :block] = share
            else:
                weights[head, :, block:] = share
            total[part] = total[part] + dot_nn(share, value_one[:seen])
    scale_row = jnp.where(
        lax.broadcasted_iota(jnp.int32, (1, TILE), 1) < head_dim,
        scales[2 * pair],
        scales[2 * pair + 1],
    )
    for part in range(2):
        mixed[part * block : (part + 1) * block, :] = total[part]
        scaled[part * block : (part + 1) * block, :] = (total[part] * scale_row).astype(BF16)


def attend(length, scales, projected):
    rows, width3 = projected.shape
    width = width3 // 3
    pairs = width // TILE
    block = rows // 2
    return call(
        attend_body,
        (pairs,),
        [
            pl.BlockSpec((rows, TILE), lambda pair, *_: (0, pair)),
            pl.BlockSpec((rows, TILE), lambda pair, *_: (0, pairs + pair)),
            pl.BlockSpec((rows, TILE), lambda pair, *_: (0, 2 * pairs + pair)),
        ],
        [
            pl.BlockSpec((rows, TILE), lambda pair, *_: (0, pair)),
            pl.BlockSpec((rows, TILE), lambda pair, *_: (0, pair)),
            pl.BlockSpec((2, block, 3 * block), lambda pair, *_: (pair, 0, 0)),
        ],
        [
            jax.ShapeDtypeStruct((rows, width), F32),
            jax.ShapeDtypeStruct((rows, width), BF16),
            jax.ShapeDtypeStruct((2 * pairs, block, 3 * block), BF16),
        ],
        flops=4 * rows * rows * width,
        bytes_accessed=20 * rows * width,
        scalars=2,
    )(length, scales, projected, projected, projected)


def attend_back_body(
    core, queries, keys, values, mixed, grads, weights, normed, _, __, out, sent_q, sent_k, sent_v, turned
):
    @pl.when(pl.program_id(0) == 0)
    def _():
        turn_rows(normed, turned, 1 - core[0])

    rows = queries.shape[0]
    head_dim = TILE // 2
    block = rows // 2
    lane = lax.broadcasted_iota(jnp.int32, (rows, TILE), 1)
    zero = jnp.zeros((rows, TILE), BF16)
    query, key, value, grad = queries[...], keys[...], values[...], grads[...]
    both = grad.astype(F32) * mixed[...]
    q_total = [jnp.zeros((block, TILE), F32) for _ in range(2)]
    k_total = [jnp.zeros((block, TILE), F32) for _ in range(2)]
    v_total = [jnp.zeros((block, TILE), F32) for _ in range(2)]
    for head in range(2):
        mine = (lane < head_dim) if head == 0 else (lane >= head_dim)
        query_one = jnp.where(mine, query, zero)
        key_one = jnp.where(mine, key, zero)
        grad_one = jnp.where(mine, grad, zero)
        delta = jnp.sum(jnp.where(mine, both, 0.0), axis=1, keepdims=True)
        for part in range(2):
            at = part * block
            seen = at + block
            share = weights[head, :, :block] if part == 0 else weights[head, :, block:]
            into = dot_nt(grad_one[at:seen], value[:seen])
            slope = (share.astype(F32) * (into - delta[at:seen])).astype(BF16)
            q_total[part] = q_total[part] + dot_nn(slope, key_one[:seen])
            k_new = dot_tn(slope, query_one[at:seen])
            v_new = dot_tn(share, grad_one[at:seen])
            for into_part in range(part + 1):
                cut = slice(into_part * block, (into_part + 1) * block)
                k_total[into_part] = k_total[into_part] + k_new[cut]
                v_total[into_part] = v_total[into_part] + v_new[cut]
    root = 1.0 / math.sqrt(head_dim)
    low_q = (jnp.concatenate(q_total, axis=0) * root).astype(BF16)
    low_k = (jnp.concatenate(k_total, axis=0) * root).astype(BF16)
    low_v = jnp.concatenate(v_total, axis=0).astype(BF16)
    out[0], out[1], out[2] = low_q, low_k, low_v
    values = dot_nn(turned[...], jnp.concatenate([low_q, low_k, low_v], axis=1)).astype(BF16)
    for which, sent in enumerate((sent_q, sent_k, sent_v)):
        sent[...] = values[:, which * TILE : (which + 1) * TILE]


def attend_back(core, projected, mixed, grads, weights, normed, wait):
    rows, width3 = projected.shape
    width = width3 // 3
    half = width // 2
    pairs = width // TILE
    block = rows // 2
    by_pair = pl.BlockSpec((rows, TILE), lambda pair, *_: (0, pair))
    return call(
        attend_back_body,
        (pairs,),
        [
            by_pair,
            pl.BlockSpec((rows, TILE), lambda pair, *_: (0, pairs + pair)),
            pl.BlockSpec((rows, TILE), lambda pair, *_: (0, 2 * pairs + pair)),
            by_pair,
            by_pair,
            pl.BlockSpec((2, block, 3 * block), lambda pair, *_: (pair, 0, 0)),
            whole((rows, width)),
            *after(*wait),
        ],
        [
            pl.BlockSpec((3, rows, TILE), lambda pair, *_: (0, 0, pair)),
            *[pl.BlockSpec((half, TILE), lambda pair, *_: (0, pair)) for _ in range(3)],
        ],
        [
            jax.ShapeDtypeStruct((3, rows, width), BF16),
            *[jax.ShapeDtypeStruct((half, width), BF16) for _ in range(3)],
        ],
        scratch=[pltpu.VMEM((half, rows), BF16)],
        flops=10 * rows * rows * width,
        bytes_accessed=24 * rows * width,
        scalars=1,
    )(core, projected, projected, projected, mixed, grads, weights, normed, *wait)


def branch_body(core, scaled, own, other, tokens, vectors, branch, attended, normed, parts):
    parts[0], parts[1] = split_parity(scaled[...])
    me = core[0]
    value = dot_nn(parts[me], own[...]) + dot_nn(parts[1 - me], other[...]) + vectors[6:7, :]
    branch[...] = value
    centered, spread = row_stats(value)
    total = tokens[...].astype(F32) + centered * spread * vectors[4:5, :] + vectors[5:6, :]
    attended[...] = total
    centered, spread = row_stats(total)
    normed[...] = (centered * spread * vectors[7:8, :] + vectors[8:9, :]).astype(BF16)


def branch_out(core, scaled, weights, tokens, vectors):
    rows, width = scaled.shape
    block = rows // 4
    by_row = pl.BlockSpec((block, width), lambda at, *_: (at, 0))
    fourth = pl.BlockSpec((width // 2, width), lambda at, *_: (0, 1))
    return call(
        branch_body,
        (rows // block,),
        [by_row, fourth, fourth, by_row, whole(vectors.shape)],
        [by_row, by_row, by_row],
        [
            jax.ShapeDtypeStruct((rows, width), F32),
            jax.ShapeDtypeStruct((rows, width), F32),
            jax.ShapeDtypeStruct((rows, width), BF16),
        ],
        scratch=[pltpu.VMEM((2, block, width // 2), BF16)],
        flops=2 * rows * width * width,
        bytes_accessed=2 * width * width + 14 * rows * width,
        scalars=1,
    )(core, scaled, *weights[2:], tokens, vectors)


def branch_back_body(
    core,
    grad_attended,
    branch,
    own,
    other,
    mixed,
    scales,
    vectors,
    scaled,
    grad_branch,
    grad_mixed,
    sums,
    sent,
    staying,
    parts,
    lows,
    turned,
):
    at = pl.program_id(0)

    @pl.when(at == 0)
    def _():
        sums[...] = jnp.zeros_like(sums)

    grad = grad_attended[...]
    centered, spread = row_stats(branch[...])
    unit = centered * spread
    low = norm_back(grad * vectors[4:5, :], unit, spread).astype(BF16)
    grad_branch[...] = low
    lows[at] = low
    me = core[0]
    parts[me] = dot_nt(low, own[...])
    parts[1 - me] = dot_nt(low, other[...])
    grad_scaled = join_parity(parts[0], parts[1])
    grad_mixed[...] = (grad_scaled * scales[0:1, :]).astype(BF16)
    sums[0:1, :] += jnp.sum(grad * unit, axis=0, keepdims=True)
    sums[1:2, :] += jnp.sum(grad, axis=0, keepdims=True)
    sums[2:3, :] += jnp.sum(low.astype(F32), axis=0, keepdims=True)
    sums[3:4, :] += jnp.sum(grad_scaled * mixed[...], axis=0, keepdims=True)

    @pl.when(at == pl.num_programs(0) - 1)
    def _():
        right = lows[...].reshape(scaled.shape)
        turn_rows(scaled, turned, 1 - me)
        sent[...] = dot_nn(turned[...], right).astype(BF16)
        turn_rows(scaled, turned, me)
        staying[...] = dot_nn(turned[...], right)


def branch_back(core, grad_attended, branch, weights, mixed, scales, vectors, scaled, *wait):
    rows, width = branch.shape
    block = rows // 4
    by_row = pl.BlockSpec((block, width), lambda at, *_: (at, 0))
    fourth = pl.BlockSpec((width // 2, width), lambda at, *_: (0, 1))
    return call(
        branch_back_body,
        (rows // block,),
        [
            by_row,
            by_row,
            fourth,
            fourth,
            by_row,
            whole(scales.shape),
            whole(vectors.shape),
            whole(scaled.shape),
            *after(*wait),
        ],
        [by_row, by_row, whole((8, width)), whole((width // 2, width)), whole((width // 2, width))],
        [
            jax.ShapeDtypeStruct((rows, width), BF16),
            jax.ShapeDtypeStruct((rows, width), BF16),
            jax.ShapeDtypeStruct((8, width), F32),
            jax.ShapeDtypeStruct((width // 2, width), BF16),
            jax.ShapeDtypeStruct((width // 2, width), F32),
        ],
        scratch=[
            pltpu.VMEM((2, block, width // 2), F32),
            pltpu.VMEM((rows // block, block, width), BF16),
            pltpu.VMEM((width // 2, rows), BF16),
        ],
        flops=4 * rows * width * width,
        bytes_accessed=2 * width * width + 16 * rows * width,
        scalars=1,
    )(core, grad_attended, branch, *weights[2:], mixed, scales, vectors, scaled, *wait)


def send_part(values, step, firsts, first, second):
    @pl.when(step < firsts)
    def _():
        first[...] = values.astype(BF16)

    @pl.when(step >= firsts)
    def _():
        second[...] = by_owner(values, second.shape[0]).astype(BF16)


def part_specs(half, plane, start, firsts):
    return [
        pl.BlockSpec((half, 1024), lambda at, *_: (0, jnp.clip(at - start, 0, firsts - 1))),
        pl.BlockSpec(
            (plane, half // plane, 1024),
            lambda at, *_: (0, 0, jnp.clip(at - start - firsts, 0, 3 - firsts)),
        ),
    ]


def part_shapes(half, plane, firsts):
    return [
        jax.ShapeDtypeStruct((half, firsts * 1024), BF16),
        jax.ShapeDtypeStruct((plane, half // plane, (4 - firsts) * 1024), BF16),
    ]


def forward_ffn_body(
    steps,
    normed,
    attended,
    vectors,
    rows_of,
    up,
    down,
    upstream,
    output,
    top,
    kept,
    slope,
    stats,
    sent_first,
    sent_second,
    held,
    total,
    sums,
    turned,
):
    at = pl.program_id(0)
    width = held.shape[2]

    @pl.when(at == 0)
    def _():
        turn_all(upstream, turned)
        sums[...] = jnp.zeros_like(sums)

    @pl.when(at < steps)
    def _():
        hidden = dot_nn(normed[...], up[...]) + rows_of[0:1, :]
        cdf = 0.5 + 0.5 * lax.erf(hidden * math.sqrt(0.5))
        value = hidden * cdf
        slope[...] = (
            cdf + hidden * (jnp.exp(-0.5 * hidden * hidden) * (1.0 / math.sqrt(2.0 * math.pi)))
        ).astype(BF16)
        held[at] = value
        kept[...] = value.astype(BF16)
        sums[...] += lane_sum(value)

    @pl.when(at == steps)
    def _():
        count = steps * width
        mean = jnp.sum(sums[...], axis=1, keepdims=True) * (1.0 / count)
        square = jnp.zeros(sums.shape, F32)
        for block in range(steps):
            centered = held[block] - mean
            square = square + lane_sum(centered * centered)
        spread = lax.rsqrt(jnp.sum(square, axis=1, keepdims=True) * (1.0 / count) + EPS)
        stats[:, :TILE] = jnp.broadcast_to(mean, sums.shape)
        stats[:, TILE:] = jnp.broadcast_to(spread, sums.shape)
        total[...] = attended[...] + vectors[21:22, :]

    @pl.when(at >= steps)
    def _():
        mean = stats[:, 0:1]
        spread = stats[:, TILE : TILE + 1]
        value = held[at - steps]
        low = ((value - mean) * spread * rows_of[1:2, :] + rows_of[2:3, :]).astype(BF16)
        top[...] = low
        total[...] += dot_nt(low, down[...])
        send_part(dot_nn(turned[...], low), at - steps, DOWN_FIRSTS, sent_first, sent_second)

    @pl.when(at == 2 * steps - 1)
    def _():
        output[...] = total[...].astype(BF16)


def forward_ffn(plane, normed, attended, vectors, wide_rows, both, upstream):
    rows, width = attended.shape
    hidden = both.shape[1] // 2
    block = 1024
    steps = hidden // block
    early = lambda at, *_: (0, jnp.minimum(at, steps - 1))
    late = lambda at, *_: (0, jnp.maximum(at - steps, 0))
    return call(
        functools.partial(forward_ffn_body, steps),
        (2 * steps,),
        [
            whole((rows, width)),
            whole((rows, width)),
            whole(vectors.shape),
            pl.BlockSpec((8, block), lambda at, *_: (0, lax.rem(at, steps))),
            pl.BlockSpec((width, block), early),
            pl.BlockSpec((width, block), lambda at, *_: (0, steps + jnp.maximum(at - steps, 0))),
            whole((rows, width)),
        ],
        [
            whole((rows, width)),
            pl.BlockSpec((rows, block), late),
            pl.BlockSpec((rows, block), early),
            pl.BlockSpec((rows, block), early),
            whole((rows, 2 * TILE)),
            *part_specs(width, plane, steps, DOWN_FIRSTS),
        ],
        [
            jax.ShapeDtypeStruct((rows, width), BF16),
            jax.ShapeDtypeStruct((rows, hidden), BF16),
            jax.ShapeDtypeStruct((rows, hidden), BF16),
            jax.ShapeDtypeStruct((rows, hidden), BF16),
            jax.ShapeDtypeStruct((rows, 2 * TILE), F32),
            *part_shapes(width, plane, DOWN_FIRSTS),
        ],
        scratch=[
            pltpu.VMEM((steps, rows, block), F32),
            pltpu.VMEM((rows, width), F32),
            pltpu.VMEM((rows, TILE), F32),
            pltpu.VMEM((width, rows), BF16),
        ],
        flops=6 * rows * width * hidden,
        bytes_accessed=4 * width * hidden + 6 * rows * hidden,
    )(normed, attended, vectors, wide_rows, both, both, upstream)


def backward_ffn_body(
    steps,
    core,
    upstream,
    attended,
    vectors,
    rows_of,
    stats,
    kept,
    slope,
    down,
    up,
    normed,
    _,
    grad_attended,
    grad_hidden,
    wide_sums,
    sums,
    sent_first,
    sent_second,
    held,
    total,
    first,
    second,
    turned,
):
    at = pl.program_id(0)
    count = steps * held.shape[2]
    mean = stats[:, 0:1]
    spread = stats[:, TILE : TILE + 1]

    @pl.when(at == 0)
    def _():
        turn_rows(normed, turned, 1 - core[0])
        first[...] = jnp.zeros_like(first)
        second[...] = jnp.zeros_like(second)
        total[...] = jnp.zeros_like(total)
        wide_sums[...] = jnp.zeros_like(wide_sums)

    @pl.when(at < steps)
    def _():
        grad = dot_nn(upstream[...], down[...])
        unit = (kept[...].astype(F32) - mean) * spread
        both = grad * unit
        wide_sums[at, 0:1, :] = jnp.sum(both, axis=0, keepdims=True)
        wide_sums[at, 1:2, :] = jnp.sum(grad, axis=0, keepdims=True)
        gain = rows_of[1:2, :]
        held[at] = grad * gain
        first[...] += lane_sum(grad * gain)
        second[...] += lane_sum(both * gain)

    @pl.when(at == steps)
    def _():
        scale = 1.0 / count
        first[...] = jnp.broadcast_to(
            jnp.sum(first[...], axis=1, keepdims=True) * scale, first.shape
        )
        second[...] = jnp.broadcast_to(
            jnp.sum(second[...], axis=1, keepdims=True) * scale, second.shape
        )

    @pl.when(at >= steps)
    def _():
        unit = (kept[...].astype(F32) - mean) * spread
        grad = spread * (held[at - steps] - first[:, 0:1] - unit * second[:, 0:1])
        low = (grad * slope[...].astype(F32)).astype(BF16)
        grad_hidden[...] = low
        wide_sums[at - steps, 2:3, :] = jnp.sum(low.astype(F32), axis=0, keepdims=True)
        total[...] += dot_nt(low, up[...])
        send_part(dot_nn(turned[...], low), at - steps, UP_FIRSTS, sent_first, sent_second)

    @pl.when(at == 2 * steps - 1)
    def _():
        grad = total[...]
        centered, mid_spread = row_stats(attended[...])
        unit = centered * mid_spread
        top = upstream[...].astype(F32)
        grad_attended[...] = top + norm_back(grad * vectors[7:8, :], unit, mid_spread)
        sums[0:1, :] = jnp.sum(grad * unit, axis=0, keepdims=True)
        sums[1:2, :] = jnp.sum(grad, axis=0, keepdims=True)
        sums[2:3, :] = jnp.sum(top, axis=0, keepdims=True)
        sums[3:8, :] = jnp.zeros((5, sums.shape[1]), F32)


def backward_ffn(
    core, plane, upstream, attended, vectors, wide_rows, stats, kept, slope, both, normed, wait
):
    rows, width = attended.shape
    hidden = both.shape[1] // 2
    block = 1024
    steps = hidden // block
    late = lambda at, *_: (0, jnp.maximum(at - steps, 0))
    turn = lambda at, *_: (0, lax.rem(at, steps))
    return call(
        functools.partial(backward_ffn_body, steps),
        (2 * steps,),
        [
            whole((rows, width)),
            whole((rows, width)),
            whole(vectors.shape),
            pl.BlockSpec((8, block), turn),
            whole((rows, 2 * TILE)),
            pl.BlockSpec((rows, block), turn),
            pl.BlockSpec((rows, block), late),
            pl.BlockSpec((width, block), lambda at, *_: (0, steps + jnp.minimum(at, steps - 1))),
            pl.BlockSpec((width, block), late),
            whole((rows, width)),
            *after(wait),
        ],
        [
            whole((rows, width)),
            pl.BlockSpec((rows, block), late),
            whole((steps, 8, block)),
            whole((8, width)),
            *part_specs(width // 2, plane, steps, UP_FIRSTS),
        ],
        [
            jax.ShapeDtypeStruct((rows, width), F32),
            jax.ShapeDtypeStruct((rows, hidden), BF16),
            jax.ShapeDtypeStruct((steps, 8, block), F32),
            jax.ShapeDtypeStruct((8, width), F32),
            *part_shapes(width // 2, plane, UP_FIRSTS),
        ],
        scratch=[
            pltpu.VMEM((steps, rows, block), F32),
            pltpu.VMEM((rows, width), F32),
            pltpu.VMEM((rows, TILE), F32),
            pltpu.VMEM((rows, TILE), F32),
            pltpu.VMEM((width // 2, rows), BF16),
        ],
        flops=5 * rows * width * hidden,
        bytes_accessed=4 * width * hidden + 8 * rows * hidden,
        scalars=1,
    )(core, upstream, attended, vectors, wide_rows, stats, kept, slope, both, both, normed, wait)


def input_back_body(
    core,
    grads,
    own_qk,
    other_qk,
    own_vo,
    other_vo,
    tokens,
    grad_attended,
    vectors,
    branch_sums,
    mid_sums,
    wide_sums,
    _,
    input_grad,
    turned,
    parts,
    sums,
):
    part = pl.program_id(0)
    me = core[0]
    grad_part = grads[...]

    @pl.when(part == 0)
    def _():
        parts[me] = dot_nt(grad_part, own_qk[...])
        parts[1 - me] = dot_nt(grad_part, other_qk[...])
        sums[...] = jnp.zeros_like(sums)
        sums[2:3, :] = jnp.sum(grad_part.astype(F32), axis=0, keepdims=True)

    @pl.when(part == 1)
    def _():
        parts[me] += dot_nt(grad_part, own_qk[...])
        parts[1 - me] += dot_nt(grad_part, other_qk[...])

    @pl.when(part == 2)
    def _():
        parts[me] += dot_nt(grad_part, own_vo[...])
        parts[1 - me] += dot_nt(grad_part, other_vo[...])
        grad = join_parity(parts[0], parts[1])
        centered, spread = row_stats(tokens[...].astype(F32))
        unit = centered * spread
        input_grad[...] = grad_attended[...] + norm_back(grad * vectors[0:1, :], unit, spread)
        sums[0:1, :] = jnp.sum(grad * unit, axis=0, keepdims=True)
        sums[1:2, :] = jnp.sum(grad, axis=0, keepdims=True)
        sums[3:4, :] = jnp.sum(grad_part.astype(F32), axis=0, keepdims=True)
        sums[4:7, :] = branch_sums[0:3, :]
        sums[7:9, :] = mid_sums[0:2, :]
        for row in range(wide_sums.shape[0]):
            sums[9 + row : 10 + row, :] = wide_sums[row, 2:3, :]
            sums[13 + row : 14 + row, :] = wide_sums[row, 0:1, :]
            sums[17 + row : 18 + row, :] = wide_sums[row, 1:2, :]
        sums[21:22, :] = mid_sums[2:3, :]
        width = sums.shape[1]
        head_dim = TILE // 2
        picks = (
            lax.broadcasted_iota(jnp.int32, (width, TILE), 0) // head_dim + HEAD_AT
            == lax.broadcasted_iota(jnp.int32, (width, TILE), 1)
        ).astype(F32)
        heads = lax.dot_general(
            branch_sums[...],
            picks,
            (((1,), (0,)), ((), ())),
            precision=HIGHEST,
            preferred_element_type=F32,
        )[3:4, :]
        for block in range(turned.shape[0]):
            turned[block] = (
                jnp.transpose(sums[:, block * TILE : (block + 1) * TILE]) + heads
            )


def input_back(core, grads, weights, tokens, grad_attended, vectors, sums, wait):
    rows, width = tokens.shape
    full = whole((rows, width))
    third = pl.BlockSpec((width // 2, width), lambda part, *_: (0, jnp.minimum(part, 1)))
    last = pl.BlockSpec((width // 2, width), lambda part, *_: (0, 0))
    return call(
        input_back_body,
        (3,),
        [
            pl.BlockSpec((None, rows, width), lambda part, *_: (part, 0, 0)),
            third,
            third,
            last,
            last,
            full,
            full,
            whole(vectors.shape),
            *[whole(item.shape) for item in sums],
            *after(wait),
        ],
        [full, whole((width // TILE, TILE, TILE))],
        [
            jax.ShapeDtypeStruct((rows, width), F32),
            jax.ShapeDtypeStruct((width // TILE, TILE, TILE), F32),
        ],
        scratch=[pltpu.VMEM((2, rows, width // 2), F32), pltpu.VMEM((TILE, width), F32)],
        flops=6 * rows * width * width,
        bytes_accessed=6 * width * width + 16 * rows * width,
        scalars=1,
    )(core, grads, *weights, tokens, grad_attended, vectors, *sums, wait)


def outer_body(firsts, more, core, left, right, add_first, add_second, *refs):
    first, second, turned = refs[-3:]
    at = pl.program_id(0)

    @pl.when(at == 0)
    def _():
        turn_rows(left, turned, core[0])

    value = dot_nn(turned[...], right[...])

    @pl.when(at < firsts)
    def _():
        first[...] = (value + add_first[...].astype(F32)).astype(BF16)

    if more:

        @pl.when(at == firsts)
        def _():
            first[...] = (refs[0][...] + refs[1][...].astype(F32)).astype(BF16)

    @pl.when(at >= firsts)
    def _():
        second[...] = (
            by_owner(value, second.shape[0]) + add_second[...].astype(F32)
        ).astype(BF16)


def outer(core, left, right, add, wait=(), more=()):
    rows, width = left.shape
    half = width // 2
    block = 1024
    add_first, add_second = add
    plane, owned = add_second.shape[:2]
    firsts = UP_FIRSTS
    seconds = add_second.shape[2] // block
    right_spec = pl.BlockSpec((rows, block), lambda at, *_: (0, at))
    add_spec = pl.BlockSpec((half, block), lambda at, *_: (0, jnp.clip(at, 0, firsts - 1)))
    second_spec = pl.BlockSpec(
        (plane, owned, block), lambda at, *_: (0, 0, jnp.clip(at - firsts, 0, seconds - 1))
    )
    kinds = firsts + len(more) // 2
    out_specs = [
        pl.BlockSpec((half, block), lambda at, *_: (0, jnp.clip(at, 0, kinds - 1))),
        second_spec,
    ]
    out_shape = [
        jax.ShapeDtypeStruct((half, kinds * block), BF16),
        jax.ShapeDtypeStruct(add_second.shape, BF16),
    ]
    return call(
        functools.partial(outer_body, firsts, len(more) > 0),
        (firsts + seconds,),
        [
            whole((rows, width)),
            right_spec,
            add_spec,
            second_spec,
            *[whole(item.shape) for item in more],
            *after(*wait),
        ],
        out_specs,
        out_shape,
        scratch=[pltpu.VMEM((half, rows), BF16)],
        flops=2 * rows * half * block * (firsts + seconds),
        bytes_accessed=6 * half * block * (firsts + seconds),
        scalars=1,
    )(core, left, right, add_first, add_second, *more, *wait)


def outer_stack_body(core, left, right, *refs):
    adds, (first, last, turned) = refs[:3], refs[-3:]
    at = pl.program_id(0)

    @pl.when(at == 0)
    def _():
        turn_rows(left, turned, core[0])

    value = dot_nn(turned[...], right[...])
    for which, add in enumerate(adds):

        @pl.when(at == which)
        def _(add=add):
            out = first if which < 2 else last
            out[...] = (value + add[...].astype(F32)).astype(BF16)


def outer_stack(core, left, rights, adds, *wait):
    count, rows, width = rights.shape
    half = width // 2
    return call(
        outer_stack_body,
        (count,),
        [
            whole((rows, width)),
            pl.BlockSpec((None, rows, width), lambda at, *_: (at, 0, 0)),
            *[whole((half, width)) for _ in adds],
            *after(*wait),
        ],
        [
            pl.BlockSpec((half, width), lambda at, *_: (0, jnp.minimum(at, count - 2))),
            whole((half, width)),
        ],
        [
            jax.ShapeDtypeStruct((half, (count - 1) * width), BF16),
            jax.ShapeDtypeStruct((half, width), BF16),
        ],
        scratch=[pltpu.VMEM((half, rows), BF16)],
        flops=2 * rows * half * width * count,
        bytes_accessed=6 * half * width * count,
        scalars=1,
    )(core, left, rights, *adds, *wait)


def to_slots_body(perm, early, late, last, rest, *refs):
    grad_qkv, grad_out, grad_up, grad_down, slots, tiles = refs
    width = grad_out.shape[1]
    half = 2 * width
    grad_out[...] = early[:, half : half + width]
    grad_qkv[:, :half] = late[...]
    grad_qkv[:, half:] = last[:, :width]
    grad_down[:, : DOWN_FIRSTS * width] = early[:, half + width :]
    grad_down[:, DOWN_FIRSTS * width :] = rest[:, :width]
    grad_up[:, :half] = early[:, :half]
    grad_up[:, half:] = rest[:, width : width + half]
    column = 0
    for result in (grad_qkv, grad_out, grad_up, grad_down):
        for at in range(0, result.shape[1], TILE):
            tiles[column] = result[:, at : at + TILE]
            column += 1
    planes, pairs = slots.shape[:2]
    for slot in range(planes * pairs):
        pair = [tiles[perm[2 * slot + which]] for which in range(2)]
        slots[slot // pairs, slot % pairs] = jnp.concatenate(pair, axis=0).astype(BF16)


def to_slots(perm, early, late, last, rest, plane, widths):
    arrays = [early, late, last, rest]
    pairs = perm.shape[0] // (2 * plane)
    shapes = [jax.ShapeDtypeStruct((8, columns), F32) for columns in widths]
    shapes.append(jax.ShapeDtypeStruct((plane, pairs, 16, TILE), BF16))
    return call(
        to_slots_body,
        (1,),
        [whole(item.shape) for item in arrays],
        [whole(item.shape) for item in shapes],
        shapes,
        scratch=[pltpu.VMEM((perm.shape[0], 8, TILE), F32)],
        bytes_accessed=8 * 8 * sum(widths),
        scalars=1,
    )(perm, *arrays)


def update_body(grads, left_stats, right_stats, left_roots, right_roots, left_new, right_new, back):
    planes, pairs = grads.shape[:2]
    for pair in range(pairs):
        block = grads[:, pair].astype(F32)
        moved = []
        for which in range(2):
            slot = 2 * pair + which
            grad = block[:, which * 8 : which * 8 + 8, :].reshape(TILE, TILE)
            low = grad.astype(BF16)
            left_new[slot] = DECAY * left_stats[slot] + (1.0 - DECAY) * dot_nt(low, low)
            right_new[slot] = DECAY * right_stats[slot] + (1.0 - DECAY) * dot_tn(low, low)
            step = jnp.dot(grad, right_roots[slot], precision=HIGHEST, preferred_element_type=F32)
            step = jnp.dot(left_roots[slot], step, precision=HIGHEST, preferred_element_type=F32)
            moved.append(step.reshape(planes, 8, TILE))
        back[:, pair] = jnp.concatenate(moved, axis=1).astype(BF16)


def update(grads, left_stats, right_stats, left_roots, right_roots):
    arrays = [item[0] for item in (left_stats, right_stats, left_roots, right_roots)]
    stats = jax.ShapeDtypeStruct(arrays[0].shape, F32)
    left_new, right_new, back = call(
        update_body,
        (1,),
        [whole(grads.shape)] + [whole(item.shape) for item in arrays],
        [whole(stats.shape), whole(stats.shape), whole(grads.shape)],
        [stats, stats, jax.ShapeDtypeStruct(grads.shape, BF16)],
        bytes_accessed=24 * arrays[0].size,
    )(grads, *arrays)
    return left_new[None], right_new[None], back


def apply_body(perm, moved, *refs):
    olds, news, tiles = refs[:4], refs[4:8], refs[8]
    pairs = moved.shape[1]
    for slot in range(moved.shape[0] * pairs):
        value = moved[slot // pairs, slot % pairs].astype(F32)
        tiles[perm[2 * slot]] = value[:8]
        tiles[perm[2 * slot + 1]] = value[8:]
    column = 0
    for old, new in zip(olds, news):
        for at in range(0, old.shape[1], TILE):
            cut = slice(at, at + TILE)
            new[:, cut] = old[:, cut] - RATE_MATRIX * tiles[column]
            column += 1


def apply_steps(perm, moved, weights):
    shapes = [jax.ShapeDtypeStruct(item.shape, F32) for item in weights]
    return call(
        apply_body,
        (1,),
        [whole(moved.shape)] + [whole(item.shape) for item in weights],
        [whole(item.shape) for item in shapes],
        shapes,
        scratch=[pltpu.VMEM((perm.shape[0], 8, TILE), F32)],
        bytes_accessed=10 * 8 * TILE * perm.shape[0],
        scalars=1,
    )(perm, moved, *weights)


def swap_cores(values):
    return lax.ppermute(values, "core", [(0, 1), (1, 0)])


def take_core(values, core):
    return lax.dynamic_slice_in_dim(values, core, 1, 1, allow_negative_indices=False)[:, 0]


def turn_chips(values, step):
    count = lax.axis_size("x")
    return lax.ppermute(values, "x", [(at, (at + step) % count) for at in range(count)])


def sum_parts(parts):
    return jnp.sum(parts.astype(F32), axis=0)


def shards(
    tokens,
    cotangent,
    lengths,
    valid,
    owner_perm,
    w_qkv,
    w_out,
    w_up,
    w_down,
    vectors,
    head_scale,
    left_stats,
    right_stats,
    left_roots,
    right_roots,
    vector_stats,
    head_stats,
):
    rows, width = tokens.shape
    heads = head_scale.shape[0]
    hidden = w_up.shape[1]
    ratio = hidden // width
    shard = w_up.shape[0]
    plane = lax.axis_size("fsdp")
    chips = lax.axis_size("x")
    core = lax.axis_index("core")
    core_arg = core.astype(jnp.int32).reshape(1)

    both = lax.all_gather(
        jnp.concatenate([w_up.astype(BF16), w_down.astype(BF16)], axis=1),
        ("x", "core", "fsdp"),
        axis=0,
        tiled=True,
    )
    low_qk = jnp.concatenate(
        [
            w_qkv[:, : 2 * width].astype(BF16),
            jnp.pad(vectors.astype(BF16).T, ((0, 0), (0, TILE - vectors.shape[0]))),
        ],
        axis=1,
    )
    low_vo = jnp.concatenate([w_qkv[:, 2 * width :].astype(BF16), w_out.astype(BF16)], axis=1)

    def to_plane(part, concat):
        spread = jnp.broadcast_to(part[None], (plane,) + part.shape)
        return lax.all_to_all(spread, "fsdp", split_axis=0, concat_axis=concat, tiled=True)

    place = lax.axis_index("x")

    def roll_chips(parts, start):
        twice = jnp.concatenate([parts, parts], axis=0)
        begin = [start] + [0] * (parts.ndim - 1)
        return lax.dynamic_slice(twice, begin, parts.shape, allow_negative_indices=False)

    def in_order(parts):
        return roll_chips(jnp.stack(parts[::-1]), chips - 1 - place)

    def to_chips(part):
        return in_order([part] + [turn_chips(part, step) for step in range(1, chips)])

    def across_chips(parts):
        ahead = roll_chips(parts, place)
        return [ahead[0]] + [turn_chips(ahead[step], step) for step in range(1, chips)]

    own_vo = to_plane(to_chips(low_vo), 2).reshape(width // 2, -1)
    own_qk = to_chips(to_plane(low_qk, 0).reshape(plane * shard, -1)).reshape(width // 2, -1)
    other_qk, other_vo = swap_cores(own_qk), swap_cores(own_vo)
    weights = (own_qk, other_qk, own_vo, other_vo)
    vector_at = 2 * width
    vector_pair = jnp.stack([own_qk[:, vector_at:], other_qk[:, vector_at:]])
    vector_pair = jnp.where(core == 0, vector_pair, vector_pair[::-1])
    vector_rows = (
        vector_pair.reshape(2, -1, TILE, TILE)
        .transpose(1, 0, 2, 3)
        .reshape(width, TILE)
        .T[:24]
        .astype(F32)
    )
    wide_rows = jnp.concatenate(
        [
            vector_rows[9 : 9 + 3 * ratio].reshape(3, hidden),
            jnp.zeros((5, hidden), F32),
        ],
        axis=0,
    )
    upstream = jnp.where(valid[:, None] != 0, cotangent, jnp.zeros_like(cotangent))
    scales = jnp.broadcast_to(jnp.repeat(head_scale, width // heads)[None], (8, width))

    normed, projected = project(core_arg, tokens, vector_rows, weights)
    mixed, scaled, attention = attend(lengths, head_scale, projected)
    branch, attended, normed_mid = branch_out(core_arg, scaled, weights, tokens, vector_rows)
    output, normed_top, kept, slope, stats, down_first, down_second = forward_ffn(
        plane, normed_mid, attended, vector_rows, wide_rows, both, upstream
    )

    def over_x(part):
        return lax.psum_scatter(part, "x", scatter_dimension=0, tiled=True)

    def over_plane(part):
        return sum_parts(
            lax.all_to_all(
                part.reshape(plane, shard, -1), "fsdp", split_axis=0, concat_axis=0, tiled=True
            )
        )

    def plane_first(part):
        total = lax.all_to_all(part, "fsdp", split_axis=0, concat_axis=0, tiled=True)
        return sum_parts(total)

    down_chips = lax.psum_scatter(down_first, ("x", "core"), scatter_dimension=0, tiled=True)
    down_rest = plane_first(down_second)
    grad_attended, grad_hidden, wide_sums, mid_sums, *sent_up = backward_ffn(
        core_arg,
        plane,
        upstream,
        attended,
        vector_rows,
        wide_rows,
        stats,
        kept,
        slope,
        both,
        normed_mid,
        down_second,
    )
    grad_branch, grad_mixed, branch_sums, out_sent, out_stays = branch_back(
        core_arg,
        grad_attended,
        branch,
        weights,
        mixed,
        scales,
        vector_rows,
        scaled,
    )
    up_first, up_second = outer(
        core_arg,
        normed_mid,
        grad_hidden,
        [swap_cores(part) for part in sent_up],
        wait=(grad_branch, down_rest),
        more=(out_stays, swap_cores(out_sent)),
    )
    up_rest = plane_first(up_second)
    up_chips = over_x(up_first)
    grads, *sent_attn = attend_back(
        core_arg,
        projected,
        mixed,
        grad_mixed,
        attention,
        normed,
        (up_second, down_chips),
    )
    input_grad, turned = input_back(
        core_arg,
        grads,
        weights,
        tokens,
        grad_attended,
        vector_rows,
        (branch_sums, mid_sums, wide_sums),
        up_second,
    )

    turned = turned.reshape(chips, 2, TILE, TILE)
    half_sums = take_core(turned, core) + swap_cores(take_core(turned, 1 - core))
    query_key, value_last = outer_stack(
        core_arg, normed, grads, [swap_cores(part) for part in sent_attn], half_sums, up_rest
    )

    early_parts = over_plane(jnp.concatenate([up_chips, down_chips], axis=1))
    half_sums, down_rest, up_rest, early_parts = lax.optimization_barrier(
        (half_sums, down_rest, up_rest, early_parts)
    )
    small = jnp.sum(in_order(across_chips(half_sums)), axis=0)
    down_rest = down_rest.reshape(chips, 2, shard, -1)
    down_rest = take_core(down_rest, core) + swap_cores(
        take_core(down_rest, 1 - core).astype(BF16)
    ).astype(F32)
    rest = jnp.concatenate([down_rest, up_rest.reshape(chips, shard, -1)], axis=2)
    rest = across_chips(rest.astype(BF16))
    rest = sum(part.astype(F32) for part in rest)
    late_parts = over_plane(over_x(query_key))
    last_parts = over_plane(jnp.concatenate([over_x(value_last), small.astype(BF16)], axis=1))
    small = last_parts[:, width:]
    vector_grads = small.T[: vectors.shape[0]]
    head_total = small[0, HEAD_AT : HEAD_AT + heads]

    masters = (w_qkv, w_out, w_up, w_down)
    grad_qkv, grad_out, grad_up, grad_down, slots = to_slots(
        owner_perm,
        early_parts,
        late_parts,
        last_parts,
        rest,
        plane,
        [item.shape[1] for item in masters],
    )
    slots = lax.all_to_all(slots, "fsdp", split_axis=0, concat_axis=0, tiled=True)
    left_new, right_new, back = update(slots, left_stats, right_stats, left_roots, right_roots)
    back = lax.all_to_all(back, "fsdp", split_axis=0, concat_axis=0, tiled=True)
    new_qkv, new_out, new_up, new_down = apply_steps(owner_perm, back, masters)
    vector_stats_new = DECAY * vector_stats + (1.0 - DECAY) * vector_grads * vector_grads
    vectors_new = vectors - RATE_VECTOR * vector_grads * lax.rsqrt(vector_stats_new)
    head_stats_new = DECAY * head_stats + (1.0 - DECAY) * head_total * head_total
    head_new = head_scale - RATE_VECTOR * head_total * lax.rsqrt(head_stats_new)
    return (
        output,
        input_grad,
        grad_qkv,
        grad_out,
        grad_up,
        grad_down,
        vector_grads,
        head_total,
        left_new,
        right_new,
        new_qkv,
        new_out,
        new_up,
        new_down,
        vector_stats_new,
        vectors_new,
        head_stats_new,
        head_new,
    )


def solution(mesh):
    everywhere = ("x", "core", "fsdp")
    by_rows = P(everywhere, None)
    by_columns = P(None, everywhere)
    by_block = P(("x", "core"), "fsdp", None, None)
    dp, fsdp = mesh.devices.shape
    mesh = jax.sharding.Mesh(mesh.devices.reshape(dp // 2, 2, fsdp), everywhere)
    return jax.shard_map(
        shards,
        mesh=mesh,
        in_specs=(
            (by_rows, by_rows, P(everywhere), P(everywhere), P())
            + (by_rows,) * 4
            + (by_columns, P())
            + (by_block,) * 4
            + (by_columns, P())
        ),
        out_specs=(
            (by_rows,) * 6
            + (by_columns, P())
            + (by_block,) * 2
            + (by_rows,) * 4
            + (by_columns, by_columns, P(), P())
        ),
        check_vma=False,
    )
```

```python
import functools
import math

import jax
import jax.numpy as jnp
from jax import lax
from jax.experimental import pallas as pl
from jax.experimental.pallas import tpu as pltpu
from jax.sharding import PartitionSpec as P

TILE = 128
EPS = 1e-05
DECAY = 0.5
RATE_MATRIX = 0.1
RATE_VECTOR = 0.3
HIGHEST = lax.Precision.HIGHEST
HEAD_AT = 24
DOWN_FIRSTS = 3
UP_FIRSTS = 2
VMEM_BYTES = 56 * 1024 * 1024
F32 = jnp.float32
BF16 = jnp.bfloat16


def dot_nn(left, right):
    return lax.dot_general(left, right, (((1,), (0,)), ((), ())), preferred_element_type=F32)


def dot_nt(left, right):
    return lax.dot_general(left, right, (((1,), (1,)), ((), ())), preferred_element_type=F32)


def dot_tn(left, right):
    return lax.dot_general(left, right, (((0,), (0,)), ((), ())), preferred_element_type=F32)


def row_stats(values):
    mean = jnp.mean(values, axis=-1, keepdims=True)
    centered = values - mean
    spread = lax.rsqrt(jnp.mean(centered * centered, axis=-1, keepdims=True) + EPS)
    return centered, spread


def norm_back(scaled_grad, unit, spread):
    mean_grad = jnp.mean(scaled_grad, axis=-1, keepdims=True)
    mean_both = jnp.mean(scaled_grad * unit, axis=-1, keepdims=True)
    return spread * (scaled_grad - mean_grad - unit * mean_both)


def lane_sum(values):
    total = values[:, :TILE]
    for at in range(TILE, values.shape[1], TILE):
        total = total + values[:, at : at + TILE]
    return total


def call(body, grid, in_specs, out_specs, out_shape, scratch=(), flops=0, bytes_accessed=0, scalars=0):
    return pl.pallas_call(
        body,
        out_shape=out_shape,
        grid_spec=pltpu.PrefetchScalarGridSpec(
            num_scalar_prefetch=scalars,
            grid=grid,
            in_specs=in_specs,
            out_specs=out_specs,
            scratch_shapes=list(scratch),
        ),
        compiler_params=pltpu.CompilerParams(vmem_limit_bytes=VMEM_BYTES),
        cost_estimate=pl.CostEstimate(
            flops=flops, bytes_accessed=bytes_accessed, transcendentals=0
        ),
    )


def whole(shape):
    return pl.BlockSpec(shape, lambda *_: (0,) * len(shape))


def after(*arrays):
    return [pl.BlockSpec(memory_space=pl.ANY) for _ in arrays]


def split_parity(values):
    blocks = [values[:, at : at + TILE] for at in range(0, values.shape[1], TILE)]
    return jnp.concatenate(blocks[0::2], axis=1), jnp.concatenate(blocks[1::2], axis=1)


def join_parity(even, odd):
    blocks = []
    for at in range(0, even.shape[1], TILE):
        blocks += [even[:, at : at + TILE], odd[:, at : at + TILE]]
    return jnp.concatenate(blocks, axis=1)


def turn_rows(left, turned, parity):
    for block in range(turned.shape[0] // TILE):
        at = pl.multiple_of((2 * block + parity) * TILE, TILE)
        turned[block * TILE : (block + 1) * TILE, :] = jnp.transpose(left[:, pl.ds(at, TILE)])


def turn_all(left, turned):
    for at in range(0, turned.shape[0], TILE):
        turned[at : at + TILE, :] = jnp.transpose(left[:, at : at + TILE])


def by_owner(values, plane):
    rows, columns = values.shape
    chips = rows // (8 * plane)
    values = values.reshape(chips, plane, 8, columns)
    return jnp.concatenate([values[chip] for chip in range(chips)], axis=1)


def project_body(
    core, tokens, vectors, own_qk, other_qk, own_vo, other_vo, normed, projected, parts
):
    part = pl.program_id(0)

    @pl.when(part == 0)
    def _():
        centered, spread = row_stats(tokens[...].astype(F32))
        low = (centered * spread * vectors[0:1, :] + vectors[1:2, :]).astype(BF16)
        normed[...] = low
        parts[0], parts[1] = split_parity(low)

    gate_q = jnp.where(part == 0, 1.0, 0.0).astype(F32)
    gate_v = jnp.where(part == 2, 1.0, 0.0).astype(F32)
    bias = gate_q * vectors[2:3, :] + gate_v * vectors[3:4, :]
    me = core[0]

    @pl.when(part < 2)
    def _():
        projected[...] = (
            dot_nn(parts[me], own_qk[...]) + dot_nn(parts[1 - me], other_qk[...]) + bias
        ).astype(BF16)

    @pl.when(part == 2)
    def _():
        projected[...] = (
            dot_nn(parts[me], own_vo[...]) + dot_nn(parts[1 - me], other_vo[...]) + bias
        ).astype(BF16)


def project(core, tokens, vectors, weights):
    rows, width = tokens.shape
    parts = 3
    third = pl.BlockSpec((width // 2, width), lambda part, *_: (0, jnp.minimum(part, 1)))
    last = pl.BlockSpec((width // 2, width), lambda part, *_: (0, 0))
    return call(
        project_body,
        (parts,),
        [whole((rows, width)), whole(vectors.shape), third, third, last, last],
        [whole((rows, width)), pl.BlockSpec((rows, width), lambda part, *_: (0, part))],
        [
            jax.ShapeDtypeStruct((rows, width), BF16),
            jax.ShapeDtypeStruct((rows, parts * width), BF16),
        ],
        scratch=[pltpu.VMEM((2, rows, width // 2), BF16)],
        flops=2 * rows * width * width * parts,
        bytes_accessed=2 * width * width * parts,
        scalars=1,
    )(core, tokens, vectors, *weights)


def attend_body(length, scales, queries, keys, values, mixed, scaled, weights):
    rows = queries.shape[0]
    head_dim = TILE // 2
    pair = pl.program_id(0)
    block = rows // 2
    lane = lax.broadcasted_iota(jnp.int32, (rows, TILE), 1)
    spot = lax.broadcasted_iota(jnp.int32, (rows, TILE), 0)
    hidden_key = jnp.where(spot < length[0], 0.0, -1e30).astype(BF16)
    one = jnp.ones((rows, TILE), BF16)
    zero = jnp.zeros((rows, TILE), BF16)
    query = queries[...] * jnp.asarray(1.0 / math.sqrt(head_dim), BF16)
    key = keys[...]
    value = values[...]
    causal = lax.broadcasted_iota(jnp.int32, (block, block), 1) <= lax.broadcasted_iota(
        jnp.int32, (block, block), 0
    )
    total = [jnp.zeros((block, TILE), F32) for _ in range(2)]
    for head in range(2):
        mine = (lane < head_dim) if head == 0 else (lane >= head_dim)
        spare = lane == (head_dim if head == 0 else 0)
        query_one = jnp.where(mine, query, jnp.where(spare, one, zero))
        key_one = jnp.where(mine, key, jnp.where(spare, hidden_key, zero))
        value_one = jnp.where(mine, value, zero)
        for part in range(2):
            seen = (part + 1) * block
            score = dot_nt(query_one[part * block : seen], key_one[:seen])
            last = jnp.where(causal, score[:, part * block :], -1e30)
            score = last if part == 0 else jnp.concatenate([score[:, :block], last], axis=1)
            top = jnp.max(score, axis=1, keepdims=True)
            grown = jnp.exp(score - top)
            share = (grown * (1.0 / jnp.sum(grown, axis=1, keepdims=True))).astype(BF16)
            if part == 0:
                weights[head, :, :block] = share
            else:
                weights[head, :, block:] = share
            total[part] = total[part] + dot_nn(share, value_one[:seen])
    scale_row = jnp.where(
        lax.broadcasted_iota(jnp.int32, (1, TILE), 1) < head_dim,
        scales[2 * pair],
        scales[2 * pair + 1],
    )
    for part in range(2):
        mixed[part * block : (part + 1) * block, :] = total[part]
        scaled[part * block : (part + 1) * block, :] = (total[part] * scale_row).astype(BF16)


def attend(length, scales, projected):
    rows, width3 = projected.shape
    width = width3 // 3
    pairs = width // TILE
    block = rows // 2
    return call(
        attend_body,
        (pairs,),
        [
            pl.BlockSpec((rows, TILE), lambda pair, *_: (0, pair)),
            pl.BlockSpec((rows, TILE), lambda pair, *_: (0, pairs + pair)),
            pl.BlockSpec((rows, TILE), lambda pair, *_: (0, 2 * pairs + pair)),
        ],
        [
            pl.BlockSpec((rows, TILE), lambda pair, *_: (0, pair)),
            pl.BlockSpec((rows, TILE), lambda pair, *_: (0, pair)),
            pl.BlockSpec((2, block, 3 * block), lambda pair, *_: (pair, 0, 0)),
        ],
        [
            jax.ShapeDtypeStruct((rows, width), F32),
            jax.ShapeDtypeStruct((rows, width), BF16),
            jax.ShapeDtypeStruct((2 * pairs, block, 3 * block), BF16),
        ],
        flops=4 * rows * rows * width,
        bytes_accessed=20 * rows * width,
        scalars=2,
    )(length, scales, projected, projected, projected)


def attend_back_body(
    core, queries, keys, values, mixed, grads, weights, normed, _, __, out, sent_q, sent_k, sent_v, turned
):
    @pl.when(pl.program_id(0) == 0)
    def _():
        turn_rows(normed, turned, 1 - core[0])

    rows = queries.shape[0]
    head_dim = TILE // 2
    block = rows // 2
    lane = lax.broadcasted_iota(jnp.int32, (rows, TILE), 1)
    zero = jnp.zeros((rows, TILE), BF16)
    query, key, value, grad = queries[...], keys[...], values[...], grads[...]
    both = grad.astype(F32) * mixed[...]
    q_total = [jnp.zeros((block, TILE), F32) for _ in range(2)]
    k_total = [jnp.zeros((block, TILE), F32) for _ in range(2)]
    v_total = [jnp.zeros((block, TILE), F32) for _ in range(2)]
    for head in range(2):
        mine = (lane < head_dim) if head == 0 else (lane >= head_dim)
        query_one = jnp.where(mine, query, zero)
        key_one = jnp.where(mine, key, zero)
        grad_one = jnp.where(mine, grad, zero)
        delta = jnp.sum(jnp.where(mine, both, 0.0), axis=1, keepdims=True)
        for part in range(2):
            at = part * block
            seen = at + block
            share = weights[head, :, :block] if part == 0 else weights[head, :, block:]
            into = dot_nt(grad_one[at:seen], value[:seen])
            slope = (share.astype(F32) * (into - delta[at:seen])).astype(BF16)
            q_total[part] = q_total[part] + dot_nn(slope, key_one[:seen])
            k_new = dot_tn(slope, query_one[at:seen])
            v_new = dot_tn(share, grad_one[at:seen])
            for into_part in range(part + 1):
                cut = slice(into_part * block, (into_part + 1) * block)
                k_total[into_part] = k_total[into_part] + k_new[cut]
                v_total[into_part] = v_total[into_part] + v_new[cut]
    root = 1.0 / math.sqrt(head_dim)
    low_q = (jnp.concatenate(q_total, axis=0) * root).astype(BF16)
    low_k = (jnp.concatenate(k_total, axis=0) * root).astype(BF16)
    low_v = jnp.concatenate(v_total, axis=0).astype(BF16)
    out[0], out[1], out[2] = low_q, low_k, low_v
    values = dot_nn(turned[...], jnp.concatenate([low_q, low_k, low_v], axis=1)).astype(BF16)
    for which, sent in enumerate((sent_q, sent_k, sent_v)):
        sent[...] = values[:, which * TILE : (which + 1) * TILE]


def attend_back(core, projected, mixed, grads, weights, normed, wait):
    rows, width3 = projected.shape
    width = width3 // 3
    half = width // 2
    pairs = width // TILE
    block = rows // 2
    by_pair = pl.BlockSpec((rows, TILE), lambda pair, *_: (0, pair))
    return call(
        attend_back_body,
        (pairs,),
        [
            by_pair,
            pl.BlockSpec((rows, TILE), lambda pair, *_: (0, pairs + pair)),
            pl.BlockSpec((rows, TILE), lambda pair, *_: (0, 2 * pairs + pair)),
            by_pair,
            by_pair,
            pl.BlockSpec((2, block, 3 * block), lambda pair, *_: (pair, 0, 0)),
            whole((rows, width)),
            *after(*wait),
        ],
        [
            pl.BlockSpec((3, rows, TILE), lambda pair, *_: (0, 0, pair)),
            *[pl.BlockSpec((half, TILE), lambda pair, *_: (0, pair)) for _ in range(3)],
        ],
        [
            jax.ShapeDtypeStruct((3, rows, width), BF16),
            *[jax.ShapeDtypeStruct((half, width), BF16) for _ in range(3)],
        ],
        scratch=[pltpu.VMEM((half, rows), BF16)],
        flops=10 * rows * rows * width,
        bytes_accessed=24 * rows * width,
        scalars=1,
    )(core, projected, projected, projected, mixed, grads, weights, normed, *wait)


def branch_body(core, scaled, own, other, tokens, vectors, branch, attended, normed, parts):
    parts[0], parts[1] = split_parity(scaled[...])
    me = core[0]
    value = dot_nn(parts[me], own[...]) + dot_nn(parts[1 - me], other[...]) + vectors[6:7, :]
    branch[...] = value
    centered, spread = row_stats(value)
    total = tokens[...].astype(F32) + centered * spread * vectors[4:5, :] + vectors[5:6, :]
    attended[...] = total
    centered, spread = row_stats(total)
    normed[...] = (centered * spread * vectors[7:8, :] + vectors[8:9, :]).astype(BF16)


def branch_out(core, scaled, weights, tokens, vectors):
    rows, width = scaled.shape
    block = rows // 4
    by_row = pl.BlockSpec((block, width), lambda at, *_: (at, 0))
    fourth = pl.BlockSpec((width // 2, width), lambda at, *_: (0, 1))
    return call(
        branch_body,
        (rows // block,),
        [by_row, fourth, fourth, by_row, whole(vectors.shape)],
        [by_row, by_row, by_row],
        [
            jax.ShapeDtypeStruct((rows, width), F32),
            jax.ShapeDtypeStruct((rows, width), F32),
            jax.ShapeDtypeStruct((rows, width), BF16),
        ],
        scratch=[pltpu.VMEM((2, block, width // 2), BF16)],
        flops=2 * rows * width * width,
        bytes_accessed=2 * width * width + 14 * rows * width,
        scalars=1,
    )(core, scaled, *weights[2:], tokens, vectors)


def branch_back_body(
    core,
    grad_attended,
    branch,
    own,
    other,
    mixed,
    scales,
    vectors,
    scaled,
    grad_branch,
    grad_mixed,
    sums,
    sent,
    staying,
    parts,
    lows,
    turned,
):
    at = pl.program_id(0)

    @pl.when(at == 0)
    def _():
        sums[...] = jnp.zeros_like(sums)

    grad = grad_attended[...]
    centered, spread = row_stats(branch[...])
    unit = centered * spread
    low = norm_back(grad * vectors[4:5, :], unit, spread).astype(BF16)
    grad_branch[...] = low
    lows[at] = low
    me = core[0]
    parts[me] = dot_nt(low, own[...])
    parts[1 - me] = dot_nt(low, other[...])
    grad_scaled = join_parity(parts[0], parts[1])
    grad_mixed[...] = (grad_scaled * scales[0:1, :]).astype(BF16)
    sums[0:1, :] += jnp.sum(grad * unit, axis=0, keepdims=True)
    sums[1:2, :] += jnp.sum(grad, axis=0, keepdims=True)
    sums[2:3, :] += jnp.sum(low.astype(F32), axis=0, keepdims=True)
    sums[3:4, :] += jnp.sum(grad_scaled * mixed[...], axis=0, keepdims=True)

    @pl.when(at == pl.num_programs(0) - 1)
    def _():
        right = lows[...].reshape(scaled.shape)
        turn_rows(scaled, turned, 1 - me)
        sent[...] = dot_nn(turned[...], right).astype(BF16)
        turn_rows(scaled, turned, me)
        staying[...] = dot_nn(turned[...], right)


def branch_back(core, grad_attended, branch, weights, mixed, scales, vectors, scaled, *wait):
    rows, width = branch.shape
    block = rows // 4
    by_row = pl.BlockSpec((block, width), lambda at, *_: (at, 0))
    fourth = pl.BlockSpec((width // 2, width), lambda at, *_: (0, 1))
    return call(
        branch_back_body,
        (rows // block,),
        [
            by_row,
            by_row,
            fourth,
            fourth,
            by_row,
            whole(scales.shape),
            whole(vectors.shape),
            whole(scaled.shape),
            *after(*wait),
        ],
        [by_row, by_row, whole((8, width)), whole((width // 2, width)), whole((width // 2, width))],
        [
            jax.ShapeDtypeStruct((rows, width), BF16),
            jax.ShapeDtypeStruct((rows, width), BF16),
            jax.ShapeDtypeStruct((8, width), F32),
            jax.ShapeDtypeStruct((width // 2, width), BF16),
            jax.ShapeDtypeStruct((width // 2, width), F32),
        ],
        scratch=[
            pltpu.VMEM((2, block, width // 2), F32),
            pltpu.VMEM((rows // block, block, width), BF16),
            pltpu.VMEM((width // 2, rows), BF16),
        ],
        flops=4 * rows * width * width,
        bytes_accessed=2 * width * width + 16 * rows * width,
        scalars=1,
    )(core, grad_attended, branch, *weights[2:], mixed, scales, vectors, scaled, *wait)


def send_part(values, step, firsts, first, second):
    @pl.when(step < firsts)
    def _():
        first[...] = values.astype(BF16)

    @pl.when(step >= firsts)
    def _():
        second[...] = by_owner(values, second.shape[0]).astype(BF16)


def part_specs(half, plane, start, firsts):
    return [
        pl.BlockSpec((half, 1024), lambda at, *_: (0, jnp.clip(at - start, 0, firsts - 1))),
        pl.BlockSpec(
            (plane, half // plane, 1024),
            lambda at, *_: (0, 0, jnp.clip(at - start - firsts, 0, 3 - firsts)),
        ),
    ]


def part_shapes(half, plane, firsts):
    return [
        jax.ShapeDtypeStruct((half, firsts * 1024), BF16),
        jax.ShapeDtypeStruct((plane, half // plane, (4 - firsts) * 1024), BF16),
    ]


def forward_ffn_body(
    steps,
    normed,
    attended,
    vectors,
    rows_of,
    up,
    down,
    upstream,
    output,
    kept,
    slope,
    stats,
    sent_first,
    sent_second,
    held,
    total,
    sums,
    turned,
):
    at = pl.program_id(0)
    width = held.shape[2]

    @pl.when(at == 0)
    def _():
        turn_all(upstream, turned)
        sums[...] = jnp.zeros_like(sums)

    @pl.when(at < steps)
    def _():
        hidden = dot_nn(normed[...], up[...]) + rows_of[0:1, :]
        cdf = 0.5 + 0.5 * lax.erf(hidden * math.sqrt(0.5))
        value = hidden * cdf
        slope[...] = (
            cdf + hidden * (jnp.exp(-0.5 * hidden * hidden) * (1.0 / math.sqrt(2.0 * math.pi)))
        ).astype(BF16)
        held[at] = value
        kept[...] = value.astype(BF16)
        sums[...] += lane_sum(value)

    @pl.when(at == steps)
    def _():
        count = steps * width
        mean = jnp.sum(sums[...], axis=1, keepdims=True) * (1.0 / count)
        square = jnp.zeros(sums.shape, F32)
        for block in range(steps):
            centered = held[block] - mean
            square = square + lane_sum(centered * centered)
        spread = lax.rsqrt(jnp.sum(square, axis=1, keepdims=True) * (1.0 / count) + EPS)
        stats[:, :TILE] = jnp.broadcast_to(mean, sums.shape)
        stats[:, TILE:] = jnp.broadcast_to(spread, sums.shape)
        total[...] = attended[...] + vectors[21:22, :]

    @pl.when(at >= steps)
    def _():
        mean = stats[:, 0:1]
        spread = stats[:, TILE : TILE + 1]
        value = held[at - steps]
        low = ((value - mean) * spread * rows_of[1:2, :] + rows_of[2:3, :]).astype(BF16)
        total[...] += dot_nt(low, down[...])
        send_part(dot_nn(turned[...], low), at - steps, DOWN_FIRSTS, sent_first, sent_second)

    @pl.when(at == 2 * steps - 1)
    def _():
        output[...] = total[...].astype(BF16)


def forward_ffn(plane, normed, attended, vectors, wide_rows, both, upstream):
    rows, width = attended.shape
    hidden = both.shape[1] // 2
    block = 1024
    steps = hidden // block
    early = lambda at, *_: (0, jnp.minimum(at, steps - 1))
    return call(
        functools.partial(forward_ffn_body, steps),
        (2 * steps,),
        [
            whole((rows, width)),
            whole((rows, width)),
            whole(vectors.shape),
            pl.BlockSpec((8, block), lambda at, *_: (0, lax.rem(at, steps))),
            pl.BlockSpec((width, block), early),
            pl.BlockSpec((width, block), lambda at, *_: (0, steps + jnp.maximum(at - steps, 0))),
            whole((rows, width)),
        ],
        [
            whole((rows, width)),
            pl.BlockSpec((rows, block), early),
            pl.BlockSpec((rows, block), early),
            whole((rows, 2 * TILE)),
            *part_specs(width, plane, steps, DOWN_FIRSTS),
        ],
        [
            jax.ShapeDtypeStruct((rows, width), BF16),
            jax.ShapeDtypeStruct((rows, hidden), BF16),
            jax.ShapeDtypeStruct((rows, hidden), BF16),
            jax.ShapeDtypeStruct((rows, 2 * TILE), F32),
            *part_shapes(width, plane, DOWN_FIRSTS),
        ],
        scratch=[
            pltpu.VMEM((steps, rows, block), F32),
            pltpu.VMEM((rows, width), F32),
            pltpu.VMEM((rows, TILE), F32),
            pltpu.VMEM((width, rows), BF16),
        ],
        flops=6 * rows * width * hidden,
        bytes_accessed=4 * width * hidden + 6 * rows * hidden,
    )(normed, attended, vectors, wide_rows, both, both, upstream)


def backward_ffn_body(
    steps,
    core,
    upstream,
    attended,
    vectors,
    rows_of,
    stats,
    kept,
    slope,
    down,
    up,
    normed,
    _,
    grad_attended,
    grad_hidden,
    wide_sums,
    sums,
    sent_first,
    sent_second,
    held,
    total,
    first,
    second,
    turned,
):
    at = pl.program_id(0)
    count = steps * held.shape[2]
    mean = stats[:, 0:1]
    spread = stats[:, TILE : TILE + 1]

    @pl.when(at == 0)
    def _():
        turn_rows(normed, turned, 1 - core[0])
        first[...] = jnp.zeros_like(first)
        second[...] = jnp.zeros_like(second)
        total[...] = jnp.zeros_like(total)
        wide_sums[...] = jnp.zeros_like(wide_sums)

    @pl.when(at < steps)
    def _():
        grad = dot_nn(upstream[...], down[...])
        unit = (kept[...].astype(F32) - mean) * spread
        both = grad * unit
        wide_sums[at, 0:1, :] = jnp.sum(both, axis=0, keepdims=True)
        wide_sums[at, 1:2, :] = jnp.sum(grad, axis=0, keepdims=True)
        gain = rows_of[1:2, :]
        held[at] = grad * gain
        first[...] += lane_sum(grad * gain)
        second[...] += lane_sum(both * gain)

    @pl.when(at == steps)
    def _():
        scale = 1.0 / count
        first[...] = jnp.broadcast_to(
            jnp.sum(first[...], axis=1, keepdims=True) * scale, first.shape
        )
        second[...] = jnp.broadcast_to(
            jnp.sum(second[...], axis=1, keepdims=True) * scale, second.shape
        )

    @pl.when(at >= steps)
    def _():
        unit = (kept[...].astype(F32) - mean) * spread
        grad = spread * (held[at - steps] - first[:, 0:1] - unit * second[:, 0:1])
        low = (grad * slope[...].astype(F32)).astype(BF16)
        grad_hidden[...] = low
        wide_sums[at - steps, 2:3, :] = jnp.sum(low.astype(F32), axis=0, keepdims=True)
        total[...] += dot_nt(low, up[...])
        send_part(dot_nn(turned[...], low), at - steps, UP_FIRSTS, sent_first, sent_second)

    @pl.when(at == 2 * steps - 1)
    def _():
        grad = total[...]
        centered, mid_spread = row_stats(attended[...])
        unit = centered * mid_spread
        top = upstream[...].astype(F32)
        grad_attended[...] = top + norm_back(grad * vectors[7:8, :], unit, mid_spread)
        sums[0:1, :] = jnp.sum(grad * unit, axis=0, keepdims=True)
        sums[1:2, :] = jnp.sum(grad, axis=0, keepdims=True)
        sums[2:3, :] = jnp.sum(top, axis=0, keepdims=True)
        sums[3:8, :] = jnp.zeros((5, sums.shape[1]), F32)


def backward_ffn(
    core, plane, upstream, attended, vectors, wide_rows, stats, kept, slope, both, normed, wait
):
    rows, width = attended.shape
    hidden = both.shape[1] // 2
    block = 1024
    steps = hidden // block
    late = lambda at, *_: (0, jnp.maximum(at - steps, 0))
    turn = lambda at, *_: (0, lax.rem(at, steps))
    return call(
        functools.partial(backward_ffn_body, steps),
        (2 * steps,),
        [
            whole((rows, width)),
            whole((rows, width)),
            whole(vectors.shape),
            pl.BlockSpec((8, block), turn),
            whole((rows, 2 * TILE)),
            pl.BlockSpec((rows, block), turn),
            pl.BlockSpec((rows, block), late),
            pl.BlockSpec((width, block), lambda at, *_: (0, steps + jnp.minimum(at, steps - 1))),
            pl.BlockSpec((width, block), late),
            whole((rows, width)),
            *after(wait),
        ],
        [
            whole((rows, width)),
            pl.BlockSpec((rows, block), late),
            whole((steps, 8, block)),
            whole((8, width)),
            *part_specs(width // 2, plane, steps, UP_FIRSTS),
        ],
        [
            jax.ShapeDtypeStruct((rows, width), F32),
            jax.ShapeDtypeStruct((rows, hidden), BF16),
            jax.ShapeDtypeStruct((steps, 8, block), F32),
            jax.ShapeDtypeStruct((8, width), F32),
            *part_shapes(width // 2, plane, UP_FIRSTS),
        ],
        scratch=[
            pltpu.VMEM((steps, rows, block), F32),
            pltpu.VMEM((rows, width), F32),
            pltpu.VMEM((rows, TILE), F32),
            pltpu.VMEM((rows, TILE), F32),
            pltpu.VMEM((width // 2, rows), BF16),
        ],
        flops=5 * rows * width * hidden,
        bytes_accessed=4 * width * hidden + 8 * rows * hidden,
        scalars=1,
    )(core, upstream, attended, vectors, wide_rows, stats, kept, slope, both, both, normed, wait)


def input_back_body(
    core,
    grads,
    own_qk,
    other_qk,
    own_vo,
    other_vo,
    tokens,
    grad_attended,
    vectors,
    branch_sums,
    mid_sums,
    wide_sums,
    _,
    input_grad,
    turned,
    parts,
    sums,
):
    part = pl.program_id(0)
    me = core[0]
    grad_part = grads[...]

    @pl.when(part == 0)
    def _():
        parts[me] = dot_nt(grad_part, own_qk[...])
        parts[1 - me] = dot_nt(grad_part, other_qk[...])
        sums[...] = jnp.zeros_like(sums)
        sums[2:3, :] = jnp.sum(grad_part.astype(F32), axis=0, keepdims=True)

    @pl.when(part == 1)
    def _():
        parts[me] += dot_nt(grad_part, own_qk[...])
        parts[1 - me] += dot_nt(grad_part, other_qk[...])

    @pl.when(part == 2)
    def _():
        parts[me] += dot_nt(grad_part, own_vo[...])
        parts[1 - me] += dot_nt(grad_part, other_vo[...])
        grad = join_parity(parts[0], parts[1])
        centered, spread = row_stats(tokens[...].astype(F32))
        unit = centered * spread
        input_grad[...] = grad_attended[...] + norm_back(grad * vectors[0:1, :], unit, spread)
        sums[0:1, :] = jnp.sum(grad * unit, axis=0, keepdims=True)
        sums[1:2, :] = jnp.sum(grad, axis=0, keepdims=True)
        sums[3:4, :] = jnp.sum(grad_part.astype(F32), axis=0, keepdims=True)
        sums[4:7, :] = branch_sums[0:3, :]
        sums[7:9, :] = mid_sums[0:2, :]
        for row in range(wide_sums.shape[0]):
            sums[9 + row : 10 + row, :] = wide_sums[row, 2:3, :]
            sums[13 + row : 14 + row, :] = wide_sums[row, 0:1, :]
            sums[17 + row : 18 + row, :] = wide_sums[row, 1:2, :]
        sums[21:22, :] = mid_sums[2:3, :]
        width = sums.shape[1]
        head_dim = TILE // 2
        picks = (
            lax.broadcasted_iota(jnp.int32, (width, TILE), 0) // head_dim + HEAD_AT
            == lax.broadcasted_iota(jnp.int32, (width, TILE), 1)
        ).astype(F32)
        heads = lax.dot_general(
            branch_sums[...],
            picks,
            (((1,), (0,)), ((), ())),
            precision=HIGHEST,
            preferred_element_type=F32,
        )[3:4, :]
        for block in range(turned.shape[0]):
            turned[block] = (
                jnp.transpose(sums[:, block * TILE : (block + 1) * TILE]) + heads
            )


def input_back(core, grads, weights, tokens, grad_attended, vectors, sums, wait):
    rows, width = tokens.shape
    full = whole((rows, width))
    third = pl.BlockSpec((width // 2, width), lambda part, *_: (0, jnp.minimum(part, 1)))
    last = pl.BlockSpec((width // 2, width), lambda part, *_: (0, 0))
    return call(
        input_back_body,
        (3,),
        [
            pl.BlockSpec((None, rows, width), lambda part, *_: (part, 0, 0)),
            third,
            third,
            last,
            last,
            full,
            full,
            whole(vectors.shape),
            *[whole(item.shape) for item in sums],
            *after(wait),
        ],
        [full, whole((width // TILE, TILE, TILE))],
        [
            jax.ShapeDtypeStruct((rows, width), F32),
            jax.ShapeDtypeStruct((width // TILE, TILE, TILE), F32),
        ],
        scratch=[pltpu.VMEM((2, rows, width // 2), F32), pltpu.VMEM((TILE, width), F32)],
        flops=6 * rows * width * width,
        bytes_accessed=6 * width * width + 16 * rows * width,
        scalars=1,
    )(core, grads, *weights, tokens, grad_attended, vectors, *sums, wait)


def outer_body(firsts, more, core, left, right, add_first, add_second, *refs):
    first, second, turned = refs[-3:]
    at = pl.program_id(0)

    @pl.when(at == 0)
    def _():
        turn_rows(left, turned, core[0])

    value = dot_nn(turned[...], right[...])

    @pl.when(at < firsts)
    def _():
        first[...] = (value + add_first[...].astype(F32)).astype(BF16)

    if more:

        @pl.when(at == firsts)
        def _():
            first[...] = (refs[0][...] + refs[1][...].astype(F32)).astype(BF16)

    @pl.when(at >= firsts)
    def _():
        second[...] = (
            by_owner(value, second.shape[0]) + add_second[...].astype(F32)
        ).astype(BF16)


def outer(core, left, right, add, wait=(), more=()):
    rows, width = left.shape
    half = width // 2
    block = 1024
    add_first, add_second = add
    plane, owned = add_second.shape[:2]
    firsts = UP_FIRSTS
    seconds = add_second.shape[2] // block
    right_spec = pl.BlockSpec((rows, block), lambda at, *_: (0, at))
    add_spec = pl.BlockSpec((half, block), lambda at, *_: (0, jnp.clip(at, 0, firsts - 1)))
    second_spec = pl.BlockSpec(
        (plane, owned, block), lambda at, *_: (0, 0, jnp.clip(at - firsts, 0, seconds - 1))
    )
    kinds = firsts + len(more) // 2
    out_specs = [
        pl.BlockSpec((half, block), lambda at, *_: (0, jnp.clip(at, 0, kinds - 1))),
        second_spec,
    ]
    out_shape = [
        jax.ShapeDtypeStruct((half, kinds * block), BF16),
        jax.ShapeDtypeStruct(add_second.shape, BF16),
    ]
    return call(
        functools.partial(outer_body, firsts, len(more) > 0),
        (firsts + seconds,),
        [
            whole((rows, width)),
            right_spec,
            add_spec,
            second_spec,
            *[whole(item.shape) for item in more],
            *after(*wait),
        ],
        out_specs,
        out_shape,
        scratch=[pltpu.VMEM((half, rows), BF16)],
        flops=2 * rows * half * block * (firsts + seconds),
        bytes_accessed=6 * half * block * (firsts + seconds),
        scalars=1,
    )(core, left, right, add_first, add_second, *more, *wait)


def outer_stack_body(core, left, right, *refs):
    adds, (out, turned) = refs[:3], refs[-2:]
    at = pl.program_id(0)

    @pl.when(at == 0)
    def _():
        turn_rows(left, turned, core[0])

    value = dot_nn(turned[...], right[...])
    for which, add in enumerate(adds):

        @pl.when(at == which)
        def _(add=add):
            out[...] = (value + add[...].astype(F32)).astype(BF16)


def outer_stack(core, left, rights, adds, *wait):
    count, rows, width = rights.shape
    half = width // 2
    return call(
        outer_stack_body,
        (count,),
        [
            whole((rows, width)),
            pl.BlockSpec((None, rows, width), lambda at, *_: (at, 0, 0)),
            *[whole((half, width)) for _ in adds],
            *after(*wait),
        ],
        pl.BlockSpec((half, width), lambda at, *_: (0, at)),
        jax.ShapeDtypeStruct((half, count * width), BF16),
        scratch=[pltpu.VMEM((half, rows), BF16)],
        flops=2 * rows * half * width * count,
        bytes_accessed=6 * half * width * count,
        scalars=1,
    )(core, left, rights, *adds, *wait)


def to_slots_body(perm, early, late, rest, *refs):
    grad_qkv, grad_out, grad_up, grad_down, slots, tiles = refs
    width = grad_out.shape[1]
    half = 2 * width
    grad_out[...] = early[:, half : half + width]
    grad_qkv[...] = late[:, : 3 * width]
    grad_down[:, : DOWN_FIRSTS * width] = early[:, half + width :]
    grad_down[:, DOWN_FIRSTS * width :] = rest[:, :width]
    grad_up[:, :half] = early[:, :half]
    grad_up[:, half:] = rest[:, width : width + half]
    column = 0
    for result in (grad_qkv, grad_out, grad_up, grad_down):
        for at in range(0, result.shape[1], TILE):
            tiles[column] = result[:, at : at + TILE]
            column += 1
    planes, pairs = slots.shape[:2]
    for slot in range(planes * pairs):
        pair = [tiles[perm[2 * slot + which]] for which in range(2)]
        slots[slot // pairs, slot % pairs] = jnp.concatenate(pair, axis=0).astype(BF16)


def to_slots(perm, early, late, rest, plane, widths):
    arrays = [early, late, rest]
    pairs = perm.shape[0] // (2 * plane)
    shapes = [jax.ShapeDtypeStruct((8, columns), F32) for columns in widths]
    shapes.append(jax.ShapeDtypeStruct((plane, pairs, 16, TILE), BF16))
    return call(
        to_slots_body,
        (1,),
        [whole(item.shape) for item in arrays],
        [whole(item.shape) for item in shapes],
        shapes,
        scratch=[pltpu.VMEM((perm.shape[0], 8, TILE), F32)],
        bytes_accessed=8 * 8 * sum(widths),
        scalars=1,
    )(perm, *arrays)


def update_body(grads, left_stats, right_stats, left_roots, right_roots, left_new, right_new, back):
    planes, pairs = grads.shape[:2]
    for pair in range(pairs):
        block = grads[:, pair].astype(F32)
        moved = []
        for which in range(2):
            slot = 2 * pair + which
            grad = block[:, which * 8 : which * 8 + 8, :].reshape(TILE, TILE)
            low = grad.astype(BF16)
            left_new[slot] = DECAY * left_stats[slot] + (1.0 - DECAY) * dot_nt(low, low)
            right_new[slot] = DECAY * right_stats[slot] + (1.0 - DECAY) * dot_tn(low, low)
            step = jnp.dot(grad, right_roots[slot], precision=HIGHEST, preferred_element_type=F32)
            step = jnp.dot(left_roots[slot], step, precision=HIGHEST, preferred_element_type=F32)
            moved.append(step.reshape(planes, 8, TILE))
        back[:, pair] = jnp.concatenate(moved, axis=1).astype(BF16)


def update(grads, left_stats, right_stats, left_roots, right_roots):
    arrays = [item[0] for item in (left_stats, right_stats, left_roots, right_roots)]
    stats = jax.ShapeDtypeStruct(arrays[0].shape, F32)
    left_new, right_new, back = call(
        update_body,
        (1,),
        [whole(grads.shape)] + [whole(item.shape) for item in arrays],
        [whole(stats.shape), whole(stats.shape), whole(grads.shape)],
        [stats, stats, jax.ShapeDtypeStruct(grads.shape, BF16)],
        bytes_accessed=24 * arrays[0].size,
    )(grads, *arrays)
    return left_new[None], right_new[None], back


def apply_body(perm, moved, *refs):
    olds, news, tiles = refs[:4], refs[4:8], refs[8]
    pairs = moved.shape[1]
    for slot in range(moved.shape[0] * pairs):
        value = moved[slot // pairs, slot % pairs].astype(F32)
        tiles[perm[2 * slot]] = value[:8]
        tiles[perm[2 * slot + 1]] = value[8:]
    column = 0
    for old, new in zip(olds, news):
        for at in range(0, old.shape[1], TILE):
            cut = slice(at, at + TILE)
            new[:, cut] = old[:, cut] - RATE_MATRIX * tiles[column]
            column += 1


def apply_steps(perm, moved, weights):
    shapes = [jax.ShapeDtypeStruct(item.shape, F32) for item in weights]
    return call(
        apply_body,
        (1,),
        [whole(moved.shape)] + [whole(item.shape) for item in weights],
        [whole(item.shape) for item in shapes],
        shapes,
        scratch=[pltpu.VMEM((perm.shape[0], 8, TILE), F32)],
        bytes_accessed=10 * 8 * TILE * perm.shape[0],
        scalars=1,
    )(perm, moved, *weights)


def swap_cores(values):
    return lax.ppermute(values, "core", [(0, 1), (1, 0)])


def take_core(values, core):
    return lax.dynamic_slice_in_dim(values, core, 1, 1, allow_negative_indices=False)[:, 0]


def turn_chips(values, step):
    count = lax.axis_size("x")
    return lax.ppermute(values, "x", [(at, (at + step) % count) for at in range(count)])


def sum_parts(parts):
    return jnp.sum(parts.astype(F32), axis=0)


def shards(
    tokens,
    cotangent,
    lengths,
    valid,
    owner_perm,
    w_qkv,
    w_out,
    w_up,
    w_down,
    vectors,
    head_scale,
    left_stats,
    right_stats,
    left_roots,
    right_roots,
    vector_stats,
    head_stats,
):
    rows, width = tokens.shape
    heads = head_scale.shape[0]
    hidden = w_up.shape[1]
    ratio = hidden // width
    shard = w_up.shape[0]
    plane = lax.axis_size("fsdp")
    chips = lax.axis_size("x")
    core = lax.axis_index("core")
    core_arg = core.astype(jnp.int32).reshape(1)

    both = lax.all_gather(
        jnp.concatenate([w_up.astype(BF16), w_down.astype(BF16)], axis=1),
        ("x", "core", "fsdp"),
        axis=0,
        tiled=True,
    )
    low_qk = jnp.concatenate(
        [
            w_qkv[:, : 2 * width].astype(BF16),
            jnp.pad(vectors.astype(BF16).T, ((0, 0), (0, TILE - vectors.shape[0]))),
        ],
        axis=1,
    )
    low_vo = jnp.concatenate([w_qkv[:, 2 * width :].astype(BF16), w_out.astype(BF16)], axis=1)

    def to_plane(part, concat):
        spread = jnp.broadcast_to(part[None], (plane,) + part.shape)
        return lax.all_to_all(spread, "fsdp", split_axis=0, concat_axis=concat, tiled=True)

    place = lax.axis_index("x")

    def roll_chips(parts, start):
        twice = jnp.concatenate([parts, parts], axis=0)
        begin = [start] + [0] * (parts.ndim - 1)
        return lax.dynamic_slice(twice, begin, parts.shape, allow_negative_indices=False)

    def in_order(parts):
        return roll_chips(jnp.stack(parts[::-1]), chips - 1 - place)

    def to_chips(part):
        return in_order([part] + [turn_chips(part, step) for step in range(1, chips)])

    def across_chips(parts):
        ahead = roll_chips(parts, place)
        return [ahead[0]] + [turn_chips(ahead[step], step) for step in range(1, chips)]

    own_vo = to_plane(to_chips(low_vo), 2).reshape(width // 2, -1)
    own_qk = to_chips(to_plane(low_qk, 0).reshape(plane * shard, -1)).reshape(width // 2, -1)
    other_qk, other_vo = swap_cores(own_qk), swap_cores(own_vo)
    weights = (own_qk, other_qk, own_vo, other_vo)
    vector_at = 2 * width
    vector_pair = jnp.stack([own_qk[:, vector_at:], other_qk[:, vector_at:]])
    vector_pair = jnp.where(core == 0, vector_pair, vector_pair[::-1])
    vector_rows = (
        vector_pair.reshape(2, -1, TILE, TILE)
        .transpose(1, 0, 2, 3)
        .reshape(width, TILE)
        .T[:24]
        .astype(F32)
    )
    wide_rows = jnp.concatenate(
        [
            vector_rows[9 : 9 + 3 * ratio].reshape(3, hidden),
            jnp.zeros((5, hidden), F32),
        ],
        axis=0,
    )
    upstream = jnp.where(valid[:, None] != 0, cotangent, jnp.zeros_like(cotangent))
    scales = jnp.broadcast_to(jnp.repeat(head_scale, width // heads)[None], (8, width))

    normed, projected = project(core_arg, tokens, vector_rows, weights)
    mixed, scaled, attention = attend(lengths, head_scale, projected)
    branch, attended, normed_mid = branch_out(core_arg, scaled, weights, tokens, vector_rows)
    output, kept, slope, stats, down_first, down_second = forward_ffn(
        plane, normed_mid, attended, vector_rows, wide_rows, both, upstream
    )

    def over_x(part):
        return lax.psum_scatter(part, "x", scatter_dimension=0, tiled=True)

    def over_plane(part):
        return sum_parts(
            lax.all_to_all(
                part.reshape(plane, shard, -1), "fsdp", split_axis=0, concat_axis=0, tiled=True
            )
        )

    def plane_first(part):
        total = lax.all_to_all(part, "fsdp", split_axis=0, concat_axis=0, tiled=True)
        return sum_parts(total)

    down_chips = lax.psum_scatter(down_first, ("x", "core"), scatter_dimension=0, tiled=True)
    down_rest = plane_first(down_second)
    grad_attended, grad_hidden, wide_sums, mid_sums, *sent_up = backward_ffn(
        core_arg,
        plane,
        upstream,
        attended,
        vector_rows,
        wide_rows,
        stats,
        kept,
        slope,
        both,
        normed_mid,
        down_second,
    )
    grad_branch, grad_mixed, branch_sums, out_sent, out_stays = branch_back(
        core_arg,
        grad_attended,
        branch,
        weights,
        mixed,
        scales,
        vector_rows,
        scaled,
    )
    up_first, up_second = outer(
        core_arg,
        normed_mid,
        grad_hidden,
        [swap_cores(part) for part in sent_up],
        wait=(grad_branch, down_rest),
        more=(out_stays, swap_cores(out_sent)),
    )
    up_rest = plane_first(up_second)
    up_chips = over_x(up_first)
    grads, *sent_attn = attend_back(
        core_arg,
        projected,
        mixed,
        grad_mixed,
        attention,
        normed,
        (up_second, down_chips),
    )
    input_grad, turned = input_back(
        core_arg,
        grads,
        weights,
        tokens,
        grad_attended,
        vector_rows,
        (branch_sums, mid_sums, wide_sums),
        up_second,
    )

    turned = turned.reshape(chips, 2, TILE, TILE)
    half_sums = take_core(turned, core) + swap_cores(take_core(turned, 1 - core))
    attn_first = outer_stack(
        core_arg, normed, grads, [swap_cores(part) for part in sent_attn], half_sums, up_rest
    )

    early_parts = over_plane(jnp.concatenate([up_chips, down_chips], axis=1))
    half_sums, _ = lax.optimization_barrier((half_sums, attn_first))
    down_rest, up_rest, early_parts = lax.optimization_barrier((down_rest, up_rest, early_parts))
    small = jnp.sum(in_order(across_chips(half_sums)), axis=0)
    down_rest = down_rest.reshape(chips, 2, shard, -1)
    down_rest = take_core(down_rest, core) + swap_cores(
        take_core(down_rest, 1 - core).astype(BF16)
    ).astype(F32)
    rest = jnp.concatenate([down_rest, up_rest.reshape(chips, shard, -1)], axis=2)
    rest = across_chips(rest.astype(BF16))
    rest = sum(part.astype(F32) for part in rest)
    late_parts = over_plane(jnp.concatenate([over_x(attn_first), small.astype(BF16)], axis=1))
    small = late_parts[:, 3 * width :]
    vector_grads = small.T[: vectors.shape[0]]
    head_total = small[0, HEAD_AT : HEAD_AT + heads]

    masters = (w_qkv, w_out, w_up, w_down)
    grad_qkv, grad_out, grad_up, grad_down, slots = to_slots(
        owner_perm,
        early_parts,
        late_parts,
        rest,
        plane,
        [item.shape[1] for item in masters],
    )
    slots = lax.all_to_all(slots, "fsdp", split_axis=0, concat_axis=0, tiled=True)
    left_new, right_new, back = update(slots, left_stats, right_stats, left_roots, right_roots)
    back = lax.all_to_all(back, "fsdp", split_axis=0, concat_axis=0, tiled=True)
    new_qkv, new_out, new_up, new_down = apply_steps(owner_perm, back, masters)
    vector_stats_new = DECAY * vector_stats + (1.0 - DECAY) * vector_grads * vector_grads
    vectors_new = vectors - RATE_VECTOR * vector_grads * lax.rsqrt(vector_stats_new)
    head_stats_new = DECAY * head_stats + (1.0 - DECAY) * head_total * head_total
    head_new = head_scale - RATE_VECTOR * head_total * lax.rsqrt(head_stats_new)
    return (
        output,
        input_grad,
        grad_qkv,
        grad_out,
        grad_up,
        grad_down,
        vector_grads,
        head_total,
        left_new,
        right_new,
        new_qkv,
        new_out,
        new_up,
        new_down,
        vector_stats_new,
        vectors_new,
        head_stats_new,
        head_new,
    )


def solution(mesh):
    everywhere = ("x", "core", "fsdp")
    by_rows = P(everywhere, None)
    by_columns = P(None, everywhere)
    by_block = P(("x", "core"), "fsdp", None, None)
    dp, fsdp = mesh.devices.shape
    mesh = jax.sharding.Mesh(mesh.devices.reshape(dp // 2, 2, fsdp), everywhere)
    return jax.shard_map(
        shards,
        mesh=mesh,
        in_specs=(
            (by_rows, by_rows, P(everywhere), P(everywhere), P())
            + (by_rows,) * 4
            + (by_columns, P())
            + (by_block,) * 4
            + (by_columns, P())
        ),
        out_specs=(
            (by_rows,) * 6
            + (by_columns, P())
            + (by_block,) * 2
            + (by_rows,) * 4
            + (by_columns, by_columns, P(), P())
        ),
        check_vma=False,
    )
```

```python
import functools
import math

import jax
import jax.numpy as jnp
from jax import lax
from jax.experimental import pallas as pl
from jax.experimental.pallas import tpu as pltpu
from jax.sharding import PartitionSpec as P

TILE = 128
EPS = 1e-05
DECAY = 0.5
RATE_MATRIX = 0.1
RATE_VECTOR = 0.3
HIGHEST = lax.Precision.HIGHEST
HEAD_AT = 24
UP_FIRSTS = 2
VMEM_BYTES = 56 * 1024 * 1024
F32 = jnp.float32
BF16 = jnp.bfloat16


def dot_nn(left, right):
    return lax.dot_general(left, right, (((1,), (0,)), ((), ())), preferred_element_type=F32)


def dot_nt(left, right):
    return lax.dot_general(left, right, (((1,), (1,)), ((), ())), preferred_element_type=F32)


def dot_tn(left, right):
    return lax.dot_general(left, right, (((0,), (0,)), ((), ())), preferred_element_type=F32)


def row_stats(values):
    mean = jnp.mean(values, axis=-1, keepdims=True)
    centered = values - mean
    spread = lax.rsqrt(jnp.mean(centered * centered, axis=-1, keepdims=True) + EPS)
    return centered, spread


def norm_back(scaled_grad, unit, spread):
    mean_grad = jnp.mean(scaled_grad, axis=-1, keepdims=True)
    mean_both = jnp.mean(scaled_grad * unit, axis=-1, keepdims=True)
    return spread * (scaled_grad - mean_grad - unit * mean_both)


def lane_sum(values):
    total = values[:, :TILE]
    for at in range(TILE, values.shape[1], TILE):
        total = total + values[:, at : at + TILE]
    return total


def call(body, grid, in_specs, out_specs, out_shape, scratch=(), flops=0, bytes_accessed=0, scalars=0):
    return pl.pallas_call(
        body,
        out_shape=out_shape,
        grid_spec=pltpu.PrefetchScalarGridSpec(
            num_scalar_prefetch=scalars,
            grid=grid,
            in_specs=in_specs,
            out_specs=out_specs,
            scratch_shapes=list(scratch),
        ),
        compiler_params=pltpu.CompilerParams(vmem_limit_bytes=VMEM_BYTES),
        cost_estimate=pl.CostEstimate(
            flops=flops, bytes_accessed=bytes_accessed, transcendentals=0
        ),
    )


def whole(shape):
    return pl.BlockSpec(shape, lambda *_: (0,) * len(shape))


def after(*arrays):
    return [pl.BlockSpec(memory_space=pl.ANY) for _ in arrays]


def split_parity(values):
    blocks = [values[:, at : at + TILE] for at in range(0, values.shape[1], TILE)]
    return jnp.concatenate(blocks[0::2], axis=1), jnp.concatenate(blocks[1::2], axis=1)


def join_parity(even, odd):
    blocks = []
    for at in range(0, even.shape[1], TILE):
        blocks += [even[:, at : at + TILE], odd[:, at : at + TILE]]
    return jnp.concatenate(blocks, axis=1)


def turn_rows(left, turned, parity):
    for block in range(turned.shape[0] // TILE):
        at = pl.multiple_of((2 * block + parity) * TILE, TILE)
        turned[block * TILE : (block + 1) * TILE, :] = jnp.transpose(left[:, pl.ds(at, TILE)])


def by_owner(values, plane):
    rows, columns = values.shape
    chips = rows // (8 * plane)
    values = values.reshape(chips, plane, 8, columns)
    return jnp.concatenate([values[chip] for chip in range(chips)], axis=1)


def project_body(
    core, tokens, vectors, own_qk, other_qk, own_vo, other_vo, normed, projected, parts
):
    part = pl.program_id(0)

    @pl.when(part == 0)
    def _():
        centered, spread = row_stats(tokens[...].astype(F32))
        low = (centered * spread * vectors[0:1, :] + vectors[1:2, :]).astype(BF16)
        normed[...] = low
        parts[0], parts[1] = split_parity(low)

    gate_q = jnp.where(part == 0, 1.0, 0.0).astype(F32)
    gate_v = jnp.where(part == 2, 1.0, 0.0).astype(F32)
    bias = gate_q * vectors[2:3, :] + gate_v * vectors[3:4, :]
    me = core[0]

    @pl.when(part < 2)
    def _():
        projected[...] = (
            dot_nn(parts[me], own_qk[...]) + dot_nn(parts[1 - me], other_qk[...]) + bias
        ).astype(BF16)

    @pl.when(part == 2)
    def _():
        projected[...] = (
            dot_nn(parts[me], own_vo[...]) + dot_nn(parts[1 - me], other_vo[...]) + bias
        ).astype(BF16)


def project(core, tokens, vectors, weights):
    rows, width = tokens.shape
    parts = 3
    third = pl.BlockSpec((width // 2, width), lambda part, *_: (0, jnp.minimum(part, 1)))
    last = pl.BlockSpec((width // 2, width), lambda part, *_: (0, 0))
    return call(
        project_body,
        (parts,),
        [whole((rows, width)), whole(vectors.shape), third, third, last, last],
        [whole((rows, width)), pl.BlockSpec((rows, width), lambda part, *_: (0, part))],
        [
            jax.ShapeDtypeStruct((rows, width), BF16),
            jax.ShapeDtypeStruct((rows, parts * width), BF16),
        ],
        scratch=[pltpu.VMEM((2, rows, width // 2), BF16)],
        flops=2 * rows * width * width * parts,
        bytes_accessed=2 * width * width * parts,
        scalars=1,
    )(core, tokens, vectors, *weights)


def attend_body(length, scales, queries, keys, values, mixed, scaled, weights):
    rows = queries.shape[0]
    head_dim = TILE // 2
    pair = pl.program_id(0)
    block = rows // 2
    lane = lax.broadcasted_iota(jnp.int32, (rows, TILE), 1)
    spot = lax.broadcasted_iota(jnp.int32, (rows, TILE), 0)
    hidden_key = jnp.where(spot < length[0], 0.0, -1e30).astype(BF16)
    one = jnp.ones((rows, TILE), BF16)
    zero = jnp.zeros((rows, TILE), BF16)
    query = queries[...] * jnp.asarray(1.0 / math.sqrt(head_dim), BF16)
    key = keys[...]
    value = values[...]
    causal = lax.broadcasted_iota(jnp.int32, (block, block), 1) <= lax.broadcasted_iota(
        jnp.int32, (block, block), 0
    )
    total = [jnp.zeros((block, TILE), F32) for _ in range(2)]
    for head in range(2):
        mine = (lane < head_dim) if head == 0 else (lane >= head_dim)
        spare = lane == (head_dim if head == 0 else 0)
        query_one = jnp.where(mine, query, jnp.where(spare, one, zero))
        key_one = jnp.where(mine, key, jnp.where(spare, hidden_key, zero))
        value_one = jnp.where(mine, value, zero)
        for part in range(2):
            seen = (part + 1) * block
            score = dot_nt(query_one[part * block : seen], key_one[:seen])
            last = jnp.where(causal, score[:, part * block :], -1e30)
            score = last if part == 0 else jnp.concatenate([score[:, :block], last], axis=1)
            top = jnp.max(score, axis=1, keepdims=True)
            grown = jnp.exp(score - top)
            share = (grown * (1.0 / jnp.sum(grown, axis=1, keepdims=True))).astype(BF16)
            if part == 0:
                weights[head, :, :block] = share
            else:
                weights[head, :, block:] = share
            total[part] = total[part] + dot_nn(share, value_one[:seen])
    scale_row = jnp.where(
        lax.broadcasted_iota(jnp.int32, (1, TILE), 1) < head_dim,
        scales[2 * pair],
        scales[2 * pair + 1],
    )
    for part in range(2):
        mixed[part * block : (part + 1) * block, :] = total[part]
        scaled[part * block : (part + 1) * block, :] = (total[part] * scale_row).astype(BF16)


def attend(length, scales, projected):
    rows, width3 = projected.shape
    width = width3 // 3
    pairs = width // TILE
    block = rows // 2
    return call(
        attend_body,
        (pairs,),
        [
            pl.BlockSpec((rows, TILE), lambda pair, *_: (0, pair)),
            pl.BlockSpec((rows, TILE), lambda pair, *_: (0, pairs + pair)),
            pl.BlockSpec((rows, TILE), lambda pair, *_: (0, 2 * pairs + pair)),
        ],
        [
            pl.BlockSpec((rows, TILE), lambda pair, *_: (0, pair)),
            pl.BlockSpec((rows, TILE), lambda pair, *_: (0, pair)),
            pl.BlockSpec((2, block, 3 * block), lambda pair, *_: (pair, 0, 0)),
        ],
        [
            jax.ShapeDtypeStruct((rows, width), F32),
            jax.ShapeDtypeStruct((rows, width), BF16),
            jax.ShapeDtypeStruct((2 * pairs, block, 3 * block), BF16),
        ],
        flops=4 * rows * rows * width,
        bytes_accessed=20 * rows * width,
        scalars=2,
    )(length, scales, projected, projected, projected)


def attend_back_body(
    core, queries, keys, values, mixed, grads, weights, normed, _, __, out, sent_q, sent_k, sent_v, turned
):
    @pl.when(pl.program_id(0) == 0)
    def _():
        turn_rows(normed, turned, 1 - core[0])

    rows = queries.shape[0]
    head_dim = TILE // 2
    block = rows // 2
    lane = lax.broadcasted_iota(jnp.int32, (rows, TILE), 1)
    zero = jnp.zeros((rows, TILE), BF16)
    query, key, value, grad = queries[...], keys[...], values[...], grads[...]
    both = grad.astype(F32) * mixed[...]
    q_total = [jnp.zeros((block, TILE), F32) for _ in range(2)]
    k_total = [jnp.zeros((block, TILE), F32) for _ in range(2)]
    v_total = [jnp.zeros((block, TILE), F32) for _ in range(2)]
    for head in range(2):
        mine = (lane < head_dim) if head == 0 else (lane >= head_dim)
        query_one = jnp.where(mine, query, zero)
        key_one = jnp.where(mine, key, zero)
        grad_one = jnp.where(mine, grad, zero)
        delta = jnp.sum(jnp.where(mine, both, 0.0), axis=1, keepdims=True)
        for part in range(2):
            at = part * block
            seen = at + block
            share = weights[head, :, :block] if part == 0 else weights[head, :, block:]
            into = dot_nt(grad_one[at:seen], value[:seen])
            slope = (share.astype(F32) * (into - delta[at:seen])).astype(BF16)
            q_total[part] = q_total[part] + dot_nn(slope, key_one[:seen])
            k_new = dot_tn(slope, query_one[at:seen])
            v_new = dot_tn(share, grad_one[at:seen])
            for into_part in range(part + 1):
                cut = slice(into_part * block, (into_part + 1) * block)
                k_total[into_part] = k_total[into_part] + k_new[cut]
                v_total[into_part] = v_total[into_part] + v_new[cut]
    root = 1.0 / math.sqrt(head_dim)
    low_q = (jnp.concatenate(q_total, axis=0) * root).astype(BF16)
    low_k = (jnp.concatenate(k_total, axis=0) * root).astype(BF16)
    low_v = jnp.concatenate(v_total, axis=0).astype(BF16)
    out[0], out[1], out[2] = low_q, low_k, low_v
    values = dot_nn(turned[...], jnp.concatenate([low_q, low_k, low_v], axis=1)).astype(BF16)
    for which, sent in enumerate((sent_q, sent_k, sent_v)):
        sent[...] = values[:, which * TILE : (which + 1) * TILE]


def attend_back(core, projected, mixed, grads, weights, normed, wait):
    rows, width3 = projected.shape
    width = width3 // 3
    half = width // 2
    pairs = width // TILE
    block = rows // 2
    by_pair = pl.BlockSpec((rows, TILE), lambda pair, *_: (0, pair))
    return call(
        attend_back_body,
        (pairs,),
        [
            by_pair,
            pl.BlockSpec((rows, TILE), lambda pair, *_: (0, pairs + pair)),
            pl.BlockSpec((rows, TILE), lambda pair, *_: (0, 2 * pairs + pair)),
            by_pair,
            by_pair,
            pl.BlockSpec((2, block, 3 * block), lambda pair, *_: (pair, 0, 0)),
            whole((rows, width)),
            *after(*wait),
        ],
        [
            pl.BlockSpec((3, rows, TILE), lambda pair, *_: (0, 0, pair)),
            *[pl.BlockSpec((half, TILE), lambda pair, *_: (0, pair)) for _ in range(3)],
        ],
        [
            jax.ShapeDtypeStruct((3, rows, width), BF16),
            *[jax.ShapeDtypeStruct((half, width), BF16) for _ in range(3)],
        ],
        scratch=[pltpu.VMEM((half, rows), BF16)],
        flops=10 * rows * rows * width,
        bytes_accessed=24 * rows * width,
        scalars=1,
    )(core, projected, projected, projected, mixed, grads, weights, normed, *wait)


def branch_body(core, scaled, own, other, tokens, vectors, branch, attended, normed, parts):
    parts[0], parts[1] = split_parity(scaled[...])
    me = core[0]
    value = dot_nn(parts[me], own[...]) + dot_nn(parts[1 - me], other[...]) + vectors[6:7, :]
    branch[...] = value
    centered, spread = row_stats(value)
    total = tokens[...].astype(F32) + centered * spread * vectors[4:5, :] + vectors[5:6, :]
    attended[...] = total
    centered, spread = row_stats(total)
    normed[...] = (centered * spread * vectors[7:8, :] + vectors[8:9, :]).astype(BF16)


def branch_out(core, scaled, weights, tokens, vectors):
    rows, width = scaled.shape
    block = rows // 4
    by_row = pl.BlockSpec((block, width), lambda at, *_: (at, 0))
    fourth = pl.BlockSpec((width // 2, width), lambda at, *_: (0, 1))
    return call(
        branch_body,
        (rows // block,),
        [by_row, fourth, fourth, by_row, whole(vectors.shape)],
        [by_row, by_row, by_row],
        [
            jax.ShapeDtypeStruct((rows, width), F32),
            jax.ShapeDtypeStruct((rows, width), F32),
            jax.ShapeDtypeStruct((rows, width), BF16),
        ],
        scratch=[pltpu.VMEM((2, block, width // 2), BF16)],
        flops=2 * rows * width * width,
        bytes_accessed=2 * width * width + 14 * rows * width,
        scalars=1,
    )(core, scaled, *weights[2:], tokens, vectors)


def branch_back_body(
    core,
    grad_attended,
    branch,
    own,
    other,
    mixed,
    scales,
    vectors,
    scaled,
    grad_branch,
    grad_mixed,
    sums,
    sent,
    staying,
    parts,
    lows,
    turned,
):
    at = pl.program_id(0)

    @pl.when(at == 0)
    def _():
        sums[...] = jnp.zeros_like(sums)

    grad = grad_attended[...]
    centered, spread = row_stats(branch[...])
    unit = centered * spread
    low = norm_back(grad * vectors[4:5, :], unit, spread).astype(BF16)
    grad_branch[...] = low
    lows[at] = low
    me = core[0]
    parts[me] = dot_nt(low, own[...])
    parts[1 - me] = dot_nt(low, other[...])
    grad_scaled = join_parity(parts[0], parts[1])
    grad_mixed[...] = (grad_scaled * scales[0:1, :]).astype(BF16)
    sums[0:1, :] += jnp.sum(grad * unit, axis=0, keepdims=True)
    sums[1:2, :] += jnp.sum(grad, axis=0, keepdims=True)
    sums[2:3, :] += jnp.sum(low.astype(F32), axis=0, keepdims=True)
    sums[3:4, :] += jnp.sum(grad_scaled * mixed[...], axis=0, keepdims=True)

    @pl.when(at == pl.num_programs(0) - 1)
    def _():
        right = lows[...].reshape(scaled.shape)
        turn_rows(scaled, turned, 1 - me)
        sent[...] = dot_nn(turned[...], right).astype(BF16)
        turn_rows(scaled, turned, me)
        staying[...] = dot_nn(turned[...], right)


def branch_back(core, grad_attended, branch, weights, mixed, scales, vectors, scaled, *wait):
    rows, width = branch.shape
    block = rows // 4
    by_row = pl.BlockSpec((block, width), lambda at, *_: (at, 0))
    fourth = pl.BlockSpec((width // 2, width), lambda at, *_: (0, 1))
    return call(
        branch_back_body,
        (rows // block,),
        [
            by_row,
            by_row,
            fourth,
            fourth,
            by_row,
            whole(scales.shape),
            whole(vectors.shape),
            whole(scaled.shape),
            *after(*wait),
        ],
        [by_row, by_row, whole((8, width)), whole((width // 2, width)), whole((width // 2, width))],
        [
            jax.ShapeDtypeStruct((rows, width), BF16),
            jax.ShapeDtypeStruct((rows, width), BF16),
            jax.ShapeDtypeStruct((8, width), F32),
            jax.ShapeDtypeStruct((width // 2, width), BF16),
            jax.ShapeDtypeStruct((width // 2, width), F32),
        ],
        scratch=[
            pltpu.VMEM((2, block, width // 2), F32),
            pltpu.VMEM((rows // block, block, width), BF16),
            pltpu.VMEM((width // 2, rows), BF16),
        ],
        flops=4 * rows * width * width,
        bytes_accessed=2 * width * width + 16 * rows * width,
        scalars=1,
    )(core, grad_attended, branch, *weights[2:], mixed, scales, vectors, scaled, *wait)


def send_part(values, step, firsts, first, second):
    @pl.when(step < firsts)
    def _():
        first[...] = values.astype(BF16)

    @pl.when(step >= firsts)
    def _():
        second[...] = by_owner(values, second.shape[0]).astype(BF16)


def part_specs(half, plane, start, firsts):
    return [
        pl.BlockSpec((half, 1024), lambda at, *_: (0, jnp.clip(at - start, 0, firsts - 1))),
        pl.BlockSpec(
            (plane, half // plane, 1024),
            lambda at, *_: (0, 0, jnp.clip(at - start - firsts, 0, 3 - firsts)),
        ),
    ]


def part_shapes(half, plane, firsts):
    return [
        jax.ShapeDtypeStruct((half, firsts * 1024), BF16),
        jax.ShapeDtypeStruct((plane, half // plane, (4 - firsts) * 1024), BF16),
    ]


def forward_ffn_body(
    steps,
    normed,
    attended,
    vectors,
    rows_of,
    weights,
    upstream,
    output,
    kept,
    slope,
    stats,
    sent,
    held,
    total,
    sums,
    turned,
):
    at = pl.program_id(0)
    width = held.shape[2]

    @pl.when(at == 0)
    def _():
        sums[...] = jnp.zeros_like(sums)

    @pl.when(at < steps)
    def _():
        hidden = dot_nn(normed[...], weights[...]) + rows_of[0:1, :]
        cdf = 0.5 + 0.5 * lax.erf(hidden * math.sqrt(0.5))
        value = hidden * cdf
        slope[...] = (
            cdf + hidden * (jnp.exp(-0.5 * hidden * hidden) * (1.0 / math.sqrt(2.0 * math.pi)))
        ).astype(BF16)
        held[at] = value
        kept[...] = value.astype(BF16)
        sums[...] += lane_sum(value)
        share = attended.shape[1]
        start = pl.multiple_of(at * share, share)
        total[:, pl.ds(start, share)] = attended[...] + vectors[21:22, pl.ds(start, share)]
        for block in range(0, share, TILE):
            turned[pl.ds(start + block, TILE), :] = jnp.transpose(
                upstream[:, block : block + TILE]
            )

    @pl.when(at == steps)
    def _():
        count = steps * width
        mean = jnp.sum(sums[...], axis=1, keepdims=True) * (1.0 / count)
        square = jnp.zeros(sums.shape, F32)
        for block in range(steps):
            centered = held[block] - mean
            square = square + lane_sum(centered * centered)
        spread = lax.rsqrt(jnp.sum(square, axis=1, keepdims=True) * (1.0 / count) + EPS)
        stats[:, :TILE] = jnp.broadcast_to(mean, sums.shape)
        stats[:, TILE:] = jnp.broadcast_to(spread, sums.shape)

    @pl.when(at >= steps)
    def _():
        mean = stats[:, 0:1]
        spread = stats[:, TILE : TILE + 1]
        value = held[at - steps]
        low = ((value - mean) * spread * rows_of[1:2, :] + rows_of[2:3, :]).astype(BF16)
        total[...] += dot_nt(low, weights[...])
        sent[...] = dot_nn(turned[...], low).astype(BF16)

    @pl.when(at == 2 * steps - 1)
    def _():
        output[...] = total[...].astype(BF16)


def forward_ffn(normed, attended, vectors, wide_rows, both, upstream):
    rows, width = attended.shape
    hidden = both.shape[1] // 2
    block = 1024
    steps = hidden // block
    early = lambda at, *_: (0, jnp.minimum(at, steps - 1))
    return call(
        functools.partial(forward_ffn_body, steps),
        (2 * steps,),
        [
            whole((rows, width)),
            pl.BlockSpec((rows, width // steps), early),
            whole(vectors.shape),
            pl.BlockSpec((8, block), lambda at, *_: (0, lax.rem(at, steps))),
            pl.BlockSpec((width, block), lambda at, *_: (0, at)),
            pl.BlockSpec((rows, width // steps), early),
        ],
        [
            whole((rows, width)),
            pl.BlockSpec((rows, block), early),
            pl.BlockSpec((rows, block), early),
            whole((rows, 2 * TILE)),
            pl.BlockSpec((width, block), lambda at, *_: (0, jnp.maximum(at - steps, 0))),
        ],
        [
            jax.ShapeDtypeStruct((rows, width), BF16),
            jax.ShapeDtypeStruct((rows, hidden), BF16),
            jax.ShapeDtypeStruct((rows, hidden), BF16),
            jax.ShapeDtypeStruct((rows, 2 * TILE), F32),
            jax.ShapeDtypeStruct((width, hidden), BF16),
        ],
        scratch=[
            pltpu.VMEM((steps, rows, block), F32),
            pltpu.VMEM((rows, width), F32),
            pltpu.VMEM((rows, TILE), F32),
            pltpu.VMEM((width, rows), BF16),
        ],
        flops=6 * rows * width * hidden,
        bytes_accessed=4 * width * hidden + 6 * rows * hidden,
    )(normed, attended, vectors, wide_rows, both, upstream)


def backward_ffn_body(
    steps,
    core,
    upstream,
    attended,
    vectors,
    rows_of,
    stats,
    kept,
    slope,
    weights,
    normed,
    _,
    grad_attended,
    grad_hidden,
    wide_sums,
    sums,
    sent_first,
    sent_second,
    held,
    total,
    first,
    second,
    turned,
    saved,
    units,
):
    at = pl.program_id(0)
    count = steps * held.shape[2]
    mean = stats[:, 0:1]
    spread = stats[:, TILE : TILE + 1]

    @pl.when(at == 0)
    def _():
        first[...] = jnp.zeros_like(first)
        second[...] = jnp.zeros_like(second)
        total[...] = jnp.zeros_like(total)
        wide_sums[...] = jnp.zeros_like(wide_sums)

    @pl.when(at < steps)
    def _():
        grad = dot_nn(upstream[...], weights[...])
        unit = (kept[...].astype(F32) - mean) * spread
        units[at] = unit.astype(BF16)
        both = grad * unit
        share = attended.shape[1]
        saved[:, pl.ds(pl.multiple_of(at * share, share), share)] = attended[...]
        lane = pl.multiple_of((1 - core[0]) * TILE, TILE)
        turned[pl.ds(pl.multiple_of(at * TILE, TILE), TILE), :] = jnp.transpose(
            normed[:, pl.ds(lane, TILE)]
        )
        wide_sums[at, 0:1, :] = jnp.sum(both, axis=0, keepdims=True)
        wide_sums[at, 1:2, :] = jnp.sum(grad, axis=0, keepdims=True)
        gain = rows_of[1:2, :]
        held[at] = grad * gain
        first[...] += lane_sum(grad * gain)
        second[...] += lane_sum(both * gain)

    @pl.when(at == steps)
    def _():
        scale = 1.0 / count
        first[...] = jnp.broadcast_to(
            jnp.sum(first[...], axis=1, keepdims=True) * scale, first.shape
        )
        second[...] = jnp.broadcast_to(
            jnp.sum(second[...], axis=1, keepdims=True) * scale, second.shape
        )

    @pl.when(at >= steps)
    def _():
        unit = units[at - steps].astype(F32)
        grad = spread * (held[at - steps] - first[:, 0:1] - unit * second[:, 0:1])
        low = (grad * slope[...].astype(F32)).astype(BF16)
        grad_hidden[...] = low
        wide_sums[at - steps, 2:3, :] = jnp.sum(low.astype(F32), axis=0, keepdims=True)
        total[...] += dot_nt(low, weights[...])
        send_part(dot_nn(turned[...], low), at - steps, UP_FIRSTS, sent_first, sent_second)

    @pl.when(at == 2 * steps - 1)
    def _():
        grad = total[...]
        centered, mid_spread = row_stats(saved[...])
        unit = centered * mid_spread
        top = upstream[...].astype(F32)
        grad_attended[...] = top + norm_back(grad * vectors[7:8, :], unit, mid_spread)
        sums[0:1, :] = jnp.sum(grad * unit, axis=0, keepdims=True)
        sums[1:2, :] = jnp.sum(grad, axis=0, keepdims=True)
        sums[2:3, :] = jnp.sum(top, axis=0, keepdims=True)
        sums[3:8, :] = jnp.zeros((5, sums.shape[1]), F32)


def backward_ffn(
    core, plane, upstream, attended, vectors, wide_rows, stats, kept, slope, both, normed, wait
):
    rows, width = attended.shape
    hidden = both.shape[1] // 2
    block = 1024
    steps = hidden // block
    late = lambda at, *_: (0, jnp.maximum(at - steps, 0))
    early = lambda at, *_: (0, jnp.minimum(at, steps - 1))
    turn = lambda at, *_: (0, lax.rem(at, steps))
    return call(
        functools.partial(backward_ffn_body, steps),
        (2 * steps,),
        [
            whole((rows, width)),
            pl.BlockSpec((rows, width // steps), early),
            whole(vectors.shape),
            pl.BlockSpec((8, block), turn),
            whole((rows, 2 * TILE)),
            pl.BlockSpec((rows, block), early),
            pl.BlockSpec((rows, block), late),
            pl.BlockSpec((width, block), lambda at, *_: (0, lax.rem(at + steps, 2 * steps))),
            pl.BlockSpec((rows, width // steps), early),
            *after(wait),
        ],
        [
            whole((rows, width)),
            pl.BlockSpec((rows, block), late),
            whole((steps, 8, block)),
            whole((8, width)),
            *part_specs(width // 2, plane, steps, UP_FIRSTS),
        ],
        [
            jax.ShapeDtypeStruct((rows, width), F32),
            jax.ShapeDtypeStruct((rows, hidden), BF16),
            jax.ShapeDtypeStruct((steps, 8, block), F32),
            jax.ShapeDtypeStruct((8, width), F32),
            *part_shapes(width // 2, plane, UP_FIRSTS),
        ],
        scratch=[
            pltpu.VMEM((steps, rows, block), F32),
            pltpu.VMEM((rows, width), F32),
            pltpu.VMEM((rows, TILE), F32),
            pltpu.VMEM((rows, TILE), F32),
            pltpu.VMEM((width // 2, rows), BF16),
            pltpu.VMEM((rows, width), F32),
            pltpu.VMEM((steps, rows, block), BF16),
        ],
        flops=5 * rows * width * hidden,
        bytes_accessed=4 * width * hidden + 8 * rows * hidden,
        scalars=1,
    )(core, upstream, attended, vectors, wide_rows, stats, kept, slope, both, normed, wait)


def input_back_body(
    core,
    grads,
    own_qk,
    other_qk,
    own_vo,
    other_vo,
    tokens,
    grad_attended,
    vectors,
    branch_sums,
    mid_sums,
    wide_sums,
    _,
    input_grad,
    turned,
    parts,
    sums,
):
    part = pl.program_id(0)
    me = core[0]
    grad_part = grads[...]

    @pl.when(part == 0)
    def _():
        parts[me] = dot_nt(grad_part, own_qk[...])
        parts[1 - me] = dot_nt(grad_part, other_qk[...])
        sums[...] = jnp.zeros_like(sums)
        sums[2:3, :] = jnp.sum(grad_part.astype(F32), axis=0, keepdims=True)

    @pl.when(part == 1)
    def _():
        parts[me] += dot_nt(grad_part, own_qk[...])
        parts[1 - me] += dot_nt(grad_part, other_qk[...])

    @pl.when(part == 2)
    def _():
        parts[me] += dot_nt(grad_part, own_vo[...])
        parts[1 - me] += dot_nt(grad_part, other_vo[...])
        grad = join_parity(parts[0], parts[1])
        centered, spread = row_stats(tokens[...].astype(F32))
        unit = centered * spread
        input_grad[...] = grad_attended[...] + norm_back(grad * vectors[0:1, :], unit, spread)
        sums[0:1, :] = jnp.sum(grad * unit, axis=0, keepdims=True)
        sums[1:2, :] = jnp.sum(grad, axis=0, keepdims=True)
        sums[3:4, :] = jnp.sum(grad_part.astype(F32), axis=0, keepdims=True)
        sums[4:7, :] = branch_sums[0:3, :]
        sums[7:9, :] = mid_sums[0:2, :]
        for row in range(wide_sums.shape[0]):
            sums[9 + row : 10 + row, :] = wide_sums[row, 2:3, :]
            sums[13 + row : 14 + row, :] = wide_sums[row, 0:1, :]
            sums[17 + row : 18 + row, :] = wide_sums[row, 1:2, :]
        sums[21:22, :] = mid_sums[2:3, :]
        width = sums.shape[1]
        head_dim = TILE // 2
        picks = (
            lax.broadcasted_iota(jnp.int32, (width, TILE), 0) // head_dim + HEAD_AT
            == lax.broadcasted_iota(jnp.int32, (width, TILE), 1)
        ).astype(F32)
        heads = lax.dot_general(
            branch_sums[...],
            picks,
            (((1,), (0,)), ((), ())),
            precision=HIGHEST,
            preferred_element_type=F32,
        )[3:4, :]
        for block in range(turned.shape[0]):
            turned[block] = (
                jnp.transpose(sums[:, block * TILE : (block + 1) * TILE]) + heads
            )


def input_back(core, grads, weights, tokens, grad_attended, vectors, sums, wait):
    rows, width = tokens.shape
    full = whole((rows, width))
    third = pl.BlockSpec((width // 2, width), lambda part, *_: (0, jnp.minimum(part, 1)))
    last = pl.BlockSpec((width // 2, width), lambda part, *_: (0, 0))
    return call(
        input_back_body,
        (3,),
        [
            pl.BlockSpec((None, rows, width), lambda part, *_: (part, 0, 0)),
            third,
            third,
            last,
            last,
            full,
            full,
            whole(vectors.shape),
            *[whole(item.shape) for item in sums],
            *after(wait),
        ],
        [full, whole((width // TILE, TILE, TILE))],
        [
            jax.ShapeDtypeStruct((rows, width), F32),
            jax.ShapeDtypeStruct((width // TILE, TILE, TILE), F32),
        ],
        scratch=[pltpu.VMEM((2, rows, width // 2), F32), pltpu.VMEM((TILE, width), F32)],
        flops=6 * rows * width * width,
        bytes_accessed=6 * width * width + 16 * rows * width,
        scalars=1,
    )(core, grads, *weights, tokens, grad_attended, vectors, *sums, wait)


def outer_body(firsts, more, core, left, right, add_first, add_second, *refs):
    first, second, turned = refs[-3:]
    at = pl.program_id(0)

    @pl.when(at == 0)
    def _():
        turn_rows(left, turned, core[0])

    value = dot_nn(turned[...], right[...])

    @pl.when(at < firsts)
    def _():
        first[...] = (value + add_first[...].astype(F32)).astype(BF16)

    if more:

        @pl.when(at == firsts)
        def _():
            first[...] = (refs[0][...] + refs[1][...].astype(F32)).astype(BF16)

    @pl.when(at >= firsts)
    def _():
        second[...] = (
            by_owner(value, second.shape[0]) + add_second[...].astype(F32)
        ).astype(BF16)


def outer(core, left, right, add, wait=(), more=()):
    rows, width = left.shape
    half = width // 2
    block = 1024
    add_first, add_second = add
    plane, owned = add_second.shape[:2]
    firsts = UP_FIRSTS
    seconds = add_second.shape[2] // block
    right_spec = pl.BlockSpec((rows, block), lambda at, *_: (0, at))
    add_spec = pl.BlockSpec((half, block), lambda at, *_: (0, jnp.clip(at, 0, firsts - 1)))
    second_spec = pl.BlockSpec(
        (plane, owned, block), lambda at, *_: (0, 0, jnp.clip(at - firsts, 0, seconds - 1))
    )
    kinds = firsts + len(more) // 2
    out_specs = [
        pl.BlockSpec((half, block), lambda at, *_: (0, jnp.clip(at, 0, kinds - 1))),
        second_spec,
    ]
    out_shape = [
        jax.ShapeDtypeStruct((half, kinds * block), BF16),
        jax.ShapeDtypeStruct(add_second.shape, BF16),
    ]
    return call(
        functools.partial(outer_body, firsts, len(more) > 0),
        (firsts + seconds,),
        [
            whole((rows, width)),
            right_spec,
            add_spec,
            second_spec,
            *[whole(item.shape) for item in more],
            *after(*wait),
        ],
        out_specs,
        out_shape,
        scratch=[pltpu.VMEM((half, rows), BF16)],
        flops=2 * rows * half * block * (firsts + seconds),
        bytes_accessed=6 * half * block * (firsts + seconds),
        scalars=1,
    )(core, left, right, add_first, add_second, *more, *wait)


def outer_stack_body(core, left, right, *refs):
    adds, (out, turned) = refs[:3], refs[-2:]
    at = pl.program_id(0)

    @pl.when(at == 0)
    def _():
        turn_rows(left, turned, core[0])

    value = dot_nn(turned[...], right[...])
    for which, add in enumerate(adds):

        @pl.when(at == which)
        def _(add=add):
            out[...] = (value + add[...].astype(F32)).astype(BF16)


def outer_stack(core, left, rights, adds, *wait):
    count, rows, width = rights.shape
    half = width // 2
    return call(
        outer_stack_body,
        (count,),
        [
            whole((rows, width)),
            pl.BlockSpec((None, rows, width), lambda at, *_: (at, 0, 0)),
            *[whole((half, width)) for _ in adds],
            *after(*wait),
        ],
        pl.BlockSpec((half, width), lambda at, *_: (0, at)),
        jax.ShapeDtypeStruct((half, count * width), BF16),
        scratch=[pltpu.VMEM((half, rows), BF16)],
        flops=2 * rows * half * width * count,
        bytes_accessed=6 * half * width * count,
        scalars=1,
    )(core, left, rights, *adds, *wait)


def to_slots_body(perm, early, late, rest, *refs):
    grad_qkv, grad_out, grad_up, grad_down, slots, tiles = refs
    width = grad_out.shape[1]
    half = 2 * width
    grad_out[...] = early[:, half : half + width]
    grad_qkv[...] = late[:, : 3 * width]
    grad_down[...] = early[:, half + width :]
    grad_up[:, :half] = early[:, :half]
    grad_up[:, half:] = rest[...]
    column = 0
    for result in (grad_qkv, grad_out, grad_up, grad_down):
        for at in range(0, result.shape[1], TILE):
            tiles[column] = result[:, at : at + TILE]
            column += 1
    planes, pairs = slots.shape[:2]
    for slot in range(planes * pairs):
        pair = [tiles[perm[2 * slot + which]] for which in range(2)]
        slots[slot // pairs, slot % pairs] = jnp.concatenate(pair, axis=0).astype(BF16)


def to_slots(perm, early, late, rest, plane, widths):
    arrays = [early, late, rest]
    pairs = perm.shape[0] // (2 * plane)
    shapes = [jax.ShapeDtypeStruct((8, columns), F32) for columns in widths]
    shapes.append(jax.ShapeDtypeStruct((plane, pairs, 16, TILE), BF16))
    return call(
        to_slots_body,
        (1,),
        [whole(item.shape) for item in arrays],
        [whole(item.shape) for item in shapes],
        shapes,
        scratch=[pltpu.VMEM((perm.shape[0], 8, TILE), F32)],
        bytes_accessed=8 * 8 * sum(widths),
        scalars=1,
    )(perm, *arrays)


def update_body(grads, left_stats, right_stats, left_roots, right_roots, left_new, right_new, back):
    planes, pairs = grads.shape[:2]
    for pair in range(pairs):
        block = grads[:, pair].astype(F32)
        moved = []
        for which in range(2):
            slot = 2 * pair + which
            grad = block[:, which * 8 : which * 8 + 8, :].reshape(TILE, TILE)
            low = grad.astype(BF16)
            left_new[slot] = DECAY * left_stats[slot] + (1.0 - DECAY) * dot_nt(low, low)
            right_new[slot] = DECAY * right_stats[slot] + (1.0 - DECAY) * dot_tn(low, low)
            step = jnp.dot(grad, right_roots[slot], precision=HIGHEST, preferred_element_type=F32)
            step = jnp.dot(left_roots[slot], step, precision=HIGHEST, preferred_element_type=F32)
            moved.append(step.reshape(planes, 8, TILE))
        back[:, pair] = jnp.concatenate(moved, axis=1).astype(BF16)


def update(grads, left_stats, right_stats, left_roots, right_roots):
    arrays = [item[0] for item in (left_stats, right_stats, left_roots, right_roots)]
    stats = jax.ShapeDtypeStruct(arrays[0].shape, F32)
    left_new, right_new, back = call(
        update_body,
        (1,),
        [whole(grads.shape)] + [whole(item.shape) for item in arrays],
        [whole(stats.shape), whole(stats.shape), whole(grads.shape)],
        [stats, stats, jax.ShapeDtypeStruct(grads.shape, BF16)],
        bytes_accessed=24 * arrays[0].size,
    )(grads, *arrays)
    return left_new[None], right_new[None], back


def apply_body(perm, moved, *refs):
    olds, news, tiles = refs[:4], refs[4:8], refs[8]
    pairs = moved.shape[1]
    for slot in range(moved.shape[0] * pairs):
        value = moved[slot // pairs, slot % pairs].astype(F32)
        tiles[perm[2 * slot]] = value[:8]
        tiles[perm[2 * slot + 1]] = value[8:]
    column = 0
    for old, new in zip(olds, news):
        for at in range(0, old.shape[1], TILE):
            cut = slice(at, at + TILE)
            new[:, cut] = old[:, cut] - RATE_MATRIX * tiles[column]
            column += 1


def apply_steps(perm, moved, weights):
    shapes = [jax.ShapeDtypeStruct(item.shape, F32) for item in weights]
    return call(
        apply_body,
        (1,),
        [whole(moved.shape)] + [whole(item.shape) for item in weights],
        [whole(item.shape) for item in shapes],
        shapes,
        scratch=[pltpu.VMEM((perm.shape[0], 8, TILE), F32)],
        bytes_accessed=10 * 8 * TILE * perm.shape[0],
        scalars=1,
    )(perm, moved, *weights)


def swap_cores(values):
    return lax.ppermute(values, "core", [(0, 1), (1, 0)])


def take_core(values, core):
    return lax.dynamic_slice_in_dim(values, core, 1, 1, allow_negative_indices=False)[:, 0]


def turn_chips(values, step):
    count = lax.axis_size("x")
    return lax.ppermute(values, "x", [(at, (at + step) % count) for at in range(count)])


def sum_parts(parts):
    return jnp.sum(parts.astype(F32), axis=0)


def shards(
    tokens,
    cotangent,
    lengths,
    valid,
    owner_perm,
    w_qkv,
    w_out,
    w_up,
    w_down,
    vectors,
    head_scale,
    left_stats,
    right_stats,
    left_roots,
    right_roots,
    vector_stats,
    head_stats,
):
    rows, width = tokens.shape
    heads = head_scale.shape[0]
    hidden = w_up.shape[1]
    ratio = hidden // width
    shard = w_up.shape[0]
    plane = lax.axis_size("fsdp")
    chips = lax.axis_size("x")
    core = lax.axis_index("core")
    core_arg = core.astype(jnp.int32).reshape(1)

    both = lax.all_gather(
        jnp.concatenate([w_up.astype(BF16), w_down.astype(BF16)], axis=1),
        ("x", "core", "fsdp"),
        axis=0,
        tiled=True,
    )
    low_qk = jnp.concatenate(
        [
            w_qkv[:, : 2 * width].astype(BF16),
            jnp.pad(vectors.astype(BF16).T, ((0, 0), (0, TILE - vectors.shape[0]))),
        ],
        axis=1,
    )
    low_vo = jnp.concatenate([w_qkv[:, 2 * width :].astype(BF16), w_out.astype(BF16)], axis=1)

    def to_plane(part, concat):
        spread = jnp.broadcast_to(part[None], (plane,) + part.shape)
        return lax.all_to_all(spread, "fsdp", split_axis=0, concat_axis=concat, tiled=True)

    place = lax.axis_index("x")

    def roll_chips(parts, start):
        twice = jnp.concatenate([parts, parts], axis=0)
        begin = [start] + [0] * (parts.ndim - 1)
        return lax.dynamic_slice(twice, begin, parts.shape, allow_negative_indices=False)

    def in_order(parts):
        return roll_chips(jnp.stack(parts[::-1]), chips - 1 - place)

    def to_chips(part):
        return in_order([part] + [turn_chips(part, step) for step in range(1, chips)])

    def across_chips(parts):
        ahead = roll_chips(parts, place)
        return [ahead[0]] + [turn_chips(ahead[step], step) for step in range(1, chips)]

    own_vo = to_plane(to_chips(low_vo), 2).reshape(width // 2, -1)
    own_qk = to_chips(to_plane(low_qk, 0).reshape(plane * shard, -1)).reshape(width // 2, -1)
    other_qk, other_vo = swap_cores(own_qk), swap_cores(own_vo)
    weights = (own_qk, other_qk, own_vo, other_vo)
    vector_at = 2 * width
    vector_pair = jnp.stack([own_qk[:, vector_at:], other_qk[:, vector_at:]])
    vector_pair = jnp.where(core == 0, vector_pair, vector_pair[::-1])
    vector_rows = (
        vector_pair.reshape(2, -1, TILE, TILE)
        .transpose(1, 0, 2, 3)
        .reshape(width, TILE)
        .T[:24]
        .astype(F32)
    )
    wide_rows = jnp.concatenate(
        [
            vector_rows[9 : 9 + 3 * ratio].reshape(3, hidden),
            jnp.zeros((5, hidden), F32),
        ],
        axis=0,
    )
    upstream = jnp.where(valid[:, None] != 0, cotangent, jnp.zeros_like(cotangent))
    scales = jnp.broadcast_to(jnp.repeat(head_scale, width // heads)[None], (8, width))

    normed, projected = project(core_arg, tokens, vector_rows, weights)
    mixed, scaled, attention = attend(lengths, head_scale, projected)
    branch, attended, normed_mid = branch_out(core_arg, scaled, weights, tokens, vector_rows)
    output, kept, slope, stats, down_local = forward_ffn(
        normed_mid, attended, vector_rows, wide_rows, both, upstream
    )

    def over_x(part):
        return lax.psum_scatter(part, "x", scatter_dimension=0, tiled=True)

    def over_plane(part):
        return sum_parts(
            lax.all_to_all(
                part.reshape(plane, shard, -1), "fsdp", split_axis=0, concat_axis=0, tiled=True
            )
        )

    def plane_first(part):
        total = lax.all_to_all(part, "fsdp", split_axis=0, concat_axis=0, tiled=True)
        return sum_parts(total)

    down_chips = lax.psum_scatter(down_local, ("x", "core"), scatter_dimension=0, tiled=True)
    grad_attended, grad_hidden, wide_sums, mid_sums, *sent_up = backward_ffn(
        core_arg,
        plane,
        upstream,
        attended,
        vector_rows,
        wide_rows,
        stats,
        kept,
        slope,
        both,
        normed_mid,
        down_local,
    )
    grad_branch, grad_mixed, branch_sums, out_sent, out_stays = branch_back(
        core_arg,
        grad_attended,
        branch,
        weights,
        mixed,
        scales,
        vector_rows,
        scaled,
    )
    up_first, up_second = outer(
        core_arg,
        normed_mid,
        grad_hidden,
        [swap_cores(part) for part in sent_up],
        wait=(grad_branch,),
        more=(out_stays, swap_cores(out_sent)),
    )
    up_rest = plane_first(up_second)
    up_chips = over_x(up_first)
    grads, *sent_attn = attend_back(
        core_arg,
        projected,
        mixed,
        grad_mixed,
        attention,
        normed,
        (up_second, down_chips),
    )
    input_grad, turned = input_back(
        core_arg,
        grads,
        weights,
        tokens,
        grad_attended,
        vector_rows,
        (branch_sums, mid_sums, wide_sums),
        up_second,
    )

    turned = turned.reshape(chips, 2, TILE, TILE)
    half_sums = take_core(turned, core) + swap_cores(take_core(turned, 1 - core))
    attn_first = outer_stack(
        core_arg, normed, grads, [swap_cores(part) for part in sent_attn], half_sums, up_rest
    )

    early_parts = over_plane(jnp.concatenate([up_chips, down_chips], axis=1))
    half_sums, _ = lax.optimization_barrier((half_sums, attn_first))
    up_rest, early_parts = lax.optimization_barrier((up_rest, early_parts))
    small = jnp.sum(in_order(across_chips(half_sums)), axis=0)
    rest = up_rest.reshape(chips, shard, -1)
    rest = across_chips(rest.astype(BF16))
    rest = sum(part.astype(F32) for part in rest)
    late_parts = over_plane(jnp.concatenate([over_x(attn_first), small.astype(BF16)], axis=1))
    small = late_parts[:, 3 * width :]
    vector_grads = small.T[: vectors.shape[0]]
    head_total = small[0, HEAD_AT : HEAD_AT + heads]

    masters = (w_qkv, w_out, w_up, w_down)
    grad_qkv, grad_out, grad_up, grad_down, slots = to_slots(
        owner_perm,
        early_parts,
        late_parts,
        rest,
        plane,
        [item.shape[1] for item in masters],
    )
    slots = lax.all_to_all(slots, "fsdp", split_axis=0, concat_axis=0, tiled=True)
    left_new, right_new, back = update(slots, left_stats, right_stats, left_roots, right_roots)
    back = lax.all_to_all(back, "fsdp", split_axis=0, concat_axis=0, tiled=True)
    new_qkv, new_out, new_up, new_down = apply_steps(owner_perm, back, masters)
    vector_stats_new = DECAY * vector_stats + (1.0 - DECAY) * vector_grads * vector_grads
    vectors_new = vectors - RATE_VECTOR * vector_grads * lax.rsqrt(vector_stats_new)
    head_stats_new = DECAY * head_stats + (1.0 - DECAY) * head_total * head_total
    head_new = head_scale - RATE_VECTOR * head_total * lax.rsqrt(head_stats_new)
    return (
        output,
        input_grad,
        grad_qkv,
        grad_out,
        grad_up,
        grad_down,
        vector_grads,
        head_total,
        left_new,
        right_new,
        new_qkv,
        new_out,
        new_up,
        new_down,
        vector_stats_new,
        vectors_new,
        head_stats_new,
        head_new,
    )


def solution(mesh):
    everywhere = ("x", "core", "fsdp")
    by_rows = P(everywhere, None)
    by_columns = P(None, everywhere)
    by_block = P(("x", "core"), "fsdp", None, None)
    dp, fsdp = mesh.devices.shape
    mesh = jax.sharding.Mesh(mesh.devices.reshape(dp // 2, 2, fsdp), everywhere)
    return jax.shard_map(
        shards,
        mesh=mesh,
        in_specs=(
            (by_rows, by_rows, P(everywhere), P(everywhere), P())
            + (by_rows,) * 4
            + (by_columns, P())
            + (by_block,) * 4
            + (by_columns, P())
        ),
        out_specs=(
            (by_rows,) * 6
            + (by_columns, P())
            + (by_block,) * 2
            + (by_rows,) * 4
            + (by_columns, by_columns, P(), P())
        ),
        check_vma=False,
    )
```

```python
import functools
import math

import jax
import jax.numpy as jnp
from jax import lax
from jax.experimental import pallas as pl
from jax.experimental.pallas import tpu as pltpu
from jax.sharding import PartitionSpec as P

TILE = 128
EPS = 1e-05
DECAY = 0.5
RATE_MATRIX = 0.1
RATE_VECTOR = 0.3
HIGHEST = lax.Precision.HIGHEST
HEAD_AT = 24
UP_FIRSTS = 2
VMEM_BYTES = 56 * 1024 * 1024
F32 = jnp.float32
BF16 = jnp.bfloat16


def dot_nn(left, right):
    return lax.dot_general(left, right, (((1,), (0,)), ((), ())), preferred_element_type=F32)


def dot_nt(left, right):
    return lax.dot_general(left, right, (((1,), (1,)), ((), ())), preferred_element_type=F32)


def dot_tn(left, right):
    return lax.dot_general(left, right, (((0,), (0,)), ((), ())), preferred_element_type=F32)


def row_stats(values):
    mean = jnp.mean(values, axis=-1, keepdims=True)
    centered = values - mean
    spread = lax.rsqrt(jnp.mean(centered * centered, axis=-1, keepdims=True) + EPS)
    return centered, spread


def norm_back(scaled_grad, unit, spread):
    mean_grad = jnp.mean(scaled_grad, axis=-1, keepdims=True)
    mean_both = jnp.mean(scaled_grad * unit, axis=-1, keepdims=True)
    return spread * (scaled_grad - mean_grad - unit * mean_both)


def lane_sum(values):
    total = values[:, :TILE]
    for at in range(TILE, values.shape[1], TILE):
        total = total + values[:, at : at + TILE]
    return total


def call(body, grid, in_specs, out_specs, out_shape, scratch=(), flops=0, bytes_accessed=0, scalars=0):
    return pl.pallas_call(
        body,
        out_shape=out_shape,
        grid_spec=pltpu.PrefetchScalarGridSpec(
            num_scalar_prefetch=scalars,
            grid=grid,
            in_specs=in_specs,
            out_specs=out_specs,
            scratch_shapes=list(scratch),
        ),
        compiler_params=pltpu.CompilerParams(vmem_limit_bytes=VMEM_BYTES),
        cost_estimate=pl.CostEstimate(
            flops=20 * flops, bytes_accessed=bytes_accessed, transcendentals=0
        ),
    )


def whole(shape):
    return pl.BlockSpec(shape, lambda *_: (0,) * len(shape))


def after(*arrays):
    return [pl.BlockSpec(memory_space=pl.ANY) for _ in arrays]


def split_parity(values):
    blocks = [values[:, at : at + TILE] for at in range(0, values.shape[1], TILE)]
    return jnp.concatenate(blocks[0::2], axis=1), jnp.concatenate(blocks[1::2], axis=1)


def join_parity(even, odd):
    blocks = []
    for at in range(0, even.shape[1], TILE):
        blocks += [even[:, at : at + TILE], odd[:, at : at + TILE]]
    return jnp.concatenate(blocks, axis=1)


def turn_rows(left, turned, parity):
    for block in range(turned.shape[0] // TILE):
        at = pl.multiple_of((2 * block + parity) * TILE, TILE)
        turned[block * TILE : (block + 1) * TILE, :] = jnp.transpose(left[:, pl.ds(at, TILE)])


def by_owner(values, plane):
    rows, columns = values.shape
    chips = rows // (8 * plane)
    values = values.reshape(chips, plane, 8, columns)
    return jnp.concatenate([values[chip] for chip in range(chips)], axis=1)


def project_body(
    core, tokens, vectors, own_qk, other_qk, own_vo, other_vo, normed, projected, parts
):
    part = pl.program_id(0)

    @pl.when(part == 0)
    def _():
        centered, spread = row_stats(tokens[...].astype(F32))
        low = (centered * spread * vectors[0:1, :] + vectors[1:2, :]).astype(BF16)
        normed[...] = low
        parts[0], parts[1] = split_parity(low)

    gate_q = jnp.where(part == 0, 1.0, 0.0).astype(F32)
    gate_v = jnp.where(part == 2, 1.0, 0.0).astype(F32)
    bias = gate_q * vectors[2:3, :] + gate_v * vectors[3:4, :]
    me = core[0]

    @pl.when(part < 2)
    def _():
        projected[...] = (
            dot_nn(parts[me], own_qk[...]) + dot_nn(parts[1 - me], other_qk[...]) + bias
        ).astype(BF16)

    @pl.when(part == 2)
    def _():
        projected[...] = (
            dot_nn(parts[me], own_vo[...]) + dot_nn(parts[1 - me], other_vo[...]) + bias
        ).astype(BF16)


def project(core, tokens, vectors, weights):
    rows, width = tokens.shape
    parts = 3
    third = pl.BlockSpec((width // 2, width), lambda part, *_: (0, jnp.minimum(part, 1)))
    last = pl.BlockSpec((width // 2, width), lambda part, *_: (0, 0))
    return call(
        project_body,
        (parts,),
        [whole((rows, width)), whole(vectors.shape), third, third, last, last],
        [whole((rows, width)), pl.BlockSpec((rows, width), lambda part, *_: (0, part))],
        [
            jax.ShapeDtypeStruct((rows, width), BF16),
            jax.ShapeDtypeStruct((rows, parts * width), BF16),
        ],
        scratch=[pltpu.VMEM((2, rows, width // 2), BF16)],
        flops=2 * rows * width * width * parts,
        bytes_accessed=2 * width * width * parts,
        scalars=1,
    )(core, tokens, vectors, *weights)


def attend_body(length, scales, queries, keys, values, mixed, scaled, weights):
    rows = queries.shape[0]
    head_dim = TILE // 2
    pair = pl.program_id(0)
    block = rows // 2
    lane = lax.broadcasted_iota(jnp.int32, (rows, TILE), 1)
    spot = lax.broadcasted_iota(jnp.int32, (rows, TILE), 0)
    hidden_key = jnp.where(spot < length[0], 0.0, -1e30).astype(BF16)
    one = jnp.ones((rows, TILE), BF16)
    zero = jnp.zeros((rows, TILE), BF16)
    query = queries[...] * jnp.asarray(1.0 / math.sqrt(head_dim), BF16)
    key = keys[...]
    value = values[...]
    causal = lax.broadcasted_iota(jnp.int32, (block, block), 1) <= lax.broadcasted_iota(
        jnp.int32, (block, block), 0
    )
    total = [jnp.zeros((block, TILE), F32) for _ in range(2)]
    for head in range(2):
        mine = (lane < head_dim) if head == 0 else (lane >= head_dim)
        spare = lane == (head_dim if head == 0 else 0)
        query_one = jnp.where(mine, query, jnp.where(spare, one, zero))
        key_one = jnp.where(mine, key, jnp.where(spare, hidden_key, zero))
        value_one = jnp.where(mine, value, zero)
        for part in range(2):
            seen = (part + 1) * block
            score = dot_nt(query_one[part * block : seen], key_one[:seen])
            last = jnp.where(causal, score[:, part * block :], -1e30)
            score = last if part == 0 else jnp.concatenate([score[:, :block], last], axis=1)
            top = jnp.max(score, axis=1, keepdims=True)
            grown = jnp.exp(score - top)
            share = (grown * (1.0 / jnp.sum(grown, axis=1, keepdims=True))).astype(BF16)
            if part == 0:
                weights[head, :, :block] = share
            else:
                weights[head, :, block:] = share
            total[part] = total[part] + dot_nn(share, value_one[:seen])
    scale_row = jnp.where(
        lax.broadcasted_iota(jnp.int32, (1, TILE), 1) < head_dim,
        scales[2 * pair],
        scales[2 * pair + 1],
    )
    for part in range(2):
        mixed[part * block : (part + 1) * block, :] = total[part]
        scaled[part * block : (part + 1) * block, :] = (total[part] * scale_row).astype(BF16)


def attend(length, scales, projected):
    rows, width3 = projected.shape
    width = width3 // 3
    pairs = width // TILE
    block = rows // 2
    return call(
        attend_body,
        (pairs,),
        [
            pl.BlockSpec((rows, TILE), lambda pair, *_: (0, pair)),
            pl.BlockSpec((rows, TILE), lambda pair, *_: (0, pairs + pair)),
            pl.BlockSpec((rows, TILE), lambda pair, *_: (0, 2 * pairs + pair)),
        ],
        [
            pl.BlockSpec((rows, TILE), lambda pair, *_: (0, pair)),
            pl.BlockSpec((rows, TILE), lambda pair, *_: (0, pair)),
            pl.BlockSpec((2, block, 3 * block), lambda pair, *_: (pair, 0, 0)),
        ],
        [
            jax.ShapeDtypeStruct((rows, width), F32),
            jax.ShapeDtypeStruct((rows, width), BF16),
            jax.ShapeDtypeStruct((2 * pairs, block, 3 * block), BF16),
        ],
        flops=4 * rows * rows * width,
        bytes_accessed=20 * rows * width,
        scalars=2,
    )(length, scales, projected, projected, projected)


def attend_back_body(
    queries, keys, values, mixed, grads, weights, normed, _, __, out, local, turned
):
    @pl.when(pl.program_id(0) == 0)
    def _():
        for at in range(0, turned.shape[0], TILE):
            turned[at : at + TILE, :] = jnp.transpose(normed[:, at : at + TILE])

    rows = queries.shape[0]
    head_dim = TILE // 2
    block = rows // 2
    lane = lax.broadcasted_iota(jnp.int32, (rows, TILE), 1)
    zero = jnp.zeros((rows, TILE), BF16)
    query, key, value, grad = queries[...], keys[...], values[...], grads[...]
    both = grad.astype(F32) * mixed[...]
    q_total = [jnp.zeros((block, TILE), F32) for _ in range(2)]
    k_total = [jnp.zeros((block, TILE), F32) for _ in range(2)]
    v_total = [jnp.zeros((block, TILE), F32) for _ in range(2)]
    for head in range(2):
        mine = (lane < head_dim) if head == 0 else (lane >= head_dim)
        query_one = jnp.where(mine, query, zero)
        key_one = jnp.where(mine, key, zero)
        grad_one = jnp.where(mine, grad, zero)
        delta = jnp.sum(jnp.where(mine, both, 0.0), axis=1, keepdims=True)
        for part in range(2):
            at = part * block
            seen = at + block
            share = weights[head, :, :block] if part == 0 else weights[head, :, block:]
            into = dot_nt(grad_one[at:seen], value[:seen])
            slope = (share.astype(F32) * (into - delta[at:seen])).astype(BF16)
            q_total[part] = q_total[part] + dot_nn(slope, key_one[:seen])
            k_new = dot_tn(slope, query_one[at:seen])
            v_new = dot_tn(share, grad_one[at:seen])
            for into_part in range(part + 1):
                cut = slice(into_part * block, (into_part + 1) * block)
                k_total[into_part] = k_total[into_part] + k_new[cut]
                v_total[into_part] = v_total[into_part] + v_new[cut]
    root = 1.0 / math.sqrt(head_dim)
    low_q = (jnp.concatenate(q_total, axis=0) * root).astype(BF16)
    low_k = (jnp.concatenate(k_total, axis=0) * root).astype(BF16)
    low_v = jnp.concatenate(v_total, axis=0).astype(BF16)
    out[0], out[1], out[2] = low_q, low_k, low_v
    local[...] = dot_nn(turned[...], jnp.concatenate([low_q, low_k, low_v], axis=1)).astype(BF16)


def attend_back(projected, mixed, grads, weights, normed, wait):
    rows, width3 = projected.shape
    width = width3 // 3
    pairs = width // TILE
    block = rows // 2
    by_pair = pl.BlockSpec((rows, TILE), lambda pair, *_: (0, pair))
    return call(
        attend_back_body,
        (pairs,),
        [
            by_pair,
            pl.BlockSpec((rows, TILE), lambda pair, *_: (0, pairs + pair)),
            pl.BlockSpec((rows, TILE), lambda pair, *_: (0, 2 * pairs + pair)),
            by_pair,
            by_pair,
            pl.BlockSpec((2, block, 3 * block), lambda pair, *_: (pair, 0, 0)),
            whole((rows, width)),
            *after(*wait),
        ],
        [
            pl.BlockSpec((3, rows, TILE), lambda pair, *_: (0, 0, pair)),
            pl.BlockSpec((width, 3 * TILE), lambda pair, *_: (0, pair)),
        ],
        [
            jax.ShapeDtypeStruct((3, rows, width), BF16),
            jax.ShapeDtypeStruct((width, width3), BF16),
        ],
        scratch=[pltpu.VMEM((width, rows), BF16)],
        flops=10 * rows * rows * width,
        bytes_accessed=24 * rows * width,
    )(projected, projected, projected, mixed, grads, weights, normed, *wait)


def branch_body(core, scaled, own, other, tokens, vectors, branch, attended, normed, parts):
    parts[0], parts[1] = split_parity(scaled[...])
    me = core[0]
    value = dot_nn(parts[me], own[...]) + dot_nn(parts[1 - me], other[...]) + vectors[6:7, :]
    branch[...] = value
    centered, spread = row_stats(value)
    total = tokens[...].astype(F32) + centered * spread * vectors[4:5, :] + vectors[5:6, :]
    attended[...] = total
    centered, spread = row_stats(total)
    normed[...] = (centered * spread * vectors[7:8, :] + vectors[8:9, :]).astype(BF16)


def branch_out(core, scaled, weights, tokens, vectors):
    rows, width = scaled.shape
    block = rows // 4
    by_row = pl.BlockSpec((block, width), lambda at, *_: (at, 0))
    fourth = pl.BlockSpec((width // 2, width), lambda at, *_: (0, 1))
    return call(
        branch_body,
        (rows // block,),
        [by_row, fourth, fourth, by_row, whole(vectors.shape)],
        [by_row, by_row, by_row],
        [
            jax.ShapeDtypeStruct((rows, width), F32),
            jax.ShapeDtypeStruct((rows, width), F32),
            jax.ShapeDtypeStruct((rows, width), BF16),
        ],
        scratch=[pltpu.VMEM((2, block, width // 2), BF16)],
        flops=2 * rows * width * width,
        bytes_accessed=2 * width * width + 14 * rows * width,
        scalars=1,
    )(core, scaled, *weights[2:], tokens, vectors)


def branch_back_body(
    core,
    grad_attended,
    branch,
    own,
    other,
    mixed,
    scales,
    vectors,
    scaled,
    grad_branch,
    grad_mixed,
    sums,
    sent,
    staying,
    parts,
    lows,
    turned,
):
    at = pl.program_id(0)

    @pl.when(at == 0)
    def _():
        sums[...] = jnp.zeros_like(sums)

    grad = grad_attended[...]
    centered, spread = row_stats(branch[...])
    unit = centered * spread
    low = norm_back(grad * vectors[4:5, :], unit, spread).astype(BF16)
    grad_branch[...] = low
    lows[at] = low
    me = core[0]
    parts[me] = dot_nt(low, own[...])
    parts[1 - me] = dot_nt(low, other[...])
    grad_scaled = join_parity(parts[0], parts[1])
    grad_mixed[...] = (grad_scaled * scales[0:1, :]).astype(BF16)
    sums[0:1, :] += jnp.sum(grad * unit, axis=0, keepdims=True)
    sums[1:2, :] += jnp.sum(grad, axis=0, keepdims=True)
    sums[2:3, :] += jnp.sum(low.astype(F32), axis=0, keepdims=True)
    sums[3:4, :] += jnp.sum(grad_scaled * mixed[...], axis=0, keepdims=True)

    @pl.when(at == pl.num_programs(0) - 1)
    def _():
        right = lows[...].reshape(scaled.shape)
        turn_rows(scaled, turned, 1 - me)
        sent[...] = dot_nn(turned[...], right).astype(BF16)
        turn_rows(scaled, turned, me)
        staying[...] = dot_nn(turned[...], right)


def branch_back(core, grad_attended, branch, weights, mixed, scales, vectors, scaled, *wait):
    rows, width = branch.shape
    block = rows // 4
    by_row = pl.BlockSpec((block, width), lambda at, *_: (at, 0))
    fourth = pl.BlockSpec((width // 2, width), lambda at, *_: (0, 1))
    return call(
        branch_back_body,
        (rows // block,),
        [
            by_row,
            by_row,
            fourth,
            fourth,
            by_row,
            whole(scales.shape),
            whole(vectors.shape),
            whole(scaled.shape),
            *after(*wait),
        ],
        [by_row, by_row, whole((8, width)), whole((width // 2, width)), whole((width // 2, width))],
        [
            jax.ShapeDtypeStruct((rows, width), BF16),
            jax.ShapeDtypeStruct((rows, width), BF16),
            jax.ShapeDtypeStruct((8, width), F32),
            jax.ShapeDtypeStruct((width // 2, width), BF16),
            jax.ShapeDtypeStruct((width // 2, width), F32),
        ],
        scratch=[
            pltpu.VMEM((2, block, width // 2), F32),
            pltpu.VMEM((rows // block, block, width), BF16),
            pltpu.VMEM((width // 2, rows), BF16),
        ],
        flops=4 * rows * width * width,
        bytes_accessed=2 * width * width + 16 * rows * width,
        scalars=1,
    )(core, grad_attended, branch, *weights[2:], mixed, scales, vectors, scaled, *wait)


def send_part(values, step, firsts, first, second):
    @pl.when(step < firsts)
    def _():
        first[...] = values.astype(BF16)

    @pl.when(step >= firsts)
    def _():
        second[...] = by_owner(values, second.shape[0]).astype(BF16)


def part_specs(half, plane, start, firsts):
    return [
        pl.BlockSpec((half, 1024), lambda at, *_: (0, jnp.clip(at - start, 0, firsts - 1))),
        pl.BlockSpec(
            (plane, half // plane, 1024),
            lambda at, *_: (0, 0, jnp.clip(at - start - firsts, 0, 3 - firsts)),
        ),
    ]


def part_shapes(half, plane, firsts):
    return [
        jax.ShapeDtypeStruct((half, firsts * 1024), BF16),
        jax.ShapeDtypeStruct((plane, half // plane, (4 - firsts) * 1024), BF16),
    ]


def forward_ffn_body(
    steps,
    normed,
    attended,
    vectors,
    rows_of,
    weights,
    upstream,
    output,
    kept,
    slope,
    stats,
    sent,
    held,
    total,
    sums,
    turned,
):
    at = pl.program_id(0)
    width = held.shape[2]

    @pl.when(at == 0)
    def _():
        sums[...] = jnp.zeros_like(sums)

    @pl.when(at < steps)
    def _():
        hidden = dot_nn(normed[...], weights[...]) + rows_of[0:1, :]
        cdf = 0.5 + 0.5 * lax.erf(hidden * math.sqrt(0.5))
        value = hidden * cdf
        slope[...] = (
            cdf + hidden * (jnp.exp(-0.5 * hidden * hidden) * (1.0 / math.sqrt(2.0 * math.pi)))
        ).astype(BF16)
        held[at] = value
        kept[...] = value.astype(BF16)
        sums[...] += lane_sum(value)
        share = attended.shape[1]
        start = pl.multiple_of(at * share, share)
        total[:, pl.ds(start, share)] = attended[...] + vectors[21:22, pl.ds(start, share)]
        for block in range(0, share, TILE):
            turned[pl.ds(start + block, TILE), :] = jnp.transpose(
                upstream[:, block : block + TILE]
            )

    @pl.when(at == steps)
    def _():
        count = steps * width
        mean = jnp.sum(sums[...], axis=1, keepdims=True) * (1.0 / count)
        square = jnp.zeros(sums.shape, F32)
        for block in range(steps):
            centered = held[block] - mean
            square = square + lane_sum(centered * centered)
        spread = lax.rsqrt(jnp.sum(square, axis=1, keepdims=True) * (1.0 / count) + EPS)
        stats[:, :TILE] = jnp.broadcast_to(mean, sums.shape)
        stats[:, TILE:] = jnp.broadcast_to(spread, sums.shape)

    @pl.when(at >= steps)
    def _():
        mean = stats[:, 0:1]
        spread = stats[:, TILE : TILE + 1]
        value = held[at - steps]
        low = ((value - mean) * spread * rows_of[1:2, :] + rows_of[2:3, :]).astype(BF16)
        total[...] += dot_nt(low, weights[...])
        sent[...] = dot_nn(turned[...], low).astype(BF16)

    @pl.when(at == 2 * steps - 1)
    def _():
        output[...] = total[...].astype(BF16)


def forward_ffn(normed, attended, vectors, wide_rows, both, upstream):
    rows, width = attended.shape
    hidden = both.shape[1] // 2
    block = 1024
    steps = hidden // block
    early = lambda at, *_: (0, jnp.minimum(at, steps - 1))
    return call(
        functools.partial(forward_ffn_body, steps),
        (2 * steps,),
        [
            whole((rows, width)),
            pl.BlockSpec((rows, width // steps), early),
            whole(vectors.shape),
            pl.BlockSpec((8, block), lambda at, *_: (0, lax.rem(at, steps))),
            pl.BlockSpec((width, block), lambda at, *_: (0, at)),
            pl.BlockSpec((rows, width // steps), early),
        ],
        [
            whole((rows, width)),
            pl.BlockSpec((rows, block), early),
            pl.BlockSpec((rows, block), early),
            whole((rows, 2 * TILE)),
            pl.BlockSpec((width, block), lambda at, *_: (0, jnp.maximum(at - steps, 0))),
        ],
        [
            jax.ShapeDtypeStruct((rows, width), BF16),
            jax.ShapeDtypeStruct((rows, hidden), BF16),
            jax.ShapeDtypeStruct((rows, hidden), BF16),
            jax.ShapeDtypeStruct((rows, 2 * TILE), F32),
            jax.ShapeDtypeStruct((width, hidden), BF16),
        ],
        scratch=[
            pltpu.VMEM((steps, rows, block), F32),
            pltpu.VMEM((rows, width), F32),
            pltpu.VMEM((rows, TILE), F32),
            pltpu.VMEM((width, rows), BF16),
        ],
        flops=6 * rows * width * hidden,
        bytes_accessed=4 * width * hidden + 6 * rows * hidden,
    )(normed, attended, vectors, wide_rows, both, upstream)


def backward_ffn_body(
    steps,
    core,
    upstream,
    attended,
    vectors,
    rows_of,
    stats,
    kept,
    slope,
    weights,
    normed,
    _,
    grad_attended,
    grad_hidden,
    wide_sums,
    sums,
    sent_first,
    sent_second,
    held,
    total,
    first,
    second,
    turned,
    saved,
    units,
):
    at = pl.program_id(0)
    count = steps * held.shape[2]
    mean = stats[:, 0:1]
    spread = stats[:, TILE : TILE + 1]

    @pl.when(at == 0)
    def _():
        first[...] = jnp.zeros_like(first)
        second[...] = jnp.zeros_like(second)
        total[...] = jnp.zeros_like(total)
        wide_sums[...] = jnp.zeros_like(wide_sums)

    @pl.when(at < steps)
    def _():
        grad = dot_nn(upstream[...], weights[...])
        unit = (kept[...].astype(F32) - mean) * spread
        units[at] = unit.astype(BF16)
        both = grad * unit
        share = attended.shape[1]
        saved[:, pl.ds(pl.multiple_of(at * share, share), share)] = attended[...]
        lane = pl.multiple_of((1 - core[0]) * TILE, TILE)
        turned[pl.ds(pl.multiple_of(at * TILE, TILE), TILE), :] = jnp.transpose(
            normed[:, pl.ds(lane, TILE)]
        )
        wide_sums[at, 0:1, :] = jnp.sum(both, axis=0, keepdims=True)
        wide_sums[at, 1:2, :] = jnp.sum(grad, axis=0, keepdims=True)
        gain = rows_of[1:2, :]
        held[at] = grad * gain
        first[...] += lane_sum(grad * gain)
        second[...] += lane_sum(both * gain)

    @pl.when(at == steps)
    def _():
        scale = 1.0 / count
        first[...] = jnp.broadcast_to(
            jnp.sum(first[...], axis=1, keepdims=True) * scale, first.shape
        )
        second[...] = jnp.broadcast_to(
            jnp.sum(second[...], axis=1, keepdims=True) * scale, second.shape
        )

    @pl.when(at >= steps)
    def _():
        unit = units[at - steps].astype(F32)
        grad = spread * (held[at - steps] - first[:, 0:1] - unit * second[:, 0:1])
        low = (grad * slope[...].astype(F32)).astype(BF16)
        grad_hidden[...] = low
        wide_sums[at - steps, 2:3, :] = jnp.sum(low.astype(F32), axis=0, keepdims=True)
        total[...] += dot_nt(low, weights[...])
        send_part(dot_nn(turned[...], low), at - steps, UP_FIRSTS, sent_first, sent_second)

    @pl.when(at == 2 * steps - 1)
    def _():
        grad = total[...]
        centered, mid_spread = row_stats(saved[...])
        unit = centered * mid_spread
        top = upstream[...].astype(F32)
        grad_attended[...] = top + norm_back(grad * vectors[7:8, :], unit, mid_spread)
        sums[0:1, :] = jnp.sum(grad * unit, axis=0, keepdims=True)
        sums[1:2, :] = jnp.sum(grad, axis=0, keepdims=True)
        sums[2:3, :] = jnp.sum(top, axis=0, keepdims=True)
        sums[3:8, :] = jnp.zeros((5, sums.shape[1]), F32)


def backward_ffn(
    core, plane, upstream, attended, vectors, wide_rows, stats, kept, slope, both, normed, wait
):
    rows, width = attended.shape
    hidden = both.shape[1] // 2
    block = 1024
    steps = hidden // block
    late = lambda at, *_: (0, jnp.maximum(at - steps, 0))
    early = lambda at, *_: (0, jnp.minimum(at, steps - 1))
    turn = lambda at, *_: (0, lax.rem(at, steps))
    return call(
        functools.partial(backward_ffn_body, steps),
        (2 * steps,),
        [
            whole((rows, width)),
            pl.BlockSpec((rows, width // steps), early),
            whole(vectors.shape),
            pl.BlockSpec((8, block), turn),
            whole((rows, 2 * TILE)),
            pl.BlockSpec((rows, block), early),
            pl.BlockSpec((rows, block), late),
            pl.BlockSpec((width, block), lambda at, *_: (0, lax.rem(at + steps, 2 * steps))),
            pl.BlockSpec((rows, width // steps), early),
            *after(wait),
        ],
        [
            whole((rows, width)),
            pl.BlockSpec((rows, block), late),
            whole((steps, 8, block)),
            whole((8, width)),
            *part_specs(width // 2, plane, steps, UP_FIRSTS),
        ],
        [
            jax.ShapeDtypeStruct((rows, width), F32),
            jax.ShapeDtypeStruct((rows, hidden), BF16),
            jax.ShapeDtypeStruct((steps, 8, block), F32),
            jax.ShapeDtypeStruct((8, width), F32),
            *part_shapes(width // 2, plane, UP_FIRSTS),
        ],
        scratch=[
            pltpu.VMEM((steps, rows, block), F32),
            pltpu.VMEM((rows, width), F32),
            pltpu.VMEM((rows, TILE), F32),
            pltpu.VMEM((rows, TILE), F32),
            pltpu.VMEM((width // 2, rows), BF16),
            pltpu.VMEM((rows, width), F32),
            pltpu.VMEM((steps, rows, block), BF16),
        ],
        flops=5 * rows * width * hidden,
        bytes_accessed=4 * width * hidden + 8 * rows * hidden,
        scalars=1,
    )(core, upstream, attended, vectors, wide_rows, stats, kept, slope, both, normed, wait)


def input_back_body(
    core,
    grads,
    own_qk,
    other_qk,
    own_vo,
    other_vo,
    tokens,
    grad_attended,
    vectors,
    branch_sums,
    mid_sums,
    wide_sums,
    _,
    input_grad,
    turned,
    parts,
    sums,
):
    part = pl.program_id(0)
    me = core[0]
    grad_part = grads[...]

    @pl.when(part == 0)
    def _():
        parts[me] = dot_nt(grad_part, own_qk[...])
        parts[1 - me] = dot_nt(grad_part, other_qk[...])
        sums[...] = jnp.zeros_like(sums)
        sums[2:3, :] = jnp.sum(grad_part.astype(F32), axis=0, keepdims=True)

    @pl.when(part == 1)
    def _():
        parts[me] += dot_nt(grad_part, own_qk[...])
        parts[1 - me] += dot_nt(grad_part, other_qk[...])

    @pl.when(part == 2)
    def _():
        parts[me] += dot_nt(grad_part, own_vo[...])
        parts[1 - me] += dot_nt(grad_part, other_vo[...])
        grad = join_parity(parts[0], parts[1])
        centered, spread = row_stats(tokens[...].astype(F32))
        unit = centered * spread
        input_grad[...] = grad_attended[...] + norm_back(grad * vectors[0:1, :], unit, spread)
        sums[0:1, :] = jnp.sum(grad * unit, axis=0, keepdims=True)
        sums[1:2, :] = jnp.sum(grad, axis=0, keepdims=True)
        sums[3:4, :] = jnp.sum(grad_part.astype(F32), axis=0, keepdims=True)
        sums[4:7, :] = branch_sums[0:3, :]
        sums[7:9, :] = mid_sums[0:2, :]
        for row in range(wide_sums.shape[0]):
            sums[9 + row : 10 + row, :] = wide_sums[row, 2:3, :]
            sums[13 + row : 14 + row, :] = wide_sums[row, 0:1, :]
            sums[17 + row : 18 + row, :] = wide_sums[row, 1:2, :]
        sums[21:22, :] = mid_sums[2:3, :]
        width = sums.shape[1]
        head_dim = TILE // 2
        picks = (
            lax.broadcasted_iota(jnp.int32, (width, TILE), 0) // head_dim + HEAD_AT
            == lax.broadcasted_iota(jnp.int32, (width, TILE), 1)
        ).astype(F32)
        heads = lax.dot_general(
            branch_sums[...],
            picks,
            (((1,), (0,)), ((), ())),
            precision=HIGHEST,
            preferred_element_type=F32,
        )[3:4, :]
        for block in range(turned.shape[0]):
            turned[block] = (
                jnp.transpose(sums[:, block * TILE : (block + 1) * TILE]) + heads
            )


def input_back(core, grads, weights, tokens, grad_attended, vectors, sums, wait):
    rows, width = tokens.shape
    full = whole((rows, width))
    third = pl.BlockSpec((width // 2, width), lambda part, *_: (0, jnp.minimum(part, 1)))
    last = pl.BlockSpec((width // 2, width), lambda part, *_: (0, 0))
    return call(
        input_back_body,
        (3,),
        [
            pl.BlockSpec((None, rows, width), lambda part, *_: (part, 0, 0)),
            third,
            third,
            last,
            last,
            full,
            full,
            whole(vectors.shape),
            *[whole(item.shape) for item in sums],
            *after(wait),
        ],
        [full, whole((width // TILE, TILE, TILE))],
        [
            jax.ShapeDtypeStruct((rows, width), F32),
            jax.ShapeDtypeStruct((width // TILE, TILE, TILE), F32),
        ],
        scratch=[pltpu.VMEM((2, rows, width // 2), F32), pltpu.VMEM((TILE, width), F32)],
        flops=6 * rows * width * width,
        bytes_accessed=6 * width * width + 16 * rows * width,
        scalars=1,
    )(core, grads, *weights, tokens, grad_attended, vectors, *sums, wait)


def outer_body(firsts, more, core, left, right, add_first, add_second, *refs):
    first, second, turned = refs[-3:]
    at = pl.program_id(0)

    @pl.when(at == 0)
    def _():
        turn_rows(left, turned, core[0])

    value = dot_nn(turned[...], right[...])

    @pl.when(at < firsts)
    def _():
        first[...] = (value + add_first[...].astype(F32)).astype(BF16)

    if more:

        @pl.when(at == firsts)
        def _():
            first[...] = (refs[0][...] + refs[1][...].astype(F32)).astype(BF16)

    @pl.when(at >= firsts)
    def _():
        second[...] = (
            by_owner(value, second.shape[0]) + add_second[...].astype(F32)
        ).astype(BF16)


def outer(core, left, right, add, wait=(), more=()):
    rows, width = left.shape
    half = width // 2
    block = 1024
    add_first, add_second = add
    plane, owned = add_second.shape[:2]
    firsts = UP_FIRSTS
    seconds = add_second.shape[2] // block
    right_spec = pl.BlockSpec((rows, block), lambda at, *_: (0, at))
    add_spec = pl.BlockSpec((half, block), lambda at, *_: (0, jnp.clip(at, 0, firsts - 1)))
    second_spec = pl.BlockSpec(
        (plane, owned, block), lambda at, *_: (0, 0, jnp.clip(at - firsts, 0, seconds - 1))
    )
    kinds = firsts + len(more) // 2
    out_specs = [
        pl.BlockSpec((half, block), lambda at, *_: (0, jnp.clip(at, 0, kinds - 1))),
        second_spec,
    ]
    out_shape = [
        jax.ShapeDtypeStruct((half, kinds * block), BF16),
        jax.ShapeDtypeStruct(add_second.shape, BF16),
    ]
    return call(
        functools.partial(outer_body, firsts, len(more) > 0),
        (firsts + seconds,),
        [
            whole((rows, width)),
            right_spec,
            add_spec,
            second_spec,
            *[whole(item.shape) for item in more],
            *after(*wait),
        ],
        out_specs,
        out_shape,
        scratch=[pltpu.VMEM((half, rows), BF16)],
        flops=2 * rows * half * block * (firsts + seconds),
        bytes_accessed=6 * half * block * (firsts + seconds),
        scalars=1,
    )(core, left, right, add_first, add_second, *more, *wait)


def to_slots_body(perm, early, late, rest, *refs):
    grad_qkv, grad_out, grad_up, grad_down, slots, tiles = refs
    width = grad_out.shape[1]
    half = 2 * width
    grad_out[...] = early[:, half : half + width]
    for pair in range(width // TILE):
        for which in range(3):
            at = (3 * pair + which) * TILE
            to = which * width + pair * TILE
            grad_qkv[:, to : to + TILE] = late[:, at : at + TILE]
    grad_down[...] = early[:, half + width :]
    grad_up[:, :half] = early[:, :half]
    grad_up[:, half:] = rest[...]
    column = 0
    for result in (grad_qkv, grad_out, grad_up, grad_down):
        for at in range(0, result.shape[1], TILE):
            tiles[column] = result[:, at : at + TILE]
            column += 1
    planes, pairs = slots.shape[:2]
    for slot in range(planes * pairs):
        pair = [tiles[perm[2 * slot + which]] for which in range(2)]
        slots[slot // pairs, slot % pairs] = jnp.concatenate(pair, axis=0).astype(BF16)


def to_slots(perm, early, late, rest, plane, widths):
    arrays = [early, late, rest]
    pairs = perm.shape[0] // (2 * plane)
    shapes = [jax.ShapeDtypeStruct((8, columns), F32) for columns in widths]
    shapes.append(jax.ShapeDtypeStruct((plane, pairs, 16, TILE), BF16))
    return call(
        to_slots_body,
        (1,),
        [whole(item.shape) for item in arrays],
        [whole(item.shape) for item in shapes],
        shapes,
        scratch=[pltpu.VMEM((perm.shape[0], 8, TILE), F32)],
        bytes_accessed=8 * 8 * sum(widths),
        scalars=1,
    )(perm, *arrays)


def update_body(grads, left_stats, right_stats, left_roots, right_roots, left_new, right_new, back):
    planes, pairs = grads.shape[:2]
    for pair in range(pairs):
        block = grads[:, pair].astype(F32)
        moved = []
        for which in range(2):
            slot = 2 * pair + which
            grad = block[:, which * 8 : which * 8 + 8, :].reshape(TILE, TILE)
            low = grad.astype(BF16)
            left_new[slot] = DECAY * left_stats[slot] + (1.0 - DECAY) * dot_nt(low, low)
            right_new[slot] = DECAY * right_stats[slot] + (1.0 - DECAY) * dot_tn(low, low)
            step = jnp.dot(grad, right_roots[slot], precision=HIGHEST, preferred_element_type=F32)
            step = jnp.dot(left_roots[slot], step, precision=HIGHEST, preferred_element_type=F32)
            moved.append(step.reshape(planes, 8, TILE))
        back[:, pair] = jnp.concatenate(moved, axis=1).astype(BF16)


def update(grads, left_stats, right_stats, left_roots, right_roots):
    arrays = [item[0] for item in (left_stats, right_stats, left_roots, right_roots)]
    stats = jax.ShapeDtypeStruct(arrays[0].shape, F32)
    left_new, right_new, back = call(
        update_body,
        (1,),
        [whole(grads.shape)] + [whole(item.shape) for item in arrays],
        [whole(stats.shape), whole(stats.shape), whole(grads.shape)],
        [stats, stats, jax.ShapeDtypeStruct(grads.shape, BF16)],
        bytes_accessed=24 * arrays[0].size,
    )(grads, *arrays)
    return left_new[None], right_new[None], back


def apply_body(perm, moved, *refs):
    olds, news, tiles = refs[:4], refs[4:8], refs[8]
    pairs = moved.shape[1]
    for slot in range(moved.shape[0] * pairs):
        value = moved[slot // pairs, slot % pairs].astype(F32)
        tiles[perm[2 * slot]] = value[:8]
        tiles[perm[2 * slot + 1]] = value[8:]
    column = 0
    for old, new in zip(olds, news):
        for at in range(0, old.shape[1], TILE):
            cut = slice(at, at + TILE)
            new[:, cut] = old[:, cut] - RATE_MATRIX * tiles[column]
            column += 1


def apply_steps(perm, moved, weights):
    shapes = [jax.ShapeDtypeStruct(item.shape, F32) for item in weights]
    return call(
        apply_body,
        (1,),
        [whole(moved.shape)] + [whole(item.shape) for item in weights],
        [whole(item.shape) for item in shapes],
        shapes,
        scratch=[pltpu.VMEM((perm.shape[0], 8, TILE), F32)],
        bytes_accessed=10 * 8 * TILE * perm.shape[0],
        scalars=1,
    )(perm, moved, *weights)


def swap_cores(values):
    return lax.ppermute(values, "core", [(0, 1), (1, 0)])


def take_core(values, core):
    return lax.dynamic_slice_in_dim(values, core, 1, 1, allow_negative_indices=False)[:, 0]


def turn_chips(values, step):
    count = lax.axis_size("x")
    return lax.ppermute(values, "x", [(at, (at + step) % count) for at in range(count)])


def sum_parts(parts):
    return jnp.sum(parts.astype(F32), axis=0)


def shards(
    tokens,
    cotangent,
    lengths,
    valid,
    owner_perm,
    w_qkv,
    w_out,
    w_up,
    w_down,
    vectors,
    head_scale,
    left_stats,
    right_stats,
    left_roots,
    right_roots,
    vector_stats,
    head_stats,
):
    rows, width = tokens.shape
    heads = head_scale.shape[0]
    hidden = w_up.shape[1]
    ratio = hidden // width
    shard = w_up.shape[0]
    plane = lax.axis_size("fsdp")
    chips = lax.axis_size("x")
    core = lax.axis_index("core")
    core_arg = core.astype(jnp.int32).reshape(1)

    both = lax.all_gather(
        jnp.concatenate([w_up.astype(BF16), w_down.astype(BF16)], axis=1),
        ("x", "core", "fsdp"),
        axis=0,
        tiled=True,
    )
    low_qk = jnp.concatenate(
        [
            w_qkv[:, : 2 * width].astype(BF16),
            jnp.pad(vectors.astype(BF16).T, ((0, 0), (0, TILE - vectors.shape[0]))),
        ],
        axis=1,
    )
    low_vo = jnp.concatenate([w_qkv[:, 2 * width :].astype(BF16), w_out.astype(BF16)], axis=1)

    def to_plane(part, concat):
        spread = jnp.broadcast_to(part[None], (plane,) + part.shape)
        return lax.all_to_all(spread, "fsdp", split_axis=0, concat_axis=concat, tiled=True)

    place = lax.axis_index("x")

    def roll_chips(parts, start):
        twice = jnp.concatenate([parts, parts], axis=0)
        begin = [start] + [0] * (parts.ndim - 1)
        return lax.dynamic_slice(twice, begin, parts.shape, allow_negative_indices=False)

    def in_order(parts):
        return roll_chips(jnp.stack(parts[::-1]), chips - 1 - place)

    def to_chips(part):
        return in_order([part] + [turn_chips(part, step) for step in range(1, chips)])

    def across_chips(parts):
        ahead = roll_chips(parts, place)
        return [ahead[0]] + [turn_chips(ahead[step], step) for step in range(1, chips)]

    own_vo = to_plane(to_chips(low_vo), 2).reshape(width // 2, -1)
    own_qk = to_chips(to_plane(low_qk, 0).reshape(plane * shard, -1)).reshape(width // 2, -1)
    other_qk, other_vo = swap_cores(own_qk), swap_cores(own_vo)
    weights = (own_qk, other_qk, own_vo, other_vo)
    vector_at = 2 * width
    vector_pair = jnp.stack([own_qk[:, vector_at:], other_qk[:, vector_at:]])
    vector_pair = jnp.where(core == 0, vector_pair, vector_pair[::-1])
    vector_rows = (
        vector_pair.reshape(2, -1, TILE, TILE)
        .transpose(1, 0, 2, 3)
        .reshape(width, TILE)
        .T[:24]
        .astype(F32)
    )
    wide_rows = jnp.concatenate(
        [
            vector_rows[9 : 9 + 3 * ratio].reshape(3, hidden),
            jnp.zeros((5, hidden), F32),
        ],
        axis=0,
    )
    upstream = jnp.where(valid[:, None] != 0, cotangent, jnp.zeros_like(cotangent))
    scales = jnp.broadcast_to(jnp.repeat(head_scale, width // heads)[None], (8, width))

    normed, projected = project(core_arg, tokens, vector_rows, weights)
    mixed, scaled, attention = attend(lengths, head_scale, projected)
    branch, attended, normed_mid = branch_out(core_arg, scaled, weights, tokens, vector_rows)
    output, kept, slope, stats, down_local = forward_ffn(
        normed_mid, attended, vector_rows, wide_rows, both, upstream
    )

    def over_x(part):
        return lax.psum_scatter(part, "x", scatter_dimension=0, tiled=True)

    def over_plane(part):
        return sum_parts(
            lax.all_to_all(
                part.reshape(plane, shard, -1), "fsdp", split_axis=0, concat_axis=0, tiled=True
            )
        )

    def plane_first(part):
        total = lax.all_to_all(part, "fsdp", split_axis=0, concat_axis=0, tiled=True)
        return sum_parts(total)

    down_chips = lax.psum_scatter(down_local, ("x", "core"), scatter_dimension=0, tiled=True)
    grad_attended, grad_hidden, wide_sums, mid_sums, *sent_up = backward_ffn(
        core_arg,
        plane,
        upstream,
        attended,
        vector_rows,
        wide_rows,
        stats,
        kept,
        slope,
        both,
        normed_mid,
        down_local,
    )
    grad_branch, grad_mixed, branch_sums, out_sent, out_stays = branch_back(
        core_arg,
        grad_attended,
        branch,
        weights,
        mixed,
        scales,
        vector_rows,
        scaled,
    )
    up_first, up_second = outer(
        core_arg,
        normed_mid,
        grad_hidden,
        [swap_cores(part) for part in sent_up],
        wait=(grad_branch,),
        more=(out_stays, swap_cores(out_sent)),
    )
    up_rest = plane_first(up_second)
    up_chips = over_x(up_first)
    grads, attn_local = attend_back(
        projected,
        mixed,
        grad_mixed,
        attention,
        normed,
        (up_second, down_chips),
    )
    input_grad, turned = input_back(
        core_arg,
        grads,
        weights,
        tokens,
        grad_attended,
        vector_rows,
        (branch_sums, mid_sums, wide_sums),
        up_rest,
    )

    turned = turned.reshape(chips, 2, TILE, TILE)
    half_sums = take_core(turned, core) + swap_cores(take_core(turned, 1 - core))
    attn_chips = lax.psum_scatter(attn_local, ("x", "core"), scatter_dimension=0, tiled=True)

    early_parts = over_plane(jnp.concatenate([up_chips, down_chips], axis=1))
    half_sums, up_rest, early_parts = lax.optimization_barrier((half_sums, up_rest, early_parts))
    small = jnp.sum(in_order(across_chips(half_sums)), axis=0)
    rest = up_rest.reshape(chips, shard, -1)
    rest = across_chips(rest.astype(BF16))
    rest = sum(part.astype(F32) for part in rest)
    late_parts = over_plane(jnp.concatenate([attn_chips, small.astype(BF16)], axis=1))
    small = late_parts[:, 3 * width :]
    vector_grads = small.T[: vectors.shape[0]]
    head_total = small[0, HEAD_AT : HEAD_AT + heads]

    masters = (w_qkv, w_out, w_up, w_down)
    grad_qkv, grad_out, grad_up, grad_down, slots = to_slots(
        owner_perm,
        early_parts,
        late_parts,
        rest,
        plane,
        [item.shape[1] for item in masters],
    )
    slots = lax.all_to_all(slots, "fsdp", split_axis=0, concat_axis=0, tiled=True)
    left_new, right_new, back = update(slots, left_stats, right_stats, left_roots, right_roots)
    back = lax.all_to_all(back, "fsdp", split_axis=0, concat_axis=0, tiled=True)
    new_qkv, new_out, new_up, new_down = apply_steps(owner_perm, back, masters)
    vector_stats_new = DECAY * vector_stats + (1.0 - DECAY) * vector_grads * vector_grads
    vectors_new = vectors - RATE_VECTOR * vector_grads * lax.rsqrt(vector_stats_new)
    head_stats_new = DECAY * head_stats + (1.0 - DECAY) * head_total * head_total
    head_new = head_scale - RATE_VECTOR * head_total * lax.rsqrt(head_stats_new)
    return (
        output,
        input_grad,
        grad_qkv,
        grad_out,
        grad_up,
        grad_down,
        vector_grads,
        head_total,
        left_new,
        right_new,
        new_qkv,
        new_out,
        new_up,
        new_down,
        vector_stats_new,
        vectors_new,
        head_stats_new,
        head_new,
    )


def solution(mesh):
    everywhere = ("x", "core", "fsdp")
    by_rows = P(everywhere, None)
    by_columns = P(None, everywhere)
    by_block = P(("x", "core"), "fsdp", None, None)
    dp, fsdp = mesh.devices.shape
    mesh = jax.sharding.Mesh(mesh.devices.reshape(dp // 2, 2, fsdp), everywhere)
    return jax.shard_map(
        shards,
        mesh=mesh,
        in_specs=(
            (by_rows, by_rows, P(everywhere), P(everywhere), P())
            + (by_rows,) * 4
            + (by_columns, P())
            + (by_block,) * 4
            + (by_columns, P())
        ),
        out_specs=(
            (by_rows,) * 6
            + (by_columns, P())
            + (by_block,) * 2
            + (by_rows,) * 4
            + (by_columns, by_columns, P(), P())
        ),
        check_vma=False,
    )
```

```python
import functools
import math

import jax
import jax.numpy as jnp
from jax import lax
from jax.experimental import pallas as pl
from jax.experimental.pallas import tpu as pltpu
from jax.sharding import PartitionSpec as P

TILE = 128
EPS = 1e-05
DECAY = 0.5
RATE_MATRIX = 0.1
RATE_VECTOR = 0.3
HIGHEST = lax.Precision.HIGHEST
HEAD_AT = 24
UP_FIRSTS = 2
VMEM_BYTES = 56 * 1024 * 1024
F32 = jnp.float32
BF16 = jnp.bfloat16


def dot_nn(left, right):
    return lax.dot_general(left, right, (((1,), (0,)), ((), ())), preferred_element_type=F32)


def dot_nt(left, right):
    return lax.dot_general(left, right, (((1,), (1,)), ((), ())), preferred_element_type=F32)


def dot_tn(left, right):
    return lax.dot_general(left, right, (((0,), (0,)), ((), ())), preferred_element_type=F32)


def row_stats(values):
    mean = jnp.mean(values, axis=-1, keepdims=True)
    centered = values - mean
    spread = lax.rsqrt(jnp.mean(centered * centered, axis=-1, keepdims=True) + EPS)
    return centered, spread


def norm_back(scaled_grad, unit, spread):
    mean_grad = jnp.mean(scaled_grad, axis=-1, keepdims=True)
    mean_both = jnp.mean(scaled_grad * unit, axis=-1, keepdims=True)
    return spread * (scaled_grad - mean_grad - unit * mean_both)


def lane_sum(values):
    total = values[:, :TILE]
    for at in range(TILE, values.shape[1], TILE):
        total = total + values[:, at : at + TILE]
    return total


def call(body, grid, in_specs, out_specs, out_shape, scratch=(), flops=0, bytes_accessed=0, scalars=0):
    return pl.pallas_call(
        body,
        out_shape=out_shape,
        grid_spec=pltpu.PrefetchScalarGridSpec(
            num_scalar_prefetch=scalars,
            grid=grid,
            in_specs=in_specs,
            out_specs=out_specs,
            scratch_shapes=list(scratch),
        ),
        compiler_params=pltpu.CompilerParams(vmem_limit_bytes=VMEM_BYTES),
        cost_estimate=pl.CostEstimate(
            flops=20 * flops, bytes_accessed=bytes_accessed, transcendentals=0
        ),
    )


def whole(shape):
    return pl.BlockSpec(shape, lambda *_: (0,) * len(shape))


def after(*arrays):
    return [pl.BlockSpec(memory_space=pl.ANY) for _ in arrays]


def split_parity(values):
    blocks = [values[:, at : at + TILE] for at in range(0, values.shape[1], TILE)]
    return jnp.concatenate(blocks[0::2], axis=1), jnp.concatenate(blocks[1::2], axis=1)


def join_parity(even, odd):
    blocks = []
    for at in range(0, even.shape[1], TILE):
        blocks += [even[:, at : at + TILE], odd[:, at : at + TILE]]
    return jnp.concatenate(blocks, axis=1)


def turn_rows(left, turned, parity):
    for block in range(turned.shape[0] // TILE):
        at = pl.multiple_of((2 * block + parity) * TILE, TILE)
        turned[block * TILE : (block + 1) * TILE, :] = jnp.transpose(left[:, pl.ds(at, TILE)])


def by_owner(values, plane):
    rows, columns = values.shape
    chips = rows // (8 * plane)
    values = values.reshape(chips, plane, 8, columns)
    return jnp.concatenate([values[chip] for chip in range(chips)], axis=1)


def project_body(
    core, tokens, vectors, own_qk, other_qk, own_vo, other_vo, normed, projected, parts
):
    part = pl.program_id(0)

    @pl.when(part == 0)
    def _():
        centered, spread = row_stats(tokens[...].astype(F32))
        low = (centered * spread * vectors[0:1, :] + vectors[1:2, :]).astype(BF16)
        normed[...] = low
        parts[0], parts[1] = split_parity(low)

    gate_q = jnp.where(part == 0, 1.0, 0.0).astype(F32)
    gate_v = jnp.where(part == 2, 1.0, 0.0).astype(F32)
    bias = gate_q * vectors[2:3, :] + gate_v * vectors[3:4, :]
    me = core[0]

    @pl.when(part < 2)
    def _():
        projected[...] = (
            dot_nn(parts[me], own_qk[...]) + dot_nn(parts[1 - me], other_qk[...]) + bias
        ).astype(BF16)

    @pl.when(part == 2)
    def _():
        projected[...] = (
            dot_nn(parts[me], own_vo[...]) + dot_nn(parts[1 - me], other_vo[...]) + bias
        ).astype(BF16)


def project(core, tokens, vectors, weights):
    rows, width = tokens.shape
    parts = 3
    third = pl.BlockSpec((width // 2, width), lambda part, *_: (0, jnp.minimum(part, 1)))
    last = pl.BlockSpec((width // 2, width), lambda part, *_: (0, 0))
    return call(
        project_body,
        (parts,),
        [whole((rows, width)), whole(vectors.shape), third, third, last, last],
        [whole((rows, width)), pl.BlockSpec((rows, width), lambda part, *_: (0, part))],
        [
            jax.ShapeDtypeStruct((rows, width), BF16),
            jax.ShapeDtypeStruct((rows, parts * width), BF16),
        ],
        scratch=[pltpu.VMEM((2, rows, width // 2), BF16)],
        flops=2 * rows * width * width * parts,
        bytes_accessed=2 * width * width * parts,
        scalars=1,
    )(core, tokens, vectors, *weights)


def attend_body(length, scales, queries, keys, values, mixed, scaled, weights):
    rows = queries.shape[0]
    head_dim = TILE // 2
    pair = pl.program_id(0)
    block = rows // 2
    lane = lax.broadcasted_iota(jnp.int32, (rows, TILE), 1)
    spot = lax.broadcasted_iota(jnp.int32, (rows, TILE), 0)
    hidden_key = jnp.where(spot < length[0], 0.0, -1e30).astype(BF16)
    one = jnp.ones((rows, TILE), BF16)
    zero = jnp.zeros((rows, TILE), BF16)
    query = queries[...] * jnp.asarray(1.0 / math.sqrt(head_dim), BF16)
    key = keys[...]
    value = values[...]
    causal = lax.broadcasted_iota(jnp.int32, (block, block), 1) <= lax.broadcasted_iota(
        jnp.int32, (block, block), 0
    )
    total = [jnp.zeros((block, TILE), F32) for _ in range(2)]
    for head in range(2):
        mine = (lane < head_dim) if head == 0 else (lane >= head_dim)
        spare = lane == (head_dim if head == 0 else 0)
        query_one = jnp.where(mine, query, jnp.where(spare, one, zero))
        key_one = jnp.where(mine, key, jnp.where(spare, hidden_key, zero))
        value_one = jnp.where(mine, value, zero)
        for part in range(2):
            seen = (part + 1) * block
            score = dot_nt(query_one[part * block : seen], key_one[:seen])
            last = jnp.where(causal, score[:, part * block :], -1e30)
            score = last if part == 0 else jnp.concatenate([score[:, :block], last], axis=1)
            top = jnp.max(score, axis=1, keepdims=True)
            grown = jnp.exp(score - top)
            share = (grown * (1.0 / jnp.sum(grown, axis=1, keepdims=True))).astype(BF16)
            if part == 0:
                weights[head, :, :block] = share
            else:
                weights[head, :, block:] = share
            total[part] = total[part] + dot_nn(share, value_one[:seen])
    scale_row = jnp.where(
        lax.broadcasted_iota(jnp.int32, (1, TILE), 1) < head_dim,
        scales[2 * pair],
        scales[2 * pair + 1],
    )
    for part in range(2):
        mixed[part * block : (part + 1) * block, :] = total[part]
        scaled[part * block : (part + 1) * block, :] = (total[part] * scale_row).astype(BF16)


def attend(length, scales, projected):
    rows, width3 = projected.shape
    width = width3 // 3
    pairs = width // TILE
    block = rows // 2
    return call(
        attend_body,
        (pairs,),
        [
            pl.BlockSpec((rows, TILE), lambda pair, *_: (0, pair)),
            pl.BlockSpec((rows, TILE), lambda pair, *_: (0, pairs + pair)),
            pl.BlockSpec((rows, TILE), lambda pair, *_: (0, 2 * pairs + pair)),
        ],
        [
            pl.BlockSpec((rows, TILE), lambda pair, *_: (0, pair)),
            pl.BlockSpec((rows, TILE), lambda pair, *_: (0, pair)),
            pl.BlockSpec((2, block, 3 * block), lambda pair, *_: (pair, 0, 0)),
        ],
        [
            jax.ShapeDtypeStruct((rows, width), F32),
            jax.ShapeDtypeStruct((rows, width), BF16),
            jax.ShapeDtypeStruct((2 * pairs, block, 3 * block), BF16),
        ],
        flops=4 * rows * rows * width,
        bytes_accessed=20 * rows * width,
        scalars=2,
    )(length, scales, projected, projected, projected)


def attend_back_body(
    queries, keys, values, mixed, grads, weights, normed, _, __, out, local, turned
):
    @pl.when(pl.program_id(0) == 0)
    def _():
        for at in range(0, turned.shape[0], TILE):
            turned[at : at + TILE, :] = jnp.transpose(normed[:, at : at + TILE])

    rows = queries.shape[0]
    head_dim = TILE // 2
    block = rows // 2
    lane = lax.broadcasted_iota(jnp.int32, (rows, TILE), 1)
    zero = jnp.zeros((rows, TILE), BF16)
    query, key, value, grad = queries[...], keys[...], values[...], grads[...]
    both = grad.astype(F32) * mixed[...]
    q_total = [jnp.zeros((block, TILE), F32) for _ in range(2)]
    k_total = [jnp.zeros((block, TILE), F32) for _ in range(2)]
    v_total = [jnp.zeros((block, TILE), F32) for _ in range(2)]
    for head in range(2):
        mine = (lane < head_dim) if head == 0 else (lane >= head_dim)
        query_one = jnp.where(mine, query, zero)
        key_one = jnp.where(mine, key, zero)
        grad_one = jnp.where(mine, grad, zero)
        delta = jnp.sum(jnp.where(mine, both, 0.0), axis=1, keepdims=True)
        for part in range(2):
            at = part * block
            seen = at + block
            share = weights[head, :, :block] if part == 0 else weights[head, :, block:]
            into = dot_nt(grad_one[at:seen], value[:seen])
            slope = (share.astype(F32) * (into - delta[at:seen])).astype(BF16)
            q_total[part] = q_total[part] + dot_nn(slope, key_one[:seen])
            k_new = dot_tn(slope, query_one[at:seen])
            v_new = dot_tn(share, grad_one[at:seen])
            for into_part in range(part + 1):
                cut = slice(into_part * block, (into_part + 1) * block)
                k_total[into_part] = k_total[into_part] + k_new[cut]
                v_total[into_part] = v_total[into_part] + v_new[cut]
    root = 1.0 / math.sqrt(head_dim)
    low_q = (jnp.concatenate(q_total, axis=0) * root).astype(BF16)
    low_k = (jnp.concatenate(k_total, axis=0) * root).astype(BF16)
    low_v = jnp.concatenate(v_total, axis=0).astype(BF16)
    out[0], out[1], out[2] = low_q, low_k, low_v
    local[...] = dot_nn(turned[...], jnp.concatenate([low_q, low_k, low_v], axis=1)).astype(BF16)


def attend_back(projected, mixed, grads, weights, normed, wait):
    rows, width3 = projected.shape
    width = width3 // 3
    pairs = width // TILE
    block = rows // 2
    by_pair = pl.BlockSpec((rows, TILE), lambda pair, *_: (0, pair))
    return call(
        attend_back_body,
        (pairs,),
        [
            by_pair,
            pl.BlockSpec((rows, TILE), lambda pair, *_: (0, pairs + pair)),
            pl.BlockSpec((rows, TILE), lambda pair, *_: (0, 2 * pairs + pair)),
            by_pair,
            by_pair,
            pl.BlockSpec((2, block, 3 * block), lambda pair, *_: (pair, 0, 0)),
            whole((rows, width)),
            *after(*wait),
        ],
        [
            pl.BlockSpec((3, rows, TILE), lambda pair, *_: (0, 0, pair)),
            pl.BlockSpec((width, 3 * TILE), lambda pair, *_: (0, pair)),
        ],
        [
            jax.ShapeDtypeStruct((3, rows, width), BF16),
            jax.ShapeDtypeStruct((width, width3), BF16),
        ],
        scratch=[pltpu.VMEM((width, rows), BF16)],
        flops=10 * rows * rows * width,
        bytes_accessed=24 * rows * width,
    )(projected, projected, projected, mixed, grads, weights, normed, *wait)


def branch_body(core, scaled, own, other, tokens, vectors, branch, attended, normed, parts):
    parts[0], parts[1] = split_parity(scaled[...])
    me = core[0]
    value = dot_nn(parts[me], own[...]) + dot_nn(parts[1 - me], other[...]) + vectors[6:7, :]
    branch[...] = value
    centered, spread = row_stats(value)
    total = tokens[...].astype(F32) + centered * spread * vectors[4:5, :] + vectors[5:6, :]
    attended[...] = total
    centered, spread = row_stats(total)
    normed[...] = (centered * spread * vectors[7:8, :] + vectors[8:9, :]).astype(BF16)


def branch_out(core, scaled, weights, tokens, vectors):
    rows, width = scaled.shape
    block = rows // 4
    by_row = pl.BlockSpec((block, width), lambda at, *_: (at, 0))
    fourth = pl.BlockSpec((width // 2, width), lambda at, *_: (0, 1))
    return call(
        branch_body,
        (rows // block,),
        [by_row, fourth, fourth, by_row, whole(vectors.shape)],
        [by_row, by_row, by_row],
        [
            jax.ShapeDtypeStruct((rows, width), F32),
            jax.ShapeDtypeStruct((rows, width), F32),
            jax.ShapeDtypeStruct((rows, width), BF16),
        ],
        scratch=[pltpu.VMEM((2, block, width // 2), BF16)],
        flops=2 * rows * width * width,
        bytes_accessed=2 * width * width + 14 * rows * width,
        scalars=1,
    )(core, scaled, *weights[2:], tokens, vectors)


def branch_back_body(
    core,
    grad_attended,
    branch,
    own,
    other,
    mixed,
    scales,
    vectors,
    scaled,
    grad_branch,
    grad_mixed,
    sums,
    sent,
    staying,
    parts,
    lows,
    turned,
):
    at = pl.program_id(0)

    @pl.when(at == 0)
    def _():
        sums[...] = jnp.zeros_like(sums)

    grad = grad_attended[...]
    centered, spread = row_stats(branch[...])
    unit = centered * spread
    low = norm_back(grad * vectors[4:5, :], unit, spread).astype(BF16)
    grad_branch[...] = low
    lows[at] = low
    me = core[0]
    parts[me] = dot_nt(low, own[...])
    parts[1 - me] = dot_nt(low, other[...])
    grad_scaled = join_parity(parts[0], parts[1])
    grad_mixed[...] = (grad_scaled * scales[0:1, :]).astype(BF16)
    sums[0:1, :] += jnp.sum(grad * unit, axis=0, keepdims=True)
    sums[1:2, :] += jnp.sum(grad, axis=0, keepdims=True)
    sums[2:3, :] += jnp.sum(low.astype(F32), axis=0, keepdims=True)
    sums[3:4, :] += jnp.sum(grad_scaled * mixed[...], axis=0, keepdims=True)

    @pl.when(at == pl.num_programs(0) - 1)
    def _():
        right = lows[...].reshape(scaled.shape)
        turn_rows(scaled, turned, 1 - me)
        sent[...] = dot_nn(turned[...], right).astype(BF16)
        turn_rows(scaled, turned, me)
        staying[...] = dot_nn(turned[...], right)


def branch_back(core, grad_attended, branch, weights, mixed, scales, vectors, scaled, *wait):
    rows, width = branch.shape
    block = rows // 4
    by_row = pl.BlockSpec((block, width), lambda at, *_: (at, 0))
    fourth = pl.BlockSpec((width // 2, width), lambda at, *_: (0, 1))
    return call(
        branch_back_body,
        (rows // block,),
        [
            by_row,
            by_row,
            fourth,
            fourth,
            by_row,
            whole(scales.shape),
            whole(vectors.shape),
            whole(scaled.shape),
            *after(*wait),
        ],
        [by_row, by_row, whole((8, width)), whole((width // 2, width)), whole((width // 2, width))],
        [
            jax.ShapeDtypeStruct((rows, width), BF16),
            jax.ShapeDtypeStruct((rows, width), BF16),
            jax.ShapeDtypeStruct((8, width), F32),
            jax.ShapeDtypeStruct((width // 2, width), BF16),
            jax.ShapeDtypeStruct((width // 2, width), F32),
        ],
        scratch=[
            pltpu.VMEM((2, block, width // 2), F32),
            pltpu.VMEM((rows // block, block, width), BF16),
            pltpu.VMEM((width // 2, rows), BF16),
        ],
        flops=4 * rows * width * width,
        bytes_accessed=2 * width * width + 16 * rows * width,
        scalars=1,
    )(core, grad_attended, branch, *weights[2:], mixed, scales, vectors, scaled, *wait)


def send_part(values, step, firsts, first, second):
    @pl.when(step < firsts)
    def _():
        first[...] = values.astype(BF16)

    @pl.when(step >= firsts)
    def _():
        second[...] = by_owner(values, second.shape[0]).astype(BF16)


def part_specs(half, plane, start, firsts):
    return [
        pl.BlockSpec((half, 1024), lambda at, *_: (0, jnp.clip(at - start, 0, firsts - 1))),
        pl.BlockSpec(
            (plane, half // plane, 1024),
            lambda at, *_: (0, 0, jnp.clip(at - start - firsts, 0, 3 - firsts)),
        ),
    ]


def part_shapes(half, plane, firsts):
    return [
        jax.ShapeDtypeStruct((half, firsts * 1024), BF16),
        jax.ShapeDtypeStruct((plane, half // plane, (4 - firsts) * 1024), BF16),
    ]


def forward_ffn_body(
    steps,
    normed,
    attended,
    vectors,
    rows_of,
    weights,
    upstream,
    output,
    kept,
    slope,
    stats,
    sent,
    held,
    total,
    sums,
    turned,
):
    at = pl.program_id(0)
    width = held.shape[2]

    @pl.when(at == 0)
    def _():
        sums[...] = jnp.zeros_like(sums)

    @pl.when(at < steps)
    def _():
        hidden = dot_nn(normed[...], weights[...]) + rows_of[0:1, :]
        cdf = 0.5 + 0.5 * lax.erf(hidden * math.sqrt(0.5))
        value = hidden * cdf
        slope[...] = (
            cdf + hidden * (jnp.exp(-0.5 * hidden * hidden) * (1.0 / math.sqrt(2.0 * math.pi)))
        ).astype(BF16)
        held[at] = value
        kept[...] = value.astype(BF16)
        sums[...] += lane_sum(value)
        share = attended.shape[1]
        start = pl.multiple_of(at * share, share)
        total[:, pl.ds(start, share)] = attended[...] + vectors[21:22, pl.ds(start, share)]
        for block in range(0, share, TILE):
            turned[pl.ds(start + block, TILE), :] = jnp.transpose(
                upstream[:, block : block + TILE]
            )

    @pl.when(at == steps)
    def _():
        count = steps * width
        mean = jnp.sum(sums[...], axis=1, keepdims=True) * (1.0 / count)
        square = jnp.zeros(sums.shape, F32)
        for block in range(steps):
            centered = held[block] - mean
            square = square + lane_sum(centered * centered)
        spread = lax.rsqrt(jnp.sum(square, axis=1, keepdims=True) * (1.0 / count) + EPS)
        stats[:, :TILE] = jnp.broadcast_to(mean, sums.shape)
        stats[:, TILE:] = jnp.broadcast_to(spread, sums.shape)

    @pl.when(at >= steps)
    def _():
        mean = stats[:, 0:1]
        spread = stats[:, TILE : TILE + 1]
        value = held[at - steps]
        low = ((value - mean) * spread * rows_of[1:2, :] + rows_of[2:3, :]).astype(BF16)
        total[...] += dot_nt(low, weights[...])
        sent[...] = dot_nn(turned[...], low).astype(BF16)

    @pl.when(at == 2 * steps - 1)
    def _():
        output[...] = total[...].astype(BF16)


def forward_ffn(normed, attended, vectors, wide_rows, both, upstream):
    rows, width = attended.shape
    hidden = both.shape[1] // 2
    block = 1024
    steps = hidden // block
    early = lambda at, *_: (0, jnp.minimum(at, steps - 1))
    return call(
        functools.partial(forward_ffn_body, steps),
        (2 * steps,),
        [
            whole((rows, width)),
            pl.BlockSpec((rows, width // steps), early),
            whole(vectors.shape),
            pl.BlockSpec((8, block), lambda at, *_: (0, lax.rem(at, steps))),
            pl.BlockSpec((width, block), lambda at, *_: (0, at)),
            pl.BlockSpec((rows, width // steps), early),
        ],
        [
            whole((rows, width)),
            pl.BlockSpec((rows, block), early),
            pl.BlockSpec((rows, block), early),
            whole((rows, 2 * TILE)),
            pl.BlockSpec((width, block), lambda at, *_: (0, jnp.maximum(at - steps, 0))),
        ],
        [
            jax.ShapeDtypeStruct((rows, width), BF16),
            jax.ShapeDtypeStruct((rows, hidden), BF16),
            jax.ShapeDtypeStruct((rows, hidden), BF16),
            jax.ShapeDtypeStruct((rows, 2 * TILE), F32),
            jax.ShapeDtypeStruct((width, hidden), BF16),
        ],
        scratch=[
            pltpu.VMEM((steps, rows, block), F32),
            pltpu.VMEM((rows, width), F32),
            pltpu.VMEM((rows, TILE), F32),
            pltpu.VMEM((width, rows), BF16),
        ],
        flops=6 * rows * width * hidden,
        bytes_accessed=4 * width * hidden + 6 * rows * hidden,
    )(normed, attended, vectors, wide_rows, both, upstream)


def backward_ffn_body(
    steps,
    core,
    upstream,
    attended,
    vectors,
    rows_of,
    stats,
    kept,
    slope,
    weights,
    normed,
    _,
    grad_attended,
    grad_hidden,
    wide_sums,
    sums,
    sent_first,
    sent_second,
    held,
    total,
    first,
    second,
    turned,
    saved,
    units,
):
    at = pl.program_id(0)
    count = steps * held.shape[2]
    mean = stats[:, 0:1]
    spread = stats[:, TILE : TILE + 1]

    @pl.when(at == 0)
    def _():
        first[...] = jnp.zeros_like(first)
        second[...] = jnp.zeros_like(second)
        total[...] = jnp.zeros_like(total)
        wide_sums[...] = jnp.zeros_like(wide_sums)

    @pl.when(at < steps)
    def _():
        grad = dot_nn(upstream[...], weights[...])
        unit = (kept[...].astype(F32) - mean) * spread
        units[at] = unit.astype(BF16)
        both = grad * unit
        share = attended.shape[1]
        saved[:, pl.ds(pl.multiple_of(at * share, share), share)] = attended[...]
        lane = pl.multiple_of((1 - core[0]) * TILE, TILE)
        turned[pl.ds(pl.multiple_of(at * TILE, TILE), TILE), :] = jnp.transpose(
            normed[:, pl.ds(lane, TILE)]
        )
        wide_sums[at, 0:1, :] = jnp.sum(both, axis=0, keepdims=True)
        wide_sums[at, 1:2, :] = jnp.sum(grad, axis=0, keepdims=True)
        gain = rows_of[1:2, :]
        held[at] = grad * gain
        first[...] += lane_sum(grad * gain)
        second[...] += lane_sum(both * gain)

    @pl.when(at == steps)
    def _():
        scale = 1.0 / count
        first[...] = jnp.broadcast_to(
            jnp.sum(first[...], axis=1, keepdims=True) * scale, first.shape
        )
        second[...] = jnp.broadcast_to(
            jnp.sum(second[...], axis=1, keepdims=True) * scale, second.shape
        )

    @pl.when(at >= steps)
    def _():
        unit = units[at - steps].astype(F32)
        grad = spread * (held[at - steps] - first[:, 0:1] - unit * second[:, 0:1])
        low = (grad * slope[...].astype(F32)).astype(BF16)
        grad_hidden[...] = low
        wide_sums[at - steps, 2:3, :] = jnp.sum(low.astype(F32), axis=0, keepdims=True)
        total[...] += dot_nt(low, weights[...])
        send_part(dot_nn(turned[...], low), at - steps, UP_FIRSTS, sent_first, sent_second)

    @pl.when(at == 2 * steps - 1)
    def _():
        grad = total[...]
        centered, mid_spread = row_stats(saved[...])
        unit = centered * mid_spread
        top = upstream[...].astype(F32)
        grad_attended[...] = top + norm_back(grad * vectors[7:8, :], unit, mid_spread)
        sums[0:1, :] = jnp.sum(grad * unit, axis=0, keepdims=True)
        sums[1:2, :] = jnp.sum(grad, axis=0, keepdims=True)
        sums[2:3, :] = jnp.sum(top, axis=0, keepdims=True)
        sums[3:8, :] = jnp.zeros((5, sums.shape[1]), F32)


def backward_ffn(
    core, plane, upstream, attended, vectors, wide_rows, stats, kept, slope, both, normed, wait
):
    rows, width = attended.shape
    hidden = both.shape[1] // 2
    block = 1024
    steps = hidden // block
    late = lambda at, *_: (0, jnp.maximum(at - steps, 0))
    early = lambda at, *_: (0, jnp.minimum(at, steps - 1))
    turn = lambda at, *_: (0, lax.rem(at, steps))
    return call(
        functools.partial(backward_ffn_body, steps),
        (2 * steps,),
        [
            whole((rows, width)),
            pl.BlockSpec((rows, width // steps), early),
            whole(vectors.shape),
            pl.BlockSpec((8, block), turn),
            whole((rows, 2 * TILE)),
            pl.BlockSpec((rows, block), early),
            pl.BlockSpec((rows, block), late),
            pl.BlockSpec((width, block), lambda at, *_: (0, lax.rem(at + steps, 2 * steps))),
            pl.BlockSpec((rows, width // steps), early),
            *after(wait),
        ],
        [
            whole((rows, width)),
            pl.BlockSpec((rows, block), late),
            whole((steps, 8, block)),
            whole((8, width)),
            *part_specs(width // 2, plane, steps, UP_FIRSTS),
        ],
        [
            jax.ShapeDtypeStruct((rows, width), F32),
            jax.ShapeDtypeStruct((rows, hidden), BF16),
            jax.ShapeDtypeStruct((steps, 8, block), F32),
            jax.ShapeDtypeStruct((8, width), F32),
            *part_shapes(width // 2, plane, UP_FIRSTS),
        ],
        scratch=[
            pltpu.VMEM((steps, rows, block), F32),
            pltpu.VMEM((rows, width), F32),
            pltpu.VMEM((rows, TILE), F32),
            pltpu.VMEM((rows, TILE), F32),
            pltpu.VMEM((width // 2, rows), BF16),
            pltpu.VMEM((rows, width), F32),
            pltpu.VMEM((steps, rows, block), BF16),
        ],
        flops=5 * rows * width * hidden,
        bytes_accessed=4 * width * hidden + 8 * rows * hidden,
        scalars=1,
    )(core, upstream, attended, vectors, wide_rows, stats, kept, slope, both, normed, wait)


def input_back_body(
    core,
    grads,
    own_qk,
    other_qk,
    own_vo,
    other_vo,
    tokens,
    grad_attended,
    vectors,
    branch_sums,
    mid_sums,
    wide_sums,
    _,
    input_grad,
    turned,
    parts,
    sums,
):
    part = pl.program_id(0)
    me = core[0]
    grad_part = grads[...]

    @pl.when(part == 0)
    def _():
        parts[me] = dot_nt(grad_part, own_qk[...])
        parts[1 - me] = dot_nt(grad_part, other_qk[...])
        sums[...] = jnp.zeros_like(sums)
        sums[2:3, :] = jnp.sum(grad_part.astype(F32), axis=0, keepdims=True)

    @pl.when(part == 1)
    def _():
        parts[me] += dot_nt(grad_part, own_qk[...])
        parts[1 - me] += dot_nt(grad_part, other_qk[...])

    @pl.when(part == 2)
    def _():
        parts[me] += dot_nt(grad_part, own_vo[...])
        parts[1 - me] += dot_nt(grad_part, other_vo[...])
        grad = join_parity(parts[0], parts[1])
        centered, spread = row_stats(tokens[...].astype(F32))
        unit = centered * spread
        input_grad[...] = grad_attended[...] + norm_back(grad * vectors[0:1, :], unit, spread)
        sums[0:1, :] = jnp.sum(grad * unit, axis=0, keepdims=True)
        sums[1:2, :] = jnp.sum(grad, axis=0, keepdims=True)
        sums[3:4, :] = jnp.sum(grad_part.astype(F32), axis=0, keepdims=True)
        sums[4:7, :] = branch_sums[0:3, :]
        sums[7:9, :] = mid_sums[0:2, :]
        for row in range(wide_sums.shape[0]):
            sums[9 + row : 10 + row, :] = wide_sums[row, 2:3, :]
            sums[13 + row : 14 + row, :] = wide_sums[row, 0:1, :]
            sums[17 + row : 18 + row, :] = wide_sums[row, 1:2, :]
        sums[21:22, :] = mid_sums[2:3, :]
        width = sums.shape[1]
        head_dim = TILE // 2
        picks = (
            lax.broadcasted_iota(jnp.int32, (width, TILE), 0) // head_dim + HEAD_AT
            == lax.broadcasted_iota(jnp.int32, (width, TILE), 1)
        ).astype(F32)
        heads = lax.dot_general(
            branch_sums[...],
            picks,
            (((1,), (0,)), ((), ())),
            precision=HIGHEST,
            preferred_element_type=F32,
        )[3:4, :]
        for block in range(turned.shape[0]):
            turned[block] = (
                jnp.transpose(sums[:, block * TILE : (block + 1) * TILE]) + heads
            )


def input_back(core, grads, weights, tokens, grad_attended, vectors, sums, wait):
    rows, width = tokens.shape
    full = whole((rows, width))
    third = pl.BlockSpec((width // 2, width), lambda part, *_: (0, jnp.minimum(part, 1)))
    last = pl.BlockSpec((width // 2, width), lambda part, *_: (0, 0))
    return call(
        input_back_body,
        (3,),
        [
            pl.BlockSpec((None, rows, width), lambda part, *_: (part, 0, 0)),
            third,
            third,
            last,
            last,
            full,
            full,
            whole(vectors.shape),
            *[whole(item.shape) for item in sums],
            *after(wait),
        ],
        [full, whole((width // TILE, TILE, TILE))],
        [
            jax.ShapeDtypeStruct((rows, width), F32),
            jax.ShapeDtypeStruct((width // TILE, TILE, TILE), F32),
        ],
        scratch=[pltpu.VMEM((2, rows, width // 2), F32), pltpu.VMEM((TILE, width), F32)],
        flops=6 * rows * width * width,
        bytes_accessed=6 * width * width + 16 * rows * width,
        scalars=1,
    )(core, grads, *weights, tokens, grad_attended, vectors, *sums, wait)


def outer_body(firsts, more, core, left, right, add_first, add_second, *refs):
    first, second, turned = refs[-3:]
    at = pl.program_id(0)

    @pl.when(at == 0)
    def _():
        turn_rows(left, turned, core[0])

    value = dot_nn(turned[...], right[...])

    @pl.when(at < firsts)
    def _():
        first[...] = (value + add_first[...].astype(F32)).astype(BF16)

    if more:

        @pl.when(at == firsts)
        def _():
            first[...] = (refs[0][...] + refs[1][...].astype(F32)).astype(BF16)

    @pl.when(at >= firsts)
    def _():
        second[...] = (
            by_owner(value, second.shape[0]) + add_second[...].astype(F32)
        ).astype(BF16)


def outer(core, left, right, add, wait=(), more=()):
    rows, width = left.shape
    half = width // 2
    block = 1024
    add_first, add_second = add
    plane, owned = add_second.shape[:2]
    firsts = UP_FIRSTS
    seconds = add_second.shape[2] // block
    right_spec = pl.BlockSpec((rows, block), lambda at, *_: (0, at))
    add_spec = pl.BlockSpec((half, block), lambda at, *_: (0, jnp.clip(at, 0, firsts - 1)))
    second_spec = pl.BlockSpec(
        (plane, owned, block), lambda at, *_: (0, 0, jnp.clip(at - firsts, 0, seconds - 1))
    )
    kinds = firsts + len(more) // 2
    out_specs = [
        pl.BlockSpec((half, block), lambda at, *_: (0, jnp.clip(at, 0, kinds - 1))),
        second_spec,
    ]
    out_shape = [
        jax.ShapeDtypeStruct((half, kinds * block), BF16),
        jax.ShapeDtypeStruct(add_second.shape, BF16),
    ]
    return call(
        functools.partial(outer_body, firsts, len(more) > 0),
        (firsts + seconds,),
        [
            whole((rows, width)),
            right_spec,
            add_spec,
            second_spec,
            *[whole(item.shape) for item in more],
            *after(*wait),
        ],
        out_specs,
        out_shape,
        scratch=[pltpu.VMEM((half, rows), BF16)],
        flops=2 * rows * half * block * (firsts + seconds),
        bytes_accessed=6 * half * block * (firsts + seconds),
        scalars=1,
    )(core, left, right, add_first, add_second, *more, *wait)


def to_slots_body(perm, early, late, rest, small, *refs):
    grad_qkv, grad_out, grad_up, grad_down, slots, tiles = refs
    width = grad_out.shape[1]
    half = 2 * width
    grad_out[...] = early[:, half : half + width]
    for pair in range(width // TILE):
        for which in range(3):
            at = (3 * pair + which) * TILE
            to = which * width + pair * TILE
            grad_qkv[:, to : to + TILE] = late[:, at : at + TILE]
    grad_down[...] = early[:, half + width :]
    grad_up[:, :half] = early[:, :half]
    grad_up[:, half:] = rest[...]
    column = 0
    for result in (grad_qkv, grad_out, grad_up, grad_down):
        for at in range(0, result.shape[1], TILE):
            tiles[column] = result[:, at : at + TILE]
            column += 1
    planes, pairs = slots.shape[0], slots.shape[1] - 1
    for slot in range(planes * pairs):
        pair = [tiles[perm[2 * slot + which]] for which in range(2)]
        slots[slot // pairs, slot % pairs] = jnp.concatenate(pair, axis=0).astype(BF16)
    rounded = small[...].astype(BF16).astype(F32)
    slots[:, pairs] = jnp.concatenate([rounded, small[...] - rounded], axis=1).astype(BF16)


def to_slots(perm, early, late, rest, small, plane, widths):
    arrays = [early, late, rest, small]
    pairs = perm.shape[0] // (2 * plane)
    shapes = [jax.ShapeDtypeStruct((8, columns), F32) for columns in widths]
    shapes.append(jax.ShapeDtypeStruct((plane, pairs + 1, 16, TILE), BF16))
    return call(
        to_slots_body,
        (1,),
        [whole(item.shape) for item in arrays],
        [whole(item.shape) for item in shapes],
        shapes,
        scratch=[pltpu.VMEM((perm.shape[0], 8, TILE), F32)],
        bytes_accessed=8 * 8 * sum(widths),
        scalars=1,
    )(perm, *arrays)


def update_body(grads, left_stats, right_stats, left_roots, right_roots, left_new, right_new, back):
    planes, pairs = back.shape[:2]
    for pair in range(pairs):
        block = grads[:, pair].astype(F32)
        moved = []
        for which in range(2):
            slot = 2 * pair + which
            grad = block[:, which * 8 : which * 8 + 8, :].reshape(TILE, TILE)
            low = grad.astype(BF16)
            left_new[slot] = DECAY * left_stats[slot] + (1.0 - DECAY) * dot_nt(low, low)
            right_new[slot] = DECAY * right_stats[slot] + (1.0 - DECAY) * dot_tn(low, low)
            step = jnp.dot(grad, right_roots[slot], precision=HIGHEST, preferred_element_type=F32)
            step = jnp.dot(left_roots[slot], step, precision=HIGHEST, preferred_element_type=F32)
            moved.append(step.reshape(planes, 8, TILE))
        back[:, pair] = jnp.concatenate(moved, axis=1).astype(BF16)


def update(grads, left_stats, right_stats, left_roots, right_roots):
    arrays = [item[0] for item in (left_stats, right_stats, left_roots, right_roots)]
    stats = jax.ShapeDtypeStruct(arrays[0].shape, F32)
    moved = (grads.shape[0], arrays[0].shape[0] // 2, 16, TILE)
    left_new, right_new, back = call(
        update_body,
        (1,),
        [whole(grads.shape)] + [whole(item.shape) for item in arrays],
        [whole(stats.shape), whole(stats.shape), whole(moved)],
        [stats, stats, jax.ShapeDtypeStruct(moved, BF16)],
        bytes_accessed=24 * arrays[0].size,
    )(grads, *arrays)
    return left_new[None], right_new[None], back


def apply_body(perm, moved, *refs):
    olds, news, tiles = refs[:4], refs[4:8], refs[8]
    pairs = moved.shape[1]
    for slot in range(moved.shape[0] * pairs):
        value = moved[slot // pairs, slot % pairs].astype(F32)
        tiles[perm[2 * slot]] = value[:8]
        tiles[perm[2 * slot + 1]] = value[8:]
    column = 0
    for old, new in zip(olds, news):
        for at in range(0, old.shape[1], TILE):
            cut = slice(at, at + TILE)
            new[:, cut] = old[:, cut] - RATE_MATRIX * tiles[column]
            column += 1


def apply_steps(perm, moved, weights):
    shapes = [jax.ShapeDtypeStruct(item.shape, F32) for item in weights]
    return call(
        apply_body,
        (1,),
        [whole(moved.shape)] + [whole(item.shape) for item in weights],
        [whole(item.shape) for item in shapes],
        shapes,
        scratch=[pltpu.VMEM((perm.shape[0], 8, TILE), F32)],
        bytes_accessed=10 * 8 * TILE * perm.shape[0],
        scalars=1,
    )(perm, moved, *weights)


def swap_cores(values):
    return lax.ppermute(values, "core", [(0, 1), (1, 0)])


def take_core(values, core):
    return lax.dynamic_slice_in_dim(values, core, 1, 1, allow_negative_indices=False)[:, 0]


def turn_chips(values, step):
    count = lax.axis_size("x")
    return lax.ppermute(values, "x", [(at, (at + step) % count) for at in range(count)])


def sum_parts(parts):
    return jnp.sum(parts.astype(F32), axis=0)


def shards(
    tokens,
    cotangent,
    lengths,
    valid,
    owner_perm,
    w_qkv,
    w_out,
    w_up,
    w_down,
    vectors,
    head_scale,
    left_stats,
    right_stats,
    left_roots,
    right_roots,
    vector_stats,
    head_stats,
):
    rows, width = tokens.shape
    heads = head_scale.shape[0]
    hidden = w_up.shape[1]
    ratio = hidden // width
    shard = w_up.shape[0]
    plane = lax.axis_size("fsdp")
    chips = lax.axis_size("x")
    core = lax.axis_index("core")
    core_arg = core.astype(jnp.int32).reshape(1)

    both = lax.all_gather(
        jnp.concatenate([w_up.astype(BF16), w_down.astype(BF16)], axis=1),
        ("x", "core", "fsdp"),
        axis=0,
        tiled=True,
    )
    low_qk = jnp.concatenate(
        [
            w_qkv[:, : 2 * width].astype(BF16),
            jnp.pad(vectors.astype(BF16).T, ((0, 0), (0, TILE - vectors.shape[0]))),
        ],
        axis=1,
    )
    low_vo = jnp.concatenate([w_qkv[:, 2 * width :].astype(BF16), w_out.astype(BF16)], axis=1)

    def to_plane(part, concat):
        spread = jnp.broadcast_to(part[None], (plane,) + part.shape)
        return lax.all_to_all(spread, "fsdp", split_axis=0, concat_axis=concat, tiled=True)

    place = lax.axis_index("x")

    def roll_chips(parts, start):
        twice = jnp.concatenate([parts, parts], axis=0)
        begin = [start] + [0] * (parts.ndim - 1)
        return lax.dynamic_slice(twice, begin, parts.shape, allow_negative_indices=False)

    def in_order(parts):
        return roll_chips(jnp.stack(parts[::-1]), chips - 1 - place)

    def to_chips(part):
        return in_order([part] + [turn_chips(part, step) for step in range(1, chips)])

    def across_chips(parts):
        ahead = roll_chips(parts, place)
        return [ahead[0]] + [turn_chips(ahead[step], step) for step in range(1, chips)]

    own_vo = to_plane(to_chips(low_vo), 2).reshape(width // 2, -1)
    own_qk = to_chips(to_plane(low_qk, 0).reshape(plane * shard, -1)).reshape(width // 2, -1)
    other_qk, other_vo = swap_cores(own_qk), swap_cores(own_vo)
    weights = (own_qk, other_qk, own_vo, other_vo)
    vector_at = 2 * width
    vector_pair = jnp.stack([own_qk[:, vector_at:], other_qk[:, vector_at:]])
    vector_pair = jnp.where(core == 0, vector_pair, vector_pair[::-1])
    vector_rows = (
        vector_pair.reshape(2, -1, TILE, TILE)
        .transpose(1, 0, 2, 3)
        .reshape(width, TILE)
        .T[:24]
        .astype(F32)
    )
    wide_rows = jnp.concatenate(
        [
            vector_rows[9 : 9 + 3 * ratio].reshape(3, hidden),
            jnp.zeros((5, hidden), F32),
        ],
        axis=0,
    )
    upstream = jnp.where(valid[:, None] != 0, cotangent, jnp.zeros_like(cotangent))
    scales = jnp.broadcast_to(jnp.repeat(head_scale, width // heads)[None], (8, width))

    normed, projected = project(core_arg, tokens, vector_rows, weights)
    mixed, scaled, attention = attend(lengths, head_scale, projected)
    branch, attended, normed_mid = branch_out(core_arg, scaled, weights, tokens, vector_rows)
    output, kept, slope, stats, down_local = forward_ffn(
        normed_mid, attended, vector_rows, wide_rows, both, upstream
    )

    def over_x(part):
        return lax.psum_scatter(part, "x", scatter_dimension=0, tiled=True)

    def over_plane(part):
        return sum_parts(
            lax.all_to_all(
                part.reshape(plane, shard, -1), "fsdp", split_axis=0, concat_axis=0, tiled=True
            )
        )

    def plane_first(part):
        total = lax.all_to_all(part, "fsdp", split_axis=0, concat_axis=0, tiled=True)
        return sum_parts(total)

    down_chips = lax.psum_scatter(down_local, ("x", "core"), scatter_dimension=0, tiled=True)
    grad_attended, grad_hidden, wide_sums, mid_sums, *sent_up = backward_ffn(
        core_arg,
        plane,
        upstream,
        attended,
        vector_rows,
        wide_rows,
        stats,
        kept,
        slope,
        both,
        normed_mid,
        down_local,
    )
    grad_branch, grad_mixed, branch_sums, out_sent, out_stays = branch_back(
        core_arg,
        grad_attended,
        branch,
        weights,
        mixed,
        scales,
        vector_rows,
        scaled,
    )
    up_first, up_second = outer(
        core_arg,
        normed_mid,
        grad_hidden,
        [swap_cores(part) for part in sent_up],
        wait=(grad_branch,),
        more=(out_stays, swap_cores(out_sent)),
    )
    up_rest = plane_first(up_second)
    up_chips = over_x(up_first)
    grads, attn_local = attend_back(
        projected,
        mixed,
        grad_mixed,
        attention,
        normed,
        (up_second, down_chips),
    )
    input_grad, turned = input_back(
        core_arg,
        grads,
        weights,
        tokens,
        grad_attended,
        vector_rows,
        (branch_sums, mid_sums, wide_sums),
        up_rest,
    )

    turned = turned.reshape(chips, 2, TILE, TILE)
    half_sums = take_core(turned, core) + swap_cores(take_core(turned, 1 - core))
    attn_chips = lax.psum_scatter(attn_local, ("x", "core"), scatter_dimension=0, tiled=True)

    early_parts = over_plane(jnp.concatenate([up_chips, down_chips], axis=1))
    half_sums, up_rest, early_parts = lax.optimization_barrier((half_sums, up_rest, early_parts))
    small = jnp.sum(in_order(across_chips(half_sums)), axis=0)
    rest = up_rest.reshape(chips, shard, -1)
    rest = across_chips(rest.astype(BF16))
    rest = sum(part.astype(F32) for part in rest)
    late_parts = over_plane(attn_chips)

    masters = (w_qkv, w_out, w_up, w_down)
    grad_qkv, grad_out, grad_up, grad_down, slots = to_slots(
        owner_perm,
        early_parts,
        late_parts,
        rest,
        small.reshape(plane, shard, TILE),
        plane,
        [item.shape[1] for item in masters],
    )
    slots = lax.all_to_all(slots, "fsdp", split_axis=0, concat_axis=0, tiled=True)
    small = sum_parts(slots[:, -1])
    small = small[:shard] + small[shard:]
    vector_grads = small.T[: vectors.shape[0]]
    head_total = small[0, HEAD_AT : HEAD_AT + heads]
    left_new, right_new, back = update(slots, left_stats, right_stats, left_roots, right_roots)
    back = lax.all_to_all(back, "fsdp", split_axis=0, concat_axis=0, tiled=True)
    new_qkv, new_out, new_up, new_down = apply_steps(owner_perm, back, masters)
    vector_stats_new = DECAY * vector_stats + (1.0 - DECAY) * vector_grads * vector_grads
    vectors_new = vectors - RATE_VECTOR * vector_grads * lax.rsqrt(vector_stats_new)
    head_stats_new = DECAY * head_stats + (1.0 - DECAY) * head_total * head_total
    head_new = head_scale - RATE_VECTOR * head_total * lax.rsqrt(head_stats_new)
    return (
        output,
        input_grad,
        grad_qkv,
        grad_out,
        grad_up,
        grad_down,
        vector_grads,
        head_total,
        left_new,
        right_new,
        new_qkv,
        new_out,
        new_up,
        new_down,
        vector_stats_new,
        vectors_new,
        head_stats_new,
        head_new,
    )


def solution(mesh):
    everywhere = ("x", "core", "fsdp")
    by_rows = P(everywhere, None)
    by_columns = P(None, everywhere)
    by_block = P(("x", "core"), "fsdp", None, None)
    dp, fsdp = mesh.devices.shape
    mesh = jax.sharding.Mesh(mesh.devices.reshape(dp // 2, 2, fsdp), everywhere)
    return jax.shard_map(
        shards,
        mesh=mesh,
        in_specs=(
            (by_rows, by_rows, P(everywhere), P(everywhere), P())
            + (by_rows,) * 4
            + (by_columns, P())
            + (by_block,) * 4
            + (by_columns, P())
        ),
        out_specs=(
            (by_rows,) * 6
            + (by_columns, P())
            + (by_block,) * 2
            + (by_rows,) * 4
            + (by_columns, by_columns, P(), P())
        ),
        check_vma=False,
    )
```
